32 devices in a mesh: dp: 8 (over y, x, core), mp: 4 (over z).
Axes of the slice: x: 2, y: 2, z: 4, core: 2. Of those that a mesh axis runs over, the one named last changes fastest.
Arguments:
- byte_input: bfloat16 [4, 128, 8192], P(None, 'dp'), may hold values from -6 to 6
- seq_lengths: int32 [4, 3], replicated, may hold values from 9 to 80, as said below
- patch_weight: bfloat16 [8, 1024, 1024], P('mp'), may hold values from -0.0625 to 0.0625
- norm_in_gain: float32 [1024], replicated, may hold values from 0.5 to 1.5
- in_weight: bfloat16 [4, 1024, 1288], P('mp'), may hold values from -0.1875 to 0.1875
- conv_weight: float32 [4, 768, 4], P('mp'), may hold values from -3 to 3
- conv_bias: float32 [4, 768], P('mp'), may hold values from -3 to 3
- step_bias: float32 [4, 8], P('mp'), may hold values from -3 to 0.5
- log_decay: float32 [4, 8], P('mp'), may hold values from -4.5 to 0
- skip_gain: float32 [4, 8], P('mp'), may hold values from 0.5 to 1.5
- group_gain: float32 [4, 512], P('mp'), may hold values from 0.5 to 1.5
- out_weight: bfloat16 [4, 512, 1024], P('mp'), may hold values from -0.125 to 0.125
- attn_gain: float32 [1024], replicated, may hold values from 0.5 to 1.5
- qkv_weight: bfloat16 [3, 1024, 1024], P(None, None, 'mp'), may hold values from -0.1875 to 0.1875
- attn_out_weight: bfloat16 [1024, 1024], P('mp'), may hold values from -0.375 to 0.375
- ffn_gain: float32 [1024], replicated, may hold values from 0.5 to 1.5
- ffn_weight: bfloat16 [3, 1024, 4096], P(None, 'mp', 'dp'), may hold values from -0.1875 to 0.1875
- out_grad: bfloat16 [4, 1024, 1024], P(None, 'dp'), may hold values from -6 to 6
Outputs:
- block_out: bfloat16 [4, 1024, 1024], P(None, 'dp', 'mp')
- input_grad: float32 [4, 128, 8192], P(None, 'dp', 'mp')
- grad_patch_weight: float32 [8, 1024, 1024], P('mp', 'dp')
- grad_norm_in_gain: float32 [1024], P('dp')
- grad_in_weight: float32 [4, 1024, 1288], P('mp', 'dp')
- grad_conv_weight: float32 [4, 768, 4], P('mp', 'dp')
- grad_conv_bias: float32 [4, 768], P('mp', 'dp')
- grad_step_bias: float32 [4, 8], P('mp')
- grad_log_decay: float32 [4, 8], P('mp')
- grad_skip_gain: float32 [4, 8], P('mp')
- grad_group_gain: float32 [4, 512], P('mp', 'dp')
- grad_out_weight: float32 [4, 512, 1024], P('mp', 'dp')
- grad_attn_gain: float32 [1024], P('dp')
- grad_qkv_weight: float32 [3, 1024, 1024], P(None, 'dp', 'mp')
- grad_attn_out_weight: float32 [1024, 1024], P('mp', 'dp')
- grad_ffn_gain: float32 [1024], P('dp')
- grad_ffn_weight: float32 [3, 1024, 4096], P(None, 'mp', 'dp')
The draws below stay inside these ranges and needn't reach their ends.
Inputs may be any that keep to these rules, and one draw needn't show every extreme that they name: `seq_lengths`: lengths count patches of 8 bytes; every length is at least 1. In each micro-batch the three sequences lie end to end from patch 0 in this order and are followed by 1 to 8 patches of padding; the first holds more than half of the 128 patches, the third 16 to 31. In some micro-batch the first holds exactly the maximum.
All inputs are finite; a program needn't handle non-finite values.
Results may differ from the reference program's by a relative error of at most 0.02.
Values may be sent and summed in bfloat16 or wider, within the bound.
A program may use at most 256 MiB of HBM per device.

```python
import jax
import jax.numpy as jnp
from jax import lax

D = 1024
DIN = 2048
STATE = 128
ATT_HEADS = 16
FF = 4096
PATCH = 8
CONV = 4
GROUPS = 4
SEQS = 3
MICRO = 4
PATCH_DEV = 16
MB_PATCHES = 128
MB_BYTES = 1024
GROUP_WIDTH = 512
GROUP_HEADS = 8
HEAD_DIM = 64
ATT_DIM = 64
CONV_CH = 768
IN_COLS = 1288


def draw_seq_lengths(key, part):
    key = jax.random.fold_in(key, 7)
    sub_keys = jax.random.split(key, 4)
    padding = jax.random.randint(sub_keys[0], (MICRO,), 1, PATCH_DEV // 2 + 1)
    shortest = jax.random.randint(sub_keys[1], (MICRO,), PATCH_DEV, 2 * PATCH_DEV)
    upper_len = MB_PATCHES // 2 + PATCH_DEV
    longest = jax.random.randint(sub_keys[2], (MICRO,), MB_PATCHES // 2 + 1, upper_len + 1)
    chosen = jax.random.randint(sub_keys[3], (), 0, MICRO)
    longest = jnp.where(jnp.arange(MICRO) == chosen, upper_len, longest)
    middle = MB_PATCHES - padding - shortest - longest
    return jnp.stack([longest, middle, shortest], axis=1).astype(jnp.int32)


def level_of(own_key, dims, cuts, least, high):
    gain, own = 1.0, jax.random.fold_in(own_key, 6)
    for axis_at, blocks in cuts:
        heights = jnp.exp(jax.random.uniform(jax.random.fold_in(own, axis_at), (blocks,), jnp.float32, least / len(cuts), high / len(cuts)))
        gain = gain * jnp.repeat(heights, dims[axis_at] // blocks).reshape([-1 if axis == axis_at else 1 for axis in range(len(dims))])
    return gain


def normal_values(rng, extent, deviation, most, shards=(), kind=jnp.bfloat16):
    values = deviation * jax.random.normal(rng, extent, jnp.float32)
    if shards:
        values = values * level_of(rng, extent, shards, -0.22, 0.18)
    return jnp.clip(values, -most, most).astype(kind)


def setup_inputs(seed: int = 0) -> dict:
    arg_keys = jax.random.split(jax.random.key(seed), 19)
    return {
        "byte_input": normal_values(arg_keys[0], (MICRO, MB_PATCHES, PATCH * D), 1.0, 6.0, ((1, 8),)),
        "seq_lengths": draw_seq_lengths(jax.random.fold_in(arg_keys[18], 71), 0),
        "patch_weight": normal_values(arg_keys[2], (PATCH, D, D), (PATCH * D) ** -0.5, 0.0625, ((0, 4),)),
        "norm_in_gain": jnp.clip(1.0 + 0.1 * jax.random.normal(arg_keys[3], (D,), jnp.float32), 0.5, 1.5),
        "in_weight": normal_values(arg_keys[4], (GROUPS, D, IN_COLS), D ** -0.5, 0.1875, ((0, 4),)),
        "conv_weight": normal_values(arg_keys[5], (GROUPS, CONV_CH, CONV), CONV ** -0.5, 3.0, ((0, 4),), jnp.float32),
        "conv_bias": normal_values(arg_keys[6], (GROUPS, CONV_CH), 0.5, 3.0, ((0, 4),), jnp.float32),
        "step_bias": jnp.clip(-3.0 + 3.5 * jax.random.uniform(arg_keys[7], (GROUPS, GROUP_HEADS), jnp.float32) ** level_of(arg_keys[7], (GROUPS, GROUP_HEADS), ((0, 4),), -0.2, 0.2), -3.0, 0.5),
        "log_decay": jnp.clip(-4.5 + 4.5 * jax.random.uniform(arg_keys[8], (GROUPS, GROUP_HEADS), jnp.float32) ** level_of(arg_keys[8], (GROUPS, GROUP_HEADS), ((0, 4),), -0.2, 0.2), -4.5, 0.0),
        "skip_gain": jnp.clip(0.5 + 1.0 * jax.random.uniform(arg_keys[9], (GROUPS, GROUP_HEADS), jnp.float32) ** level_of(arg_keys[9], (GROUPS, GROUP_HEADS), ((0, 4),), -0.2, 0.2), 0.5, 1.5),
        "group_gain": jnp.clip(1.0 + 0.1 * jax.random.normal(arg_keys[10], (GROUPS, GROUP_WIDTH), jnp.float32), 0.5, 1.5),
        "out_weight": normal_values(arg_keys[11], (GROUPS, GROUP_WIDTH, D), DIN ** -0.5, 0.125, ((0, 4),)),
        "attn_gain": jnp.clip(1.0 + 0.1 * jax.random.normal(arg_keys[12], (D,), jnp.float32), 0.5, 1.5),
        "qkv_weight": normal_values(arg_keys[13], (3, D, D), D ** -0.5, 0.1875, ((2, 4),)),
        "attn_out_weight": normal_values(arg_keys[14], (D, D), (D // 4) ** -0.5, 0.375, ((0, 4),)),
        "ffn_gain": jnp.clip(1.0 + 0.1 * jax.random.normal(arg_keys[15], (D,), jnp.float32), 0.5, 1.5),
        "ffn_weight": normal_values(arg_keys[16], (3, D, FF), D ** -0.5, 0.1875, ((1, 4), (2, 8))),
        "out_grad": normal_values(arg_keys[17], (MICRO, MB_BYTES, D), 1.0, 6.0, ((1, 8),)),
    }


@jax.custom_vjp
def low(v):
    return lax.optimization_barrier(v.astype(jnp.bfloat16)).astype(jnp.float32)

@jax.custom_vjp
def low_back(v):
    return v

def low_keep(v):
    return (low(v), None)

def low_pass(kept, grad):
    return (grad,)

def back_keep(v):
    return (v, None)

def back_low(kept, grad):
    return (low(grad),)
low.defvjp(low_keep, low_pass)
low_back.defvjp(back_keep, back_low)
norm_eps = 1e-06
highest = lax.Precision.HIGHEST
large_negative = -1e+30

def rms_scale(values, scale_gain):
    return values * lax.rsqrt(lax.optimization_barrier(jnp.mean(values * values, axis=-1, keepdims=True)) + norm_eps) * scale_gain

def segment_ids(seq_lengths, first_patch, patch_count):
    seq_ends = jnp.cumsum(seq_lengths).astype(jnp.int32)
    places = first_patch + jnp.arange(patch_count, dtype=jnp.int32)
    return lax.optimization_barrier(jnp.sum((places[:, None] >= seq_ends[None, :]).astype(jnp.int32), axis=1)).astype(jnp.int32)

def block_terms(values, inputs, outputs, step_sizes, log_decays, segment, previous):
    running = jnp.cumsum(log_decays, axis=0)
    block_len = segment.shape[0]
    ordinal = jnp.arange(block_len)
    same_seg = (segment[:, None] == segment[None, :]) & (ordinal[None, :] <= ordinal[:, None])
    log_gap = running[:, None] - running[None, :]
    pair_mask = same_seg[:, :, None, None]
    decays = jnp.where(pair_mask, jnp.exp(jnp.where(pair_mask, log_gap, 0.0)), 0.0)
    inner_prod = jnp.einsum('tgn,sgn->tsg', outputs, inputs, precision=highest)
    weights = decays * inner_prod[:, :, :, None] * step_sizes[None]
    within = jnp.einsum('tsgh,sghe->tghe', weights, values, precision=highest)
    carry_weight = jnp.exp(running) * (segment == previous).astype(jnp.float32)[:, None, None]
    last_seg = segment[block_len - 1]
    to_end = jnp.exp(running[block_len - 1][None] - running) * (segment == last_seg).astype(jnp.float32)[:, None, None] * step_sizes
    local_state = jnp.einsum('sgh,sghe,sgn->ghen', to_end, values, inputs, precision=highest)
    through = jnp.exp(running[block_len - 1]) * (last_seg == previous).astype(jnp.float32)
    return (within, carry_weight, local_state, through)

def micro_forward(stream_in, seq_lengths, params):
    patch_weight, norm_in_gain, in_weight, conv_weight, conv_bias, step_bias, log_decay, skip_gain, group_gain, out_weight, attn_gain, qkv_weight, attn_out_weight, ffn_gain, ffn_weight = params
    patches = stream_in.shape[0]
    segment = segment_ids(seq_lengths, 0, patches)
    valid = jnp.repeat((segment < SEQS).astype(jnp.float32), PATCH)
    global_in = low_back(jnp.einsum('pkd,kde->pe', stream_in.reshape(patches, PATCH, D), patch_weight, precision=highest))
    normed_in = low(rms_scale(global_in, norm_in_gain))
    projected = low_back(jnp.einsum('pd,gdc->pgc', normed_in, in_weight, precision=highest))
    gate_part = projected[:, :, :GROUP_WIDTH]
    conv_in = projected[:, :, GROUP_WIDTH:GROUP_WIDTH + CONV_CH]
    step_raw = projected[:, :, GROUP_WIDTH + CONV_CH:]
    conv_out = conv_bias[None]
    for lag_index in range(CONV):
        lag_len = CONV - 1 - lag_index
        shifted = jnp.concatenate([jnp.zeros((lag_len, GROUPS, CONV_CH), jnp.float32), conv_in[:patches - lag_len]], axis=0)
        seg_shift = jnp.concatenate([jnp.full((lag_len,), -1, jnp.int32), segment[:patches - lag_len]], axis=0)
        keep_mask = (seg_shift == segment).astype(jnp.float32)[:, None, None]
        conv_out = conv_out + shifted * keep_mask * conv_weight[:, :, lag_index][None]
    activated = jax.nn.silu(conv_out)
    values = activated[:, :, :GROUP_WIDTH].reshape(patches, GROUPS, GROUP_HEADS, HEAD_DIM)
    inputs = activated[:, :, GROUP_WIDTH:GROUP_WIDTH + STATE]
    outputs = activated[:, :, GROUP_WIDTH + STATE:]
    step_sizes = jax.nn.softplus(step_raw + step_bias[None])
    log_decays = -step_sizes * jnp.exp(log_decay)[None]
    blocks = patches // PATCH_DEV

    def blockify(tensor):
        return tensor.reshape((blocks, PATCH_DEV) + tensor.shape[1:])
    starts = jnp.arange(blocks, dtype=jnp.int32) * PATCH_DEV
    previous = jnp.where(starts > 0, segment[jnp.maximum(starts - 1, 0)], -1).astype(jnp.int32)

    def block_step(carry_state, pieces):
        block_values, block_inputs, block_outputs, block_steps, block_decays, block_seg, block_prev = pieces
        within, carry_weight, local_state, through = block_terms(block_values, block_inputs, block_outputs, block_steps, block_decays, block_seg, block_prev)
        carried = carry_weight[..., None] * jnp.einsum('ghen,tgn->tghe', carry_state, block_outputs, precision=highest)
        result = within + carried + skip_gain[None, :, :, None] * block_values
        return (through[:, :, None, None] * carry_state + local_state, result)
    zero_state = jnp.zeros((GROUPS, GROUP_HEADS, HEAD_DIM, STATE), jnp.float32)
    final_state, scanned = lax.scan(jax.checkpoint(block_step), zero_state, (blockify(values), blockify(inputs), blockify(outputs), blockify(step_sizes), blockify(log_decays), blockify(segment), previous))
    mixer_y = scanned.reshape(patches, GROUPS, GROUP_WIDTH)
    gated_out = mixer_y * jax.nn.silu(gate_part)
    group_normed = low(rms_scale(gated_out, group_gain[None]))
    mixer_out = low_back(jnp.einsum('pgc,gcd->pd', group_normed, out_weight, precision=highest))
    global_out = global_in + mixer_out
    byte_rows = patches * PATCH
    local_in = stream_in.reshape(byte_rows, D) + jnp.repeat(global_out, PATCH, axis=0)
    attn_in = low(rms_scale(local_in, attn_gain))
    qkv_all = low(low_back(jnp.einsum('td,kde->kte', attn_in, qkv_weight, precision=highest)))
    shaped = qkv_all.reshape(3, patches, PATCH, ATT_HEADS, ATT_DIM)
    scores = jnp.einsum('pihe,pjhe->phij', shaped[0], shaped[1], precision=highest) * ATT_DIM ** (-0.5)
    causal = jnp.tril(jnp.ones((PATCH, PATCH), jnp.bool_))
    scores = jnp.where(causal[None, None], scores, large_negative)
    attn_probs = low(jax.nn.softmax(scores, axis=-1))
    heads_out = low(jnp.einsum('phij,pjhe->pihe', attn_probs, shaped[2], precision=highest)).reshape(byte_rows, D)
    attn_branch = low_back(jnp.dot(heads_out, attn_out_weight, precision=highest))
    after_attn = local_in + attn_branch
    ffn_in = low(rms_scale(after_attn, ffn_gain))
    gate_up = low_back(jnp.einsum('td,kdf->ktf', ffn_in, ffn_weight[:2], precision=highest))
    hidden = low(jax.nn.silu(gate_up[0]) * gate_up[1])
    ffn_out = jnp.einsum('tf,df->td', hidden, ffn_weight[2], precision=highest)
    return (after_attn + ffn_out) * valid[:, None]

def reference(byte_input, seq_lengths, patch_weight, norm_in_gain, in_weight, conv_weight, conv_bias, step_bias, log_decay, skip_gain, group_gain, out_weight, attn_gain, qkv_weight, attn_out_weight, ffn_gain, ffn_weight, out_grad):
    weights = tuple((tensor.astype(jnp.float32) for tensor in (patch_weight, norm_in_gain, in_weight, conv_weight, conv_bias, step_bias, log_decay, skip_gain, group_gain, out_weight, attn_gain, qkv_weight, attn_out_weight, ffn_gain, ffn_weight)))

    def forward(stream_all, params):
        return jnp.stack([micro_forward(stream_all[micro_index], seq_lengths[micro_index], params) for micro_index in range(MICRO)])
    block_out, pull_back = jax.vjp(forward, byte_input.astype(jnp.float32), weights)
    input_grad, weight_grads = pull_back(out_grad.astype(jnp.float32))
    return (block_out.astype(jnp.bfloat16), input_grad, weight_grads[0], weight_grads[1], weight_grads[2], weight_grads[3], weight_grads[4], weight_grads[5], weight_grads[6], weight_grads[7], weight_grads[8], weight_grads[9], weight_grads[10], weight_grads[11], weight_grads[12], weight_grads[13], weight_grads[14])
```

```python
from functools import partial

import jax
import jax.numpy as jnp
from jax import lax
from jax.experimental import pallas as pl
from jax.experimental.pallas import tpu as pltpu
from jax.sharding import PartitionSpec as P

STATE = 128
CONV = 4
SEQS = 3
GROUP_WIDTH = 512
GROUP_HEADS = 8
HEAD_DIM = 64
ATT_DIM = 64
CONV_CH = 768

norm_eps = 1e-06
highest = lax.Precision.HIGHEST
large_negative = -1e30
f32 = jnp.float32
bf16 = jnp.bfloat16
MESH = pl.DeviceIdType.MESH
VMEM = pl.BlockSpec(memory_space=pltpu.VMEM)
SMEM = pl.BlockSpec(memory_space=pltpu.SMEM)
DMA = pltpu.SemaphoreType.DMA


def dot(a, b, dims=((1,), (0,)), precision=None):
    return lax.dot_general(
        a, b, (dims, ((), ())), preferred_element_type=f32, precision=precision
    )


def inv_rms(values):
    return lax.rsqrt(jnp.mean(values * values, axis=-1, keepdims=True) + norm_eps)


def rms_back(values, gain, upstream):
    scale = inv_rms(values)
    weighted = upstream * gain
    inner = jnp.mean(weighted * values, axis=-1, keepdims=True)
    back = scale * weighted - values * (inner * scale * scale * scale)
    return back, upstream * (values * scale)


def silu_pair(values):
    sig = jax.nn.sigmoid(values)
    return values * sig, sig * (1.0 + values * (1.0 - sig))


def rcopy(src, dst, send_sem, recv_sem, dp, mp):
    return pltpu.make_async_remote_copy(
        src_ref=src,
        dst_ref=dst,
        send_sem=send_sem,
        recv_sem=recv_sem,
        device_id={"dp": dp, "mp": mp},
        device_id_type=MESH,
    )


def greet(barrier, dp, mp):
    pl.semaphore_signal(barrier, inc=1, device_id={"dp": dp, "mp": mp}, device_id_type=MESH)


def plain_params(mib=56):
    return pltpu.CompilerParams(vmem_limit_bytes=mib * 2**20)


def remote_params(cid, mib=40):
    return pltpu.CompilerParams(
        collective_id=cid, has_side_effects=True, vmem_limit_bytes=mib * 2**20
    )


def embed_kernel(n, mpn, own, weight, gain, total_out, normed_out, part, recv, low, normed, ss1, rs1, ss2, rs2):
    i, j = lax.axis_index("dp"), lax.axis_index("mp")
    reps = n // mpn
    m = i // reps
    inside = m == j
    barrier = pltpu.get_barrier_semaphore()
    for d in range(1, mpn):
        greet(barrier, i, (j + d) % mpn)
    for s in range(n):
        @pl.when(jnp.logical_not((s == i) & inside))
        def _():
            greet(barrier, s, m)
    rows = part.shape[1]
    sums = dot(own[...], weight[...])
    for t in range(mpn):
        part[t] = sums[t * rows : (t + 1) * rows]
    pl.semaphore_wait(barrier, mpn - 1 + reps * mpn - inside.astype(jnp.int32))
    first = []
    for d in range(1, mpn):
        t = (j + d) % mpn
        copy = rcopy(part.at[t], recv.at[j], ss1.at[t], rs1.at[j], i, t)
        copy.start()
        first.append(copy)
    total = part[j]
    for d in range(1, mpn):
        s = (j + d) % mpn
        rcopy(part.at[s], recv.at[s], ss1.at[s], rs1.at[s], i, s).wait_recv()
        total = total + recv[s]
    total_out[...] = total
    low[...] = (total * inv_rms(total) * gain[...]).astype(bf16)
    for h in range(reps):
        for t in range(mpn):
            q = h * mpn + t
            here = (j * reps + h == i) & (t == j)

            @pl.when(jnp.logical_not(here))
            def _():
                rcopy(low, normed.at[i], ss2.at[q], rs2.at[i], j * reps + h, t).start()

            @pl.when(here)
            def _():
                normed[i] = low[...]
    for s in range(n):
        @pl.when(jnp.logical_not((s == i) & inside))
        def _():
            rcopy(low, normed.at[s], ss2.at[0], rs2.at[s], s, m).wait_recv()
    normed_out[...] = normed[...]
    for copy in first:
        copy.wait_send()
    for h in range(reps):
        for t in range(mpn):
            q = h * mpn + t

            @pl.when(jnp.logical_not((j * reps + h == i) & (t == j)))
            def _():
                rcopy(low, normed.at[i], ss2.at[q], rs2.at[i], j * reps + h, t).wait_send()


def embed(n, mpn, own, weight, gain):
    rows, dim = own.shape[0] // mpn, weight.shape[1]
    reps = n // mpn
    return pl.pallas_call(
        partial(embed_kernel, n, mpn),
        out_shape=(
            jax.ShapeDtypeStruct((rows, dim), f32),
            jax.ShapeDtypeStruct((n, rows, dim), bf16),
        ),
        in_specs=[VMEM] * 3,
        out_specs=(VMEM, VMEM),
        scratch_shapes=[
            pltpu.VMEM((mpn, rows, dim), f32),
            pltpu.VMEM((mpn, rows, dim), f32),
            pltpu.VMEM((rows, dim), bf16),
            pltpu.VMEM((n, rows, dim), bf16),
            DMA((mpn,)),
            DMA((mpn,)),
            DMA((reps * mpn,)),
            DMA((n,)),
        ],
        compiler_params=remote_params(0),
        name="embed",
    )(own, weight, gain)


def seg_starts(lengths, places):
    end0 = lengths[0]
    end1 = end0 + lengths[1]
    end2 = end1 + lengths[2]
    return jnp.where(
        places >= end2, end2, jnp.where(places >= end1, end1, jnp.where(places >= end0, end0, 0))
    )


def conv_taps(conv_in, pos, lag):
    moved = conv_in if lag == 0 else pltpu.roll(conv_in, lag, 0)
    return jnp.where(pos >= lag, moved, 0.0)


def mixer_state(lengths, projected, conv_weight, conv_bias, step_bias, log_decay):
    patches = projected.shape[0]
    places = lax.broadcasted_iota(jnp.int32, (patches, 1), 0)
    start = seg_starts(lengths, places)
    pos = places - start
    conv_in = projected[:, GROUP_WIDTH : GROUP_WIDTH + CONV_CH]
    conv_out = conv_bias
    for lag in range(CONV):
        conv_out = conv_out + conv_taps(conv_in, pos, lag) * conv_weight[CONV - 1 - lag][None]
    step_raw = projected[:, GROUP_WIDTH + CONV_CH :] + step_bias
    step = jnp.maximum(step_raw, 0.0) + jnp.log1p(jnp.exp(-jnp.abs(step_raw)))
    logd = -step * jnp.exp(log_decay)
    across = lax.broadcasted_iota(jnp.int32, (patches, patches), 1)
    down = lax.broadcasted_iota(jnp.int32, (patches, patches), 0)
    mask = (across >= start) & (across <= down)
    running = dot(mask.astype(f32), logd, precision=highest)
    return pos, conv_in, conv_out, step_raw, step, logd, mask, running


def head_decay(mask, running, running_t, h):
    return jnp.exp(
        jnp.where(mask, running[:, h : h + 1] - running_t[h : h + 1, :], large_negative)
    )


def mixer_fwd_kernel(
    lengths, normed, in_weight, conv_weight, conv_bias, step_bias, log_decay, skip, group_gain, out_weight,
    proj_out, y_out, low_out, part_out,
):
    projected = dot(normed[...], in_weight[...])
    proj_out[...] = projected
    _, _, conv_out, _, step, _, mask, running = mixer_state(
        lengths, projected, conv_weight[...], conv_bias[...], step_bias[...], log_decay[...]
    )
    act = conv_out * jax.nn.sigmoid(conv_out)
    inputs = act[:, GROUP_WIDTH : GROUP_WIDTH + STATE]
    outputs = act[:, GROUP_WIDTH + STATE :]
    inner = dot(outputs, inputs, ((1,), (1,)))
    running_t, step_t = running.T, step.T
    pair = 2 * HEAD_DIM
    lane = lax.broadcasted_iota(jnp.int32, (1, pair), 1)
    pieces = []
    for c in range(GROUP_WIDTH // pair):
        values = act[:, c * pair : (c + 1) * pair]
        got = []
        for h in (2 * c, 2 * c + 1):
            weights = head_decay(mask, running, running_t, h) * inner * step_t[h : h + 1, :]
            got.append(dot(weights, values))
        pieces.append(jnp.where(lane < HEAD_DIM, got[0], got[1]))
    y = jnp.concatenate(pieces, axis=1) + skip[...] * act[:, :GROUP_WIDTH]
    y_out[...] = y
    gate = projected[:, :GROUP_WIDTH]
    gated = y * (gate * jax.nn.sigmoid(gate))
    low = (gated * inv_rms(gated) * group_gain[...]).astype(bf16)
    low_out[...] = low
    part_out[...] = dot(low, out_weight[...])


def mixer_fwd(lengths, normed, in_weight, conv_weight, conv_bias, step_bias, log_decay, skip, group_gain, out_weight):
    patches, dim = normed.shape
    return pl.pallas_call(
        mixer_fwd_kernel,
        out_shape=(
            jax.ShapeDtypeStruct((patches, in_weight.shape[1]), f32),
            jax.ShapeDtypeStruct((patches, GROUP_WIDTH), f32),
            jax.ShapeDtypeStruct((patches, GROUP_WIDTH), bf16),
            jax.ShapeDtypeStruct((patches, dim), f32),
        ),
        in_specs=[SMEM] + [VMEM] * 9,
        out_specs=(VMEM,) * 4,
        compiler_params=plain_params(),
        name="mixer_fwd",
    )(lengths, normed, in_weight, conv_weight, conv_bias, step_bias, log_decay, skip, group_gain, out_weight)


def mixer_bwd_kernel(
    half, lengths, g_mixer, normed_half, projected_ref, y_ref, low_half, in_weight, conv_weight, conv_bias,
    step_bias, log_decay, skip, group_gain, out_weight,
    part_out, in_grad, out_grad, small,
):
    projected = projected_ref[...]
    pos, conv_in, conv_out, step_raw, step, logd, mask, running = mixer_state(
        lengths, projected, conv_weight[...], conv_bias[...], step_bias[...], log_decay[...]
    )
    act, act_slope = silu_pair(conv_out)
    inputs = act[:, GROUP_WIDTH : GROUP_WIDTH + STATE]
    outputs = act[:, GROUP_WIDTH + STATE :]
    inner = dot(outputs, inputs, ((1,), (1,)))
    running_t, step_t = running.T, step.T
    upstream = g_mixer[...]
    out_grad[...] = dot(low_half[...], upstream, ((0,), (0,))).astype(bf16)
    normed_grad = dot(upstream, out_weight[...], ((1,), (1,)))
    y = y_ref[...]
    gate = projected[:, :GROUP_WIDTH]
    gate_act, gate_slope = silu_pair(gate)
    gated_grad, gain_rows = rms_back(y * gate_act, group_gain[...], normed_grad)
    y_grad = gated_grad * gate_act
    gate_grad = gated_grad * y * gate_slope
    values = act[:, :GROUP_WIDTH]
    skip_cols = jnp.sum(y_grad * values, axis=0, keepdims=True)
    pair = 2 * HEAD_DIM
    lane = lax.broadcasted_iota(jnp.int32, (1, pair), 1)
    inner_grad = jnp.zeros_like(inner)
    value_pieces, row_sums, col_sums = [], [], []
    for c in range(GROUP_WIDTH // pair):
        at = slice(c * pair, (c + 1) * pair)
        got = []
        for h in (2 * c, 2 * c + 1):
            own = (lane < HEAD_DIM) if h % 2 == 0 else (lane >= HEAD_DIM)
            mine = jnp.where(own, y_grad[:, at], 0.0)
            decay = head_decay(mask, running, running_t, h)
            step_row = step_t[h : h + 1, :]
            weight_grad = dot(mine, values[:, at], ((1,), (1,))) * decay
            scaled = weight_grad * step_row
            inner_grad = inner_grad + scaled
            col_sums.append(jnp.sum(weight_grad * inner, axis=0, keepdims=True))
            row_sums.append(jnp.sum(scaled * inner, axis=1, keepdims=True))
            weights = decay * inner * step_row
            got.append(dot(weights, mine, ((0,), (0,))))
        value_pieces.append(got[0] + got[1])
    values_grad = jnp.concatenate(value_pieces, axis=1) + skip[...] * y_grad
    inputs_grad = dot(inner_grad, outputs, ((0,), (0,)))
    outputs_grad = dot(inner_grad, inputs)
    col_grad = jnp.concatenate(col_sums, axis=0).T
    running_grad = jnp.concatenate(row_sums, axis=1) - col_grad * step
    logd_grad = dot(mask.astype(f32), running_grad, ((0,), (0,)), precision=highest)
    step_grad = (col_grad - logd_grad * jnp.exp(log_decay[...])) * jax.nn.sigmoid(step_raw)
    conv_grad = jnp.concatenate([values_grad, inputs_grad, outputs_grad], axis=1) * act_slope
    patches = projected.shape[0]
    conv_in_grad = jnp.zeros_like(conv_grad)
    small[...] = jnp.zeros_like(small)
    for lag in range(CONV):
        small[CONV - 1 - lag : CONV - lag, :] = jnp.sum(
            conv_grad * conv_taps(conv_in, pos, lag), axis=0, keepdims=True
        )
        kept = jnp.where(pos >= lag, conv_grad, 0.0) * conv_weight[CONV - 1 - lag][None]
        conv_in_grad = conv_in_grad + (kept if lag == 0 else pltpu.roll(kept, patches - lag, 0))
    small[CONV : CONV + 1, :] = jnp.sum(conv_grad, axis=0, keepdims=True)
    small[CONV + 1 : CONV + 2, :GROUP_WIDTH] = jnp.sum(gain_rows, axis=0, keepdims=True)
    small[CONV + 2 : CONV + 3, :GROUP_WIDTH] = skip_cols
    small[CONV + 3 : CONV + 4, :GROUP_HEADS] = jnp.sum(step_grad, axis=0, keepdims=True)
    small[CONV + 4 : CONV + 5, :GROUP_HEADS] = jnp.sum(logd_grad * logd, axis=0, keepdims=True)
    proj_grad = jnp.concatenate([gate_grad, conv_in_grad, step_grad], axis=1).astype(bf16)
    in_grad[...] = dot(normed_half[...], proj_grad, ((0,), (0,))).astype(bf16)
    part_out[...] = dot(proj_grad, in_weight[...], ((1,), (1,)))


def mixer_bwd(
    lengths, g_mixer, normed_half, projected, y, low_half, in_weight, conv_weight, conv_bias,
    step_bias, log_decay, skip, group_gain, out_weight,
):
    patches, dim = g_mixer.shape
    return pl.pallas_call(
        partial(mixer_bwd_kernel, None),
        out_shape=(
            jax.ShapeDtypeStruct((patches, dim), f32),
            jax.ShapeDtypeStruct((normed_half.shape[1], in_weight.shape[1]), bf16),
            jax.ShapeDtypeStruct((low_half.shape[1], dim), bf16),
            jax.ShapeDtypeStruct((16, CONV_CH), f32),
        ),
        in_specs=[SMEM] + [VMEM] * 13,
        out_specs=(VMEM,) * 4,
        compiler_params=plain_params(),
        name="mixer_bwd",
    )(
        lengths, g_mixer, normed_half, projected, y, low_half, in_weight, conv_weight, conv_bias,
        step_bias, log_decay, skip, group_gain, out_weight,
    )


def to_owner_greet(barrier, n, mpn, i, j):
    reps = n // mpn
    inside = i // reps == j
    for s in range(mpn):
        @pl.when(jnp.logical_not(inside & (s == j)))
        def _():
            greet(barrier, j * reps + i % reps, s)
    return n // reps - inside.astype(jnp.int32)


def to_owner_copy(n, mpn, i, j, q, part, recv, ss, rs):
    reps = n // mpn
    block = q * reps + i % reps
    return rcopy(part.at[block], recv.at[j], ss.at[q], rs.at[j], block, i // reps)


def to_owner_start(n, mpn, i, j, part, recv, ss, rs):
    reps = n // mpn
    m = i // reps
    for q in range(n // reps):
        block = q * reps + i % reps

        @pl.when(jnp.logical_not((block == i) & (m == j)))
        def _():
            to_owner_copy(n, mpn, i, j, q, part, recv, ss, rs).start()

    @pl.when(m == j)
    def _():
        recv[j] = part[i]


def to_owner_recv(n, mpn, i, j, part, recv, ss, rs):
    reps = n // mpn
    for s in range(mpn):
        @pl.when(jnp.logical_not((i // reps == j) & (s == j)))
        def _():
            rcopy(part.at[0], recv.at[s], ss.at[0], rs.at[s], j * reps + i % reps, s).wait_recv()


def to_owner_sent(n, mpn, i, j, part, recv, ss, rs):
    reps = n // mpn
    for q in range(n // reps):
        @pl.when(jnp.logical_not((q * reps + i % reps == i) & (i // reps == j)))
        def _():
            to_owner_copy(n, mpn, i, j, q, part, recv, ss, rs).wait_send()


def mix_out_kernel(n, mpn, part, global_in, all_out, recv, own, everyone, ss1, rs1, ss2, rs2):
    i, j = lax.axis_index("dp"), lax.axis_index("mp")
    barrier = pltpu.get_barrier_semaphore()
    count = to_owner_greet(barrier, n, mpn, i, j)
    for d in range(1, mpn):
        greet(barrier, i, (j + d) % mpn)
    pl.semaphore_wait(barrier, mpn - 1 + count)
    to_owner_start(n, mpn, i, j, part, recv, ss1, rs1)
    to_owner_recv(n, mpn, i, j, part, recv, ss1, rs1)
    total = global_in[...]
    for s in range(mpn):
        total = total + recv[s]
    own[...] = total
    everyone[j] = total
    copies = []
    for d in range(1, mpn):
        t = (j + d) % mpn
        copy = rcopy(own, everyone.at[j], ss2.at[t], rs2.at[j], i, t)
        copy.start()
        copies.append(copy)
    for d in range(1, mpn):
        s = (j + d) % mpn
        rcopy(own, everyone.at[s], ss2.at[s], rs2.at[s], i, s).wait_recv()
    all_out[...] = everyone[...]
    to_owner_sent(n, mpn, i, j, part, recv, ss1, rs1)
    for copy in copies:
        copy.wait_send()


def mix_out(n, mpn, part, global_in):
    rows, dim = global_in.shape
    return pl.pallas_call(
        partial(mix_out_kernel, n, mpn),
        out_shape=jax.ShapeDtypeStruct((mpn, rows, dim), f32),
        in_specs=[VMEM] * 2,
        out_specs=VMEM,
        scratch_shapes=[
            pltpu.VMEM((mpn, rows, dim), f32),
            pltpu.VMEM((rows, dim), f32),
            pltpu.VMEM((mpn, rows, dim), f32),
            DMA((mpn,)),
            DMA((mpn,)),
            DMA((mpn,)),
            DMA((mpn,)),
        ],
        compiler_params=remote_params(1),
        name="mix_out",
    )(part, global_in)


def slab_rows(bytes_ref, m, patch_out, k, dim):
    return bytes_ref[m, :, k * dim : (k + 1) * dim].astype(f32) + patch_out


def att_mask(rows, patches):
    across = lax.broadcasted_iota(jnp.int32, (rows, rows), 1)
    down = lax.broadcasted_iota(jnp.int32, (rows, rows), 0)
    return (across % patches == down % patches) & (across <= down)


def att_fwd_kernel(bytes_in, patch_out, gain, qkv_weight, out_weight, attn_in, qkv_out, heads_out, part):
    micro, patches, cols = bytes_in.shape
    dim = gain.shape[1]
    slabs = cols // dim
    rows = slabs * patches
    width = qkv_weight.shape[2]
    mask = att_mask(rows, patches)
    pair = 2 * ATT_DIM
    lane = lax.broadcasted_iota(jnp.int32, (1, pair), 1)

    def step(m, _):
        for k in range(slabs):
            here = slab_rows(bytes_in, m, patch_out[m], k, dim)
            attn_in[m, k * patches : (k + 1) * patches, :] = (
                here * inv_rms(here) * gain[...]
            ).astype(bf16)
        got = attn_in[m]
        for w in range(3):
            qkv_out[w, m] = dot(got, qkv_weight[w]).astype(bf16)
        for c in range(width // pair):
            at = slice(c * pair, (c + 1) * pair)
            query, key, value = qkv_out[0, m, :, at], qkv_out[1, m, :, at], qkv_out[2, m, :, at]
            res = []
            for own in (lane < ATT_DIM, lane >= ATT_DIM):
                mine = jnp.where(own, query, jnp.zeros_like(query))
                scores = dot(mine, key, ((1,), (1,))) * ATT_DIM ** (-0.5)
                scores = jnp.where(mask, scores, large_negative)
                probs = jnp.exp(scores - jnp.max(scores, axis=1, keepdims=True))
                probs = probs / jnp.sum(probs, axis=1, keepdims=True)
                res.append(dot(probs.astype(bf16), value))
            heads_out[m, :, at] = jnp.where(lane < ATT_DIM, res[0], res[1]).astype(bf16)
        part[m] = dot(heads_out[m], out_weight[...]).astype(bf16)
        return 0

    lax.fori_loop(0, micro, step, 0)


def att_fwd(bytes_in, patch_out, gain, qkv_weight, out_weight):
    micro, patches, cols = bytes_in.shape
    dim, width = qkv_weight.shape[1:]
    rows = patches * (cols // dim)
    return pl.pallas_call(
        att_fwd_kernel,
        out_shape=(
            jax.ShapeDtypeStruct((micro, rows, dim), bf16),
            jax.ShapeDtypeStruct((3, micro, rows, width), bf16),
            jax.ShapeDtypeStruct((micro, rows, width), bf16),
            jax.ShapeDtypeStruct((micro, rows, dim), bf16),
        ),
        in_specs=[VMEM] * 5,
        out_specs=(VMEM,) * 4,
        compiler_params=plain_params(),
        name="att_fwd",
    )(bytes_in, patch_out, gain, qkv_weight, out_weight)


def att_bwd_kernel(branch, attn_in, qkv, heads, qkv_weight, out_weight, part, qkv_grad, out_grad, low):
    micro, rows, dim = branch.shape
    width = out_weight.shape[0]
    patches = rows // 8
    mask = att_mask(rows, patches)
    pair = 2 * ATT_DIM
    lane = lax.broadcasted_iota(jnp.int32, (1, pair), 1)

    def step(m, _):
        heads_grad = dot(branch[m], out_weight[...], ((1,), (1,)))
        for c in range(width // pair):
            at = slice(c * pair, (c + 1) * pair)
            query, key, value = qkv[0, m, :, at], qkv[1, m, :, at], qkv[2, m, :, at]
            up = heads_grad[:, at].astype(bf16)
            got = [[], [], []]
            for own in (lane < ATT_DIM, lane >= ATT_DIM):
                mine = jnp.where(own, query, jnp.zeros_like(query))
                scores = dot(mine, key, ((1,), (1,))) * ATT_DIM ** (-0.5)
                scores = jnp.where(mask, scores, large_negative)
                probs = jnp.exp(scores - jnp.max(scores, axis=1, keepdims=True))
                probs = probs / jnp.sum(probs, axis=1, keepdims=True)
                my_up = jnp.where(own, up, jnp.zeros_like(up))
                probs_grad = dot(my_up, value, ((1,), (1,)))
                inner = jnp.sum(probs * probs_grad, axis=1, keepdims=True)
                score_grad = (probs * (probs_grad - inner) * ATT_DIM ** (-0.5)).astype(bf16)
                got[0].append(dot(score_grad, key))
                got[1].append(dot(score_grad, mine, ((0,), (0,))))
                got[2].append(dot(probs.astype(bf16), my_up, ((0,), (0,))))
            low[0, m, :, at] = jnp.where(lane < ATT_DIM, got[0][0], got[0][1]).astype(bf16)
            low[1, m, :, at] = (got[1][0] + got[1][1]).astype(bf16)
            low[2, m, :, at] = (got[2][0] + got[2][1]).astype(bf16)
        total = dot(low[0, m], qkv_weight[0], ((1,), (1,)))
        total = total + dot(low[1, m], qkv_weight[1], ((1,), (1,)))
        total = total + dot(low[2, m], qkv_weight[2], ((1,), (1,)))
        part[m] = total.astype(bf16)
        return 0

    lax.fori_loop(0, micro, step, 0)
    everything = attn_in[...].reshape(micro * rows, dim)
    for w in range(3):
        qkv_grad[w] = dot(everything, low[w].reshape(micro * rows, width), ((0,), (0,))).astype(bf16)
    out_grad[...] = dot(
        heads[...].reshape(micro * rows, width), branch[...].reshape(micro * rows, dim), ((0,), (0,))
    ).astype(bf16)


def att_bwd(branch, attn_in, qkv, heads, qkv_weight, out_weight):
    micro, rows, dim = branch.shape
    width = out_weight.shape[0]
    return pl.pallas_call(
        att_bwd_kernel,
        out_shape=(
            jax.ShapeDtypeStruct((micro, rows, dim), bf16),
            jax.ShapeDtypeStruct((3, dim, width), bf16),
            jax.ShapeDtypeStruct((width, dim), bf16),
        ),
        in_specs=[VMEM] * 6,
        out_specs=(VMEM,) * 3,
        scratch_shapes=[pltpu.VMEM((3, micro, rows, width), bf16)],
        compiler_params=plain_params(),
        name="att_bwd",
    )(branch, attn_in, qkv, heads, qkv_weight, out_weight)


def after_att_kernel(
    n, mpn, part, own_bytes, patch_out, gain, after_out, all_out, recv, low, everyone, ss1, rs1, ss2, rs2, ss3,
):
    i, j = lax.axis_index("dp"), lax.axis_index("mp")
    c, mine = i % 2, i // 2
    other = i + 1 - 2 * c
    barrier = pltpu.get_barrier_semaphore()
    for d in range(1, mpn):
        greet(barrier, i, (j + d) % mpn)
    greet(barrier, other, j)
    for d in range(1, n // 2):
        greet(barrier, (mine + d) % (n // 2) * 2 + c, j)
    pl.semaphore_wait(barrier, mpn - 1 + n // 2)
    copies = []
    for d in range(1, mpn):
        t = (j + d) % mpn
        copy = rcopy(part.at[t], recv.at[j], ss1.at[t], rs1.at[j], i, t)
        copy.start()
        copies.append(copy)
    patches, dim = patch_out.shape
    for k in range(part.shape[1] // patches):
        rows = slice(k * patches, (k + 1) * patches)
        after_out[rows, :] = (
            own_bytes[:, k * dim : (k + 1) * dim].astype(f32) + patch_out[...] + part[j, rows, :].astype(f32)
        )
    for d in range(1, mpn):
        s = (j + d) % mpn
        rcopy(part.at[s], recv.at[s], ss1.at[s], rs1.at[s], i, s).wait_recv()
        after_out[...] += recv[s].astype(f32)
    after = after_out[...]
    low[...] = (after * inv_rms(after) * gain[...]).astype(bf16)
    for d in range(1, n // 2):
        q = (mine + d) % (n // 2)
        copy = rcopy(low, everyone.at[i], ss2.at[q], rs2.at[i], q * 2 + c, j)
        copy.start()
        copies.append(copy)
    copy = rcopy(low, everyone.at[i], ss3.at[mine], rs2.at[i], other, j)
    copy.start()
    copies.append(copy)
    everyone[i] = low[...]
    for d in range(1, n // 2):
        q = (mine + n // 2 - d) % (n // 2)
        s = q * 2 + c
        rcopy(low, everyone.at[s], ss2.at[q], rs2.at[s], s, j).wait_recv()
        copy = rcopy(everyone.at[s], everyone.at[s], ss3.at[q], rs2.at[s], other, j)
        copy.start()
        copies.append(copy)
    for q in range(n // 2):
        s = q * 2 + 1 - c
        rcopy(low, everyone.at[s], ss3.at[q], rs2.at[s], other, j).wait_recv()
    all_out[...] = everyone[...]
    for copy in copies:
        copy.wait_send()


def after_att(n, mpn, part, own_bytes, patch_out, gain):
    _, rows, dim = part.shape
    return pl.pallas_call(
        partial(after_att_kernel, n, mpn),
        out_shape=(
            jax.ShapeDtypeStruct((rows, dim), f32),
            jax.ShapeDtypeStruct((n, rows, dim), bf16),
        ),
        in_specs=[VMEM] * 4,
        out_specs=(VMEM, VMEM),
        scratch_shapes=[
            pltpu.VMEM((mpn, rows, dim), bf16),
            pltpu.VMEM((rows, dim), bf16),
            pltpu.VMEM((n, rows, dim), bf16),
            DMA((mpn,)),
            DMA((mpn,)),
            DMA((n // 2,)),
            DMA((n,)),
            DMA((n // 2,)),
        ],
        compiler_params=remote_params(2),
        name="after_att",
    )(part, own_bytes, patch_out, gain)


def ffn_kernel(rows_in, grads_in, weight, down_out, in_grad, weight_grad, gate_low, up_low, hidden_low):
    blocks, rows, dim = rows_in.shape

    def step(b, _):
        here, up = rows_in[b], grads_in[b]
        gate = dot(here, weight[0])
        other = dot(here, weight[1])
        act, slope = silu_pair(gate)
        hidden = (act * other).astype(bf16)
        hidden_low[b] = hidden
        down_out[b] = dot(hidden, weight[2], ((1,), (1,))).astype(bf16)
        hidden_grad = dot(up, weight[2])
        gate_grad = (hidden_grad * other * slope).astype(bf16)
        up_grad = (hidden_grad * act).astype(bf16)
        gate_low[b] = gate_grad
        up_low[b] = up_grad
        back = dot(gate_grad, weight[0], ((1,), (1,))) + dot(up_grad, weight[1], ((1,), (1,)))
        in_grad[b] = back.astype(bf16)
        return 0

    lax.fori_loop(0, blocks, step, 0)
    hidden = weight.shape[2]
    everything = rows_in[...].reshape(blocks * rows, dim)
    weight_grad[0] = dot(everything, gate_low[...].reshape(blocks * rows, hidden), ((0,), (0,))).astype(bf16)
    weight_grad[1] = dot(everything, up_low[...].reshape(blocks * rows, hidden), ((0,), (0,))).astype(bf16)
    weight_grad[2] = dot(
        grads_in[...].reshape(blocks * rows, dim), hidden_low[...].reshape(blocks * rows, hidden), ((0,), (0,))
    ).astype(bf16)


def ffn(rows_in, grads_in, weight):
    blocks, rows, dim = rows_in.shape
    hidden = weight.shape[2]
    return pl.pallas_call(
        ffn_kernel,
        out_shape=(
            jax.ShapeDtypeStruct((blocks, rows, dim), bf16),
            jax.ShapeDtypeStruct((blocks, rows, dim), bf16),
            jax.ShapeDtypeStruct((3, dim, hidden), bf16),
        ),
        in_specs=[VMEM] * 3,
        out_specs=(VMEM,) * 3,
        scratch_shapes=[pltpu.VMEM((blocks, rows, hidden), bf16)] * 3,
        compiler_params=plain_params(60),
        name="ffn",
    )(rows_in, grads_in, weight)


def ffn_back_kernel(
    n, mpn, in_part, down_part, after_ref, own_grad, valid, gain,
    after_grad_out, branch_out, block_out, gain_out,
    pre, held, recv, branch, ssa, rsa, ssb, rsb, ss2, rs2,
):
    i, j = lax.axis_index("dp"), lax.axis_index("mp")
    c, mine = i % 2, i // 2
    other = i + 1 - 2 * c
    half = n // 2
    barrier = pltpu.get_barrier_semaphore()
    for d in range(1, mpn):
        greet(barrier, i, (j + d) % mpn)
    greet(barrier, other, j)
    for d in range(1, half):
        greet(barrier, (mine + d) % half * 2 + c, j)
    pl.semaphore_wait(barrier, mpn - 1 + half)
    copies = []
    for w, part in enumerate((in_part, down_part)):
        for d in range(1, half + 1):
            q = (mine + d) % half
            copy = rcopy(part.at[q * 2 + 1 - c], pre.at[w, q], ssa.at[w, q], rsa.at[w, q], other, j)
            copy.start()
            copies.append(copy)

    def spread(w, part):
        for d in range(1, half):
            q = (mine + d) % half
            rcopy(part.at[0], pre.at[w, q], ssa.at[w, q], rsa.at[w, q], other, j).wait_recv()
            held[w, q] = (part[q * 2 + c].astype(f32) + pre[w, q].astype(f32)).astype(bf16)
            copy = rcopy(held.at[w, q], recv.at[w, mine], ssb.at[w, q], rsb.at[w, mine], q * 2 + c, j)
            copy.start()
            copies.append(copy)

    def gathered(w, part):
        rcopy(part.at[0], pre.at[w, mine], ssa.at[w, mine], rsa.at[w, mine], other, j).wait_recv()
        total = part[i].astype(f32) + pre[w, mine].astype(f32)
        for d in range(1, half):
            q = (mine + d) % half
            rcopy(held.at[w, q], recv.at[w, q], ssb.at[w, q], rsb.at[w, q], q * 2 + c, j).wait_recv()
            total = total + recv[w, q].astype(f32)
        return total

    spread(0, in_part)
    after = after_ref[...]
    back, gain_rows = rms_back(after, gain[...], gathered(0, in_part))
    after_grad = own_grad[...].astype(f32) + back
    after_grad_out[...] = after_grad
    branch[j] = after_grad.astype(bf16)
    for d in range(1, mpn):
        t = (j + d) % mpn
        copy = rcopy(branch.at[j], branch.at[j], ss2.at[t], rs2.at[j], i, t)
        copy.start()
        copies.append(copy)
    spread(1, down_part)
    gain_out[...] = jnp.sum(gain_rows, axis=0, keepdims=True)
    block_out[...] = ((after_ref[...] + gathered(1, down_part)) * valid[...]).astype(bf16)
    for d in range(1, mpn):
        s = (j + d) % mpn
        rcopy(branch.at[s], branch.at[s], ss2.at[s], rs2.at[s], i, s).wait_recv()
    branch_out[...] = branch[...]
    for copy in copies:
        copy.wait_send()


def ffn_back(n, mpn, in_part, down_part, after, own_grad, valid, gain):
    _, rows, dim = in_part.shape
    half = n // 2
    return pl.pallas_call(
        partial(ffn_back_kernel, n, mpn),
        out_shape=(
            jax.ShapeDtypeStruct((rows, dim), f32),
            jax.ShapeDtypeStruct((mpn, rows, dim), bf16),
            jax.ShapeDtypeStruct((rows, dim), bf16),
            jax.ShapeDtypeStruct((1, dim), f32),
        ),
        in_specs=[VMEM] * 6,
        out_specs=(VMEM,) * 4,
        scratch_shapes=[
            pltpu.VMEM((2, half, rows, dim), bf16),
            pltpu.VMEM((2, half, rows, dim), bf16),
            pltpu.VMEM((2, half, rows, dim), bf16),
            pltpu.VMEM((mpn, rows, dim), bf16),
            DMA((2, half)),
            DMA((2, half)),
            DMA((2, half)),
            DMA((2, half)),
            DMA((mpn,)),
            DMA((mpn,)),
        ],
        compiler_params=remote_params(3, 58),
        name="ffn_back",
    )(in_part, down_part, after, own_grad, valid, gain)


def att_back_kernel(
    n, mpn, part, own_bytes, patch_out, after_grad, block_low, gain,
    local_out, block_out, global_out, mixer_out, gain_out,
    recv, local, local_in, local_all, block_all, low, mixer, ss1, rs1, ss2, rs2, ss3, rs3, ss4, rs4,
):
    i, j = lax.axis_index("dp"), lax.axis_index("mp")
    reps = n // mpn
    m = i // reps
    inside = m == j
    barrier = pltpu.get_barrier_semaphore()
    for d in range(1, mpn):
        greet(barrier, i, (j + d) % mpn)
    for s in range(n):
        @pl.when(jnp.logical_not((s == i) & inside))
        def _():
            greet(barrier, s, m)
    pl.semaphore_wait(barrier, mpn - 1 + reps * mpn - inside.astype(jnp.int32))
    copies = []
    for d in range(1, mpn):
        t = (j + d) % mpn
        copy = rcopy(part.at[t], recv.at[j], ss1.at[t], rs1.at[j], i, t)
        copy.start()
        copies.append(copy)
    for d in range(1, mpn):
        t = (j + d) % mpn
        copy = rcopy(block_low.at[t], block_all.at[j], ss3.at[t], rs3.at[j], i, t)
        copy.start()
        copies.append(copy)
    block_all[j] = block_low[j]
    patches, dim = patch_out.shape
    rows_all = part.shape[1]
    slabs = rows_all // patches
    for k in range(slabs):
        rows = slice(k * patches, (k + 1) * patches)
        local_in[rows, :] = own_bytes[:, k * dim : (k + 1) * dim].astype(f32) + patch_out[...]
    total = part[j].astype(f32)
    for d in range(1, mpn):
        s = (j + d) % mpn
        rcopy(part.at[s], recv.at[s], ss1.at[s], rs1.at[s], i, s).wait_recv()
        total = total + recv[s].astype(f32)
    back, gain_rows = rms_back(local_in[...], gain[...], total)
    local_grad = after_grad[...] + back
    global_grad = local_grad[:patches]
    for k in range(1, slabs):
        global_grad = global_grad + local_grad[k * patches : (k + 1) * patches]
    global_out[...] = global_grad
    low[...] = global_grad.astype(bf16)
    for h in range(reps):
        for t in range(mpn):
            q = h * mpn + t
            here = (j * reps + h == i) & (t == j)

            @pl.when(jnp.logical_not(here))
            def _():
                rcopy(low, mixer.at[i], ss2.at[q], rs2.at[i], j * reps + h, t).start()

            @pl.when(here)
            def _():
                mixer[i] = low[...]
    per = rows_all // mpn
    for t in range(mpn):
        local[t] = local_grad[t * per : (t + 1) * per].astype(bf16)
    for d in range(1, mpn):
        t = (j + d) % mpn
        copy = rcopy(local.at[t], local_all.at[j], ss4.at[t], rs4.at[j], i, t)
        copy.start()
        copies.append(copy)
    local_all[j] = local[j]
    gain_out[...] = jnp.sum(gain_rows, axis=0, keepdims=True)
    for s in range(n):
        @pl.when(jnp.logical_not((s == i) & inside))
        def _():
            rcopy(low, mixer.at[s], ss2.at[0], rs2.at[s], s, m).wait_recv()
    mixer_out[...] = mixer[...]
    for d in range(1, mpn):
        s = (j + d) % mpn
        rcopy(block_low.at[s], block_all.at[s], ss3.at[s], rs3.at[s], i, s).wait_recv()
        rcopy(local.at[s], local_all.at[s], ss4.at[s], rs4.at[s], i, s).wait_recv()
    block_out[...] = block_all[...]
    local_out[...] = local_all[...]
    for copy in copies:
        copy.wait_send()
    for h in range(reps):
        for t in range(mpn):
            q = h * mpn + t

            @pl.when(jnp.logical_not((j * reps + h == i) & (t == j)))
            def _():
                rcopy(low, mixer.at[i], ss2.at[q], rs2.at[i], j * reps + h, t).wait_send()


def att_back(n, mpn, part, own_bytes, patch_out, after_grad, block_low, gain):
    _, rows, dim = part.shape
    patches = patch_out.shape[0]
    reps = n // mpn
    cols = block_low.shape[2]
    return pl.pallas_call(
        partial(att_back_kernel, n, mpn),
        out_shape=(
            jax.ShapeDtypeStruct((mpn, rows // mpn, dim), bf16),
            jax.ShapeDtypeStruct((mpn, rows, cols), bf16),
            jax.ShapeDtypeStruct((patches, dim), f32),
            jax.ShapeDtypeStruct((n, patches, dim), bf16),
            jax.ShapeDtypeStruct((1, dim), f32),
        ),
        in_specs=[VMEM] * 6,
        out_specs=(VMEM,) * 5,
        scratch_shapes=[
            pltpu.VMEM((mpn, rows, dim), bf16),
            pltpu.VMEM((mpn, rows // mpn, dim), bf16),
            pltpu.VMEM((rows, dim), f32),
            pltpu.VMEM((mpn, rows // mpn, dim), bf16),
            pltpu.VMEM((mpn, rows, cols), bf16),
            pltpu.VMEM((patches, dim), bf16),
            pltpu.VMEM((n, patches, dim), bf16),
            DMA((mpn,)),
            DMA((mpn,)),
            DMA((reps * mpn,)),
            DMA((n,)),
            DMA((mpn,)),
            DMA((mpn,)),
            DMA((mpn,)),
            DMA((mpn,)),
        ],
        compiler_params=remote_params(4),
        name="att_back",
    )(part, own_bytes, patch_out, after_grad, block_low, gain)


def mix_back_kernel(
    n, mpn, part, global_in, global_grad, gain, in_part, out_part, small_part, gains_part,
    all_out, in_out, out_out, small_out, gains_out,
    recv, line, plane, in_recv, out_recv, small_recv, gains_held, gains_line, gains_plane, gains_pair,
    ss1, rs1, ss2, rs2, ss3, rs3, ss4, ssi, rsi, sso, rso, sss, rss, ssg, rsg, ssh, rsh, ssp, rsp,
):
    i, j = lax.axis_index("dp"), lax.axis_index("mp")
    reps = n // mpn
    m, h = i // reps, i % reps
    share = n // reps
    c, mine = i % 2, i // 2
    other = i + 1 - 2 * c
    half = n // 2
    group = i // share
    barrier = pltpu.get_barrier_semaphore()
    count = to_owner_greet(barrier, n, mpn, i, j)
    for d in range(1, mpn):
        greet(barrier, i, (j + d) % mpn)
    greet(barrier, other, j)
    for d in range(1, half):
        greet(barrier, (mine + d) % half * 2 + c, j)
    for t in range(mpn):
        @pl.when(t * reps + group != i)
        def _():
            greet(barrier, t * reps + group, j)
    self_share = (group == h).astype(jnp.int32)
    pl.semaphore_wait(barrier, count + mpn - 1 + half + share - self_share)
    to_owner_start(n, mpn, i, j, part, recv, ss1, rs1)

    bundles = (
        (in_part, in_recv, ssi, rsi),
        (out_part, out_recv, sso, rso),
        (small_part, small_recv, sss, rss),
    )

    def bundle_copy(src, dst, ss, rs, e):
        source = src if src is small_part else src.at[e]
        return rcopy(source, dst.at[m], ss.at[e], rs.at[m], h * share + e, j)

    for e in range(share):
        @pl.when(h * share + e != i)
        def _():
            for src, dst, ss, rs in bundles:
                bundle_copy(src, dst, ss, rs, e).start()

        @pl.when(h * share + e == i)
        def _():
            for src, dst, ss, rs in bundles:
                dst[m] = src[...] if src is small_part else src[e]

    to_owner_recv(n, mpn, i, j, part, recv, ss1, rs1)
    total = recv[0]
    for s in range(1, mpn):
        total = total + recv[s]
    back, gain_rows = rms_back(global_in[...], gain[...], total)
    line[j] = (global_grad[...] + back).astype(bf16)
    copies = []
    for d in range(1, mpn):
        t = (j + d) % mpn
        copy = rcopy(line.at[j], line.at[j], ss2.at[t], rs2.at[j], i, t)
        copy.start()
        copies.append(copy)
    gains_held[...] = gains_part[...]
    gains_held[0:1, :] = jnp.sum(gain_rows, axis=0, keepdims=True)
    gains_line[j] = gains_held[...]
    for d in range(1, mpn):
        t = (j + d) % mpn
        copy = rcopy(gains_held, gains_line.at[j], ssg.at[t], rsg.at[j], i, t)
        copy.start()
        copies.append(copy)
    for d in range(1, mpn):
        s = (j + d) % mpn
        rcopy(line.at[s], line.at[s], ss2.at[s], rs2.at[s], i, s).wait_recv()
    for d in range(1, half):
        q = (mine + d) % half
        copy = rcopy(line, plane.at[i], ss3.at[q], rs3.at[i], q * 2 + c, j)
        copy.start()
        copies.append(copy)
    copy = rcopy(line, plane.at[i], ss4.at[mine], rs3.at[i], other, j)
    copy.start()
    copies.append(copy)
    plane[i] = line[...]
    for d in range(1, mpn):
        s = (j + d) % mpn
        rcopy(gains_held, gains_line.at[s], ssg.at[s], rsg.at[s], i, s).wait_recv()
    gains_plane[mine] = sum(gains_line[s] for s in range(mpn))
    for d in range(1, half):
        q = (mine + d) % half
        copy = rcopy(gains_plane.at[mine], gains_plane.at[mine], ssh.at[q], rsh.at[mine], q * 2 + c, j)
        copy.start()
        copies.append(copy)
    for d in range(1, half):
        q = (mine + half - d) % half
        s = q * 2 + c
        rcopy(line, plane.at[s], ss3.at[q], rs3.at[s], s, j).wait_recv()
        copy = rcopy(plane.at[s], plane.at[s], ss4.at[q], rs3.at[s], other, j)
        copy.start()
        copies.append(copy)
    for d in range(1, half):
        q = (mine + d) % half
        rcopy(gains_plane.at[q], gains_plane.at[q], ssh.at[q], rsh.at[q], q * 2 + c, j).wait_recv()
    gains_pair[0] = sum(gains_plane[s] for s in range(half))
    copy = rcopy(gains_pair.at[0], gains_pair.at[1], ssp.at[0], rsp.at[0], other, j)
    copy.start()
    copies.append(copy)
    for q in range(half):
        s = q * 2 + 1 - c
        rcopy(line, plane.at[s], ss4.at[q], rs3.at[s], other, j).wait_recv()
    all_out[...] = plane[...]
    for t in range(mpn):
        @pl.when(t * reps + group != i)
        def _():
            for src, dst, ss, rs in bundles:
                source = src if src is small_part else src.at[0]
                rcopy(source, dst.at[t], ss.at[0], rs.at[t], t * reps + group, j).wait_recv()
    in_out[...] = sum(in_recv[t].astype(f32) for t in range(mpn))
    out_out[...] = sum(out_recv[t].astype(f32) for t in range(mpn))
    small_out[...] = sum(small_recv[t] for t in range(mpn))
    rcopy(gains_pair.at[0], gains_pair.at[1], ssp.at[0], rsp.at[0], other, j).wait_recv()
    gains_out[...] = gains_pair[0] + gains_pair[1]
    to_owner_sent(n, mpn, i, j, part, recv, ss1, rs1)
    for copy in copies:
        copy.wait_send()
    for e in range(share):
        @pl.when(h * share + e != i)
        def _():
            for src, dst, ss, rs in bundles:
                bundle_copy(src, dst, ss, rs, e).wait_send()


def mix_back(n, mpn, part, global_in, global_grad, gain, in_part, out_part, small_part, gains_part):
    rows, dim = global_in.shape
    half, share = n // 2, mpn
    return pl.pallas_call(
        partial(mix_back_kernel, n, mpn),
        out_shape=(
            jax.ShapeDtypeStruct((n, mpn, rows, dim), bf16),
            jax.ShapeDtypeStruct(in_part.shape[1:], f32),
            jax.ShapeDtypeStruct(out_part.shape[1:], f32),
            jax.ShapeDtypeStruct(small_part.shape, f32),
            jax.ShapeDtypeStruct(gains_part.shape, f32),
        ),
        in_specs=[VMEM] * 8,
        out_specs=(VMEM,) * 5,
        scratch_shapes=[
            pltpu.VMEM((mpn, rows, dim), f32),
            pltpu.VMEM((mpn, rows, dim), bf16),
            pltpu.VMEM((n, mpn, rows, dim), bf16),
            pltpu.VMEM((mpn,) + in_part.shape[1:], bf16),
            pltpu.VMEM((mpn,) + out_part.shape[1:], bf16),
            pltpu.VMEM((mpn,) + small_part.shape, f32),
            pltpu.VMEM(gains_part.shape, f32),
            pltpu.VMEM((mpn,) + gains_part.shape, f32),
            pltpu.VMEM((half,) + gains_part.shape, f32),
            pltpu.VMEM((2,) + gains_part.shape, f32),
            DMA((mpn,)), DMA((mpn,)),
            DMA((mpn,)), DMA((mpn,)),
            DMA((half,)), DMA((n,)),
            DMA((half,)),
            DMA((share,)), DMA((mpn,)),
            DMA((share,)), DMA((mpn,)),
            DMA((share,)), DMA((mpn,)),
            DMA((mpn,)), DMA((mpn,)),
            DMA((half,)), DMA((half,)),
            DMA((1,)), DMA((1,)),
        ],
        compiler_params=remote_params(5),
        name="mix_back",
    )(part, global_in, global_grad, gain, in_part, out_part, small_part, gains_part)


def patch_back_kernel(everyone, own, bytes_part, weight, local, weight_grad, input_grad):
    weight_grad[...] = dot(bytes_part[...], everyone[...], ((0,), (0,)))
    piece = dot(own[...], weight[...], ((1,), (1,)))
    micro, positions, patches, dim = local.shape
    for m in range(micro):
        for k in range(positions):
            input_grad[m, :, k * dim : (k + 1) * dim] = (
                piece[m * patches : (m + 1) * patches, k * dim : (k + 1) * dim]
                + local[m, k].astype(f32)
            )


def patch_back(everyone, own, bytes_part, weight, local):
    micro, positions, patches, dim = local.shape
    return pl.pallas_call(
        patch_back_kernel,
        out_shape=(
            jax.ShapeDtypeStruct((bytes_part.shape[1], dim), f32),
            jax.ShapeDtypeStruct((micro, patches, positions * dim), f32),
        ),
        in_specs=[VMEM] * 5,
        out_specs=(VMEM,) * 2,
        compiler_params=plain_params(),
        name="patch_back",
    )(everyone, own, bytes_part, weight, local)


def body(
    byte_input,
    seq_lengths,
    patch_weight,
    norm_in_gain,
    in_weight,
    conv_weight,
    conv_bias,
    step_bias,
    log_decay,
    skip_gain,
    group_gain,
    out_weight,
    attn_gain,
    qkv_weight,
    attn_out_weight,
    ffn_gain,
    ffn_weight,
    out_grad,
):
    micro, patches, cols = byte_input.shape
    dim = norm_in_gain.shape[0]
    patch_len = cols // dim
    positions = patch_weight.shape[0]
    own_cols = positions * dim
    n, mpn = lax.axis_size("dp"), lax.axis_size("mp")
    i, j = lax.axis_index("dp"), lax.axis_index("mp")
    reps = n // mpn
    share = n // reps
    part_cols = qkv_weight.shape[2]

    weight_cols = lax.all_gather(ffn_weight, "mp", axis=1, tiled=True)
    own_input = lax.dynamic_slice_in_dim(byte_input, j * own_cols, own_cols, 2)
    own_input = own_input.reshape(micro * patches, own_cols)
    lengths_own = lax.dynamic_index_in_dim(seq_lengths, j, 0, keepdims=False)
    ends = jnp.sum(lengths_own)
    places = i * patches + jnp.arange(patches, dtype=jnp.int32)
    valid = jnp.tile((places < ends).astype(f32), patch_len)[:, None]
    own_grad = lax.dynamic_index_in_dim(out_grad, j, 0, keepdims=False)
    own_grad = own_grad.reshape(patches, patch_len, dim).swapaxes(0, 1).reshape(patch_len * patches, dim)
    own_grad = jnp.where(valid > 0, own_grad, jnp.zeros_like(own_grad))
    grad_rows = lax.all_gather(own_grad, "dp")
    input_all = lax.all_gather(own_input, "dp")
    feature = dim // n
    bytes_part = lax.dynamic_slice_in_dim(
        input_all.reshape(n * micro * patches, positions, dim), i * feature, feature, 2
    ).reshape(n * micro * patches, positions * feature)

    pw = patch_weight.reshape(own_cols, dim)
    row = lambda v: v.reshape(1, -1)
    global_in, normed = embed(n, mpn, own_input, pw, row(norm_in_gain))
    normed = normed.reshape(n * patches, dim)
    lengths_mix = lax.dynamic_index_in_dim(seq_lengths, i // reps, 0, keepdims=False)
    in_w, out_w = in_weight[0], out_weight[0]
    taps = conv_weight[0].T
    skip_cols = row(jnp.repeat(skip_gain[0], HEAD_DIM))
    mixer_params = (taps, conv_bias, step_bias, log_decay, skip_cols, group_gain)
    projected, mixer_y, mixer_low, mixer_part = mixer_fwd(lengths_mix, normed, in_w, *mixer_params, out_w)
    global_out = mix_out(n, mpn, mixer_part.reshape(n, patches, dim), global_in)
    attn_in, qkv, heads, branch_part = att_fwd(
        byte_input, global_out, row(attn_gain), qkv_weight, attn_out_weight
    )
    own_bytes = lax.dynamic_index_in_dim(byte_input, j, 0, keepdims=False)
    own_global = lax.dynamic_index_in_dim(global_out, j, 0, keepdims=False)
    after, ffn_rows = after_att(n, mpn, branch_part, own_bytes, own_global, row(ffn_gain))
    down_part, ffn_in_part, ffn_grad_part = ffn(ffn_rows, grad_rows, weight_cols)
    ffn_grad = lax.psum_scatter(ffn_grad_part, "mp", scatter_dimension=1, tiled=True)
    after_grad, branch, block_low, ffn_gain_part = ffn_back(
        n, mpn, ffn_in_part, down_part, after, own_grad, valid, row(ffn_gain)
    )
    att_part, qkv_grad_part, out_grad_part = att_bwd(branch, attn_in, qkv, heads, qkv_weight, attn_out_weight)
    qkv_grad = lax.psum_scatter(qkv_grad_part, "dp", scatter_dimension=1, tiled=True)
    attn_out_grad = lax.psum_scatter(out_grad_part, "dp", scatter_dimension=1, tiled=True)
    block_cols = block_low.reshape(patch_len * patches, mpn, part_cols).swapaxes(0, 1)
    local, block_all, global_grad, g_mixer, attn_gain_part = att_back(
        n, mpn, att_part, own_bytes, own_global, after_grad, block_cols, row(attn_gain)
    )
    rank = i % reps
    normed_half = lax.dynamic_slice_in_dim(normed, rank * (dim // reps), dim // reps, 1)
    low_half = lax.dynamic_slice_in_dim(mixer_low, rank * (GROUP_WIDTH // reps), GROUP_WIDTH // reps, 1)
    normed_part, in_part, out_part, small_part = mixer_bwd(
        lengths_mix, g_mixer.reshape(n * patches, dim), normed_half, projected, mixer_y, low_half,
        in_w, *mixer_params, out_w,
    )
    gains_part = jnp.concatenate(
        [jnp.zeros((1, dim), f32), attn_gain_part, ffn_gain_part, jnp.zeros((5, dim), f32)], axis=0
    )
    everyone, in_grad, out_w_grad, small, gains = mix_back(
        n, mpn, normed_part.reshape(n, patches, dim), global_in, global_grad, row(norm_in_gain),
        in_part.reshape(share, dim // n, in_w.shape[1]), out_part.reshape(share, GROUP_WIDTH // n, dim),
        small_part, gains_part,
    )
    own_all = lax.dynamic_index_in_dim(everyone, i, 0, keepdims=False)
    patch_grad, input_grad = patch_back(
        everyone.reshape(n * micro * patches, dim), own_all.reshape(micro * patches, dim), bytes_part, pw,
        local.reshape(micro, positions, patches, dim),
    )

    block = block_all.reshape(micro, patch_len, patches, part_cols).swapaxes(1, 2)
    block = block.reshape(micro, patches * patch_len, part_cols)

    def mine(array, axis):
        size = array.shape[axis] // n
        return lax.dynamic_slice_in_dim(array, i * size, size, axis)

    conv_w_grad = mine(small[:CONV].T[None], 1)
    return (
        block,
        input_grad,
        patch_grad.reshape(positions, feature, dim),
        mine(gains[0], 0),
        in_grad[None],
        conv_w_grad,
        mine(small[CONV : CONV + 1], 1),
        small[CONV + 3 : CONV + 4, :GROUP_HEADS],
        small[CONV + 4 : CONV + 5, :GROUP_HEADS],
        jnp.sum(small[CONV + 2, :GROUP_WIDTH].reshape(1, GROUP_HEADS, HEAD_DIM), axis=2),
        mine(small[CONV + 1 : CONV + 2, :GROUP_WIDTH], 1),
        out_w_grad[None],
        mine(gains[1], 0),
        qkv_grad.astype(f32),
        attn_out_grad.astype(f32),
        mine(gains[2], 0),
        ffn_grad.astype(f32),
    )


def solution(mesh):
    in_specs = (
        P(None, "dp", None),
        P(),
        P("mp", None, None),
        P(),
        P("mp", None, None),
        P("mp", None, None),
        P("mp", None),
        P("mp", None),
        P("mp", None),
        P("mp", None),
        P("mp", None),
        P("mp", None, None),
        P(),
        P(None, None, "mp"),
        P("mp", None),
        P(),
        P(None, "mp", "dp"),
        P(None, "dp", None),
    )
    out_specs = (
        P(None, "dp", "mp"),
        P(None, "dp", "mp"),
        P("mp", "dp", None),
        P("dp"),
        P("mp", "dp", None),
        P("mp", "dp", None),
        P("mp", "dp"),
        P("mp", None),
        P("mp", None),
        P("mp", None),
        P("mp", "dp"),
        P("mp", "dp", None),
        P("dp"),
        P(None, "dp", "mp"),
        P("mp", "dp"),
        P("dp"),
        P(None, "mp", "dp"),
    )
    return jax.shard_map(body, mesh=mesh, in_specs=in_specs, out_specs=out_specs, check_vma=False)
```

```python
from functools import partial
from types import SimpleNamespace

import jax
import jax.numpy as jnp
from jax import lax
from jax.experimental import pallas as pl
from jax.experimental.pallas import tpu as pltpu
from jax.sharding import PartitionSpec as P

STATE = 128
CONV = 4
SEQS = 3
GROUP_WIDTH = 512
GROUP_HEADS = 8
HEAD_DIM = 64
ATT_DIM = 64
CONV_CH = 768

norm_eps = 1e-06
highest = lax.Precision.HIGHEST
large_negative = -1e30
f32 = jnp.float32
bf16 = jnp.bfloat16
MESH = pl.DeviceIdType.MESH
VMEM = pl.BlockSpec(memory_space=pltpu.VMEM)
ANY = pl.BlockSpec(memory_space=pl.ANY)
SMEM = pl.BlockSpec(memory_space=pltpu.SMEM)
DMA = pltpu.SemaphoreType.DMA
WEIGHT_CUTS = 4
GRAD_CUTS = 4
SPILL_BYTES = 4 * 2**20


def dot(a, b, dims=((1,), (0,)), precision=None):
    return lax.dot_general(
        a, b, (dims, ((), ())), preferred_element_type=f32, precision=precision
    )


def inv_rms(values):
    return lax.rsqrt(jnp.mean(values * values, axis=-1, keepdims=True) + norm_eps)


def rms_back(values, gain, upstream):
    scale = inv_rms(values)
    weighted = upstream * gain
    inner = jnp.mean(weighted * values, axis=-1, keepdims=True)
    back = scale * weighted - values * (inner * scale * scale * scale)
    return back, upstream * (values * scale)


def silu_pair(values):
    sig = jax.nn.sigmoid(values)
    return values * sig, sig * (1.0 + values * (1.0 - sig))


def rcopy(src, dst, send_sem, recv_sem, dp, mp):
    return pltpu.make_async_remote_copy(
        src_ref=src,
        dst_ref=dst,
        send_sem=send_sem,
        recv_sem=recv_sem,
        device_id={"dp": dp, "mp": mp},
        device_id_type=MESH,
    )


def greet(barrier, dp, mp):
    pl.semaphore_signal(barrier, inc=1, device_id={"dp": dp, "mp": mp}, device_id_type=MESH)


def plain_params(mib=56):
    return pltpu.CompilerParams(vmem_limit_bytes=mib * 2**20)


def remote_params(cid, mib=40):
    return pltpu.CompilerParams(
        collective_id=cid, has_side_effects=True, vmem_limit_bytes=mib * 2**20
    )


def launch(name, kernel, ins, outs, scratch, params):
    names = [*ins, *outs, *scratch]

    def run(*refs):
        kernel(SimpleNamespace(**dict(zip(names, refs))))

    results = pl.pallas_call(
        run,
        out_shape=tuple(jax.ShapeDtypeStruct(shape, dtype) for shape, dtype, _ in outs.values()),
        in_specs=[spec for _, spec in ins.values()],
        out_specs=tuple(spec for _, _, spec in outs.values()),
        scratch_shapes=list(scratch.values()),
        compiler_params=params,
        name=name,
    )(*[array for array, _ in ins.values()])
    return SimpleNamespace(**dict(zip(outs, results)))


def place_of(n, mpn):
    i, j = lax.axis_index("dp"), lax.axis_index("mp")
    reps = n // mpn
    return SimpleNamespace(
        n=n, mpn=mpn, i=i, j=j, reps=reps, share=n // reps, half=n // 2,
        m=i // reps, h=i % reps, c=i % 2, mine=i // 2, other=i + 1 - 2 * (i % 2), inside=i // reps == j,
    )


def greet_all(p, barrier):
    for d in range(1, p.mpn):
        greet(barrier, p.i, (p.j + d) % p.mpn)
    for d in range(1, p.n):
        greet(barrier, (p.i + d) % p.n, p.j)
    for s in range(p.n):
        @pl.when(jnp.logical_not((s == p.i) & p.inside))
        def _():
            greet(barrier, s, p.m)
    for h in range(p.reps):
        for t in range(p.mpn):
            @pl.when(jnp.logical_not((p.j * p.reps + h == p.i) & (t == p.j)))
            def _():
                greet(barrier, p.j * p.reps + h, t)
    return p.mpn + 3 * p.n - 2 - 2 * p.inside.astype(jnp.int32)


def mp_start(p, src, dst, ss, rs):
    copies = []
    for d in range(1, p.mpn):
        t = (p.j + d) % p.mpn
        copy = rcopy(src(t), dst(p.j), ss.at[t], rs.at[p.j], p.i, t)
        copy.start()
        copies.append(copy)
    return copies


def mp_wait(p, d, dst, ss, rs):
    s = (p.j + d) % p.mpn
    rcopy(dst(s), dst(s), ss.at[s], rs.at[s], p.i, s).wait_recv()
    return s


def plane_start(p, own, slot, ss, rs, ssr):
    copies = []
    for d in range(1, p.half):
        q = (p.mine + d) % p.half
        copies.append(rcopy(own, slot(p.i), ss.at[q], rs.at[p.i], q * 2 + p.c, p.j))
    copies.append(rcopy(own, slot(p.i), ssr.at[p.mine], rs.at[p.i], p.other, p.j))
    for copy in copies:
        copy.start()
    return copies


def plane_relay(p, slot, ss, rs, ssr):
    copies = []
    for d in range(1, p.half):
        q = (p.mine + p.half - d) % p.half
        s = q * 2 + p.c
        rcopy(slot(s), slot(s), ss.at[q], rs.at[s], s, p.j).wait_recv()
        copy = rcopy(slot(s), slot(s), ssr.at[q], rs.at[s], p.other, p.j)
        copy.start()
        copies.append(copy)
    return copies


def plane_finish(p, slot, rs, ssr):
    for q in range(p.half):
        s = q * 2 + 1 - p.c
        rcopy(slot(s), slot(s), ssr.at[q], rs.at[s], p.other, p.j).wait_recv()


def reduce_start(p, block, pre, ssa, rsa):
    copies = []
    for d in range(1, p.half + 1):
        q = (p.mine + d) % p.half
        copy = rcopy(block(q * 2 + 1 - p.c), pre.at[q], ssa.at[q], rsa.at[q], p.other, p.j)
        copy.start()
        copies.append(copy)
    return copies


def cast_start(p, low, dst, ss, rs):
    for h in range(p.reps):
        for t in range(p.mpn):
            here = (p.j * p.reps + h == p.i) & (t == p.j)

            @pl.when(jnp.logical_not(here))
            def _():
                rcopy(low, dst.at[p.i], ss.at[h * p.mpn + t], rs.at[p.i], p.j * p.reps + h, t).start()

            @pl.when(here)
            def _():
                dst[p.i] = low[...]


def cast_wait(p, low, dst, ss, rs):
    for s in range(p.n):
        @pl.when(jnp.logical_not((s == p.i) & p.inside))
        def _():
            rcopy(low, dst.at[s], ss.at[0], rs.at[s], s, p.m).wait_recv()


def cast_sent(p, low, dst, ss, rs):
    for h in range(p.reps):
        for t in range(p.mpn):
            @pl.when(jnp.logical_not((p.j * p.reps + h == p.i) & (t == p.j)))
            def _():
                rcopy(low, dst.at[p.i], ss.at[h * p.mpn + t], rs.at[p.i], p.j * p.reps + h, t).wait_send()


def owner_copy(p, q, part, recv, ss, rs):
    block = q * p.reps + p.h
    return block, rcopy(part.at[block], recv.at[p.j], ss.at[q], rs.at[p.j], block, p.m)


def owner_start(p, part, recv, ss, rs):
    for q in range(p.share):
        block, copy = owner_copy(p, q, part, recv, ss, rs)

        @pl.when(jnp.logical_not((block == p.i) & p.inside))
        def _():
            copy.start()

    @pl.when(p.inside)
    def _():
        recv[p.j] = part[p.i]


def owner_wait(p, part, recv, ss, rs):
    for s in range(p.mpn):
        @pl.when(jnp.logical_not(p.inside & (s == p.j)))
        def _():
            rcopy(part.at[0], recv.at[s], ss.at[0], rs.at[s], p.j * p.reps + p.h, s).wait_recv()


def owner_sent(p, part, recv, ss, rs):
    for q in range(p.share):
        block, copy = owner_copy(p, q, part, recv, ss, rs)

        @pl.when(jnp.logical_not((block == p.i) & p.inside))
        def _():
            copy.wait_send()


class Bulk:
    def __init__(self, p, pieces):
        self.p, self.pieces, self.done, self.copies = p, pieces, 0, []

    def go(self, count):
        for src, dst, ss, rs in self.pieces[self.done : self.done + count]:
            self.copies += mp_start(self.p, src, dst, ss, rs)
        self.done += count

    def finish(self):
        self.go(len(self.pieces) - self.done)
        for src, dst, ss, rs in self.pieces:
            for d in range(1, self.p.mpn):
                mp_wait(self.p, d, dst, ss, rs)


def perm_matrix(rows, patches, per, limit):
    at = lax.broadcasted_iota(jnp.int32, (rows, rows), 0)
    source = lax.broadcasted_iota(jnp.int32, (rows, rows), 1)
    return ((source == (at % patches) * per + at // patches) & (at % patches < limit)).astype(bf16)


def seg_starts(lengths, places):
    end0 = lengths[0]
    end1 = end0 + lengths[1]
    end2 = end1 + lengths[2]
    return jnp.where(
        places >= end2, end2, jnp.where(places >= end1, end1, jnp.where(places >= end0, end0, 0))
    )


def conv_taps(conv_in, pos, lag):
    moved = conv_in if lag == 0 else pltpu.roll(conv_in, lag, 0)
    return jnp.where(pos >= lag, moved, 0.0)


def mixer_state(lengths, projected, conv_weight, conv_bias, step_bias, log_decay):
    patches = projected.shape[0]
    places = lax.broadcasted_iota(jnp.int32, (patches, 1), 0)
    start = seg_starts(lengths, places)
    pos = places - start
    conv_in = projected[:, GROUP_WIDTH : GROUP_WIDTH + CONV_CH]
    conv_out = conv_bias
    for lag in range(CONV):
        conv_out = conv_out + conv_taps(conv_in, pos, lag) * conv_weight[CONV - 1 - lag][None]
    step_raw = projected[:, GROUP_WIDTH + CONV_CH :] + step_bias
    step = jnp.maximum(step_raw, 0.0) + jnp.log1p(jnp.exp(-jnp.abs(step_raw)))
    logd = -step * jnp.exp(log_decay)
    across = lax.broadcasted_iota(jnp.int32, (patches, patches), 1)
    down = lax.broadcasted_iota(jnp.int32, (patches, patches), 0)
    mask = (across >= start) & (across <= down)
    running = dot(mask.astype(f32), logd, precision=highest)
    return pos, conv_in, conv_out, step_raw, step, logd, mask, running


def head_decay(mask, running, running_t, h):
    return jnp.exp(
        jnp.where(mask, running[:, h : h + 1] - running_t[h : h + 1, :], large_negative)
    )


def att_mask(rows, patches):
    across = lax.broadcasted_iota(jnp.int32, (rows, rows), 1)
    down = lax.broadcasted_iota(jnp.int32, (rows, rows), 0)
    return (across % patches == down % patches) & (across <= down)


def soft_rows(mask, query, key):
    scores = dot(query, key, ((1,), (1,))) * ATT_DIM ** (-0.5)
    scores = jnp.where(mask, scores, large_negative)
    probs = jnp.exp(scores - jnp.max(scores, axis=1, keepdims=True))
    return probs / jnp.sum(probs, axis=1, keepdims=True)


def mixer_fwd(r, lengths, normed):
    projected = dot(normed, r.in_v[...], ((1,), (1,)))
    r.projected[...] = projected
    _, _, conv_out, _, step, _, mask, running = mixer_state(
        lengths, projected, r.taps[...], r.conv_bias[...], r.step_bias[...], r.log_decay[...]
    )
    act = conv_out * jax.nn.sigmoid(conv_out)
    inputs = act[:, GROUP_WIDTH : GROUP_WIDTH + STATE]
    outputs = act[:, GROUP_WIDTH + STATE :]
    inner = dot(outputs, inputs, ((1,), (1,)))
    running_t, step_t = running.T, step.T
    pair = 2 * HEAD_DIM
    lane = lax.broadcasted_iota(jnp.int32, (1, pair), 1)
    pieces = []
    for c in range(GROUP_WIDTH // pair):
        values = act[:, c * pair : (c + 1) * pair]
        got = []
        for h in (2 * c, 2 * c + 1):
            weights = head_decay(mask, running, running_t, h) * inner * step_t[h : h + 1, :]
            got.append(dot(weights, values))
        pieces.append(jnp.where(lane < HEAD_DIM, got[0], got[1]))
    y = jnp.concatenate(pieces, axis=1) + r.skip[...] * act[:, :GROUP_WIDTH]
    r.mixer_y[...] = y
    gate = projected[:, :GROUP_WIDTH]
    gated = y * (gate * jax.nn.sigmoid(gate))
    low = (gated * inv_rms(gated) * r.group_gain[...]).astype(bf16)
    r.mixer_low[...] = low
    return dot(low, r.out_v[...])


def forward_kernel(n, mpn, r):
    p = place_of(n, mpn)
    i, j = p.i, p.j
    micro, patches, own_cols = r.own.shape
    positions, dim = r.pw.shape[0], r.pw.shape[1]
    slabs = r.bytes_v.shape[2] // dim
    rows = slabs * patches
    features = r.bytes_part.shape[-1]
    loads = 0

    def local(src, dst):
        nonlocal loads
        copy = pltpu.make_async_copy(src, dst, r.sem_load.at[loads])
        loads += 1
        copy.start()
        return copy

    load_own = local(r.byte_input.at[:, :, pl.ds(pl.multiple_of(j * own_cols, 128), own_cols)], r.own)
    load_pw = [local(r.patch_weight.at[k], r.pw.at[k]) for k in range(positions)]
    load_grad = local(r.out_grad.at[j], r.grad_raw)
    load_in = local(r.in_weight, r.in_v)
    load_out = local(r.out_weight, r.out_v)
    load_bytes = local(r.byte_input, r.bytes_v)
    load_qkv = local(r.qkv_weight, r.qkv_v)
    keep_w = local(r.ffn_weight, r.w_all.at[j])

    barrier = pltpu.get_barrier_semaphore()
    count = greet_all(p, barrier)
    load_own.wait()
    sums = None
    for k in range(positions):
        load_pw[k].wait()
        term = dot(r.own[:, :, k * dim : (k + 1) * dim].reshape(micro * patches, dim), r.pw[k])
        sums = term if sums is None else sums + term
    for t in range(micro):
        r.part[t] = sums[t * patches : (t + 1) * patches]
    load_grad.wait()
    lengths = lambda m: (r.seq_lengths[m, 0], r.seq_lengths[m, 1], r.seq_lengths[m, 2])
    l0, l1, l2 = lengths(j)
    perm = perm_matrix(rows, patches, slabs, l0 + l1 + l2 - i * patches)
    r.own_grad[...] = dot(perm, r.grad_raw[...]).astype(bf16)
    pl.semaphore_wait(barrier, count)

    sent = mp_start(p, lambda t: r.part.at[t], lambda s: r.recv.at[s], r.ss1, r.rs1)
    grad_slot = lambda s: r.grad_rows.at[s]
    sent += plane_start(p, r.own_grad, grad_slot, r.ssg, r.rsg, r.ssgr)
    keep_grad = local(r.own_grad, r.grad_rows.at[i])
    step = r.w_all.shape[2] // WEIGHT_CUTS
    pieces = []
    for w in range(3):
        for k in range(WEIGHT_CUTS):
            at = slice(k * step, (k + 1) * step)
            pieces.append((
                lambda t, w=w, at=at: r.ffn_weight.at[w, at],
                lambda s, w=w, at=at: r.w_all.at[s, w, at],
                r.ssw.at[w, k],
                r.rsw.at[w, k],
            ))
    bulk = Bulk(p, pieces)
    bulk.go(1)
    total = r.part[j]
    for d in range(1, mpn):
        total = total + r.recv[mp_wait(p, d, lambda s: r.recv.at[s], r.ss1, r.rs1)]
    r.global_in[...] = total
    r.low[...] = (total * inv_rms(total) * r.norm_in_gain[...]).astype(bf16)
    cast_start(p, r.low, r.normed, r.ss2, r.rs2)
    for d in range(1, n):
        t = (i + d) % n
        for k in range(positions):
            first = k * dim + t * (dim // n) // features * features
            copy = rcopy(
                r.own.at[:, :, pl.ds(pl.multiple_of(first, 128), features)],
                r.bytes_part.at[i, k], r.ssb.at[t, k], r.rsb.at[i, k], t, j,
            )
            copy.start()
            sent.append(copy)
    kept = []
    for k in range(positions):
        first = k * dim + i * (dim // n) // features * features
        kept.append(local(r.own.at[:, :, pl.ds(pl.multiple_of(first, 128), features)], r.bytes_part.at[i, k]))
    piece_rows = r.ao_full.shape[2]
    ao_own = r.out_proj.at[pl.ds(pl.multiple_of(i * piece_rows, piece_rows), piece_rows)]
    ao_slot = lambda s: r.ao_full.at[i, s]
    kept_ao = local(ao_own, r.ao_full.at[i, j])
    bulk.go(1)
    load_in.wait()
    load_out.wait()
    cast_wait(p, r.low, r.normed, r.ss2, r.rs2)
    sent += mp_start(p, lambda t: ao_own, ao_slot, r.ssa, r.rsa)
    bulk.go(1)

    part = mixer_fwd(r, lengths(p.m), r.normed[...].reshape(n * patches, dim))
    for b in range(n):
        r.mix_part[b] = part[b * patches : (b + 1) * patches]
    owner_start(p, r.mix_part, r.mix_recv, r.ss3, r.rs3)
    kept_ao.wait()
    for d in range(1, mpn):
        mp_wait(p, d, ao_slot, r.ssa, r.rsa)
    ao_block = lambda s: r.ao_full.at[s]
    sent += plane_start(p, r.ao_full.at[i], ao_block, r.ssap, r.rsap, r.ssar)
    owner_wait(p, r.mix_part, r.mix_recv, r.ss3, r.rs3)
    total = r.global_in[...]
    for s in range(mpn):
        total = total + r.mix_recv[s]
    r.global_own[...] = total
    r.patch_all[j] = total
    sent += mp_start(p, lambda t: r.global_own, lambda s: r.patch_all.at[s], r.ss4, r.rs4)
    bulk.go(2)
    sent += plane_relay(p, grad_slot, r.ssg, r.rsg, r.ssgr)
    load_bytes.wait()
    load_qkv.wait()
    for d in range(1, mpn):
        mp_wait(p, d, lambda s: r.patch_all.at[s], r.ss4, r.rs4)

    mask = att_mask(rows, patches)
    pair = 2 * ATT_DIM
    width = r.qkv_v.shape[2]
    lane = lax.broadcasted_iota(jnp.int32, (1, pair), 1)

    def heads_copy(t):
        return rcopy(r.heads.at[t], r.heads_own.at[j], r.ss5.at[t], r.rs5.at[j], i, t)

    def one_micro(d, _):
        m = (j + d) % mpn
        for k in range(slabs):
            here = r.bytes_v[m, :, k * dim : (k + 1) * dim].astype(f32) + r.patch_all[m]
            r.attn_in[m, k * patches : (k + 1) * patches, :] = (
                here * inv_rms(here) * r.attn_gain[...]
            ).astype(bf16)
        got = r.attn_in[m]
        for w in range(3):
            r.qkv[w, m] = dot(got, r.qkv_v[w]).astype(bf16)
        for c in range(width // pair):
            at = slice(c * pair, (c + 1) * pair)
            query, key, value = r.qkv[0, m, :, at], r.qkv[1, m, :, at], r.qkv[2, m, :, at]
            res = []
            for own in (lane < ATT_DIM, lane >= ATT_DIM):
                probs = soft_rows(mask, jnp.where(own, query, jnp.zeros_like(query)), key)
                res.append(dot(probs.astype(bf16), value))
            r.heads[m, :, at] = jnp.where(lane < ATT_DIM, res[0], res[1]).astype(bf16)

        @pl.when(d < mpn)
        def _():
            heads_copy(m).start()

        return 0

    lax.fori_loop(1, mpn + 1, one_micro, 0)
    bulk.go(len(pieces))
    r.heads_own[j] = r.heads[j]
    sent += plane_relay(p, ao_block, r.ssap, r.rsap, r.ssar)
    plane_finish(p, ao_block, r.rsap, r.ssar)
    for k in range(slabs):
        here = r.bytes_v[j, :, k * dim : (k + 1) * dim].astype(f32) + r.global_own[...]
        r.after[k * patches : (k + 1) * patches, :] = here
    branch = None
    for d in range(mpn):
        s = j if d == 0 else mp_wait(p, d, lambda s: r.heads_own.at[s], r.ss5, r.rs5)
        for b in range(n):
            at = slice(b * piece_rows, (b + 1) * piece_rows)
            r.ao_sorted[s, at, :] = r.ao_full[b, s]
        term = dot(r.heads_own[s], r.ao_sorted[s])
        branch = term if branch is None else branch + term
    after = r.after[...] + branch
    r.after[...] = after
    r.ffn_own[...] = (after * inv_rms(after) * r.ffn_gain[...]).astype(bf16)
    row_slot = lambda s: r.ffn_rows.at[s]
    sent += plane_start(p, r.ffn_own, row_slot, r.ssf, r.rsf, r.ssfr)
    keep_rows = local(r.ffn_own, r.ffn_rows.at[i])
    plane_finish(p, grad_slot, r.rsg, r.ssgr)
    for d in range(1, n):
        s = (i + d) % n
        for k in range(positions):
            rcopy(r.bytes_part.at[s, k], r.bytes_part.at[s, k], r.ssb.at[s, k], r.rsb.at[s, k], s, j).wait_recv()
    sent += plane_relay(p, row_slot, r.ssf, r.rsf, r.ssfr)
    plane_finish(p, row_slot, r.rsf, r.ssfr)
    bulk.finish()
    for copy in [keep_w, keep_grad, keep_rows] + kept:
        copy.wait()
    for copy in sent + bulk.copies:
        copy.wait_send()
    cast_sent(p, r.low, r.normed, r.ss2, r.rs2)
    owner_sent(p, r.mix_part, r.mix_recv, r.ss3, r.rs3)
    for d in range(1, mpn):
        heads_copy((j + d) % mpn).wait_send()


def forward(n, mpn, a):
    micro, patches, cols = a.byte_input.shape
    dim = a.norm_in_gain.shape[1]
    slabs = cols // dim
    rows = patches * slabs
    positions = a.patch_weight.shape[0]
    width = a.qkv_weight.shape[2]
    hidden = a.ffn_weight.shape[2]
    columns = a.in_weight.shape[0]
    features = max(dim // n, 128)
    ao_rows = a.attn_out_weight.shape[0]
    piece = ao_rows // n
    half = n // 2
    seq = n * patches
    ins = dict(
        seq_lengths=(a.seq_lengths, SMEM),
        byte_input=(a.byte_input, ANY), patch_weight=(a.patch_weight, ANY), out_grad=(a.out_grad, ANY),
        in_weight=(a.in_weight, ANY), out_weight=(a.out_weight, ANY), qkv_weight=(a.qkv_weight, ANY),
        out_proj=(a.attn_out_weight, ANY), ffn_weight=(a.ffn_weight, ANY),
        norm_in_gain=(a.norm_in_gain, VMEM), taps=(a.taps, VMEM), conv_bias=(a.conv_bias, VMEM),
        step_bias=(a.step_bias, VMEM), log_decay=(a.log_decay, VMEM), skip=(a.skip, VMEM),
        group_gain=(a.group_gain, VMEM), attn_gain=(a.attn_gain, VMEM), ffn_gain=(a.ffn_gain, VMEM),
    )
    outs = dict(
        grad_rows=((n, rows, dim), bf16, ANY),
        ffn_rows=((n, rows, dim), bf16, ANY),
        w_all=((mpn,) + a.ffn_weight.shape, bf16, ANY),
        bytes_part=((n, positions, micro, patches, features), bf16, ANY),
        own_grad=((rows, dim), bf16, VMEM),
        after=((rows, dim), f32, VMEM),
        heads_own=((mpn, rows, width), bf16, VMEM),
        qkv=((3, micro, rows, width), bf16, VMEM),
        attn_in=((micro, rows, dim), bf16, VMEM),
        ao_sorted=((mpn, ao_rows, dim), bf16, VMEM),
        global_in=((patches, dim), f32, VMEM),
        global_own=((patches, dim), f32, VMEM),
        normed=((n, patches, dim), bf16, VMEM),
        projected=((seq, columns), f32, VMEM),
        mixer_y=((seq, GROUP_WIDTH), f32, VMEM),
        mixer_low=((seq, GROUP_WIDTH), bf16, VMEM),
    )
    scratch = dict(
        own=pltpu.VMEM((micro, patches, positions * dim), bf16),
        pw=pltpu.VMEM(a.patch_weight.shape, bf16),
        grad_raw=pltpu.VMEM((rows, dim), bf16),
        in_v=pltpu.VMEM(a.in_weight.shape, bf16),
        out_v=pltpu.VMEM(a.out_weight.shape, bf16),
        bytes_v=pltpu.VMEM(a.byte_input.shape, bf16),
        qkv_v=pltpu.VMEM(a.qkv_weight.shape, bf16),
        part=pltpu.VMEM((micro, patches, dim), f32),
        recv=pltpu.VMEM((mpn, patches, dim), f32),
        low=pltpu.VMEM((patches, dim), bf16),
        ao_full=pltpu.VMEM((n, mpn, piece, dim), bf16),
        mix_part=pltpu.VMEM((n, patches, dim), f32),
        mix_recv=pltpu.VMEM((mpn, patches, dim), f32),
        patch_all=pltpu.VMEM((mpn, patches, dim), f32),
        heads=pltpu.VMEM((micro, rows, width), bf16),
        ffn_own=pltpu.VMEM((rows, dim), bf16),
        sem_load=DMA((16,)),
        ss1=DMA((mpn,)), rs1=DMA((mpn,)), ss2=DMA((n,)), rs2=DMA((n,)), ss3=DMA((mpn,)), rs3=DMA((mpn,)),
        ss4=DMA((mpn,)), rs4=DMA((mpn,)), ss5=DMA((mpn,)), rs5=DMA((mpn,)),
        ssg=DMA((half,)), rsg=DMA((n,)), ssgr=DMA((half,)),
        ssf=DMA((half,)), rsf=DMA((n,)), ssfr=DMA((half,)),
        ssb=DMA((n, positions)), rsb=DMA((n, positions)),
        ssa=DMA((mpn,)), rsa=DMA((mpn,)), ssap=DMA((half,)), rsap=DMA((n,)), ssar=DMA((half,)),
        ssw=DMA((3, WEIGHT_CUTS, mpn)), rsw=DMA((3, WEIGHT_CUTS, mpn)),
    )
    return launch("forward", partial(forward_kernel, n, mpn), ins, outs, scratch, remote_params(0, 60))


def ffn_kernel(rows_in, grads_in, parts, down_out, in_grad, weight_grad, weight, gate_low, up_low, hidden_low):
    blocks, rows, dim = rows_in.shape
    per = parts.shape[2]
    for s in range(parts.shape[0]):
        for w in range(3):
            weight[w, s * per : (s + 1) * per, :] = parts[s, w]

    def step(b, _):
        here, up = rows_in[b], grads_in[b]
        gate = dot(here, weight[0])
        other = dot(here, weight[1])
        act, slope = silu_pair(gate)
        hidden = (act * other).astype(bf16)
        hidden_low[b] = hidden
        down_out[b] = dot(hidden, weight[2], ((1,), (1,))).astype(bf16)
        hidden_grad = dot(up, weight[2])
        gate_grad = (hidden_grad * other * slope).astype(bf16)
        up_grad = (hidden_grad * act).astype(bf16)
        gate_low[b] = gate_grad
        up_low[b] = up_grad
        back = dot(gate_grad, weight[0], ((1,), (1,))) + dot(up_grad, weight[1], ((1,), (1,)))
        in_grad[b] = back.astype(bf16)
        return 0

    lax.fori_loop(0, blocks, step, 0)
    hidden = weight.shape[2]
    everything = rows_in[...].reshape(blocks * rows, dim)
    weight_grad[0] = dot(everything, gate_low[...].reshape(blocks * rows, hidden), ((0,), (0,))).astype(bf16)
    weight_grad[1] = dot(everything, up_low[...].reshape(blocks * rows, hidden), ((0,), (0,))).astype(bf16)
    weight_grad[2] = dot(
        grads_in[...].reshape(blocks * rows, dim), hidden_low[...].reshape(blocks * rows, hidden), ((0,), (0,))
    ).astype(bf16)


def ffn(rows_in, grads_in, parts):
    blocks, rows, dim = rows_in.shape
    hidden = parts.shape[3]
    return pl.pallas_call(
        ffn_kernel,
        out_shape=(
            jax.ShapeDtypeStruct((blocks, rows, dim), bf16),
            jax.ShapeDtypeStruct((blocks, rows, dim), bf16),
            jax.ShapeDtypeStruct((3, dim, hidden), bf16),
        ),
        in_specs=[VMEM] * 3,
        out_specs=(VMEM,) * 3,
        scratch_shapes=[pltpu.VMEM((3, dim, hidden), bf16)] + [pltpu.VMEM((blocks, rows, hidden), bf16)] * 3,
        compiler_params=plain_params(60),
        name="ffn",
    )(rows_in, grads_in, parts)


def mixer_bwd(r, p, lengths, upstream):
    projected = r.projected[...]
    patches = projected.shape[0]
    pos, conv_in, conv_out, step_raw, step, logd, mask, running = mixer_state(
        lengths, projected, r.taps[...], r.conv_bias[...], r.step_bias[...], r.log_decay[...]
    )
    act, act_slope = silu_pair(conv_out)
    inputs = act[:, GROUP_WIDTH : GROUP_WIDTH + STATE]
    outputs = act[:, GROUP_WIDTH + STATE :]
    inner = dot(outputs, inputs, ((1,), (1,)))
    running_t, step_t = running.T, step.T
    normed_grad = dot(upstream, r.out_v[...], ((1,), (1,)))
    y = r.mixer_y[...]
    gate = projected[:, :GROUP_WIDTH]
    gate_act, gate_slope = silu_pair(gate)
    gated_grad, gain_rows = rms_back(y * gate_act, r.group_gain[...], normed_grad)
    y_grad = gated_grad * gate_act
    gate_grad = gated_grad * y * gate_slope
    values = act[:, :GROUP_WIDTH]
    skip_cols = jnp.sum(y_grad * values, axis=0, keepdims=True)
    pair = 2 * HEAD_DIM
    lane = lax.broadcasted_iota(jnp.int32, (1, pair), 1)
    inner_grad = jnp.zeros_like(inner)
    value_pieces, row_sums, col_sums = [], [], []
    for c in range(GROUP_WIDTH // pair):
        at = slice(c * pair, (c + 1) * pair)
        got = []
        for h in (2 * c, 2 * c + 1):
            own = (lane < HEAD_DIM) if h % 2 == 0 else (lane >= HEAD_DIM)
            mine = jnp.where(own, y_grad[:, at], 0.0)
            decay = head_decay(mask, running, running_t, h)
            step_row = step_t[h : h + 1, :]
            weight_grad = dot(mine, values[:, at], ((1,), (1,))) * decay
            scaled = weight_grad * step_row
            inner_grad = inner_grad + scaled
            col_sums.append(jnp.sum(weight_grad * inner, axis=0, keepdims=True))
            row_sums.append(jnp.sum(scaled * inner, axis=1, keepdims=True))
            weights = decay * inner * step_row
            got.append(dot(weights, mine, ((0,), (0,))))
        value_pieces.append(got[0] + got[1])
    values_grad = jnp.concatenate(value_pieces, axis=1) + r.skip[...] * y_grad
    inputs_grad = dot(inner_grad, outputs, ((0,), (0,)))
    outputs_grad = dot(inner_grad, inputs)
    col_grad = jnp.concatenate(col_sums, axis=0).T
    running_grad = jnp.concatenate(row_sums, axis=1) - col_grad * step
    logd_grad = dot(mask.astype(f32), running_grad, ((0,), (0,)), precision=highest)
    step_grad = (col_grad - logd_grad * jnp.exp(r.log_decay[...])) * jax.nn.sigmoid(step_raw)
    conv_grad = jnp.concatenate([values_grad, inputs_grad, outputs_grad], axis=1) * act_slope
    conv_in_grad = jnp.zeros_like(conv_grad)
    small = r.small_part
    small[...] = jnp.zeros(small.shape, f32)
    for lag in range(CONV):
        small[CONV - 1 - lag : CONV - lag, :] = jnp.sum(
            conv_grad * conv_taps(conv_in, pos, lag), axis=0, keepdims=True
        )
        kept = jnp.where(pos >= lag, conv_grad, 0.0) * r.taps[CONV - 1 - lag : CONV - lag, :]
        conv_in_grad = conv_in_grad + (kept if lag == 0 else pltpu.roll(kept, patches - lag, 0))
    small[CONV : CONV + 1, :] = jnp.sum(conv_grad, axis=0, keepdims=True)
    small[CONV + 1 : CONV + 2, :GROUP_WIDTH] = jnp.sum(gain_rows, axis=0, keepdims=True)
    small[CONV + 2 : CONV + 3, :GROUP_WIDTH] = skip_cols
    small[CONV + 3 : CONV + 4, :GROUP_HEADS] = jnp.sum(step_grad, axis=0, keepdims=True)
    small[CONV + 4 : CONV + 5, :GROUP_HEADS] = jnp.sum(logd_grad * logd, axis=0, keepdims=True)
    return jnp.concatenate([gate_grad, conv_in_grad, step_grad], axis=1).astype(bf16)


def backward_kernel(n, mpn, spill, r):
    p = place_of(n, mpn)
    i, j = p.i, p.j
    micro, rows, dim = r.attn_in.shape
    patches = r.global_own.shape[0]
    slabs = rows // patches
    width = r.qkv_v.shape[2]
    feature = dim // n
    per = dim // mpn
    loads = 0

    def local(src, dst):
        nonlocal loads
        copy = pltpu.make_async_copy(src, dst, r.sem_load.at[loads])
        loads += 1
        copy.start()
        return copy

    def read(view):
        if not spill:
            return view[...]
        copy = pltpu.make_async_copy(view, r.stage.at[0], r.sem_stage.at[0])
        copy.start()
        copy.wait()
        return r.stage[0]

    def write(view, value):
        if not spill:
            view[...] = value
            return
        r.stage[1] = value
        copy = pltpu.make_async_copy(r.stage.at[1], view, r.sem_stage.at[1])
        copy.start()
        copy.wait()

    keep_w = local(r.w_grad.at[:, pl.ds(pl.multiple_of(j * per, per), per)], r.g_recv.at[j])
    load_bytes = local(r.byte_input.at[j], r.own_bytes)
    load_qkv = local(r.qkv_weight, r.qkv_v)
    load_out = local(r.out_weight, r.out_v)
    load_in = local(r.in_weight, r.in_v)
    barrier = pltpu.get_barrier_semaphore()
    pl.semaphore_wait(barrier, greet_all(p, barrier))

    def reduction(block, value, pre, recv, ss, plain):
        ssa, rsa, ssb, rsb = (ss.at[k] for k in range(4))
        get = (lambda view: view[...]) if plain else read
        put = (lambda view, v: view.__setitem__(..., v)) if plain else write

        def spread():
            copies = []
            for d in range(1, p.half):
                q = (p.mine + d) % p.half
                rcopy(pre.at[q], pre.at[q], ssa.at[q], rsa.at[q], p.other, j).wait_recv()
                total = value(q * 2 + p.c).astype(f32)
                put(pre.at[q], (total + get(pre.at[q]).astype(f32)).astype(bf16))
                copy = rcopy(pre.at[q], recv.at[p.mine], ssb.at[q], rsb.at[p.mine], q * 2 + p.c, j)
                copy.start()
                copies.append(copy)
            return copies

        def finish():
            mine = p.mine
            rcopy(pre.at[mine], pre.at[mine], ssa.at[mine], rsa.at[mine], p.other, j).wait_recv()
            total = value(i).astype(f32)
            total = total + get(pre.at[mine]).astype(f32)
            for d in range(1, p.half):
                q = (mine + d) % p.half
                rcopy(recv.at[q], recv.at[q], ssb.at[q], rsb.at[q], q * 2 + p.c, j).wait_recv()
                total = total + get(recv.at[q]).astype(f32)
            return total

        return SimpleNamespace(
            start=lambda: reduce_start(p, block, pre, ssa, rsa), spread=spread, finish=finish
        )

    block_in = lambda s: r.in_part.at[s]
    block_down = lambda s: r.down_part.at[s]
    at_feature = lambda s: pl.ds(pl.multiple_of(s * feature, feature), feature)
    block_ao = lambda s: r.ao_part.at[at_feature(s)]
    block_qkv = lambda s: r.qkv_part.at[:, at_feature(s)]
    sum_in = reduction(block_in, lambda s: read(block_in(s)), r.in_pre, r.in_recv, r.ss_in, False)
    sum_down = reduction(block_down, lambda s: read(block_down(s)), r.down_pre, r.down_recv, r.ss_down, False)
    sum_ao = reduction(block_ao, lambda s: block_ao(s)[...], r.ao_pre, r.ao_recv, r.ss_ao, True)
    sum_qkv = reduction(block_qkv, lambda s: block_qkv(s)[...], r.qkv_pre, r.qkv_recv, r.ss_qkv, True)

    pieces = []
    step = per // GRAD_CUTS
    for w in range(3):
        for k in range(GRAD_CUTS):
            pieces.append((
                lambda t, w=w, k=k: r.w_grad.at[w, pl.ds(pl.multiple_of(t * per + k * step, step), step)],
                lambda s, w=w, k=k: r.g_recv.at[s, w, k * step : (k + 1) * step],
                r.ssw.at[w, k],
                r.rsw.at[w, k],
            ))
    bulk = Bulk(p, pieces)

    sent = sum_in.start()
    bulk.go(1)
    sent += sum_in.spread()
    sent += sum_down.start()
    bulk.go(2)
    load_bytes.wait()
    for k in range(slabs):
        r.local_in[k * patches : (k + 1) * patches, :] = (
            r.own_bytes[:, k * dim : (k + 1) * dim].astype(f32) + r.global_own[...]
        )
    after = r.after[...]
    back, gain_rows = rms_back(after, r.ffn_gain[...], sum_in.finish())
    after_grad = r.own_grad[...].astype(f32) + back
    r.after_grad[...] = after_grad
    r.gains[...] = jnp.zeros(r.gains.shape, f32)
    r.gains[2:3, :] = jnp.sum(gain_rows, axis=0, keepdims=True)
    r.branch[...] = after_grad.astype(bf16)
    for d in range(mpn):
        t = (j + d) % mpn
        r.up[t] = dot(r.branch[...], r.ao_sorted[t], ((1,), (1,))).astype(bf16)
    sent += mp_start(p, lambda t: r.up.at[t], lambda s: r.up_recv.at[s], r.ss1, r.rs1)
    r.up_recv[j] = r.up[j]
    sent += sum_down.spread()
    load_qkv.wait()

    mask = att_mask(rows, patches)
    pair = 2 * ATT_DIM
    lane = lax.broadcasted_iota(jnp.int32, (1, pair), 1)

    def part_copy(t):
        return rcopy(r.att_part.at[t], r.att_recv.at[j], r.ss2.at[t], r.rs2.at[j], i, t)

    def one_micro(d, _):
        m = (j + d) % mpn

        @pl.when(d > 0)
        def _():
            rcopy(r.up_recv.at[m], r.up_recv.at[m], r.ss1.at[m], r.rs1.at[m], i, m).wait_recv()

        for c in range(width // pair):
            at = slice(c * pair, (c + 1) * pair)
            query, key, value = r.qkv[0, m, :, at], r.qkv[1, m, :, at], r.qkv[2, m, :, at]
            up = r.up_recv[m, :, at]
            got = [[], [], []]
            for own in (lane < ATT_DIM, lane >= ATT_DIM):
                mine = jnp.where(own, query, jnp.zeros_like(query))
                probs = soft_rows(mask, mine, key)
                my_up = jnp.where(own, up, jnp.zeros_like(up))
                probs_grad = dot(my_up, value, ((1,), (1,)))
                inner = jnp.sum(probs * probs_grad, axis=1, keepdims=True)
                score_grad = (probs * (probs_grad - inner) * ATT_DIM ** (-0.5)).astype(bf16)
                got[0].append(dot(score_grad, key))
                got[1].append(dot(score_grad, mine, ((0,), (0,))))
                got[2].append(dot(probs.astype(bf16), my_up, ((0,), (0,))))
            r.qkv_low[0, m, :, at] = jnp.where(lane < ATT_DIM, got[0][0], got[0][1]).astype(bf16)
            r.qkv_low[1, m, :, at] = (got[1][0] + got[1][1]).astype(bf16)
            r.qkv_low[2, m, :, at] = (got[2][0] + got[2][1]).astype(bf16)
        total = dot(r.qkv_low[0, m], r.qkv_v[0], ((1,), (1,)))
        total = total + dot(r.qkv_low[1, m], r.qkv_v[1], ((1,), (1,)))
        total = total + dot(r.qkv_low[2, m], r.qkv_v[2], ((1,), (1,)))
        r.att_part[m] = total.astype(bf16)

        @pl.when(d > 0)
        def _():
            part_copy(m).start()

        return 0

    lax.fori_loop(0, mpn, one_micro, 0)

    everything = r.attn_in[...].reshape(micro * rows, dim)
    for w in range(3):
        r.qkv_part[w] = dot(
            everything, r.qkv_low[w].reshape(micro * rows, width), ((0,), (0,))
        ).astype(bf16)
    sent += sum_qkv.start()
    for t in range(mpn):
        r.ao_part[:, t * width : (t + 1) * width] = dot(
            r.branch[...], r.heads_own[t], ((0,), (0,))
        ).astype(bf16)
    sent += sum_ao.start()
    lengths = lambda m: (r.seq_lengths[m, 0], r.seq_lengths[m, 1], r.seq_lengths[m, 2])
    l0, l1, l2 = lengths(j)
    perm = perm_matrix(rows, patches, slabs, l0 + l1 + l2 - i * patches)
    block = (r.after[...] + sum_down.finish()).astype(bf16)
    block = dot(perm, block, ((0,), (0,))).astype(bf16)
    for t in range(mpn):
        r.block[t] = block[:, t * width : (t + 1) * width]
    sent += sum_qkv.spread()
    total = r.att_part[j].astype(f32)
    for d in range(1, mpn):
        total = total + r.att_recv[mp_wait(p, d, lambda s: r.att_recv.at[s], r.ss2, r.rs2)].astype(f32)
    back, gain_rows = rms_back(r.local_in[...], r.attn_gain[...], total)
    local_grad = r.after_grad[...] + back
    global_grad = local_grad[:patches]
    for k in range(1, slabs):
        global_grad = global_grad + local_grad[k * patches : (k + 1) * patches]
    r.global_grad[...] = global_grad
    r.low[...] = global_grad.astype(bf16)
    cast_start(p, r.low, r.mixer, r.ss3, r.rs3)
    r.gains[1:2, :] = jnp.sum(gain_rows, axis=0, keepdims=True)
    share_rows = rows // mpn
    for t in range(mpn):
        r.local[t] = local_grad[t * share_rows : (t + 1) * share_rows].astype(bf16)
    load_out.wait()
    load_in.wait()
    cast_wait(p, r.low, r.mixer, r.ss3, r.rs3)
    bulk.go(2)
    sent += sum_ao.spread()

    upstream = r.mixer[...].reshape(n * patches, dim)
    proj_grad = mixer_bwd(r, p, lengths(p.m), upstream)
    part = dot(proj_grad, r.in_v[...])
    for b in range(n):
        r.mix_part[b] = part[b * patches : (b + 1) * patches]
    owner_start(p, r.mix_part, r.mix_recv, r.ss4, r.rs4)

    half_cols = dim // p.reps
    normed_half = r.normed[:, :, pl.ds(pl.multiple_of(p.h * half_cols, half_cols), half_cols)]
    in_grad = dot(proj_grad, normed_half.reshape(n * patches, half_cols), ((0,), (0,))).astype(bf16)
    columns = in_grad.shape[0]
    for e in range(p.share):
        r.in_w_part[e, :columns, :] = in_grad[:, e * feature : (e + 1) * feature]
        r.in_w_part[e, columns:, :] = jnp.zeros((r.in_w_part.shape[1] - columns, feature), bf16)
    out_grad = dot(r.mixer_low[...], upstream, ((0,), (0,))).astype(bf16)
    group_rows = GROUP_WIDTH // n
    for e in range(n):
        r.out_w_part[e] = out_grad[e * group_rows : (e + 1) * group_rows]
    bundles = (
        (lambda e: r.in_w_part.at[e], r.in_w_recv, r.ssi, r.rsi),
        (lambda e: r.out_w_part.at[p.h * p.share + e], r.out_w_recv, r.sso, r.rso),
        (lambda e: r.small_part, r.small_recv, r.sss, r.rss),
    )

    def bundle_copies(e):
        return [
            rcopy(src(e), dst.at[p.m], ss.at[e], rs.at[p.m], p.h * p.share + e, j)
            for src, dst, ss, rs in bundles
        ]

    def start_bundles():
        for e in range(p.share):
            @pl.when(p.h * p.share + e != i)
            def _():
                for copy in bundle_copies(e):
                    copy.start()

            @pl.when(p.h * p.share + e == i)
            def _():
                r.in_w_recv[p.m] = r.in_w_part[e]
                r.out_w_recv[p.m] = r.out_w_part[i]
                r.small_recv[p.m] = r.small_part[...]

    owner_wait(p, r.mix_part, r.mix_recv, r.ss4, r.rs4)
    total = r.mix_recv[0]
    for s in range(1, mpn):
        total = total + r.mix_recv[s]
    back, gain_rows = rms_back(r.global_in[...], r.norm_in_gain[...], total)
    r.line[j] = (r.global_grad[...] + back).astype(bf16)
    sent += mp_start(p, lambda t: r.line.at[j], lambda s: r.line.at[s], r.ss5, r.rs5)
    r.gains[0:1, :] = jnp.sum(gain_rows, axis=0, keepdims=True)
    r.gains_line[j] = r.gains[...]
    sent += mp_start(p, lambda t: r.gains, lambda s: r.gains_line.at[s], r.ssg, r.rsg)
    sent += mp_start(p, lambda t: r.local.at[t], lambda s: r.local_all.at[s], r.ss6, r.rs6)
    sent += mp_start(p, lambda t: r.block.at[t], lambda s: r.block_all.at[s], r.ss7, r.rs7)
    r.local_all[j] = r.local[j]
    r.block_all[j] = r.block[j]
    for d in range(1, mpn):
        mp_wait(p, d, lambda s: r.line.at[s], r.ss5, r.rs5)
    slot = lambda s: r.plane.at[s]
    sent += plane_start(p, r.line, slot, r.ssp, r.rsp, r.sspr)
    keep_line = local(r.line, r.plane.at[i])
    start_bundles()
    r.qkv_sum[...] = sum_qkv.finish()
    ao = sum_ao.finish().astype(bf16)
    for t in range(mpn):
        r.ao[t] = ao[:, t * width : (t + 1) * width]
    sent += mp_start(p, lambda t: r.ao.at[t], lambda s: r.ao_all.at[s], r.ss8, r.rs8)
    r.ao_all[j] = r.ao[j]
    bulk.go(len(pieces))
    for d in range(1, mpn):
        mp_wait(p, d, lambda s: r.gains_line.at[s], r.ssg, r.rsg)
    r.gains_plane[p.mine] = sum(r.gains_line[s] for s in range(mpn))
    for d in range(1, p.half):
        q = (p.mine + d) % p.half
        copy = rcopy(
            r.gains_plane.at[p.mine], r.gains_plane.at[p.mine], r.ssh.at[q], r.rsh.at[p.mine], q * 2 + p.c, j
        )
        copy.start()
        sent.append(copy)
    sent += plane_relay(p, slot, r.ssp, r.rsp, r.sspr)
    for d in range(1, p.half):
        q = (p.mine + d) % p.half
        rcopy(r.gains_plane.at[q], r.gains_plane.at[q], r.ssh.at[q], r.rsh.at[q], q * 2 + p.c, j).wait_recv()
    r.gains_pair[0] = sum(r.gains_plane[s] for s in range(p.half))
    pair_copy = rcopy(r.gains_pair.at[0], r.gains_pair.at[1], r.ssq.at[0], r.rsq.at[0], p.other, j)
    pair_copy.start()
    plane_finish(p, slot, r.rsp, r.sspr)
    for d in range(1, mpn):
        mp_wait(p, d, lambda s: r.local_all.at[s], r.ss6, r.rs6)
        mp_wait(p, d, lambda s: r.block_all.at[s], r.ss7, r.rs7)
        mp_wait(p, d, lambda s: r.ao_all.at[s], r.ss8, r.rs8)
    group = i // p.share
    for t in range(mpn):
        @pl.when(t * p.reps + group != i)
        def _():
            for src, dst, ss, rs in bundles:
                rcopy(src(0), dst.at[t], ss.at[0], rs.at[t], t * p.reps + group, j).wait_recv()
    pair_copy.wait()
    r.gains_all[...] = r.gains_pair[0] + r.gains_pair[1]
    bulk.finish()
    keep_w.wait()
    keep_line.wait()
    for copy in sent + bulk.copies:
        copy.wait_send()
    cast_sent(p, r.low, r.mixer, r.ss3, r.rs3)
    owner_sent(p, r.mix_part, r.mix_recv, r.ss4, r.rs4)
    for d in range(1, mpn):
        part_copy((j + d) % mpn).wait_send()
    for e in range(p.share):
        @pl.when(p.h * p.share + e != i)
        def _():
            for copy in bundle_copies(e):
                copy.wait_send()


def backward(n, mpn, a):
    micro, rows, dim = a.attn_in.shape
    patches = a.global_own.shape[0]
    width = a.qkv_weight.shape[2]
    hidden = a.w_grad.shape[2]
    columns = a.in_weight.shape[0]
    half, share = n // 2, mpn
    feature = dim // n
    per = dim // mpn
    seq = n * patches
    spill = n * rows * dim * 2 > SPILL_BYTES
    ins = dict(seq_lengths=(a.seq_lengths, SMEM))
    for name in ("byte_input", "w_grad", "in_weight", "out_weight", "qkv_weight"):
        ins[name] = (getattr(a, name), ANY)
    for name in ("in_part", "down_part"):
        ins[name] = (getattr(a, name), ANY if spill else VMEM)
    for name in (
        "after", "own_grad", "heads_own", "qkv", "attn_in", "ao_sorted", "global_in", "global_own", "normed",
        "projected", "mixer_y", "mixer_low", "norm_in_gain", "taps", "conv_bias", "step_bias", "log_decay",
        "skip", "group_gain", "attn_gain", "ffn_gain",
    ):
        ins[name] = (getattr(a, name), VMEM)
    padded = (columns + 15) // 16 * 16
    outs = dict(
        g_recv=((mpn, 3, per, hidden), bf16, ANY),
        plane=((n, mpn, patches, dim), bf16, ANY),
        qkv_sum=((3, feature, width), f32, VMEM),
        ao_all=((mpn, feature, width), bf16, VMEM),
        in_w_recv=((mpn, padded, feature), bf16, VMEM),
        out_w_recv=((mpn, GROUP_WIDTH // n, dim), bf16, VMEM),
        small_recv=((mpn, 16, CONV_CH), f32, VMEM),
        gains_all=((8, dim), f32, VMEM),
        local_all=((mpn, rows // mpn, dim), bf16, VMEM),
        block_all=((mpn, rows, width), bf16, VMEM),
    )
    scratch = {}
    for name in ("in_pre", "in_recv", "down_pre", "down_recv"):
        if spill:
            outs[name] = ((half, rows, dim), bf16, ANY)
        else:
            scratch[name] = pltpu.VMEM((half, rows, dim), bf16)
    if spill:
        scratch.update(stage=pltpu.VMEM((2, rows, dim), bf16), sem_stage=DMA((2,)))
    scratch.update(
        own_bytes=pltpu.VMEM(a.byte_input.shape[1:], bf16),
        in_v=pltpu.VMEM(a.in_weight.shape, bf16),
        out_v=pltpu.VMEM(a.out_weight.shape, bf16),
        qkv_v=pltpu.VMEM(a.qkv_weight.shape, bf16),
        local_in=pltpu.VMEM((rows, dim), f32),
        after_grad=pltpu.VMEM((rows, dim), f32),
        branch=pltpu.VMEM((rows, dim), bf16),
        up=pltpu.VMEM((mpn, rows, width), bf16),
        up_recv=pltpu.VMEM((mpn, rows, width), bf16),
        qkv_low=pltpu.VMEM((3, micro, rows, width), bf16),
        att_part=pltpu.VMEM((micro, rows, dim), bf16),
        att_recv=pltpu.VMEM((mpn, rows, dim), bf16),
        qkv_part=pltpu.VMEM((3, dim, width), bf16),
        qkv_pre=pltpu.VMEM((half, 3, feature, width), bf16),
        qkv_recv=pltpu.VMEM((half, 3, feature, width), bf16),
        ao_part=pltpu.VMEM((dim, mpn * width), bf16),
        ao_pre=pltpu.VMEM((half, feature, mpn * width), bf16),
        ao_recv=pltpu.VMEM((half, feature, mpn * width), bf16),
        ao=pltpu.VMEM((mpn, feature, width), bf16),
        block=pltpu.VMEM((mpn, rows, width), bf16),
        local=pltpu.VMEM((mpn, rows // mpn, dim), bf16),
        low=pltpu.VMEM((patches, dim), bf16),
        global_grad=pltpu.VMEM((patches, dim), f32),
        mixer=pltpu.VMEM((n, patches, dim), bf16),
        mix_part=pltpu.VMEM((n, patches, dim), f32),
        mix_recv=pltpu.VMEM((mpn, patches, dim), f32),
        line=pltpu.VMEM((mpn, patches, dim), bf16),
        in_w_part=pltpu.VMEM((share, padded, feature), bf16),
        out_w_part=pltpu.VMEM((n, GROUP_WIDTH // n, dim), bf16),
        small_part=pltpu.VMEM((16, CONV_CH), f32),
        gains=pltpu.VMEM((8, dim), f32),
        gains_line=pltpu.VMEM((mpn, 8, dim), f32),
        gains_plane=pltpu.VMEM((half, 8, dim), f32),
        gains_pair=pltpu.VMEM((2, 8, dim), f32),
        sem_load=DMA((8,)),
        ss_in=DMA((4, half)), ss_down=DMA((4, half)), ss_ao=DMA((4, half)), ss_qkv=DMA((4, half)),
        ss1=DMA((mpn,)), rs1=DMA((mpn,)), ss2=DMA((mpn,)), rs2=DMA((mpn,)), ss3=DMA((n,)), rs3=DMA((n,)),
        ss4=DMA((mpn,)), rs4=DMA((mpn,)), ss5=DMA((mpn,)), rs5=DMA((mpn,)), ss6=DMA((mpn,)), rs6=DMA((mpn,)),
        ss7=DMA((mpn,)), rs7=DMA((mpn,)), ss8=DMA((mpn,)), rs8=DMA((mpn,)),
        ssp=DMA((half,)), rsp=DMA((n,)), sspr=DMA((half,)),
        ssg=DMA((mpn,)), rsg=DMA((mpn,)), ssh=DMA((half,)), rsh=DMA((half,)), ssq=DMA((1,)), rsq=DMA((1,)),
        ssi=DMA((share,)), rsi=DMA((mpn,)), sso=DMA((share,)), rso=DMA((mpn,)),
        sss=DMA((share,)), rss=DMA((mpn,)),
        ssw=DMA((3, GRAD_CUTS, mpn)), rsw=DMA((3, GRAD_CUTS, mpn)),
    )
    return launch("backward", partial(backward_kernel, n, mpn, spill), ins, outs, scratch, remote_params(1, 60))


def finish_kernel(r):
    i = lax.axis_index("dp")
    mpn, patches, dim = r.plane.shape[1:]
    n = r.plane.shape[0]
    features = r.bytes_part.shape[-1]
    positions = r.patch_weight.shape[0]
    feature = dim // n
    everyone = r.plane[...].reshape(n * mpn * patches, dim)
    own = r.plane[i].reshape(mpn * patches, dim)
    for k in range(positions):
        mine = r.bytes_part[:, k].reshape(n * mpn * patches, features)
        got = dot(mine, everyone, ((0,), (0,)))
        if features != feature:
            cut = features // feature
            got = sum(
                jnp.where(i % cut == e, got[e * feature : (e + 1) * feature], 0.0) for e in range(cut)
            )
        r.patch_grad[k] = got
        piece = dot(own, r.patch_weight[k], ((1,), (1,)))
        for m in range(mpn):
            r.input_grad[m, :, k * dim : (k + 1) * dim] = (
                piece[m * patches : (m + 1) * patches]
                + r.local_all[m, k * patches : (k + 1) * patches, :].astype(f32)
            )
    for w in range(3):
        r.ffn_grad[w] = sum(r.g_recv[s, w].astype(f32) for s in range(mpn))
    r.ao_grad[...] = sum(r.ao_all[s].astype(f32) for s in range(mpn)).T
    columns = r.in_grad.shape[0]
    r.in_grad[...] = sum(r.in_w_recv[s, :columns, :].astype(f32) for s in range(mpn))
    r.out_grad[...] = sum(r.out_w_recv[s].astype(f32) for s in range(mpn))
    small = sum(r.small_recv[s] for s in range(mpn))

    def chosen(values, size):
        whole = values.shape[1]
        at = lax.broadcasted_iota(jnp.int32, (whole, size), 0)
        want = lax.broadcasted_iota(jnp.int32, (whole, size), 1) + i * size
        return dot(values, (at == want).astype(f32), precision=highest)

    conv = chosen(small, CONV_CH // n)
    r.conv_w_grad[...] = conv[:CONV]
    r.conv_b_grad[...] = conv[CONV : CONV + 1]
    group = chosen(small[:, :GROUP_WIDTH], GROUP_WIDTH // n)
    r.group_grad[...] = group[CONV + 1 : CONV + 2]
    heads = lax.broadcasted_iota(jnp.int32, (GROUP_WIDTH, GROUP_HEADS), 0) // HEAD_DIM
    pick = heads == lax.broadcasted_iota(jnp.int32, (GROUP_WIDTH, GROUP_HEADS), 1)
    skip = dot(small[:, :GROUP_WIDTH], pick.astype(f32), precision=highest)
    r.skip_grad[...] = skip[CONV + 2 : CONV + 3]
    r.step_grad[...] = small[CONV + 3 : CONV + 4, :GROUP_HEADS]
    r.decay_grad[...] = small[CONV + 4 : CONV + 5, :GROUP_HEADS]
    gains = chosen(r.gains_all[...], feature)
    r.norm_in_grad[...] = gains[0:1]
    r.attn_gain_grad[...] = gains[1:2]
    r.ffn_gain_grad[...] = gains[2:3]
    r.qkv_grad[...] = r.qkv_sum[...]
    r.block_out[...] = r.block_all[...]


def finish(a):
    n, mpn, patches, dim = a.plane.shape
    positions = a.patch_weight.shape[0]
    feature = dim // n
    columns = a.in_weight.shape[0]
    names = (
        "plane", "bytes_part", "patch_weight", "local_all", "g_recv", "ao_all", "in_w_recv", "out_w_recv",
        "small_recv", "gains_all", "qkv_sum", "block_all",
    )
    row = lambda size: ((1, size), f32, VMEM)
    outs = dict(
        patch_grad=((positions, feature, dim), f32, VMEM),
        input_grad=((mpn, patches, positions * dim), f32, VMEM),
        ffn_grad=(a.g_recv.shape[1:], f32, VMEM),
        ao_grad=(a.ao_all.shape[:0:-1], f32, VMEM),
        in_grad=((columns, feature), f32, VMEM),
        out_grad=(a.out_w_recv.shape[1:], f32, VMEM),
        conv_w_grad=((CONV, CONV_CH // n), f32, VMEM),
        conv_b_grad=row(CONV_CH // n),
        group_grad=row(GROUP_WIDTH // n),
        skip_grad=row(GROUP_HEADS),
        step_grad=row(GROUP_HEADS),
        decay_grad=row(GROUP_HEADS),
        norm_in_grad=row(feature),
        attn_gain_grad=row(feature),
        ffn_gain_grad=row(feature),
        qkv_grad=(a.qkv_sum.shape, f32, VMEM),
        block_out=(a.block_all.shape, bf16, VMEM),
    )
    ins = {name: (getattr(a, name), VMEM) for name in names}
    return launch("finish", finish_kernel, ins, outs, {}, plain_params())


def body(
    byte_input,
    seq_lengths,
    patch_weight,
    norm_in_gain,
    in_weight,
    conv_weight,
    conv_bias,
    step_bias,
    log_decay,
    skip_gain,
    group_gain,
    out_weight,
    attn_gain,
    qkv_weight,
    attn_out_weight,
    ffn_gain,
    ffn_weight,
    out_grad,
):
    n, mpn = lax.axis_size("dp"), lax.axis_size("mp")
    row = lambda v: v.reshape(1, -1)
    a = SimpleNamespace(
        byte_input=byte_input,
        seq_lengths=seq_lengths,
        patch_weight=patch_weight,
        norm_in_gain=row(norm_in_gain),
        in_weight=in_weight[0].T,
        taps=conv_weight[0].T,
        conv_bias=conv_bias,
        step_bias=step_bias,
        log_decay=log_decay,
        skip=row(jnp.repeat(skip_gain[0], HEAD_DIM)),
        group_gain=group_gain,
        out_weight=out_weight[0],
        attn_gain=row(attn_gain),
        qkv_weight=qkv_weight,
        attn_out_weight=attn_out_weight,
        ffn_gain=row(ffn_gain),
        ffn_weight=ffn_weight,
        out_grad=out_grad,
    )
    a.__dict__.update(forward(n, mpn, a).__dict__)
    a.down_part, a.in_part, a.w_grad = ffn(a.ffn_rows, a.grad_rows, a.w_all)
    a.__dict__.update(backward(n, mpn, a).__dict__)
    f = finish(a)
    return (
        f.block_out,
        f.input_grad,
        f.patch_grad,
        f.norm_in_grad[0],
        f.in_grad.T[None],
        f.conv_w_grad.T[None],
        f.conv_b_grad,
        f.step_grad,
        f.decay_grad,
        f.skip_grad,
        f.group_grad,
        f.out_grad[None],
        f.attn_gain_grad[0],
        f.qkv_grad,
        f.ao_grad,
        f.ffn_gain_grad[0],
        f.ffn_grad,
    )


def solution(mesh):
    in_specs = (
        P(None, "dp", None),
        P(),
        P("mp", None, None),
        P(),
        P("mp", None, None),
        P("mp", None, None),
        P("mp", None),
        P("mp", None),
        P("mp", None),
        P("mp", None),
        P("mp", None),
        P("mp", None, None),
        P(),
        P(None, None, "mp"),
        P("mp", None),
        P(),
        P(None, "mp", "dp"),
        P(None, "dp", None),
    )
    out_specs = (
        P(None, "dp", "mp"),
        P(None, "dp", "mp"),
        P("mp", "dp", None),
        P("dp"),
        P("mp", "dp", None),
        P("mp", "dp", None),
        P("mp", "dp"),
        P("mp", None),
        P("mp", None),
        P("mp", None),
        P("mp", "dp"),
        P("mp", "dp", None),
        P("dp"),
        P(None, "dp", "mp"),
        P("mp", "dp"),
        P("dp"),
        P(None, "mp", "dp"),
    )
    return jax.shard_map(body, mesh=mesh, in_specs=in_specs, out_specs=out_specs, check_vma=False)
```

```python
from functools import partial
from types import SimpleNamespace

import jax
import jax.numpy as jnp
from jax import lax
from jax.experimental import pallas as pl
from jax.experimental.pallas import tpu as pltpu
from jax.sharding import PartitionSpec as P

STATE = 128
CONV = 4
SEQS = 3
GROUP_WIDTH = 512
GROUP_HEADS = 8
HEAD_DIM = 64
ATT_DIM = 64
CONV_CH = 768

norm_eps = 1e-06
highest = lax.Precision.HIGHEST
large_negative = -1e30
f32 = jnp.float32
bf16 = jnp.bfloat16
MESH = pl.DeviceIdType.MESH
VMEM = pl.BlockSpec(memory_space=pltpu.VMEM)
ANY = pl.BlockSpec(memory_space=pl.ANY)
SMEM = pl.BlockSpec(memory_space=pltpu.SMEM)
DMA = pltpu.SemaphoreType.DMA
SMALL_PARAMS = (
    "norm_in_gain", "taps", "conv_bias", "step_bias", "log_decay", "skip", "group_gain", "attn_gain", "ffn_gain"
)
SPILL_BYTES = 4 * 2**20
FFN_COLS = 256
WEIGHT_CUTS = 2
PACE = (1, 1, 1, 1, 2, 6)
PACE_FFN = 2
PACE_BACK = (1, 1, 2, 1)
BUNDLES_FIRST = True


def dot(a, b, dims=((1,), (0,)), precision=None):
    return lax.dot_general(
        a, b, (dims, ((), ())), preferred_element_type=f32, precision=precision
    )


def inv_rms(values):
    return lax.rsqrt(jnp.mean(values * values, axis=-1, keepdims=True) + norm_eps)


def rms_back(values, gain, upstream):
    scale = inv_rms(values)
    weighted = upstream * gain
    inner = jnp.mean(weighted * values, axis=-1, keepdims=True)
    back = scale * weighted - values * (inner * scale * scale * scale)
    return back, upstream * (values * scale)


def silu_pair(values):
    sig = jax.nn.sigmoid(values)
    return values * sig, sig * (1.0 + values * (1.0 - sig))


def rcopy(src, dst, send_sem, recv_sem, dp, mp):
    return pltpu.make_async_remote_copy(
        src_ref=src,
        dst_ref=dst,
        send_sem=send_sem,
        recv_sem=recv_sem,
        device_id={"dp": dp, "mp": mp},
        device_id_type=MESH,
    )


def greet(barrier, dp, mp):
    pl.semaphore_signal(barrier, inc=1, device_id={"dp": dp, "mp": mp}, device_id_type=MESH)


def plain_params(mib=56):
    return pltpu.CompilerParams(vmem_limit_bytes=mib * 2**20)


def remote_params(cid, mib=40):
    return pltpu.CompilerParams(
        collective_id=cid, has_side_effects=True, vmem_limit_bytes=mib * 2**20
    )


def launch(name, kernel, ins, outs, scratch, params):
    names = [*ins, *outs, *scratch]

    def run(*refs):
        kernel(SimpleNamespace(**dict(zip(names, refs))))

    results = pl.pallas_call(
        run,
        out_shape=tuple(jax.ShapeDtypeStruct(shape, dtype) for shape, dtype, _ in outs.values()),
        in_specs=[spec for _, spec in ins.values()],
        out_specs=tuple(spec for _, _, spec in outs.values()),
        scratch_shapes=list(scratch.values()),
        compiler_params=params,
        name=name,
    )(*[array for array, _ in ins.values()])
    return SimpleNamespace(**dict(zip(outs, results)))


def place_of(n, mpn):
    i, j = lax.axis_index("dp"), lax.axis_index("mp")
    reps = n // mpn
    return SimpleNamespace(
        n=n, mpn=mpn, i=i, j=j, reps=reps, share=n // reps, half=n // 2,
        m=i // reps, h=i % reps, c=i % 2, mine=i // 2, other=i + 1 - 2 * (i % 2), inside=i // reps == j,
    )


def greet_all(p, barrier):
    for d in range(1, p.mpn):
        greet(barrier, p.i, (p.j + d) % p.mpn)
    for d in range(1, p.n):
        greet(barrier, (p.i + d) % p.n, p.j)
    for s in range(p.n):
        @pl.when(jnp.logical_not((s == p.i) & p.inside))
        def _():
            greet(barrier, s, p.m)
    for h in range(p.reps):
        for t in range(p.mpn):
            @pl.when(jnp.logical_not((p.j * p.reps + h == p.i) & (t == p.j)))
            def _():
                greet(barrier, p.j * p.reps + h, t)
    return p.mpn + 3 * p.n - 2 - 2 * p.inside.astype(jnp.int32)


class Exchange:
    def __init__(self, p, src, dst, ss, rs):
        self.p, self.src, self.dst, self.ss, self.rs = p, src, dst, ss, rs

    def copy(self, t):
        p = self.p
        return rcopy(self.src(t), self.dst(p.j), self.ss.at[t], self.rs.at[p.j], p.i, t)

    def start(self):
        for d in range(1, self.p.mpn):
            self.copy((self.p.j + d) % self.p.mpn).start()
        return self

    def wait(self, d):
        s = (self.p.j + d) % self.p.mpn
        rcopy(self.dst(s), self.dst(s), self.ss.at[s], self.rs.at[s], self.p.i, s).wait_recv()
        return s

    def wait_all(self):
        for d in range(1, self.p.mpn):
            self.wait(d)

    def sent(self):
        for d in range(1, self.p.mpn):
            self.copy((self.p.j + d) % self.p.mpn).wait_send()


class Bulk:
    def __init__(self, exchanges):
        self.exchanges, self.begun = exchanges, 0

    def go(self, count):
        for exchange in self.exchanges[self.begun : self.begun + count]:
            exchange.start()
        self.begun += count

    def sent(self):
        for exchange in self.exchanges:
            exchange.sent()


class PlaneGather:
    def __init__(self, p, own, slot, ss, rs, ssr):
        self.p, self.own, self.slot, self.ss, self.rs, self.ssr = p, own, slot, ss, rs, ssr

    def direct(self, q):
        p = self.p
        return rcopy(self.own, self.slot(p.i), self.ss.at[q], self.rs.at[p.i], q * 2 + p.c, p.j)

    def across(self, q):
        p = self.p
        s = q * 2 + p.c
        return rcopy(self.slot(s), self.slot(s), self.ssr.at[q], self.rs.at[s], p.other, p.j)

    def own_across(self):
        p = self.p
        return rcopy(self.own, self.slot(p.i), self.ssr.at[p.mine], self.rs.at[p.i], p.other, p.j)

    def others(self):
        return [(self.p.mine + d) % self.p.half for d in range(1, self.p.half)]

    def start(self):
        self.own_across().start()
        for q in self.others():
            self.direct(q).start()
        return self

    def relay_one(self, q):
        s = q * 2 + self.p.c
        rcopy(self.slot(s), self.slot(s), self.ss.at[q], self.rs.at[s], s, self.p.j).wait_recv()
        self.across(q).start()

    def wait_across(self, q):
        s = q * 2 + 1 - self.p.c
        rcopy(self.slot(s), self.slot(s), self.ssr.at[q], self.rs.at[s], self.p.other, self.p.j).wait_recv()

    def relay(self):
        for q in reversed(self.others()):
            self.relay_one(q)

    def finish(self):
        for q in range(self.p.half):
            self.wait_across(q)

    def sent(self):
        self.own_across().wait_send()
        for q in self.others():
            self.direct(q).wait_send()
            self.across(q).wait_send()


class Reduction:
    def __init__(self, p, block, value, pre, recv, ss, get, put):
        self.p, self.block, self.value, self.pre, self.recv, self.get, self.put = p, block, value, pre, recv, get, put
        self.ssa, self.rsa, self.ssb, self.rsb = (ss.at[k] for k in range(4))

    def first(self, q):
        p = self.p
        return rcopy(self.block(q * 2 + 1 - p.c), self.pre.at[q], self.ssa.at[q], self.rsa.at[q], p.other, p.j)

    def second(self, q):
        p = self.p
        return rcopy(self.pre.at[q], self.recv.at[p.mine], self.ssb.at[q], self.rsb.at[p.mine], q * 2 + p.c, p.j)

    def others(self):
        return [(self.p.mine + d) % self.p.half for d in range(1, self.p.half)]

    def start(self):
        for q in self.others() + [self.p.mine]:
            self.first(q).start()

    def spread_one(self, q):
        p = self.p
        rcopy(self.pre.at[q], self.pre.at[q], self.ssa.at[q], self.rsa.at[q], p.other, p.j).wait_recv()
        total = self.value(q * 2 + p.c).astype(f32)
        self.put(self.pre.at[q], (total + self.get(self.pre.at[q]).astype(f32)).astype(bf16))
        self.second(q).start()

    def spread(self):
        for q in self.others():
            self.spread_one(q)

    def finish(self):
        p, mine = self.p, self.p.mine
        rcopy(self.pre.at[mine], self.pre.at[mine], self.ssa.at[mine], self.rsa.at[mine], p.other, p.j).wait_recv()
        total = self.value(p.i).astype(f32)
        total = total + self.get(self.pre.at[mine]).astype(f32)
        for q in self.others():
            rcopy(self.recv.at[q], self.recv.at[q], self.ssb.at[q], self.rsb.at[q], q * 2 + p.c, p.j).wait_recv()
            total = total + self.get(self.recv.at[q]).astype(f32)
        return total

    def sent(self):
        for q in self.others() + [self.p.mine]:
            self.first(q).wait_send()
        for q in self.others():
            self.second(q).wait_send()


def plain_get(view):
    return view[...]


def plain_put(view, value):
    view[...] = value


class Cast:
    def __init__(self, p, low, dst, ss, rs):
        self.p, self.low, self.dst, self.ss, self.rs = p, low, dst, ss, rs

    def each(self, act):
        p = self.p
        for h in range(p.reps):
            for t in range(p.mpn):
                here = (p.j * p.reps + h == p.i) & (t == p.j)

                @pl.when(jnp.logical_not(here))
                def _():
                    act(rcopy(
                        self.low, self.dst.at[p.i], self.ss.at[h * p.mpn + t], self.rs.at[p.i], p.j * p.reps + h, t
                    ))

    def start(self):
        self.each(lambda copy: copy.start())

        @pl.when(self.p.inside)
        def _():
            self.dst[self.p.i] = self.low[...]

    def wait(self):
        p = self.p
        for s in range(p.n):
            @pl.when(jnp.logical_not((s == p.i) & p.inside))
            def _():
                rcopy(self.low, self.dst.at[s], self.ss.at[0], self.rs.at[s], s, p.m).wait_recv()

    def sent(self):
        self.each(lambda copy: copy.wait_send())


class ToOwner:
    def __init__(self, p, part, recv, ss, rs):
        self.p, self.part, self.recv, self.ss, self.rs = p, part, recv, ss, rs

    def each(self, act):
        p = self.p
        for q in range(p.share):
            block = q * p.reps + p.h

            @pl.when(jnp.logical_not((block == p.i) & p.inside))
            def _():
                act(rcopy(self.part.at[block], self.recv.at[p.j], self.ss.at[q], self.rs.at[p.j], block, p.m))

    def start(self):
        self.each(lambda copy: copy.start())

        @pl.when(self.p.inside)
        def _():
            self.recv[self.p.j] = self.part[self.p.i]

    def wait(self):
        p = self.p
        for s in range(p.mpn):
            @pl.when(jnp.logical_not(p.inside & (s == p.j)))
            def _():
                rcopy(
                    self.part.at[0], self.recv.at[s], self.ss.at[0], self.rs.at[s], p.j * p.reps + p.h, s
                ).wait_recv()

    def total(self):
        self.wait()
        return sum(self.recv[s].astype(f32) for s in range(self.p.mpn))

    def sent(self):
        self.each(lambda copy: copy.wait_send())


def perm_matrix(rows, patches, per, limit):
    at = lax.broadcasted_iota(jnp.int32, (rows, rows), 0)
    source = lax.broadcasted_iota(jnp.int32, (rows, rows), 1)
    return ((source == (at % patches) * per + at // patches) & (at % patches < limit)).astype(bf16)


class Loads:
    def __init__(self, sems):
        self.sems, self.count = sems, 0

    def __call__(self, src, dst):
        copy = pltpu.make_async_copy(src, dst, self.sems.at[self.count])
        self.count += 1
        copy.start()
        return copy


def own_lengths(r, m):
    return r.seq_lengths[m, 0], r.seq_lengths[m, 1], r.seq_lengths[m, 2]


def seg_starts(lengths, places):
    end0 = lengths[0]
    end1 = end0 + lengths[1]
    end2 = end1 + lengths[2]
    return jnp.where(
        places >= end2, end2, jnp.where(places >= end1, end1, jnp.where(places >= end0, end0, 0))
    )


def conv_taps(conv_in, pos, lag):
    moved = conv_in if lag == 0 else pltpu.roll(conv_in, lag, 0)
    return jnp.where(pos >= lag, moved, 0.0)


def mixer_state(lengths, projected, conv_weight, conv_bias, step_bias, log_decay):
    patches = projected.shape[0]
    places = lax.broadcasted_iota(jnp.int32, (patches, 1), 0)
    start = seg_starts(lengths, places)
    pos = places - start
    conv_in = projected[:, GROUP_WIDTH : GROUP_WIDTH + CONV_CH]
    conv_out = conv_bias
    for lag in range(CONV):
        conv_out = conv_out + conv_taps(conv_in, pos, lag) * conv_weight[CONV - 1 - lag][None]
    step_raw = projected[:, GROUP_WIDTH + CONV_CH :] + step_bias
    step = jnp.maximum(step_raw, 0.0) + jnp.log1p(jnp.exp(-jnp.abs(step_raw)))
    logd = -step * jnp.exp(log_decay)
    across = lax.broadcasted_iota(jnp.int32, (patches, patches), 1)
    down = lax.broadcasted_iota(jnp.int32, (patches, patches), 0)
    mask = (across >= start) & (across <= down)
    running = dot(mask.astype(f32), logd, precision=highest)
    return pos, conv_in, conv_out, step_raw, step, logd, mask, running


def head_decay(mask, running, running_t, h):
    return jnp.exp(
        jnp.where(mask, running[:, h : h + 1] - running_t[h : h + 1, :], large_negative)
    )


def att_mask(rows, patches):
    across = lax.broadcasted_iota(jnp.int32, (rows, rows), 1)
    down = lax.broadcasted_iota(jnp.int32, (rows, rows), 0)
    return (across % patches == down % patches) & (across <= down)


def soft_rows(mask, query, key):
    scores = dot(query, key, ((1,), (1,))) * ATT_DIM ** (-0.5)
    scores = jnp.where(mask, scores, large_negative)
    probs = jnp.exp(scores - jnp.max(scores, axis=1, keepdims=True))
    return probs / jnp.sum(probs, axis=1, keepdims=True)


def mixer_fwd(r, lengths, normed):
    projected = dot(normed, r.in_v[...], ((1,), (1,)))
    r.projected[...] = projected
    _, _, conv_out, _, step, _, mask, running = mixer_state(
        lengths, projected, r.taps[...], r.conv_bias[...], r.step_bias[...], r.log_decay[...]
    )
    act = conv_out * jax.nn.sigmoid(conv_out)
    inputs = act[:, GROUP_WIDTH : GROUP_WIDTH + STATE]
    outputs = act[:, GROUP_WIDTH + STATE :]
    inner = dot(outputs, inputs, ((1,), (1,)))
    running_t, step_t = running.T, step.T
    pair = 2 * HEAD_DIM
    lane = lax.broadcasted_iota(jnp.int32, (1, pair), 1)
    pieces = []
    for c in range(GROUP_WIDTH // pair):
        values = act[:, c * pair : (c + 1) * pair]
        got = []
        for h in (2 * c, 2 * c + 1):
            weights = head_decay(mask, running, running_t, h) * inner * step_t[h : h + 1, :]
            got.append(dot(weights, values))
        pieces.append(jnp.where(lane < HEAD_DIM, got[0], got[1]))
    y = jnp.concatenate(pieces, axis=1) + r.skip[...] * act[:, :GROUP_WIDTH]
    r.mixer_y[...] = y
    gate = projected[:, :GROUP_WIDTH]
    gated = y * (gate * jax.nn.sigmoid(gate))
    low = (gated * inv_rms(gated) * r.group_gain[...]).astype(bf16)
    r.mixer_low[...] = low
    return dot(low, r.out_v[...])


def forward_steps(p, r, load, land):
    n, mpn, i, j = p.n, p.mpn, p.i, p.j
    micro, patches, own_cols = r.own.shape
    positions, dim = r.pw.shape[0], r.pw.shape[1]
    slabs = r.bytes_v.shape[2] // dim
    rows = slabs * patches
    features = r.bytes_part.shape[-1]
    per, hidden = r.ffn_weight.shape[1:]

    load_own = load(r.byte_input.at[:, :, pl.ds(pl.multiple_of(j * own_cols, 128), own_cols)], r.own)
    load_pw = [load(r.patch_weight.at[k], r.pw.at[k]) for k in range(positions)]
    load_grad = load(r.out_grad.at[j], r.grad_raw)
    load_in = load(r.in_weight, r.in_v)
    load_out = load(r.out_weight, r.out_v)
    load_bytes = load(r.byte_input, r.bytes_v)
    load_qkv = load(r.qkv_weight, r.qkv_v)
    kept = [load(r.ffn_weight.at[w], land(j, w, slice(None), slice(None))) for w in range(3)]

    barrier = pltpu.get_barrier_semaphore()
    count = greet_all(p, barrier)
    load_own.wait()
    sums = None
    for k in range(positions):
        load_pw[k].wait()
        term = dot(r.own[:, :, k * dim : (k + 1) * dim].reshape(micro * patches, dim), r.pw[k])
        sums = term if sums is None else sums + term
    for t in range(micro):
        r.part[t] = sums[t * patches : (t + 1) * patches]
        r.part_low[t] = sums[t * patches : (t + 1) * patches].astype(bf16)
    load_grad.wait()
    perm = perm_matrix(rows, patches, slabs, sum(own_lengths(r, j)) - i * patches)
    r.own_grad[...] = dot(perm, r.grad_raw[...]).astype(bf16)
    r.grad_rows_own(i, r.own_grad[...])
    pl.semaphore_wait(barrier, count)

    embed = Exchange(p, lambda t: r.part_low.at[t], lambda s: r.recv.at[s], r.ss1, r.rs1).start()
    grads = PlaneGather(p, r.own_grad, lambda s: r.grad_rows.at[s], r.ssg, r.rsg, r.ssgr).start()
    halves = max(hidden // FFN_COLS, 1)
    cuts = WEIGHT_CUTS if per // WEIGHT_CUTS >= 16 else 1
    step = per // cuts
    pieces = []
    for hh in range(halves):
        cols = slice(hh * (hidden // halves), (hh + 1) * (hidden // halves))
        for w in range(3):
            for k in range(cuts):
                at = slice(k * step, (k + 1) * step)
                pieces.append(Exchange(
                    p,
                    lambda t, w=w, at=at, cols=cols: r.ffn_weight.at[w, at, cols],
                    lambda s, w=w, at=at, cols=cols: land(s, w, at, cols),
                    r.ssw.at[len(pieces)],
                    r.rsw.at[len(pieces)],
                ))
    bulk = Bulk(pieces)
    bulk.go(PACE[0])
    total = r.part[j]
    for d in range(1, mpn):
        total = total + r.recv[embed.wait(d)].astype(f32)
    r.global_in[...] = total
    r.low[...] = (total * inv_rms(total) * r.norm_in_gain[...]).astype(bf16)
    cast = Cast(p, r.low, r.normed, r.ss2, r.rs2)
    cast.start()
    def columns_of(t, k):
        first = k * dim + t * (dim // n) // features * features
        return r.own.at[:, :, pl.ds(pl.multiple_of(first, 128), features)]

    def bytes_copy(t, k):
        return rcopy(columns_of(t, k), r.bytes_part.at[i, k], r.ssb.at[t, k], r.rsb.at[i, k], t, j)

    for d in range(1, n):
        for k in range(positions):
            bytes_copy((i + d) % n, k).start()
    kept += [load(columns_of(i, k), r.bytes_part.at[i, k]) for k in range(positions)]
    piece = r.out_proj.shape[0] // n
    at_piece = lambda s: pl.ds(pl.multiple_of(s * piece, piece), piece)
    kept_ao = load(r.out_proj.at[at_piece(i)], r.ao_sorted.at[j, at_piece(i)])
    bulk.go(PACE[1])
    load_in.wait()
    load_out.wait()
    cast.wait()
    ao_line = Exchange(
        p, lambda t: r.out_proj.at[at_piece(i)], lambda s: r.ao_sorted.at[s, at_piece(i)], r.ssa, r.rsa
    ).start()
    bulk.go(PACE[2])

    part = mixer_fwd(r, own_lengths(r, p.m), r.normed[...].reshape(n * patches, dim))
    for b in range(n):
        r.mix_part[b] = part[b * patches : (b + 1) * patches].astype(bf16)
    to_owner = ToOwner(p, r.mix_part, r.mix_recv, r.ss3, r.rs3)
    to_owner.start()
    kept_ao.wait()
    ao_line.wait_all()
    ao_block = lambda s: r.ao_sorted.at[:, at_piece(s)]
    ao_plane = PlaneGather(p, ao_block(i), ao_block, r.ssap, r.rsap, r.ssar).start()
    total = r.global_in[...] + to_owner.total()
    r.global_own[...] = total
    r.patch_all[j] = total.astype(bf16)
    patch_line = Exchange(p, lambda t: r.patch_all.at[j], lambda s: r.patch_all.at[s], r.ss4, r.rs4).start()
    bulk.go(PACE[3])
    grads.relay()
    load_bytes.wait()
    load_qkv.wait()
    patch_line.wait_all()

    mask = att_mask(rows, patches)
    pair = 2 * ATT_DIM
    width = r.qkv_v.shape[2]
    lane = lax.broadcasted_iota(jnp.int32, (1, pair), 1)
    heads_line = Exchange(p, lambda t: r.heads.at[t], lambda s: r.heads_own.at[s], r.ss5, r.rs5)

    def one_micro(d, _):
        m = (j + d) % mpn
        for k in range(slabs):
            here = r.bytes_v[m, :, k * dim : (k + 1) * dim].astype(f32) + r.patch_all[m].astype(f32)
            r.attn_in[m, k * patches : (k + 1) * patches, :] = (
                here * inv_rms(here) * r.attn_gain[...]
            ).astype(bf16)
        got = r.attn_in[m]
        for w in range(3):
            r.qkv[w, m] = dot(got, r.qkv_v[w]).astype(bf16)
        for c in range(width // pair):
            at = slice(c * pair, (c + 1) * pair)
            query, key, value = r.qkv[0, m, :, at], r.qkv[1, m, :, at], r.qkv[2, m, :, at]
            res = []
            for own in (lane < ATT_DIM, lane >= ATT_DIM):
                probs = soft_rows(mask, jnp.where(own, query, jnp.zeros_like(query)), key)
                res.append(dot(probs.astype(bf16), value))
            r.heads[m, :, at] = jnp.where(lane < ATT_DIM, res[0], res[1]).astype(bf16)

        @pl.when(d < mpn)
        def _():
            heads_line.copy(m).start()

        return 0

    lax.fori_loop(1, mpn + 1, one_micro, 0)
    bulk.go(PACE[4])
    r.heads_own[j] = r.heads[j]
    ao_plane.relay()
    ao_plane.finish()
    for k in range(slabs):
        here = r.bytes_v[j, :, k * dim : (k + 1) * dim].astype(f32) + r.global_own[...]
        r.after[k * patches : (k + 1) * patches, :] = here
    branch = None
    for d in range(mpn):
        s = j if d == 0 else heads_line.wait(d)
        term = dot(r.heads_own[s], r.ao_sorted[s])
        branch = term if branch is None else branch + term
    after = r.after[...] + branch
    r.after[...] = after
    r.ffn_own[...] = (after * inv_rms(after) * r.ffn_gain[...]).astype(bf16)
    rows_gather = PlaneGather(p, r.ffn_own, lambda s: r.ffn_rows.at[s], r.ssf, r.rsf, r.ssfr).start()
    r.ffn_rows_own(i, r.ffn_own[...])
    bulk.go(PACE[5])

    def settle():
        for d in range(1, n):
            s = (i + d) % n
            for k in range(positions):
                rcopy(r.bytes_part.at[s, k], r.bytes_part.at[s, k], r.ssb.at[s, k], r.rsb.at[s, k], s, j).wait_recv()
        for thing in (embed, grads, bulk, cast, ao_line, to_owner, ao_plane, patch_line, heads_line, rows_gather):
            thing.sent()
        for d in range(1, n):
            for k in range(positions):
                bytes_copy((i + d) % n, k).wait_send()

    return SimpleNamespace(grads=grads, rows=rows_gather, bulk=bulk, halves=halves, kept=kept, settle=settle)


def forward_kernel(n, mpn, r):
    p = place_of(n, mpn)
    load = Loads(r.sem_load)
    kept = []
    r.grad_rows_own = lambda s, value: kept.append(load(r.own_grad, r.grad_rows.at[s]))
    r.ffn_rows_own = lambda s, value: kept.append(load(r.ffn_own, r.ffn_rows.at[s]))
    st = forward_steps(p, r, load, lambda s, w, rows, cols: r.w_all.at[s, w, rows, cols])
    st.grads.finish()
    st.rows.relay()
    st.rows.finish()
    st.bulk.go(len(st.bulk.exchanges))
    for exchange in st.bulk.exchanges:
        exchange.wait_all()
    st.settle()
    for copy in kept + st.kept:
        copy.wait()


def forward_ins(a):
    ins = dict(seq_lengths=(a.seq_lengths, SMEM))
    for name in ("byte_input", "patch_weight", "out_grad", "in_weight", "out_weight", "qkv_weight", "ffn_weight"):
        ins[name] = (getattr(a, name), ANY)
    ins["out_proj"] = (a.attn_out_weight, ANY)
    for name in SMALL_PARAMS:
        ins[name] = (getattr(a, name), VMEM)
    return ins


def forward_results(n, mpn, a):
    micro, patches, cols = a.byte_input.shape
    dim = a.norm_in_gain.shape[1]
    rows = patches * (cols // dim)
    positions = a.patch_weight.shape[0]
    width = a.qkv_weight.shape[2]
    seq = n * patches
    large = dict(
        grad_rows=((n, rows, dim), bf16),
        ffn_rows=((n, rows, dim), bf16),
        w_all=((mpn,) + a.ffn_weight.shape, bf16),
        bytes_part=((n, positions, micro, patches, max(dim // n, 128)), bf16),
    )
    small = dict(
        own_grad=((rows, dim), bf16),
        after=((rows, dim), f32),
        heads_own=((mpn, rows, width), bf16),
        qkv=((3, micro, rows, width), bf16),
        attn_in=((micro, rows, dim), bf16),
        ao_sorted=((mpn,) + a.attn_out_weight.shape, bf16),
        global_in=((patches, dim), f32),
        global_own=((patches, dim), f32),
        normed=((n, patches, dim), bf16),
        projected=((seq, a.in_weight.shape[0]), f32),
        mixer_y=((seq, GROUP_WIDTH), f32),
        mixer_low=((seq, GROUP_WIDTH), bf16),
    )
    return large, small


def forward_scratch(n, mpn, a):
    micro, patches, cols = a.byte_input.shape
    dim = a.norm_in_gain.shape[1]
    rows = patches * (cols // dim)
    positions = a.patch_weight.shape[0]
    width = a.qkv_weight.shape[2]
    half = n // 2
    pieces = max(a.ffn_weight.shape[2] // FFN_COLS, 1) * 3 * WEIGHT_CUTS
    line, plane = DMA((mpn,)), DMA((half,))
    return dict(
        own=pltpu.VMEM((micro, patches, positions * dim), bf16),
        pw=pltpu.VMEM(a.patch_weight.shape, bf16),
        grad_raw=pltpu.VMEM((rows, dim), bf16),
        in_v=pltpu.VMEM(a.in_weight.shape, bf16),
        out_v=pltpu.VMEM(a.out_weight.shape, bf16),
        bytes_v=pltpu.VMEM(a.byte_input.shape, bf16),
        qkv_v=pltpu.VMEM(a.qkv_weight.shape, bf16),
        part=pltpu.VMEM((micro, patches, dim), f32),
        part_low=pltpu.VMEM((micro, patches, dim), bf16),
        recv=pltpu.VMEM((mpn, patches, dim), bf16),
        low=pltpu.VMEM((patches, dim), bf16),
        mix_part=pltpu.VMEM((n, patches, dim), bf16),
        mix_recv=pltpu.VMEM((mpn, patches, dim), bf16),
        patch_all=pltpu.VMEM((mpn, patches, dim), bf16),
        heads=pltpu.VMEM((micro, rows, width), bf16),
        ffn_own=pltpu.VMEM((rows, dim), bf16),
        sem_load=DMA((24,)),
        ss1=line, rs1=line, ss2=DMA((n,)), rs2=DMA((n,)), ss3=line, rs3=line, ss4=line, rs4=line, ss5=line, rs5=line,
        ssg=plane, rsg=DMA((n,)), ssgr=plane, ssf=plane, rsf=DMA((n,)), ssfr=plane,
        ssb=DMA((n, positions)), rsb=DMA((n, positions)),
        ssa=line, rsa=line, ssap=plane, rsap=DMA((n,)), ssar=plane,
        ssw=DMA((pieces, mpn)), rsw=DMA((pieces, mpn)),
    )


def forward(n, mpn, a):
    large, small = forward_results(n, mpn, a)
    outs = {name: value + (ANY,) for name, value in large.items()}
    outs.update({name: value + (VMEM,) for name, value in small.items()})
    return launch(
        "forward", partial(forward_kernel, n, mpn), forward_ins(a), outs, forward_scratch(n, mpn, a),
        remote_params(0, 62),
    )


def ffn_kernel(rows_in, grads_in, parts, down_out, in_grad, weight_grad, weight, gate_low, up_low, hidden_low):
    blocks, rows, dim = rows_in.shape
    per = parts.shape[2]
    for s in range(parts.shape[0]):
        for w in range(3):
            weight[w, s * per : (s + 1) * per, :] = parts[s, w]

    def step(b, _):
        here, up = rows_in[b], grads_in[b]
        gate = dot(here, weight[0])
        other = dot(here, weight[1])
        act, slope = silu_pair(gate)
        hidden = (act * other).astype(bf16)
        hidden_low[b] = hidden
        down_out[b] = dot(hidden, weight[2], ((1,), (1,))).astype(bf16)
        hidden_grad = dot(up, weight[2])
        gate_grad = (hidden_grad * other * slope).astype(bf16)
        up_grad = (hidden_grad * act).astype(bf16)
        gate_low[b] = gate_grad
        up_low[b] = up_grad
        back = dot(gate_grad, weight[0], ((1,), (1,))) + dot(up_grad, weight[1], ((1,), (1,)))
        in_grad[b] = back.astype(bf16)
        return 0

    lax.fori_loop(0, blocks, step, 0)
    hidden = weight.shape[2]
    everything = rows_in[...].reshape(blocks * rows, dim)
    weight_grad[0] = dot(everything, gate_low[...].reshape(blocks * rows, hidden), ((0,), (0,))).astype(bf16)
    weight_grad[1] = dot(everything, up_low[...].reshape(blocks * rows, hidden), ((0,), (0,))).astype(bf16)
    weight_grad[2] = dot(
        grads_in[...].reshape(blocks * rows, dim), hidden_low[...].reshape(blocks * rows, hidden), ((0,), (0,))
    ).astype(bf16)


def ffn(rows_in, grads_in, parts):
    blocks, rows, dim = rows_in.shape
    hidden = parts.shape[3]
    return pl.pallas_call(
        ffn_kernel,
        out_shape=(
            jax.ShapeDtypeStruct((blocks, rows, dim), bf16),
            jax.ShapeDtypeStruct((blocks, rows, dim), bf16),
            jax.ShapeDtypeStruct((3, dim, hidden), bf16),
        ),
        in_specs=[VMEM] * 3,
        out_specs=(VMEM,) * 3,
        scratch_shapes=[pltpu.VMEM((3, dim, hidden), bf16)] + [pltpu.VMEM((blocks, rows, hidden), bf16)] * 3,
        compiler_params=plain_params(60),
        name="ffn",
    )(rows_in, grads_in, parts)


def mixer_bwd(r, p, lengths, upstream):
    projected = r.projected[...]
    patches = projected.shape[0]
    pos, conv_in, conv_out, step_raw, step, logd, mask, running = mixer_state(
        lengths, projected, r.taps[...], r.conv_bias[...], r.step_bias[...], r.log_decay[...]
    )
    act, act_slope = silu_pair(conv_out)
    inputs = act[:, GROUP_WIDTH : GROUP_WIDTH + STATE]
    outputs = act[:, GROUP_WIDTH + STATE :]
    inner = dot(outputs, inputs, ((1,), (1,)))
    running_t, step_t = running.T, step.T
    normed_grad = dot(upstream, r.out_v[...], ((1,), (1,)))
    y = r.mixer_y[...]
    gate = projected[:, :GROUP_WIDTH]
    gate_act, gate_slope = silu_pair(gate)
    gated_grad, gain_rows = rms_back(y * gate_act, r.group_gain[...], normed_grad)
    y_grad = gated_grad * gate_act
    gate_grad = gated_grad * y * gate_slope
    values = act[:, :GROUP_WIDTH]
    skip_cols = jnp.sum(y_grad * values, axis=0, keepdims=True)
    pair = 2 * HEAD_DIM
    lane = lax.broadcasted_iota(jnp.int32, (1, pair), 1)
    inner_grad = jnp.zeros_like(inner)
    value_pieces, row_sums, col_sums = [], [], []
    for c in range(GROUP_WIDTH // pair):
        at = slice(c * pair, (c + 1) * pair)
        got = []
        for h in (2 * c, 2 * c + 1):
            own = (lane < HEAD_DIM) if h % 2 == 0 else (lane >= HEAD_DIM)
            mine = jnp.where(own, y_grad[:, at], 0.0)
            decay = head_decay(mask, running, running_t, h)
            step_row = step_t[h : h + 1, :]
            weight_grad = dot(mine, values[:, at], ((1,), (1,))) * decay
            scaled = weight_grad * step_row
            inner_grad = inner_grad + scaled
            col_sums.append(jnp.sum(weight_grad * inner, axis=0, keepdims=True))
            row_sums.append(jnp.sum(scaled * inner, axis=1, keepdims=True))
            weights = decay * inner * step_row
            got.append(dot(weights, mine, ((0,), (0,))))
        value_pieces.append(got[0] + got[1])
    values_grad = jnp.concatenate(value_pieces, axis=1) + r.skip[...] * y_grad
    inputs_grad = dot(inner_grad, outputs, ((0,), (0,)))
    outputs_grad = dot(inner_grad, inputs)
    col_grad = jnp.concatenate(col_sums, axis=0).T
    running_grad = jnp.concatenate(row_sums, axis=1) - col_grad * step
    logd_grad = dot(mask.astype(f32), running_grad, ((0,), (0,)), precision=highest)
    step_grad = (col_grad - logd_grad * jnp.exp(r.log_decay[...])) * jax.nn.sigmoid(step_raw)
    conv_grad = jnp.concatenate([values_grad, inputs_grad, outputs_grad], axis=1) * act_slope
    conv_in_grad = jnp.zeros_like(conv_grad)
    small = r.small_part
    small[...] = jnp.zeros(small.shape, f32)
    for lag in range(CONV):
        small[CONV - 1 - lag : CONV - lag, :] = jnp.sum(
            conv_grad * conv_taps(conv_in, pos, lag), axis=0, keepdims=True
        )
        kept = jnp.where(pos >= lag, conv_grad, 0.0) * r.taps[CONV - 1 - lag : CONV - lag, :]
        conv_in_grad = conv_in_grad + (kept if lag == 0 else pltpu.roll(kept, patches - lag, 0))
    small[CONV : CONV + 1, :] = jnp.sum(conv_grad, axis=0, keepdims=True)
    small[CONV + 1 : CONV + 2, :GROUP_WIDTH] = jnp.sum(gain_rows, axis=0, keepdims=True)
    small[CONV + 2 : CONV + 3, :GROUP_WIDTH] = skip_cols
    small[CONV + 3 : CONV + 4, :GROUP_HEADS] = jnp.sum(step_grad, axis=0, keepdims=True)
    small[CONV + 4 : CONV + 5, :GROUP_HEADS] = jnp.sum(logd_grad * logd, axis=0, keepdims=True)
    return jnp.concatenate([gate_grad, conv_in_grad, step_grad], axis=1).astype(bf16)


def grad_pieces(p, r, halves, grad_of, dim, hidden):
    per = dim // p.mpn
    step = per // WEIGHT_CUTS
    pieces = []
    for hh in range(halves):
        cols = slice(hh * (hidden // halves), (hh + 1) * (hidden // halves))
        for w in range(3):
            for k in range(WEIGHT_CUTS):
                at = slice(k * step, (k + 1) * step)
                pieces.append(Exchange(
                    p,
                    lambda t, w=w, k=k, cols=cols: grad_of(
                        w, pl.ds(pl.multiple_of(t * per + k * step, step), step), cols
                    ),
                    lambda s, w=w, at=at, cols=cols: r.g_recv.at[s, w, at, cols],
                    r.bsw.at[len(pieces)],
                    r.brw.at[len(pieces)],
                ))
    return Bulk(pieces)


def ffn_sums(p, r, get, put):
    in_block = lambda s: r.in_part.at[s]
    down_block = lambda s: r.down_part.at[s]
    return (
        Reduction(p, in_block, lambda s: get(in_block(s)), r.in_pre, r.in_recv, r.bs_in, get, put),
        Reduction(p, down_block, lambda s: get(down_block(s)), r.down_pre, r.down_recv, r.bs_down, get, put),
    )


def backward_steps(p, r, load, own_slab, ready, sum_in, sum_down, bulk):
    n, mpn, i, j = p.n, p.mpn, p.i, p.j
    micro, rows, dim = r.attn_in.shape
    patches = r.global_own.shape[0]
    slabs = rows // patches
    width = r.qkv_v.shape[2]
    feature = dim // n
    at_feature = lambda s: pl.ds(pl.multiple_of(s * feature, feature), feature)
    block_ao = lambda s: r.ao_part.at[at_feature(s)]
    block_qkv = lambda s: r.qkv_part.at[:, at_feature(s)]
    sum_ao = Reduction(
        p, block_ao, lambda s: block_ao(s)[...], r.ao_pre, r.ao_recv, r.bs_ao, plain_get, plain_put
    )
    sum_qkv = Reduction(
        p, block_qkv, lambda s: block_qkv(s)[...], r.qkv_pre, r.qkv_recv, r.bs_qkv, plain_get, plain_put
    )

    ready("bytes")
    for k in range(slabs):
        r.local_in[k * patches : (k + 1) * patches, :] = own_slab(k).astype(f32) + r.global_own[...]
    after = r.after[...]
    back, gain_rows = rms_back(after, r.ffn_gain[...], sum_in.finish())
    after_grad = r.own_grad[...].astype(f32) + back
    r.after_grad[...] = after_grad
    r.gains[...] = jnp.zeros(r.gains.shape, f32)
    r.gains[2:3, :] = jnp.sum(gain_rows, axis=0, keepdims=True)
    r.branch[...] = after_grad.astype(bf16)
    up_line = Exchange(p, lambda t: r.up.at[t], lambda s: r.up_recv.at[s], r.bs1, r.br1)
    for d in range(1, mpn + 1):
        t = (j + d) % mpn
        r.up[t] = dot(r.branch[...], r.ao_sorted[t], ((1,), (1,))).astype(bf16)
        if d < mpn:
            up_line.copy(t).start()
    r.up_recv[j] = r.up[j]
    bulk.go(PACE_BACK[0])
    sum_down.spread()
    ready("qkv")

    mask = att_mask(rows, patches)
    pair = 2 * ATT_DIM
    lane = lax.broadcasted_iota(jnp.int32, (1, pair), 1)
    att_line = Exchange(p, lambda t: r.att_part.at[t], lambda s: r.att_recv.at[s], r.bs2, r.br2)

    def one_micro(d, _):
        m = (j + d) % mpn

        @pl.when(d > 0)
        def _():
            up_line.wait(d)

        for c in range(width // pair):
            at = slice(c * pair, (c + 1) * pair)
            query, key, value = r.qkv[0, m, :, at], r.qkv[1, m, :, at], r.qkv[2, m, :, at]
            up = r.up_recv[m, :, at]
            got = [[], [], []]
            for own in (lane < ATT_DIM, lane >= ATT_DIM):
                mine = jnp.where(own, query, jnp.zeros_like(query))
                probs = soft_rows(mask, mine, key)
                my_up = jnp.where(own, up, jnp.zeros_like(up))
                probs_grad = dot(my_up, value, ((1,), (1,)))
                inner = jnp.sum(probs * probs_grad, axis=1, keepdims=True)
                score_grad = (probs * (probs_grad - inner) * ATT_DIM ** (-0.5)).astype(bf16)
                got[0].append(dot(score_grad, key))
                got[1].append(dot(score_grad, mine, ((0,), (0,))))
                got[2].append(dot(probs.astype(bf16), my_up, ((0,), (0,))))
            r.qkv_low[0, m, :, at] = jnp.where(lane < ATT_DIM, got[0][0], got[0][1]).astype(bf16)
            r.qkv_low[1, m, :, at] = (got[1][0] + got[1][1]).astype(bf16)
            r.qkv_low[2, m, :, at] = (got[2][0] + got[2][1]).astype(bf16)
        total = dot(r.qkv_low[0, m], r.qkv_v[0], ((1,), (1,)))
        total = total + dot(r.qkv_low[1, m], r.qkv_v[1], ((1,), (1,)))
        total = total + dot(r.qkv_low[2, m], r.qkv_v[2], ((1,), (1,)))
        r.att_part[m] = total.astype(bf16)

        @pl.when(d > 0)
        def _():
            att_line.copy(m).start()

        return 0

    lax.fori_loop(0, mpn, one_micro, 0)

    everything = r.attn_in[...].reshape(micro * rows, dim)
    for w in range(3):
        r.qkv_part[w] = dot(
            everything, r.qkv_low[w].reshape(micro * rows, width), ((0,), (0,))
        ).astype(bf16)
    sum_qkv.start()
    for t in range(mpn):
        r.ao_part[:, t * width : (t + 1) * width] = dot(
            r.branch[...], r.heads_own[t], ((0,), (0,))
        ).astype(bf16)
    sum_ao.start()
    sum_qkv.spread()
    perm = perm_matrix(rows, patches, slabs, sum(own_lengths(r, j)) - i * patches)
    block = (r.after[...] + sum_down.finish()).astype(bf16)
    block = dot(perm, block, ((0,), (0,))).astype(bf16)
    for t in range(mpn):
        r.block[t] = block[:, t * width : (t + 1) * width]
    total = r.att_part[j].astype(f32)
    for d in range(1, mpn):
        total = total + r.att_recv[att_line.wait(d)].astype(f32)
    back, gain_rows = rms_back(r.local_in[...], r.attn_gain[...], total)
    local_grad = r.after_grad[...] + back
    global_grad = local_grad[:patches]
    for k in range(1, slabs):
        global_grad = global_grad + local_grad[k * patches : (k + 1) * patches]
    r.global_grad[...] = global_grad
    r.b_low[...] = global_grad.astype(bf16)
    cast = Cast(p, r.b_low, r.mixer, r.bs3, r.br3)
    cast.start()
    bulk.go(PACE_BACK[1])
    r.gains[1:2, :] = jnp.sum(gain_rows, axis=0, keepdims=True)
    share_rows = rows // mpn
    for t in range(mpn):
        r.local[t] = local_grad[t * share_rows : (t + 1) * share_rows].astype(bf16)
    local_line = Exchange(p, lambda t: r.local.at[t], lambda s: r.local_all.at[s], r.bs6, r.br6)
    block_line = Exchange(p, lambda t: r.block.at[t], lambda s: r.block_all.at[s], r.bs7, r.br7)
    ready("mixer")
    cast.wait()
    sum_ao.spread()
    bulk.go(PACE_BACK[2])

    upstream = r.mixer[...].reshape(n * patches, dim)
    proj_grad = mixer_bwd(r, p, own_lengths(r, p.m), upstream)
    part = dot(proj_grad, r.in_v[...])
    for b in range(n):
        r.b_part[b] = part[b * patches : (b + 1) * patches].astype(bf16)
    to_owner = ToOwner(p, r.b_part, r.b_recv, r.bs4, r.br4)
    to_owner.start()
    bulk.go(PACE_BACK[3])

    half_cols = dim // p.reps
    normed_half = r.normed[:, :, pl.ds(pl.multiple_of(p.h * half_cols, half_cols), half_cols)]
    in_grad = dot(proj_grad, normed_half.reshape(n * patches, half_cols), ((0,), (0,))).astype(bf16)
    columns = in_grad.shape[0]
    for e in range(p.share):
        r.in_w_part[e, :columns, :] = in_grad[:, e * feature : (e + 1) * feature]
        r.in_w_part[e, columns:, :] = jnp.zeros((r.in_w_part.shape[1] - columns, feature), bf16)
    out_grad = dot(r.mixer_low[...], upstream, ((0,), (0,))).astype(bf16)
    group_rows = GROUP_WIDTH // n
    for e in range(n):
        r.out_w_part[e] = out_grad[e * group_rows : (e + 1) * group_rows]
    bundles = (
        (lambda e: r.in_w_part.at[e], r.in_w_recv, r.bsi, r.bri),
        (lambda e: r.out_w_part.at[p.h * p.share + e], r.out_w_recv, r.bso, r.bro),
        (lambda e: r.small_part, r.small_recv, r.bss, r.brs),
    )

    def each_bundle(act):
        for e in range(p.share):
            @pl.when(p.h * p.share + e != i)
            def _():
                for src, dst, ss, rs in bundles:
                    act(rcopy(src(e), dst.at[p.m], ss.at[e], rs.at[p.m], p.h * p.share + e, j))

    def start_bundles():
        each_bundle(lambda copy: copy.start())
        for e in range(p.share):
            @pl.when(p.h * p.share + e == i)
            def _():
                r.in_w_recv[p.m] = r.in_w_part[e]
                r.out_w_recv[p.m] = r.out_w_part[i]
                r.small_recv[p.m] = r.small_part[...]

    if BUNDLES_FIRST:
        start_bundles()
    back, gain_rows = rms_back(r.global_in[...], r.norm_in_gain[...], to_owner.total())
    r.line[j] = (r.global_grad[...] + back).astype(bf16)
    line = Exchange(p, lambda t: r.line.at[j], lambda s: r.line.at[s], r.bs5, r.br5).start()
    r.gains[0:1, :] = jnp.sum(gain_rows, axis=0, keepdims=True)
    r.gains_line[j] = r.gains[...]
    gains_line = Exchange(p, lambda t: r.gains, lambda s: r.gains_line.at[s], r.bsg, r.brg).start()
    local_line.start()
    block_line.start()
    r.local_all[j] = r.local[j]
    r.block_all[j] = r.block[j]
    line.wait_all()
    slot = lambda s: r.plane.at[s]
    plane = PlaneGather(p, r.line, slot, r.bsp, r.brp, r.bspr).start()
    keep_line = load(r.line, r.plane.at[i])
    if not BUNDLES_FIRST:
        start_bundles()
    r.qkv_sum[...] = sum_qkv.finish()
    ao = sum_ao.finish().astype(bf16)
    for t in range(mpn):
        r.ao[t] = ao[:, t * width : (t + 1) * width]
    ao_line = Exchange(p, lambda t: r.ao.at[t], lambda s: r.ao_all.at[s], r.bs8, r.br8).start()
    r.ao_all[j] = r.ao[j]
    bulk.go(len(bulk.exchanges))
    gains_line.wait_all()
    r.gains_plane[p.mine] = sum(r.gains_line[s] for s in range(mpn))

    def gains_copy(q):
        return rcopy(
            r.gains_plane.at[p.mine], r.gains_plane.at[p.mine], r.bsh.at[q], r.brh.at[p.mine], q * 2 + p.c, j
        )

    others = [(p.mine + d) % p.half for d in range(1, p.half)]
    for q in others:
        gains_copy(q).start()
    plane.relay()
    for q in others:
        rcopy(r.gains_plane.at[q], r.gains_plane.at[q], r.bsh.at[q], r.brh.at[q], q * 2 + p.c, j).wait_recv()
    r.gains_pair[0] = sum(r.gains_plane[s] for s in range(p.half))
    pair_copy = rcopy(r.gains_pair.at[0], r.gains_pair.at[1], r.bsq.at[0], r.brq.at[0], p.other, j)
    pair_copy.start()
    plane.finish()
    local_line.wait_all()
    block_line.wait_all()
    ao_line.wait_all()
    group = i // p.share
    for t in range(mpn):
        @pl.when(t * p.reps + group != i)
        def _():
            for src, dst, ss, rs in bundles:
                rcopy(src(0), dst.at[t], ss.at[0], rs.at[t], t * p.reps + group, j).wait_recv()
    pair_copy.wait()
    r.gains_all[...] = r.gains_pair[0] + r.gains_pair[1]
    for exchange in bulk.exchanges:
        exchange.wait_all()
    keep_line.wait()
    for thing in (
        sum_in, sum_down, sum_ao, sum_qkv, bulk, up_line, att_line, cast, to_owner, line, gains_line, local_line,
        block_line, plane, ao_line,
    ):
        thing.sent()
    for q in others:
        gains_copy(q).wait_send()
    each_bundle(lambda copy: copy.wait_send())


def backward_kernel(n, mpn, spill, r):
    p = place_of(n, mpn)
    load = Loads(r.b_load)

    def read(view):
        if not spill:
            return view[...]
        copy = pltpu.make_async_copy(view, r.stage.at[0], r.sem_stage.at[0])
        copy.start()
        copy.wait()
        return r.stage[0]

    def write(view, value):
        if not spill:
            view[...] = value
            return
        r.stage[1] = value
        copy = pltpu.make_async_copy(r.stage.at[1], view, r.sem_stage.at[1])
        copy.start()
        copy.wait()

    per = r.w_grad.shape[1] // mpn
    keep_w = load(r.w_grad.at[:, pl.ds(pl.multiple_of(p.j * per, per), per)], r.g_recv.at[p.j])
    loads = dict(
        bytes=[load(r.byte_input.at[p.j], r.own_bytes)],
        qkv=[load(r.qkv_weight, r.qkv_v)],
        mixer=[load(r.out_weight, r.out_v), load(r.in_weight, r.in_v)],
    )

    def ready(what):
        for copy in loads[what]:
            copy.wait()

    barrier = pltpu.get_barrier_semaphore()
    pl.semaphore_wait(barrier, greet_all(p, barrier))
    bulk = grad_pieces(p, r, 1, lambda w, at, cols: r.w_grad.at[w, at, cols], *r.w_grad.shape[1:])
    sum_in, sum_down = ffn_sums(p, r, read, write)
    sum_in.start()
    sum_in.spread()
    sum_down.start()
    dim = r.after.shape[1]
    own_slab = lambda k: r.own_bytes[:, k * dim : (k + 1) * dim]
    backward_steps(p, r, load, own_slab, ready, sum_in, sum_down, bulk)
    keep_w.wait()


def backward_results(n, mpn, a):
    micro, patches, cols = a.byte_input.shape
    dim = a.norm_in_gain.shape[1]
    rows = patches * (cols // dim)
    width = a.qkv_weight.shape[2]
    hidden = a.ffn_weight.shape[2]
    feature = dim // n
    padded = (a.in_weight.shape[0] + 15) // 16 * 16
    return dict(
        g_recv=((mpn, 3, dim // mpn, hidden), bf16, ANY),
        plane=((n, mpn, patches, dim), bf16, ANY),
        qkv_sum=((3, feature, width), f32, VMEM),
        ao_all=((mpn, feature, width), bf16, VMEM),
        in_w_recv=((mpn, padded, feature), bf16, VMEM),
        out_w_recv=((mpn, GROUP_WIDTH // n, dim), bf16, VMEM),
        small_recv=((mpn, 16, CONV_CH), f32, VMEM),
        gains_all=((8, dim), f32, VMEM),
        local_all=((mpn, rows // mpn, dim), bf16, VMEM),
        block_all=((mpn, rows, width), bf16, VMEM),
    )


def backward_scratch(n, mpn, a):
    micro, patches, cols = a.byte_input.shape
    dim = a.norm_in_gain.shape[1]
    rows = patches * (cols // dim)
    width = a.qkv_weight.shape[2]
    hidden = a.ffn_weight.shape[2]
    half, share = n // 2, mpn
    feature = dim // n
    padded = (a.in_weight.shape[0] + 15) // 16 * 16
    pieces = max(hidden // FFN_COLS, 1) * 3 * WEIGHT_CUTS
    line, plane = DMA((mpn,)), DMA((half,))
    return dict(
        local_in=pltpu.VMEM((rows, dim), f32),
        after_grad=pltpu.VMEM((rows, dim), f32),
        branch=pltpu.VMEM((rows, dim), bf16),
        up=pltpu.VMEM((mpn, rows, width), bf16),
        up_recv=pltpu.VMEM((mpn, rows, width), bf16),
        qkv_low=pltpu.VMEM((3, micro, rows, width), bf16),
        att_part=pltpu.VMEM((micro, rows, dim), bf16),
        att_recv=pltpu.VMEM((mpn, rows, dim), bf16),
        qkv_part=pltpu.VMEM((3, dim, width), bf16),
        qkv_pre=pltpu.VMEM((half, 3, feature, width), bf16),
        qkv_recv=pltpu.VMEM((half, 3, feature, width), bf16),
        ao_part=pltpu.VMEM((dim, mpn * width), bf16),
        ao_pre=pltpu.VMEM((half, feature, mpn * width), bf16),
        ao_recv=pltpu.VMEM((half, feature, mpn * width), bf16),
        ao=pltpu.VMEM((mpn, feature, width), bf16),
        block=pltpu.VMEM((mpn, rows, width), bf16),
        local=pltpu.VMEM((mpn, rows // mpn, dim), bf16),
        b_low=pltpu.VMEM((patches, dim), bf16),
        global_grad=pltpu.VMEM((patches, dim), f32),
        mixer=pltpu.VMEM((n, patches, dim), bf16),
        b_part=pltpu.VMEM((n, patches, dim), bf16),
        b_recv=pltpu.VMEM((mpn, patches, dim), bf16),
        line=pltpu.VMEM((mpn, patches, dim), bf16),
        in_w_part=pltpu.VMEM((share, padded, feature), bf16),
        out_w_part=pltpu.VMEM((n, GROUP_WIDTH // n, dim), bf16),
        small_part=pltpu.VMEM((16, CONV_CH), f32),
        gains=pltpu.VMEM((8, dim), f32),
        gains_line=pltpu.VMEM((mpn, 8, dim), f32),
        gains_plane=pltpu.VMEM((half, 8, dim), f32),
        gains_pair=pltpu.VMEM((2, 8, dim), f32),
        b_load=DMA((16,)),
        bs_in=DMA((4, half)), bs_down=DMA((4, half)), bs_ao=DMA((4, half)), bs_qkv=DMA((4, half)),
        bs1=line, br1=line, bs2=line, br2=line, bs3=DMA((n,)), br3=DMA((n,)), bs4=line, br4=line,
        bs5=line, br5=line, bs6=line, br6=line, bs7=line, br7=line, bs8=line, br8=line,
        bsp=plane, brp=DMA((n,)), bspr=plane,
        bsg=line, brg=line, bsh=plane, brh=plane, bsq=DMA((1,)), brq=DMA((1,)),
        bsi=DMA((share,)), bri=line, bso=DMA((share,)), bro=line, bss=DMA((share,)), brs=line,
        bsw=DMA((pieces, mpn)), brw=DMA((pieces, mpn)),
    )


def sum_buffers(n, a, make):
    micro, patches, cols = a.byte_input.shape
    dim = a.norm_in_gain.shape[1]
    shape = (n // 2, patches * (cols // dim), dim)
    return {name: make(shape) for name in ("in_pre", "in_recv", "down_pre", "down_recv")}


def backward(n, mpn, a):
    spill = a.in_part.size * 2 > SPILL_BYTES
    ins = dict(seq_lengths=(a.seq_lengths, SMEM))
    for name in ("byte_input", "w_grad", "in_weight", "out_weight", "qkv_weight"):
        ins[name] = (getattr(a, name), ANY)
    for name in ("in_part", "down_part"):
        ins[name] = (getattr(a, name), ANY if spill else VMEM)
    for name in SMALL_PARAMS + (
        "after", "own_grad", "heads_own", "qkv", "attn_in", "ao_sorted", "global_in", "global_own", "normed",
        "projected", "mixer_y", "mixer_low",
    ):
        ins[name] = (getattr(a, name), VMEM)
    outs = backward_results(n, mpn, a)
    scratch = backward_scratch(n, mpn, a)
    scratch.update(
        own_bytes=pltpu.VMEM(a.byte_input.shape[1:], bf16),
        in_v=pltpu.VMEM(a.in_weight.shape, bf16),
        out_v=pltpu.VMEM(a.out_weight.shape, bf16),
        qkv_v=pltpu.VMEM(a.qkv_weight.shape, bf16),
    )
    if spill:
        outs.update(sum_buffers(n, a, lambda shape: (shape, bf16, ANY)))
        scratch.update(stage=pltpu.VMEM((2,) + a.in_part.shape[1:], bf16), sem_stage=DMA((2,)))
    else:
        scratch.update(sum_buffers(n, a, lambda shape: pltpu.VMEM(shape, bf16)))
    return launch(
        "backward", partial(backward_kernel, n, mpn, spill), ins, outs, scratch, remote_params(1, 63)
    )


def ffn_steps(p, r, st, load, sum_in, sum_down, bulk, grad_of):
    n, half = p.n, p.half
    rows, dim = r.own_grad.shape
    hidden = r.w_v.shape[2]
    cols = hidden // st.halves
    per = dim // p.mpn
    pair = 2 * rows
    st.grads.finish()
    grads_all = lambda: r.grad_rows[...].reshape(n * rows, dim)
    rows_all = lambda: r.ffn_rows[...].reshape(n * rows, dim)
    kept = []
    if st.halves == 1:
        st.rows.relay()
        st.rows.finish()
    count = len(st.bulk.exchanges) // st.halves
    for hh in range(st.halves):
        at = slice(hh * cols, (hh + 1) * cols)
        last = hh == st.halves - 1
        if last:
            st.bulk.go(len(st.bulk.exchanges))
        for exchange in st.bulk.exchanges[hh * count : (hh + 1) * count]:
            exchange.wait_all()
        if hh == 0:
            for copy in st.kept:
                copy.wait()

        def compute(q):
            here = r.ffn_rows[pl.ds(2 * q, 2)].reshape(pair, dim)
            up = r.grad_rows[pl.ds(2 * q, 2)].reshape(pair, dim)
            gate = dot(here, r.w_v[0, :, at])
            other = dot(here, r.w_v[1, :, at])
            act, slope = silu_pair(gate)
            hidden_low = (act * other).astype(bf16)
            here_at = pl.ds(pl.multiple_of(q * pair, pair), pair)
            r.hidden_low[hh, here_at, :] = hidden_low
            down = dot(hidden_low, r.w_v[2, :, at], ((1,), (1,)))
            hidden_grad = dot(up, r.w_v[2, :, at])
            gate_grad = (hidden_grad * other * slope).astype(bf16)
            up_grad = (hidden_grad * act).astype(bf16)
            r.gate_low[hh, here_at, :] = gate_grad
            r.up_low[hh, here_at, :] = up_grad
            back = dot(gate_grad, r.w_v[0, :, at], ((1,), (1,))) + dot(up_grad, r.w_v[1, :, at], ((1,), (1,)))
            if hh > 0:
                back = back + r.in_part[pl.ds(2 * q, 2)].reshape(pair, dim).astype(f32)
                down = down + r.down_part[pl.ds(2 * q, 2)].reshape(pair, dim).astype(f32)
            r.in_part[pl.ds(2 * q, 2)] = back.astype(bf16).reshape(2, rows, dim)
            r.down_part[pl.ds(2 * q, 2)] = down.astype(bf16).reshape(2, rows, dim)

        def first_pass(d, _):
            q = (p.mine + half - d) % half

            @pl.when(d > 0)
            def _():
                st.rows.relay_one(q)

            st.rows.wait_across(q)
            compute(q)
            return 0

        def last_pass(d, _):
            q = (p.mine + d) % half
            compute(q)
            sum_in.first(q).start()

            @pl.when(d > 1)
            def _():
                sum_in.spread_one((p.mine + d - 1) % half)

            return 0

        if last:
            lax.fori_loop(1, half + 1, last_pass, 0)
            sum_down.start()
        else:
            lax.fori_loop(0, half, first_pass, 0)
        everything = slice(0, dim)
        grad_of(0, everything, at)[...] = dot(rows_all(), r.gate_low[hh], ((0,), (0,))).astype(bf16)
        grad_of(1, everything, at)[...] = dot(rows_all(), r.up_low[hh], ((0,), (0,))).astype(bf16)
        grad_of(2, everything, at)[...] = dot(grads_all(), r.hidden_low[hh], ((0,), (0,))).astype(bf16)
        mine = pl.ds(pl.multiple_of(p.j * per, per), per)
        kept += [load(grad_of(w, mine, at), r.g_recv.at[p.j, w, :, at]) for w in range(3)]
        if not last:
            bulk.go(PACE_FFN)
    return kept


def layer_kernel(n, mpn, r):
    p = place_of(n, mpn)
    dim = r.after.shape[1]

    def put_rows(ref):
        def put(s, value):
            ref[s] = value

        return put

    r.grad_rows_own = put_rows(r.grad_rows)
    r.ffn_rows_own = put_rows(r.ffn_rows)
    per = r.ffn_weight.shape[1]

    def land(s, w, rows, cols):
        first = (0 if rows.start is None else rows.start) + s * per
        size = per if rows.start is None else rows.stop - rows.start
        return r.w_v.at[w, pl.ds(pl.multiple_of(first, size), size), cols]

    load = Loads(r.sem_load)
    st = forward_steps(p, r, load, land)
    hidden = r.w_v.shape[2]

    def grad_of(w, at, cols):
        first = w % 2 * hidden
        return r.pw.at[w // 2, at, first + cols.start : first + cols.stop]

    bulk = grad_pieces(p, r, st.halves, grad_of, dim, hidden)
    sum_in, sum_down = ffn_sums(p, r, plain_get, plain_put)
    load = Loads(r.b_load)
    kept = ffn_steps(p, r, st, load, sum_in, sum_down, bulk, grad_of)
    own_slab = lambda k: r.bytes_v[p.j, :, k * dim : (k + 1) * dim]
    backward_steps(p, r, load, own_slab, lambda what: None, sum_in, sum_down, bulk)
    st.settle()
    for copy in kept:
        copy.wait()


def layer(n, mpn, a):
    dim = a.norm_in_gain.shape[1]
    hidden = a.ffn_weight.shape[2]
    halves = max(hidden // FFN_COLS, 1)
    large, small = forward_results(n, mpn, a)
    rows = small["own_grad"][0][0]
    outs = dict(bytes_part=large.pop("bytes_part") + (ANY,))
    outs.update(backward_results(n, mpn, a))
    large.pop("w_all")
    scratch = forward_scratch(n, mpn, a)
    scratch.update(backward_scratch(n, mpn, a))
    for name, (shape, dtype) in (*large.items(), *small.items()):
        scratch[name] = pltpu.VMEM(shape, dtype)
    scratch.update(sum_buffers(n, a, lambda shape: pltpu.VMEM(shape, bf16)))
    scratch.update(
        w_v=pltpu.VMEM((3, dim, hidden), bf16),
        in_part=pltpu.VMEM((n, rows, dim), bf16),
        down_part=pltpu.VMEM((n, rows, dim), bf16),
        gate_low=pltpu.VMEM((halves, n * rows, hidden // halves), bf16),
        up_low=pltpu.VMEM((halves, n * rows, hidden // halves), bf16),
        hidden_low=pltpu.VMEM((halves, n * rows, hidden // halves), bf16),
    )
    return launch(
        "layer", partial(layer_kernel, n, mpn), forward_ins(a), outs, scratch, remote_params(2, 63)
    )


def finish_kernel(r):
    i = lax.axis_index("dp")
    mpn, patches, dim = r.plane.shape[1:]
    n = r.plane.shape[0]
    features = r.bytes_part.shape[-1]
    positions = r.patch_weight.shape[0]
    feature = dim // n
    everyone = r.plane[...].reshape(n * mpn * patches, dim)
    own = r.plane[i].reshape(mpn * patches, dim)
    for k in range(positions):
        mine = r.bytes_part[:, k].reshape(n * mpn * patches, features)
        got = dot(mine, everyone, ((0,), (0,)))
        if features != feature:
            cut = features // feature
            got = sum(
                jnp.where(i % cut == e, got[e * feature : (e + 1) * feature], 0.0) for e in range(cut)
            )
        r.patch_grad[k] = got
        piece = dot(own, r.patch_weight[k], ((1,), (1,)))
        for m in range(mpn):
            r.input_grad[m, :, k * dim : (k + 1) * dim] = (
                piece[m * patches : (m + 1) * patches]
                + r.local_all[m, k * patches : (k + 1) * patches, :].astype(f32)
            )
    for w in range(3):
        r.ffn_grad[w] = sum(r.g_recv[s, w].astype(f32) for s in range(mpn))
    r.ao_grad[...] = sum(r.ao_all[s].astype(f32) for s in range(mpn)).T
    columns = r.in_grad.shape[0]
    r.in_grad[...] = sum(r.in_w_recv[s, :columns, :].astype(f32) for s in range(mpn))
    r.out_grad[...] = sum(r.out_w_recv[s].astype(f32) for s in range(mpn))
    small = sum(r.small_recv[s] for s in range(mpn))

    def chosen(values, size):
        whole = values.shape[1]
        at = lax.broadcasted_iota(jnp.int32, (whole, size), 0)
        want = lax.broadcasted_iota(jnp.int32, (whole, size), 1) + i * size
        return dot(values, (at == want).astype(f32), precision=highest)

    conv = chosen(small, CONV_CH // n)
    r.conv_w_grad[...] = conv[:CONV]
    r.conv_b_grad[...] = conv[CONV : CONV + 1]
    group = chosen(small[:, :GROUP_WIDTH], GROUP_WIDTH // n)
    r.group_grad[...] = group[CONV + 1 : CONV + 2]
    heads = lax.broadcasted_iota(jnp.int32, (GROUP_WIDTH, GROUP_HEADS), 0) // HEAD_DIM
    pick = heads == lax.broadcasted_iota(jnp.int32, (GROUP_WIDTH, GROUP_HEADS), 1)
    skip = dot(small[:, :GROUP_WIDTH], pick.astype(f32), precision=highest)
    r.skip_grad[...] = skip[CONV + 2 : CONV + 3]
    r.step_grad[...] = small[CONV + 3 : CONV + 4, :GROUP_HEADS]
    r.decay_grad[...] = small[CONV + 4 : CONV + 5, :GROUP_HEADS]
    gains = chosen(r.gains_all[...], feature)
    r.norm_in_grad[...] = gains[0:1]
    r.attn_gain_grad[...] = gains[1:2]
    r.ffn_gain_grad[...] = gains[2:3]
    r.qkv_grad[...] = r.qkv_sum[...]
    r.block_out[...] = r.block_all[...]


def finish(a):
    n, mpn, patches, dim = a.plane.shape
    positions = a.patch_weight.shape[0]
    feature = dim // n
    columns = a.in_weight.shape[0]
    names = (
        "plane", "bytes_part", "patch_weight", "local_all", "g_recv", "ao_all", "in_w_recv", "out_w_recv",
        "small_recv", "gains_all", "qkv_sum", "block_all",
    )
    row = lambda size: ((1, size), f32, VMEM)
    outs = dict(
        patch_grad=((positions, feature, dim), f32, VMEM),
        input_grad=((mpn, patches, positions * dim), f32, VMEM),
        ffn_grad=(a.g_recv.shape[1:], f32, VMEM),
        ao_grad=(a.ao_all.shape[:0:-1], f32, VMEM),
        in_grad=((columns, feature), f32, VMEM),
        out_grad=(a.out_w_recv.shape[1:], f32, VMEM),
        conv_w_grad=((CONV, CONV_CH // n), f32, VMEM),
        conv_b_grad=row(CONV_CH // n),
        group_grad=row(GROUP_WIDTH // n),
        skip_grad=row(GROUP_HEADS),
        step_grad=row(GROUP_HEADS),
        decay_grad=row(GROUP_HEADS),
        norm_in_grad=row(feature),
        attn_gain_grad=row(feature),
        ffn_gain_grad=row(feature),
        qkv_grad=(a.qkv_sum.shape, f32, VMEM),
        block_out=(a.block_all.shape, bf16, VMEM),
    )
    ins = {name: (getattr(a, name), VMEM) for name in names}
    return launch("finish", finish_kernel, ins, outs, {}, plain_params())


def body(
    byte_input,
    seq_lengths,
    patch_weight,
    norm_in_gain,
    in_weight,
    conv_weight,
    conv_bias,
    step_bias,
    log_decay,
    skip_gain,
    group_gain,
    out_weight,
    attn_gain,
    qkv_weight,
    attn_out_weight,
    ffn_gain,
    ffn_weight,
    out_grad,
):
    n, mpn = lax.axis_size("dp"), lax.axis_size("mp")
    row = lambda v: v.reshape(1, -1)
    a = SimpleNamespace(
        byte_input=byte_input,
        seq_lengths=seq_lengths,
        patch_weight=patch_weight,
        norm_in_gain=row(norm_in_gain),
        in_weight=in_weight[0].T,
        taps=conv_weight[0].T,
        conv_bias=conv_bias,
        step_bias=step_bias,
        log_decay=log_decay,
        skip=row(jnp.repeat(skip_gain[0], HEAD_DIM)),
        group_gain=group_gain,
        out_weight=out_weight[0],
        attn_gain=row(attn_gain),
        qkv_weight=qkv_weight,
        attn_out_weight=attn_out_weight,
        ffn_gain=row(ffn_gain),
        ffn_weight=ffn_weight,
        out_grad=out_grad,
    )
    dim, hidden = ffn_gain.shape[0], ffn_weight.shape[2]
    if n * out_grad.shape[1] * dim * 2 <= SPILL_BYTES and 2 * hidden <= dim:
        a.__dict__.update(layer(n, mpn, a).__dict__)
    else:
        a.__dict__.update(forward(n, mpn, a).__dict__)
        a.down_part, a.in_part, a.w_grad = ffn(a.ffn_rows, a.grad_rows, a.w_all)
        a.__dict__.update(backward(n, mpn, a).__dict__)
    f = finish(a)
    return (
        f.block_out,
        f.input_grad,
        f.patch_grad,
        f.norm_in_grad[0],
        f.in_grad.T[None],
        f.conv_w_grad.T[None],
        f.conv_b_grad,
        f.step_grad,
        f.decay_grad,
        f.skip_grad,
        f.group_grad,
        f.out_grad[None],
        f.attn_gain_grad[0],
        f.qkv_grad,
        f.ao_grad,
        f.ffn_gain_grad[0],
        f.ffn_grad,
    )


def solution(mesh):
    in_specs = (
        P(None, "dp", None),
        P(),
        P("mp", None, None),
        P(),
        P("mp", None, None),
        P("mp", None, None),
        P("mp", None),
        P("mp", None),
        P("mp", None),
        P("mp", None),
        P("mp", None),
        P("mp", None, None),
        P(),
        P(None, None, "mp"),
        P("mp", None),
        P(),
        P(None, "mp", "dp"),
        P(None, "dp", None),
    )
    out_specs = (
        P(None, "dp", "mp"),
        P(None, "dp", "mp"),
        P("mp", "dp", None),
        P("dp"),
        P("mp", "dp", None),
        P("mp", "dp", None),
        P("mp", "dp"),
        P("mp", None),
        P("mp", None),
        P("mp", None),
        P("mp", "dp"),
        P("mp", "dp", None),
        P("dp"),
        P(None, "dp", "mp"),
        P("mp", "dp"),
        P("dp"),
        P(None, "mp", "dp"),
    )
    return jax.shard_map(body, mesh=mesh, in_specs=in_specs, out_specs=out_specs, check_vma=False)
```

```python
from functools import partial
from types import SimpleNamespace

import jax
import jax.numpy as jnp
from jax import lax
from jax.experimental import pallas as pl
from jax.experimental.pallas import tpu as pltpu
from jax.sharding import PartitionSpec as P

STATE = 128
CONV = 4
SEQS = 3
GROUP_WIDTH = 512
GROUP_HEADS = 8
HEAD_DIM = 64
ATT_DIM = 64
CONV_CH = 768

norm_eps = 1e-06
highest = lax.Precision.HIGHEST
large_negative = -1e30
f32 = jnp.float32
bf16 = jnp.bfloat16
MESH = pl.DeviceIdType.MESH
VMEM = pl.BlockSpec(memory_space=pltpu.VMEM)
ANY = pl.BlockSpec(memory_space=pl.ANY)
SMEM = pl.BlockSpec(memory_space=pltpu.SMEM)
DMA = pltpu.SemaphoreType.DMA
SMALL_PARAMS = (
    "norm_in_gain", "taps", "conv_bias", "step_bias", "log_decay", "skip", "group_gain", "attn_gain", "ffn_gain"
)
SPILL_BYTES = 4 * 2**20
FFN_COLS = 256
WEIGHT_CUTS = 2
PACE = (1, 1, 1, 0, 1, 3, 6)
PACE_FFN = 6
PACE_BACK = (0, 2, 2, 1, 1)


def dot(a, b, dims=((1,), (0,)), precision=None):
    return lax.dot_general(
        a, b, (dims, ((), ())), preferred_element_type=f32, precision=precision
    )


def inv_rms(values):
    return lax.rsqrt(jnp.mean(values * values, axis=-1, keepdims=True) + norm_eps)


def rms_back(values, gain, upstream):
    scale = inv_rms(values)
    weighted = upstream * gain
    inner = jnp.mean(weighted * values, axis=-1, keepdims=True)
    back = scale * weighted - values * (inner * scale * scale * scale)
    return back, upstream * (values * scale)


def silu_pair(values):
    sig = jax.nn.sigmoid(values)
    return values * sig, sig * (1.0 + values * (1.0 - sig))


def rcopy(src, dst, send_sem, recv_sem, dp, mp):
    return pltpu.make_async_remote_copy(
        src_ref=src,
        dst_ref=dst,
        send_sem=send_sem,
        recv_sem=recv_sem,
        device_id={"dp": dp, "mp": mp},
        device_id_type=MESH,
    )


def greet(barrier, dp, mp):
    pl.semaphore_signal(barrier, inc=1, device_id={"dp": dp, "mp": mp}, device_id_type=MESH)


def plain_params(mib=56):
    return pltpu.CompilerParams(vmem_limit_bytes=mib * 2**20)


def remote_params(cid, mib=40):
    return pltpu.CompilerParams(
        collective_id=cid, has_side_effects=True, vmem_limit_bytes=mib * 2**20
    )


def launch(name, kernel, ins, outs, scratch, params):
    names = [*ins, *outs, *scratch]

    def run(*refs):
        kernel(SimpleNamespace(**dict(zip(names, refs))))

    results = pl.pallas_call(
        run,
        out_shape=tuple(jax.ShapeDtypeStruct(shape, dtype) for shape, dtype, _ in outs.values()),
        in_specs=[spec for _, spec in ins.values()],
        out_specs=tuple(spec for _, _, spec in outs.values()),
        scratch_shapes=list(scratch.values()),
        compiler_params=params,
        name=name,
    )(*[array for array, _ in ins.values()])
    return SimpleNamespace(**dict(zip(outs, results)))


def place_of(n, mpn, line):
    i, j = lax.axis_index("dp"), lax.axis_index("mp")
    reps = n // mpn
    return SimpleNamespace(
        n=n, mpn=mpn, i=i, j=j, reps=reps, share=n // reps, half=n // 2,
        m=i // reps, h=i % reps, c=i % 2, mine=i // 2, other=i + 1 - 2 * (i % 2), inside=i // reps == j, line=line,
    )


def greet_all(p, barrier):
    for d in range(1, p.mpn):
        greet(barrier, p.i, (p.j + d) % p.mpn)
    for d in range(1, p.n):
        greet(barrier, (p.i + d) % p.n, p.j)
    for q in range(p.half):
        s = q * 2 + p.c

        @pl.when(jnp.logical_not((s == p.i) & p.inside))
        def _():
            greet(barrier, s, p.m)

    for h in range(0, p.reps, 2):
        for t in range(p.mpn):
            @pl.when(jnp.logical_not((p.j * p.reps + h + p.c == p.i) & (t == p.j)))
            def _():
                greet(barrier, p.j * p.reps + h + p.c, t)
    return p.mpn + p.n - 2 + p.half + p.reps // 2 * p.mpn - 2 * p.inside.astype(jnp.int32)


class Exchange:
    def __init__(self, p, src, dst, ss, rs):
        self.p, self.src, self.dst, self.ss, self.rs = p, src, dst, ss, rs

    def copy(self, t):
        p = self.p
        return rcopy(self.src(t), self.dst(p.j), self.ss.at[t], self.rs.at[p.j], p.i, t)

    def start(self):
        for d in range(1, self.p.mpn):
            self.copy((self.p.j + d) % self.p.mpn).start()
        return self

    def wait(self, d):
        s = (self.p.j + d) % self.p.mpn
        rcopy(self.dst(s), self.dst(s), self.ss.at[s], self.rs.at[s], self.p.i, s).wait_recv()
        return s

    def wait_all(self):
        for d in range(1, self.p.mpn):
            self.wait(d)

    def sent(self):
        for d in range(1, self.p.mpn):
            self.copy((self.p.j + d) % self.p.mpn).wait_send()


class LineGather(Exchange):
    def begin(self):
        for d in range(1, self.p.mpn):
            def send():
                self.copy((self.p.j + d) % self.p.mpn).start()

            self.unless_far(d, send)

    def unless_far(self, d, act):
        if d == 2 or not self.p.line:
            act()
        else:
            pl.when(self.p.j != (3 if d == 1 else 0))(act)

    def onward(self, at):
        s, t = (0, 3) if at == 2 else (3, 0)
        return rcopy(self.dst(s), self.dst(s), self.ss.at[at], self.rs.at[s], self.p.i, t)

    def relay(self):
        if not self.p.line:
            return
        for at in (1, 2):
            @pl.when(self.p.j == at)
            def _():
                self.wait(2)
                self.onward(at).start()

    def wait_all(self):
        for d in range(1, self.p.mpn):
            if d == 2 and self.p.line:
                @pl.when((self.p.j == 0) | (self.p.j == 3))
                def _():
                    self.wait(2)
            else:
                self.wait(d)

    def sent(self):
        for d in range(1, self.p.mpn):
            def done():
                self.copy((self.p.j + d) % self.p.mpn).wait_send()

            self.unless_far(d, done)
        if self.p.line:
            for at in (1, 2):
                @pl.when(self.p.j == at)
                def _():
                    self.onward(at).wait_send()


class LineReduce(Exchange):
    def __init__(self, p, src, dst, ss, rs, held, hs):
        super().__init__(p, src, dst, ss, rs)
        self.held, self.hs = held, hs

    def begin(self):
        p = self.p
        for d in range(1, p.mpn):
            t = (p.j + d) % p.mpn
            if not p.line:
                self.copy(t).start()
            elif d == 2:
                @pl.when((p.j == 0) | (p.j == 3))
                def _():
                    self.copy(t).start()
            else:
                end = 3 if d == 1 else 0

                @pl.when(p.j != end)
                def _():
                    self.copy(t).start()

                @pl.when(p.j == end)
                def _():
                    rcopy(self.src(t), self.held, self.ss.at[t], self.hs, p.i, 2 if end == 3 else 1).start()

    def send(self, t):
        p = self.p
        if not p.line:
            self.copy(t).start()
            return
        apart = jnp.abs(t - p.j)
        taking = (apart == 2) & ((p.j == 1) | (p.j == 2))

        @pl.when(apart == 3)
        def _():
            rcopy(self.src(t), self.held, self.ss.at[t], self.hs, p.i, jnp.where(p.j == 0, 1, 2)).start()

        @pl.when((apart < 3) & jnp.logical_not(taking))
        def _():
            self.copy(t).start()

        pl.when(taking)(self.relay)

    def relay(self):
        p = self.p
        if not p.line:
            return

        @pl.when((p.j == 1) | (p.j == 2))
        def _():
            t = (p.j + 2) % p.mpn
            rcopy(self.held, self.held, self.ss.at[t], self.hs, p.i, t).wait_recv()
            self.held[...] = (self.held[...].astype(f32) + self.src(t)[...].astype(f32)).astype(bf16)
            rcopy(self.held, self.dst(p.j), self.ss.at[t], self.rs.at[p.j], p.i, t).start()

    def wait_all(self):
        for d in range(1, self.p.mpn):
            if d == 2 or not self.p.line:
                self.wait(d)
            else:
                @pl.when(self.p.j != (3 if d == 1 else 0))
                def _():
                    self.wait(d)


def absent(line, j, s):
    return line & (((j == 3) & (s == 0)) | ((j == 0) & (s == 3)))


class Bulk:
    def __init__(self, exchanges):
        self.exchanges, self.begun, self.before, self.relayed = exchanges, 0, 0, 0

    def relay(self, last):
        for exchange in self.exchanges[self.relayed : last]:
            exchange.relay()
        self.relayed = max(last, self.relayed)

    def go(self, count):
        count = min(count, len(self.exchanges) - self.begun)
        self.relay(self.before)
        self.before = self.begun
        for exchange in self.exchanges[self.begun : self.begun + count]:
            exchange.begin()
        self.begun += count

    def wait(self, first, last):
        self.relay(last)
        for exchange in self.exchanges[first:last]:
            exchange.wait_all()

    def sent(self):
        for exchange in self.exchanges:
            exchange.sent()


class PlaneGather:
    def __init__(self, p, own, slot, ss, rs, ssr):
        self.p, self.own, self.slot, self.ss, self.rs, self.ssr = p, own, slot, ss, rs, ssr

    def direct(self, q):
        p = self.p
        return rcopy(self.own, self.slot(p.i), self.ss.at[q], self.rs.at[p.i], q * 2 + p.c, p.j)

    def across(self, q):
        p = self.p
        s = q * 2 + p.c
        return rcopy(self.slot(s), self.slot(s), self.ssr.at[q], self.rs.at[s], p.other, p.j)

    def own_across(self):
        p = self.p
        return rcopy(self.own, self.slot(p.i), self.ssr.at[p.mine], self.rs.at[p.i], p.other, p.j)

    def others(self):
        return [(self.p.mine + d) % self.p.half for d in range(1, self.p.half)]

    def start(self):
        self.own_across().start()
        for q in self.others():
            self.direct(q).start()
        return self

    def relay_one(self, q):
        s = q * 2 + self.p.c
        rcopy(self.slot(s), self.slot(s), self.ss.at[q], self.rs.at[s], s, self.p.j).wait_recv()
        self.across(q).start()

    def wait_across(self, q):
        s = q * 2 + 1 - self.p.c
        rcopy(self.slot(s), self.slot(s), self.ssr.at[q], self.rs.at[s], self.p.other, self.p.j).wait_recv()

    def relay(self):
        for q in reversed(self.others()):
            self.relay_one(q)

    def finish(self):
        for q in range(self.p.half):
            self.wait_across(q)

    def sent(self):
        self.own_across().wait_send()
        for q in self.others():
            self.direct(q).wait_send()
            self.across(q).wait_send()


class Reduction:
    def __init__(self, p, block, value, pre, recv, ss, get, put):
        self.p, self.block, self.value, self.pre, self.recv, self.get, self.put = p, block, value, pre, recv, get, put
        self.ssa, self.rsa, self.ssb, self.rsb = (ss.at[k] for k in range(4))

    def first(self, q):
        p = self.p
        return rcopy(self.block(q * 2 + 1 - p.c), self.pre.at[q], self.ssa.at[q], self.rsa.at[q], p.other, p.j)

    def second(self, q):
        p = self.p
        return rcopy(self.pre.at[q], self.recv.at[p.mine], self.ssb.at[q], self.rsb.at[p.mine], q * 2 + p.c, p.j)

    def others(self):
        return [(self.p.mine + d) % self.p.half for d in range(1, self.p.half)]

    def start(self):
        for q in self.others() + [self.p.mine]:
            self.first(q).start()

    def spread_one(self, q):
        p = self.p
        rcopy(self.pre.at[q], self.pre.at[q], self.ssa.at[q], self.rsa.at[q], p.other, p.j).wait_recv()
        total = self.value(q * 2 + p.c).astype(f32)
        self.put(self.pre.at[q], (total + self.get(self.pre.at[q]).astype(f32)).astype(bf16))
        self.second(q).start()

    def spread(self):
        for q in self.others():
            self.spread_one(q)

    def finish(self):
        p, mine = self.p, self.p.mine
        rcopy(self.pre.at[mine], self.pre.at[mine], self.ssa.at[mine], self.rsa.at[mine], p.other, p.j).wait_recv()
        total = self.value(p.i).astype(f32)
        total = total + self.get(self.pre.at[mine]).astype(f32)
        for q in self.others():
            rcopy(self.recv.at[q], self.recv.at[q], self.ssb.at[q], self.rsb.at[q], q * 2 + p.c, p.j).wait_recv()
            total = total + self.get(self.recv.at[q]).astype(f32)
        return total

    def sent(self):
        for q in self.others() + [self.p.mine]:
            self.first(q).wait_send()
        for q in self.others():
            self.second(q).wait_send()


def plain_get(view):
    return view[...]


def plain_put(view, value):
    view[...] = value


class Cast:
    def __init__(self, p, low, dst, ss, rs, ssr):
        self.p, self.low, self.dst, self.ss, self.rs, self.ssr = p, low, dst, ss, rs, ssr

    def each(self, act):
        p = self.p
        for h in range(0, p.reps, 2):
            for t in range(p.mpn):
                to = p.j * p.reps + h + p.c

                @pl.when(jnp.logical_not((to == p.i) & (t == p.j)))
                def _():
                    act(rcopy(self.low, self.dst.at[p.i], self.ss.at[h // 2 * p.mpn + t], self.rs.at[p.i], to, t))

    def across(self, q):
        p = self.p
        s = q * 2 + p.c
        return rcopy(self.dst.at[s], self.dst.at[s], self.ssr.at[q], self.rs.at[s], p.other, p.j)

    def start(self):
        self.each(lambda copy: copy.start())

        @pl.when(self.p.inside)
        def _():
            self.dst[self.p.i] = self.low[...]

    def wait(self):
        p = self.p
        for q in range(p.half):
            s = q * 2 + p.c

            @pl.when(jnp.logical_not((s == p.i) & p.inside))
            def _():
                rcopy(self.low, self.dst.at[s], self.ss.at[0], self.rs.at[s], s, p.m).wait_recv()

            self.across(q).start()
        for q in range(p.half):
            s = q * 2 + 1 - p.c
            rcopy(self.dst.at[s], self.dst.at[s], self.ssr.at[q], self.rs.at[s], p.other, p.j).wait_recv()

    def sent(self):
        self.each(lambda copy: copy.wait_send())
        for q in range(self.p.half):
            self.across(q).wait_send()


class ToOwner:
    def __init__(self, p, part, mid, recv, ss, rs, ss_line, rs_line):
        self.p, self.part, self.mid, self.recv, self.ss, self.rs = p, part, mid, recv, ss, rs
        self.line = Exchange(p, lambda t: mid.at[t], lambda s: recv.at[s], ss_line, rs_line)

    def each(self, act):
        p = self.p
        for q in range(p.share):
            block = q * p.reps + p.h

            @pl.when(block != p.i)
            def _():
                act(rcopy(self.part.at[block], self.mid.at[p.m], self.ss.at[q], self.rs.at[p.m], block, p.j))

    def start(self):
        self.each(lambda copy: copy.start())
        self.mid[self.p.m] = self.part[self.p.i]

    def pass_on(self):
        p = self.p
        for s in range(p.mpn):
            @pl.when(s != p.m)
            def _():
                rcopy(
                    self.part.at[0], self.mid.at[s], self.ss.at[0], self.rs.at[s], s * p.reps + p.h, p.j
                ).wait_recv()
        self.line.start()
        self.recv[p.j] = self.mid[p.j]

    def total(self):
        self.line.wait_all()
        return sum(self.recv[s].astype(f32) for s in range(self.p.mpn))

    def sent(self):
        self.each(lambda copy: copy.wait_send())
        self.line.sent()


def perm_matrix(rows, patches, per, limit):
    at = lax.broadcasted_iota(jnp.int32, (rows, rows), 0)
    source = lax.broadcasted_iota(jnp.int32, (rows, rows), 1)
    return ((source == (at % patches) * per + at // patches) & (at % patches < limit)).astype(bf16)


class Loads:
    def __init__(self, sems):
        self.sems, self.count = sems, 0

    def __call__(self, src, dst):
        copy = pltpu.make_async_copy(src, dst, self.sems.at[self.count])
        self.count += 1
        copy.start()
        return copy


def own_lengths(r, m):
    return r.seq_lengths[m, 0], r.seq_lengths[m, 1], r.seq_lengths[m, 2]


def seg_starts(lengths, places):
    end0 = lengths[0]
    end1 = end0 + lengths[1]
    end2 = end1 + lengths[2]
    return jnp.where(
        places >= end2, end2, jnp.where(places >= end1, end1, jnp.where(places >= end0, end0, 0))
    )


def conv_taps(conv_in, pos, lag):
    moved = conv_in if lag == 0 else pltpu.roll(conv_in, lag, 0)
    return jnp.where(pos >= lag, moved, 0.0)


def mixer_state(lengths, projected, conv_weight, conv_bias, step_bias, log_decay):
    patches = projected.shape[0]
    places = lax.broadcasted_iota(jnp.int32, (patches, 1), 0)
    start = seg_starts(lengths, places)
    pos = places - start
    conv_in = projected[:, GROUP_WIDTH : GROUP_WIDTH + CONV_CH]
    conv_out = conv_bias
    for lag in range(CONV):
        conv_out = conv_out + conv_taps(conv_in, pos, lag) * conv_weight[CONV - 1 - lag][None]
    step_raw = projected[:, GROUP_WIDTH + CONV_CH :] + step_bias
    step = jnp.maximum(step_raw, 0.0) + jnp.log1p(jnp.exp(-jnp.abs(step_raw)))
    logd = -step * jnp.exp(log_decay)
    across = lax.broadcasted_iota(jnp.int32, (patches, patches), 1)
    down = lax.broadcasted_iota(jnp.int32, (patches, patches), 0)
    mask = (across >= start) & (across <= down)
    running = dot(mask.astype(f32), logd, precision=highest)
    return pos, conv_in, conv_out, step_raw, step, logd, mask, running


def head_decay(mask, running, running_t, h):
    return jnp.exp(
        jnp.where(mask, running[:, h : h + 1] - running_t[h : h + 1, :], large_negative)
    )


def att_mask(rows, patches):
    across = lax.broadcasted_iota(jnp.int32, (rows, rows), 1)
    down = lax.broadcasted_iota(jnp.int32, (rows, rows), 0)
    return (across % patches == down % patches) & (across <= down)


def soft_rows(mask, query, key):
    scores = dot(query, key, ((1,), (1,))) * ATT_DIM ** (-0.5)
    scores = jnp.where(mask, scores, large_negative)
    probs = jnp.exp(scores - jnp.max(scores, axis=1, keepdims=True))
    return probs / jnp.sum(probs, axis=1, keepdims=True)


def mixer_fwd(r, lengths, normed):
    projected = dot(normed, r.in_v[...], ((1,), (1,)))
    r.projected[...] = projected
    _, _, conv_out, _, step, _, mask, running = mixer_state(
        lengths, projected, r.taps[...], r.conv_bias[...], r.step_bias[...], r.log_decay[...]
    )
    act = conv_out * jax.nn.sigmoid(conv_out)
    inputs = act[:, GROUP_WIDTH : GROUP_WIDTH + STATE]
    outputs = act[:, GROUP_WIDTH + STATE :]
    inner = dot(outputs, inputs, ((1,), (1,)))
    running_t, step_t = running.T, step.T
    pair = 2 * HEAD_DIM
    lane = lax.broadcasted_iota(jnp.int32, (1, pair), 1)
    pieces = []
    for c in range(GROUP_WIDTH // pair):
        values = act[:, c * pair : (c + 1) * pair]
        got = []
        for h in (2 * c, 2 * c + 1):
            weights = head_decay(mask, running, running_t, h) * inner * step_t[h : h + 1, :]
            got.append(dot(weights, values))
        pieces.append(jnp.where(lane < HEAD_DIM, got[0], got[1]))
    y = jnp.concatenate(pieces, axis=1) + r.skip[...] * act[:, :GROUP_WIDTH]
    r.mixer_y[...] = y
    gate = projected[:, :GROUP_WIDTH]
    gated = y * (gate * jax.nn.sigmoid(gate))
    low = (gated * inv_rms(gated) * r.group_gain[...]).astype(bf16)
    r.mixer_low[...] = low
    return dot(low, r.out_v[...])


def forward_steps(p, r, load, land):
    n, mpn, i, j = p.n, p.mpn, p.i, p.j
    micro, patches, own_cols = r.own.shape
    positions, dim = r.pw.shape[0], r.pw.shape[1]
    slabs = r.bytes_v.shape[2] // dim
    rows = slabs * patches
    features = r.bytes_part.shape[-1]
    per, hidden = r.ffn_weight.shape[1:]

    load_own = load(r.byte_input.at[:, :, pl.ds(pl.multiple_of(j * own_cols, 128), own_cols)], r.own)
    load_pw = [load(r.patch_weight.at[k], r.pw.at[k]) for k in range(positions)]
    load_grad = load(r.out_grad.at[j], r.grad_raw)
    load_in = load(r.in_weight, r.in_v)
    load_out = load(r.out_weight, r.out_v)
    load_bytes = load(r.byte_input, r.bytes_v)
    load_qkv = load(r.qkv_weight, r.qkv_v)
    kept = [load(r.ffn_weight.at[w], land(j, w, slice(None), slice(None))) for w in range(3)]

    barrier = pltpu.get_barrier_semaphore()
    count = greet_all(p, barrier)
    load_own.wait()
    sums = None
    for k in range(positions):
        load_pw[k].wait()
        term = dot(r.own[:, :, k * dim : (k + 1) * dim].reshape(micro * patches, dim), r.pw[k])
        sums = term if sums is None else sums + term
    for t in range(micro):
        r.part[t] = sums[t * patches : (t + 1) * patches]
        r.part_low[t] = sums[t * patches : (t + 1) * patches].astype(bf16)
    pl.semaphore_wait(barrier, count)

    embed = Exchange(p, lambda t: r.part_low.at[t], lambda s: r.recv.at[s], r.ss1, r.rs1).start()
    halves = max(hidden // FFN_COLS, 1)
    cuts = WEIGHT_CUTS if per // WEIGHT_CUTS >= 16 else 1
    step = per // cuts
    pieces = []
    for hh in range(halves):
        cols = slice(hh * (hidden // halves), (hh + 1) * (hidden // halves))
        for w in range(3):
            for k in range(cuts):
                at = slice(k * step, (k + 1) * step)
                pieces.append(LineGather(
                    p,
                    lambda t, w=w, at=at, cols=cols: r.ffn_weight.at[w, at, cols],
                    lambda s, w=w, at=at, cols=cols: land(s, w, at, cols),
                    r.ssw.at[len(pieces)],
                    r.rsw.at[len(pieces)],
                ))
    bulk = Bulk(pieces)
    bulk.go(PACE[0])
    load_grad.wait()
    perm = perm_matrix(rows, patches, slabs, sum(own_lengths(r, j)) - i * patches)
    r.own_grad[...] = dot(perm, r.grad_raw[...]).astype(bf16)
    r.grad_rows_own(i, r.own_grad[...])
    total = r.part[j]
    for d in range(1, mpn):
        total = total + r.recv[embed.wait(d)].astype(f32)
    r.global_in[...] = total
    r.low[...] = (total * inv_rms(total) * r.norm_in_gain[...]).astype(bf16)
    cast = Cast(p, r.low, r.normed, r.ss2, r.rs2, r.ssc)
    cast.start()
    def columns_of(t, k):
        first = k * dim + t * (dim // n) // features * features
        return r.own.at[:, :, pl.ds(pl.multiple_of(first, 128), features)]

    def bytes_copy(t, k):
        return rcopy(columns_of(t, k), r.bytes_part.at[i, k], r.ssb.at[t, k], r.rsb.at[i, k], t, j)

    for d in range(1, n):
        for k in range(positions):
            bytes_copy((i + d) % n, k).start()
    kept += [load(columns_of(i, k), r.bytes_part.at[i, k]) for k in range(positions)]
    piece = r.out_proj.shape[0] // n
    at_piece = lambda s: pl.ds(pl.multiple_of(s * piece, piece), piece)
    kept_ao = load(r.out_proj.at[at_piece(i)], r.ao_sorted.at[j, at_piece(i)])
    ao_line = LineGather(
        p, lambda t: r.out_proj.at[at_piece(i)], lambda s: r.ao_sorted.at[s, at_piece(i)], r.ssa, r.rsa
    )
    ao_line.begin()
    bulk.go(PACE[1])
    load_in.wait()
    load_out.wait()
    cast.wait()
    feature = dim // n
    blocks = max(feature, 128)

    def normed_copy(q):
        t = q * p.reps + p.h
        return rcopy(normed_block(t), r.normed_cols.at[p.m], r.ssn.at[q], r.rsn.at[p.m], t, j)

    def normed_block(t):
        return r.normed.at[:, :, pl.ds(pl.multiple_of(t * feature // blocks * blocks, 128), blocks)]

    def each_normed(act, here):
        for q in range(p.share):
            at_home = q * p.reps + p.h == i
            pl.when(jnp.logical_not(at_home))(partial(act, q))
            pl.when(at_home)(here)

    def keep_normed():
        return pltpu.make_async_copy(normed_block(i), r.normed_cols.at[p.m], r.ssn.at[p.share])

    each_normed(lambda q: normed_copy(q).start(), lambda: keep_normed().start())
    bulk.go(PACE[2])

    part = mixer_fwd(r, own_lengths(r, p.m), r.normed[...].reshape(n * patches, dim))
    for b in range(n):
        r.mix_part[b] = part[b * patches : (b + 1) * patches].astype(bf16)
    to_owner = ToOwner(p, r.mix_part, r.mix_mid, r.mix_recv, r.ss3, r.rs3, r.sso, r.rso)
    to_owner.start()
    kept_ao.wait()
    ao_line.relay()
    to_owner.pass_on()
    bulk.go(PACE[3])
    ao_line.wait_all()
    ao_block = lambda s: r.ao_sorted.at[:, at_piece(s)]
    ao_plane = PlaneGather(p, ao_block(i), ao_block, r.ssap, r.rsap, r.ssar).start()
    grads = PlaneGather(p, r.own_grad, lambda s: r.grad_rows.at[s], r.ssg, r.rsg, r.ssgr).start()
    total = r.global_in[...] + to_owner.total()
    r.global_own[...] = total
    r.patch_all[j] = total.astype(bf16)
    patch_line = Exchange(p, lambda t: r.patch_all.at[j], lambda s: r.patch_all.at[s], r.ss4, r.rs4).start()
    bulk.go(PACE[4])
    load_bytes.wait()
    load_qkv.wait()
    patch_line.wait_all()

    mask = att_mask(rows, patches)
    pair = 2 * ATT_DIM
    width = r.qkv_v.shape[2]
    lane = lax.broadcasted_iota(jnp.int32, (1, pair), 1)
    heads_line = Exchange(p, lambda t: r.heads.at[t], lambda s: r.heads_own.at[s], r.ss5, r.rs5)

    def one_micro(d, _):
        m = (j + d) % mpn
        for k in range(slabs):
            here = r.bytes_v[m, :, k * dim : (k + 1) * dim].astype(f32) + r.patch_all[m].astype(f32)
            r.attn_in[m, k * patches : (k + 1) * patches, :] = (
                here * inv_rms(here) * r.attn_gain[...]
            ).astype(bf16)
        got = r.attn_in[m]
        for w in range(3):
            r.qkv[w, m] = dot(got, r.qkv_v[w]).astype(bf16)
        for c in range(width // pair):
            at = slice(c * pair, (c + 1) * pair)
            query, key, value = r.qkv[0, m, :, at], r.qkv[1, m, :, at], r.qkv[2, m, :, at]
            res = []
            for own in (lane < ATT_DIM, lane >= ATT_DIM):
                probs = soft_rows(mask, jnp.where(own, query, jnp.zeros_like(query)), key)
                res.append(dot(probs.astype(bf16), value))
            r.heads[m, :, at] = jnp.where(lane < ATT_DIM, res[0], res[1]).astype(bf16)

        @pl.when(d < mpn)
        def _():
            heads_line.copy(m).start()

        return 0

    lax.fori_loop(1, mpn + 1, one_micro, 0)
    bulk.go(PACE[5])
    r.heads_own[j] = r.heads[j]
    ao_plane.relay()
    ao_plane.finish()
    grads.relay()
    for k in range(slabs):
        here = r.bytes_v[j, :, k * dim : (k + 1) * dim].astype(f32) + r.global_own[...]
        r.after[k * patches : (k + 1) * patches, :] = here
    branch = None
    for d in range(mpn):
        s = j if d == 0 else heads_line.wait(d)
        term = dot(r.heads_own[s], r.ao_sorted[s])
        branch = term if branch is None else branch + term
    after = r.after[...] + branch
    r.after[...] = after
    r.ffn_own[...] = (after * inv_rms(after) * r.ffn_gain[...]).astype(bf16)
    rows_gather = PlaneGather(p, r.ffn_own, lambda s: r.ffn_rows.at[s], r.ssf, r.rsf, r.ssfr).start()
    r.ffn_rows_own(i, r.ffn_own[...])
    bulk.go(PACE[6])

    def settle():
        for d in range(1, n):
            s = (i + d) % n
            for k in range(positions):
                rcopy(r.bytes_part.at[s, k], r.bytes_part.at[s, k], r.ssb.at[s, k], r.rsb.at[s, k], s, j).wait_recv()
        for s in range(mpn):
            @pl.when(s * p.reps + p.h != i)
            def _():
                rcopy(
                    r.normed_cols.at[s], r.normed_cols.at[s], r.ssn.at[0], r.rsn.at[s], s * p.reps + p.h, j
                ).wait_recv()
        each_normed(lambda q: normed_copy(q).wait_send(), lambda: keep_normed().wait())
        for thing in (embed, grads, bulk, cast, ao_line, to_owner, ao_plane, patch_line, heads_line, rows_gather):
            thing.sent()
        for d in range(1, n):
            for k in range(positions):
                bytes_copy((i + d) % n, k).wait_send()

    return SimpleNamespace(grads=grads, rows=rows_gather, bulk=bulk, halves=halves, kept=kept, settle=settle)


def forward_kernel(n, mpn, r):
    p = place_of(n, mpn, False)
    load = Loads(r.sem_load)
    kept = []
    r.grad_rows_own = lambda s, value: kept.append(load(r.own_grad, r.grad_rows.at[s]))
    r.ffn_rows_own = lambda s, value: kept.append(load(r.ffn_own, r.ffn_rows.at[s]))
    st = forward_steps(p, r, load, lambda s, w, rows, cols: r.w_all.at[s, w, rows, cols])
    st.grads.finish()
    st.rows.relay()
    st.rows.finish()
    st.bulk.go(len(st.bulk.exchanges))
    st.bulk.wait(0, len(st.bulk.exchanges))
    st.settle()
    for copy in kept + st.kept:
        copy.wait()


def forward_ins(a):
    ins = dict(seq_lengths=(a.seq_lengths, SMEM))
    for name in ("byte_input", "patch_weight", "out_grad", "in_weight", "out_weight", "qkv_weight", "ffn_weight"):
        ins[name] = (getattr(a, name), ANY)
    ins["out_proj"] = (a.attn_out_weight, ANY)
    for name in SMALL_PARAMS:
        ins[name] = (getattr(a, name), VMEM)
    return ins


def forward_results(n, mpn, a):
    micro, patches, cols = a.byte_input.shape
    dim = a.norm_in_gain.shape[1]
    rows = patches * (cols // dim)
    positions = a.patch_weight.shape[0]
    width = a.qkv_weight.shape[2]
    seq = n * patches
    large = dict(
        grad_rows=((n, rows, dim), bf16),
        ffn_rows=((n, rows, dim), bf16),
        w_all=((mpn,) + a.ffn_weight.shape, bf16),
        bytes_part=((n, positions, micro, patches, max(dim // n, 128)), bf16),
        normed_cols=((mpn, n, patches, max(dim // n, 128)), bf16),
    )
    small = dict(
        own_grad=((rows, dim), bf16),
        after=((rows, dim), f32),
        heads_own=((mpn, rows, width), bf16),
        qkv=((3, micro, rows, width), bf16),
        attn_in=((micro, rows, dim), bf16),
        ao_sorted=((mpn,) + a.attn_out_weight.shape, bf16),
        global_in=((patches, dim), f32),
        global_own=((patches, dim), f32),
        normed=((n, patches, dim), bf16),
        projected=((seq, a.in_weight.shape[0]), f32),
        mixer_y=((seq, GROUP_WIDTH), f32),
        mixer_low=((seq, GROUP_WIDTH), bf16),
    )
    return large, small


def forward_scratch(n, mpn, a):
    micro, patches, cols = a.byte_input.shape
    dim = a.norm_in_gain.shape[1]
    rows = patches * (cols // dim)
    positions = a.patch_weight.shape[0]
    width = a.qkv_weight.shape[2]
    half = n // 2
    pieces = max(a.ffn_weight.shape[2] // FFN_COLS, 1) * 3 * WEIGHT_CUTS
    line, plane = DMA((mpn,)), DMA((half,))
    return dict(
        own=pltpu.VMEM((micro, patches, positions * dim), bf16),
        pw=pltpu.VMEM(a.patch_weight.shape, bf16),
        grad_raw=pltpu.VMEM((rows, dim), bf16),
        in_v=pltpu.VMEM(a.in_weight.shape, bf16),
        out_v=pltpu.VMEM(a.out_weight.shape, bf16),
        bytes_v=pltpu.VMEM(a.byte_input.shape, bf16),
        qkv_v=pltpu.VMEM(a.qkv_weight.shape, bf16),
        part=pltpu.VMEM((micro, patches, dim), f32),
        part_low=pltpu.VMEM((micro, patches, dim), bf16),
        recv=pltpu.VMEM((mpn, patches, dim), bf16),
        low=pltpu.VMEM((patches, dim), bf16),
        mix_part=pltpu.VMEM((n, patches, dim), bf16),
        mix_mid=pltpu.VMEM((mpn, patches, dim), bf16),
        mix_recv=pltpu.VMEM((mpn, patches, dim), bf16),
        patch_all=pltpu.VMEM((mpn, patches, dim), bf16),
        heads=pltpu.VMEM((micro, rows, width), bf16),
        ffn_own=pltpu.VMEM((rows, dim), bf16),
        sem_load=DMA((32,)),
        ss1=line, rs1=line, ss2=DMA((n,)), rs2=DMA((n,)), ssc=plane, ss3=line, rs3=line, sso=line, rso=line, ss4=line, rs4=line, ss5=line, rs5=line,
        ssg=plane, rsg=DMA((n,)), ssgr=plane, ssf=plane, rsf=DMA((n,)), ssfr=plane,
        ssb=DMA((n, positions)), rsb=DMA((n, positions)),
        ssn=DMA((mpn + 1,)), rsn=line, ssa=line, rsa=line, ssap=plane, rsap=DMA((n,)), ssar=plane,
        ssw=DMA((pieces, mpn)), rsw=DMA((pieces, mpn)),
    )


def forward(n, mpn, a):
    large, small = forward_results(n, mpn, a)
    outs = {name: value + (ANY,) for name, value in large.items()}
    outs.update({name: value + (VMEM,) for name, value in small.items()})
    return launch(
        "forward", partial(forward_kernel, n, mpn), forward_ins(a), outs, forward_scratch(n, mpn, a),
        remote_params(0, 62),
    )


def ffn_kernel(rows_in, grads_in, parts, down_out, in_grad, weight_grad, weight, gate_low, up_low, hidden_low):
    blocks, rows, dim = rows_in.shape
    per = parts.shape[2]
    for s in range(parts.shape[0]):
        for w in range(3):
            weight[w, s * per : (s + 1) * per, :] = parts[s, w]

    def step(b, _):
        here, up = rows_in[b], grads_in[b]
        gate = dot(here, weight[0])
        other = dot(here, weight[1])
        act, slope = silu_pair(gate)
        hidden = (act * other).astype(bf16)
        hidden_low[b] = hidden
        down_out[b] = dot(hidden, weight[2], ((1,), (1,))).astype(bf16)
        hidden_grad = dot(up, weight[2])
        gate_grad = (hidden_grad * other * slope).astype(bf16)
        up_grad = (hidden_grad * act).astype(bf16)
        gate_low[b] = gate_grad
        up_low[b] = up_grad
        back = dot(gate_grad, weight[0], ((1,), (1,))) + dot(up_grad, weight[1], ((1,), (1,)))
        in_grad[b] = back.astype(bf16)
        return 0

    lax.fori_loop(0, blocks, step, 0)
    hidden = weight.shape[2]
    everything = rows_in[...].reshape(blocks * rows, dim)
    weight_grad[0] = dot(everything, gate_low[...].reshape(blocks * rows, hidden), ((0,), (0,))).astype(bf16)
    weight_grad[1] = dot(everything, up_low[...].reshape(blocks * rows, hidden), ((0,), (0,))).astype(bf16)
    weight_grad[2] = dot(
        grads_in[...].reshape(blocks * rows, dim), hidden_low[...].reshape(blocks * rows, hidden), ((0,), (0,))
    ).astype(bf16)


def ffn(rows_in, grads_in, parts):
    blocks, rows, dim = rows_in.shape
    hidden = parts.shape[3]
    return pl.pallas_call(
        ffn_kernel,
        out_shape=(
            jax.ShapeDtypeStruct((blocks, rows, dim), bf16),
            jax.ShapeDtypeStruct((blocks, rows, dim), bf16),
            jax.ShapeDtypeStruct((3, dim, hidden), bf16),
        ),
        in_specs=[VMEM] * 3,
        out_specs=(VMEM,) * 3,
        scratch_shapes=[pltpu.VMEM((3, dim, hidden), bf16)] + [pltpu.VMEM((blocks, rows, hidden), bf16)] * 3,
        compiler_params=plain_params(60),
        name="ffn",
    )(rows_in, grads_in, parts)


def mixer_bwd(r, p, lengths, upstream):
    projected = r.projected[...]
    patches = projected.shape[0]
    pos, conv_in, conv_out, step_raw, step, logd, mask, running = mixer_state(
        lengths, projected, r.taps[...], r.conv_bias[...], r.step_bias[...], r.log_decay[...]
    )
    act, act_slope = silu_pair(conv_out)
    inputs = act[:, GROUP_WIDTH : GROUP_WIDTH + STATE]
    outputs = act[:, GROUP_WIDTH + STATE :]
    inner = dot(outputs, inputs, ((1,), (1,)))
    running_t, step_t = running.T, step.T
    normed_grad = dot(upstream, r.out_v[...], ((1,), (1,)))
    y = r.mixer_y[...]
    gate = projected[:, :GROUP_WIDTH]
    gate_act, gate_slope = silu_pair(gate)
    gated_grad, gain_rows = rms_back(y * gate_act, r.group_gain[...], normed_grad)
    y_grad = gated_grad * gate_act
    gate_grad = gated_grad * y * gate_slope
    values = act[:, :GROUP_WIDTH]
    skip_cols = jnp.sum(y_grad * values, axis=0, keepdims=True)
    pair = 2 * HEAD_DIM
    lane = lax.broadcasted_iota(jnp.int32, (1, pair), 1)
    inner_grad = jnp.zeros_like(inner)
    value_pieces, row_sums, col_sums = [], [], []
    for c in range(GROUP_WIDTH // pair):
        at = slice(c * pair, (c + 1) * pair)
        got = []
        for h in (2 * c, 2 * c + 1):
            own = (lane < HEAD_DIM) if h % 2 == 0 else (lane >= HEAD_DIM)
            mine = jnp.where(own, y_grad[:, at], 0.0)
            decay = head_decay(mask, running, running_t, h)
            step_row = step_t[h : h + 1, :]
            weight_grad = dot(mine, values[:, at], ((1,), (1,))) * decay
            scaled = weight_grad * step_row
            inner_grad = inner_grad + scaled
            col_sums.append(jnp.sum(weight_grad * inner, axis=0, keepdims=True))
            row_sums.append(jnp.sum(scaled * inner, axis=1, keepdims=True))
            weights = decay * inner * step_row
            got.append(dot(weights, mine, ((0,), (0,))))
        value_pieces.append(got[0] + got[1])
    values_grad = jnp.concatenate(value_pieces, axis=1) + r.skip[...] * y_grad
    inputs_grad = dot(inner_grad, outputs, ((0,), (0,)))
    outputs_grad = dot(inner_grad, inputs)
    col_grad = jnp.concatenate(col_sums, axis=0).T
    running_grad = jnp.concatenate(row_sums, axis=1) - col_grad * step
    logd_grad = dot(mask.astype(f32), running_grad, ((0,), (0,)), precision=highest)
    step_grad = (col_grad - logd_grad * jnp.exp(r.log_decay[...])) * jax.nn.sigmoid(step_raw)
    conv_grad = jnp.concatenate([values_grad, inputs_grad, outputs_grad], axis=1) * act_slope
    conv_in_grad = jnp.zeros_like(conv_grad)
    small = r.small_part
    small[...] = jnp.zeros(small.shape, f32)
    for lag in range(CONV):
        small[CONV - 1 - lag : CONV - lag, :] = jnp.sum(
            conv_grad * conv_taps(conv_in, pos, lag), axis=0, keepdims=True
        )
        kept = jnp.where(pos >= lag, conv_grad, 0.0) * r.taps[CONV - 1 - lag : CONV - lag, :]
        conv_in_grad = conv_in_grad + (kept if lag == 0 else pltpu.roll(kept, patches - lag, 0))
    small[CONV : CONV + 1, :] = jnp.sum(conv_grad, axis=0, keepdims=True)
    small[CONV + 1 : CONV + 2, :GROUP_WIDTH] = jnp.sum(gain_rows, axis=0, keepdims=True)
    small[CONV + 2 : CONV + 3, :GROUP_WIDTH] = skip_cols
    small[CONV + 3 : CONV + 4, :GROUP_HEADS] = jnp.sum(step_grad, axis=0, keepdims=True)
    small[CONV + 4 : CONV + 5, :GROUP_HEADS] = jnp.sum(logd_grad * logd, axis=0, keepdims=True)
    return jnp.concatenate([gate_grad, conv_in_grad, step_grad], axis=1).astype(bf16)


def grad_pieces(p, r, halves, grad_of, dim, hidden):
    per = dim // p.mpn
    step = per // WEIGHT_CUTS
    pieces = []
    for hh in range(halves):
        cols = slice(hh * (hidden // halves), (hh + 1) * (hidden // halves))
        for w in range(3):
            for k in range(WEIGHT_CUTS):
                at = slice(k * step, (k + 1) * step)
                pieces.append(LineReduce(
                    p,
                    lambda t, w=w, k=k, cols=cols: grad_of(
                        w, pl.ds(pl.multiple_of(t * per + k * step, step), step), cols
                    ),
                    lambda s, w=w, at=at, cols=cols: r.g_recv.at[s, w, at, cols],
                    r.bsw.at[len(pieces)],
                    r.brw.at[len(pieces)],
                    r.g_held.at[len(pieces)] if p.line else None,
                    r.bsr.at[len(pieces)] if p.line else None,
                ))
    return Bulk(pieces)


def ffn_sums(p, r, get, put):
    in_block = lambda s: r.in_part.at[s]
    down_block = lambda s: r.down_part.at[s]
    return (
        Reduction(p, in_block, lambda s: get(in_block(s)), r.in_pre, r.in_recv, r.bs_in, get, put),
        Reduction(p, down_block, lambda s: get(down_block(s)), r.down_pre, r.down_recv, r.bs_down, get, put),
    )


def backward_steps(p, r, load, own_slab, ready, sum_in, sum_down, bulk):
    n, mpn, i, j = p.n, p.mpn, p.i, p.j
    micro, rows, dim = r.attn_in.shape
    patches = r.global_own.shape[0]
    slabs = rows // patches
    width = r.qkv_v.shape[2]
    feature = dim // n
    at_feature = lambda s: pl.ds(pl.multiple_of(s * feature, feature), feature)
    block_ao = lambda s: r.ao_part.at[at_feature(s)]
    block_qkv = lambda s: r.qkv_part.at[:, at_feature(s)]
    sum_ao = Reduction(
        p, block_ao, lambda s: block_ao(s)[...], r.ao_pre, r.ao_recv, r.bs_ao, plain_get, plain_put
    )
    sum_qkv = Reduction(
        p, block_qkv, lambda s: block_qkv(s)[...], r.qkv_pre, r.qkv_recv, r.bs_qkv, plain_get, plain_put
    )

    ready("bytes")
    for k in range(slabs):
        r.local_in[k * patches : (k + 1) * patches, :] = own_slab(k).astype(f32) + r.global_own[...]
    after = r.after[...]
    back, gain_rows = rms_back(after, r.ffn_gain[...], sum_in.finish())
    after_grad = r.own_grad[...].astype(f32) + back
    r.after_grad[...] = after_grad
    r.gains[...] = jnp.zeros(r.gains.shape, f32)
    r.gains[2:3, :] = jnp.sum(gain_rows, axis=0, keepdims=True)
    r.branch[...] = after_grad.astype(bf16)
    up_turn = jnp.where(j < mpn // 2, mpn - 1, 1)
    up_line = Exchange(p, lambda t: r.up.at[t], lambda s: r.up_recv.at[s], r.bs1, r.br1)
    for d in range(1, mpn + 1):
        t = (j + d * up_turn) % mpn
        r.up[t] = dot(r.branch[...], r.ao_sorted[t], ((1,), (1,))).astype(bf16)
        if d < mpn:
            up_line.copy(t).start()
    r.up_recv[j] = r.up[j]
    bulk.go(PACE_BACK[0])
    sum_down.spread()
    ready("qkv")

    mask = att_mask(rows, patches)
    pair = 2 * ATT_DIM
    lane = lax.broadcasted_iota(jnp.int32, (1, pair), 1)
    att_line = LineReduce(
        p, lambda t: r.att_part.at[t], lambda s: r.att_recv.at[s], r.bs2, r.br2,
        r.att_held if p.line else None, r.bsz.at[0],
    )
    turn = jnp.where(j < mpn // 2, mpn - 1, 1)

    def one_micro(d, _):
        m = (j + d * turn) % mpn

        @pl.when(d > 0)
        def _():
            up_line.wait(d * turn)

        for c in range(width // pair):
            at = slice(c * pair, (c + 1) * pair)
            query, key, value = r.qkv[0, m, :, at], r.qkv[1, m, :, at], r.qkv[2, m, :, at]
            up = r.up_recv[m, :, at]
            got = [[], [], []]
            for own in (lane < ATT_DIM, lane >= ATT_DIM):
                mine = jnp.where(own, query, jnp.zeros_like(query))
                probs = soft_rows(mask, mine, key)
                my_up = jnp.where(own, up, jnp.zeros_like(up))
                probs_grad = dot(my_up, value, ((1,), (1,)))
                inner = jnp.sum(probs * probs_grad, axis=1, keepdims=True)
                score_grad = (probs * (probs_grad - inner) * ATT_DIM ** (-0.5)).astype(bf16)
                got[0].append(dot(score_grad, key))
                got[1].append(dot(score_grad, mine, ((0,), (0,))))
                got[2].append(dot(probs.astype(bf16), my_up, ((0,), (0,))))
            r.qkv_low[0, m, :, at] = jnp.where(lane < ATT_DIM, got[0][0], got[0][1]).astype(bf16)
            r.qkv_low[1, m, :, at] = (got[1][0] + got[1][1]).astype(bf16)
            r.qkv_low[2, m, :, at] = (got[2][0] + got[2][1]).astype(bf16)
        total = dot(r.qkv_low[0, m], r.qkv_v[0], ((1,), (1,)))
        total = total + dot(r.qkv_low[1, m], r.qkv_v[1], ((1,), (1,)))
        total = total + dot(r.qkv_low[2, m], r.qkv_v[2], ((1,), (1,)))
        r.att_part[m] = total.astype(bf16)

        @pl.when(d > 0)
        def _():
            att_line.send(m)

        return 0

    lax.fori_loop(0, mpn, one_micro, 0)

    everything = r.attn_in[...].reshape(micro * rows, dim)
    for w in range(3):
        r.qkv_part[w] = dot(
            everything, r.qkv_low[w].reshape(micro * rows, width), ((0,), (0,))
        ).astype(bf16)
    sum_qkv.start()
    sum_qkv.spread()
    for t in range(mpn):
        r.ao_part[:, t * width : (t + 1) * width] = dot(
            r.branch[...], r.heads_own[t], ((0,), (0,))
        ).astype(bf16)
    sum_ao.start()
    perm = perm_matrix(rows, patches, slabs, sum(own_lengths(r, j)) - i * patches)
    block = (r.after[...] + sum_down.finish()).astype(bf16)
    block = dot(perm, block, ((0,), (0,))).astype(bf16)
    for t in range(mpn):
        r.block[t] = block[:, t * width : (t + 1) * width]
    total = r.att_part[j].astype(f32)
    att_line.wait_all()
    for s in range(mpn):
        total = total + jnp.where((s == j) | absent(p.line, j, s), 0.0, r.att_recv[s].astype(f32))
    back, gain_rows = rms_back(r.local_in[...], r.attn_gain[...], total)
    local_grad = r.after_grad[...] + back
    global_grad = local_grad[:patches]
    for k in range(1, slabs):
        global_grad = global_grad + local_grad[k * patches : (k + 1) * patches]
    r.global_grad[...] = global_grad
    r.b_low[...] = global_grad.astype(bf16)
    cast = Cast(p, r.b_low, r.mixer, r.bs3, r.br3, r.bsc)
    cast.start()
    sum_ao.spread()
    bulk.go(PACE_BACK[1])
    r.gains[1:2, :] = jnp.sum(gain_rows, axis=0, keepdims=True)
    share_rows = rows // mpn
    for t in range(mpn):
        r.local[t] = local_grad[t * share_rows : (t + 1) * share_rows].astype(bf16)
    local_line = Exchange(p, lambda t: r.local.at[t], lambda s: r.local_all.at[s], r.bs6, r.br6)
    block_line = Exchange(p, lambda t: r.block.at[t], lambda s: r.block_all.at[s], r.bs7, r.br7)
    ready("mixer")
    cast.wait()
    bulk.go(PACE_BACK[2])

    upstream = r.mixer[...].reshape(n * patches, dim)
    proj_grad = mixer_bwd(r, p, own_lengths(r, p.m), upstream)
    part = dot(proj_grad, r.in_v[...])
    for b in range(n):
        r.b_part[b] = part[b * patches : (b + 1) * patches].astype(bf16)
    to_owner = ToOwner(p, r.b_part, r.b_mid, r.b_recv, r.bs4, r.br4, r.bs9, r.br9)
    to_owner.start()
    bulk.go(PACE_BACK[3])

    r.proj_grad[...] = proj_grad
    size = n * patches // p.reps
    proj_own = r.proj_grad.at[pl.ds(pl.multiple_of(p.h * size, size), size)]
    proj_plane = PlaneGather(p, proj_own, lambda s: r.proj_all.at[s], r.bsi, r.bri, r.bsir).start()
    keep_proj = load(proj_own, r.proj_all.at[i])
    out_grad = dot(r.mixer_low[...], upstream, ((0,), (0,))).astype(bf16)
    group_rows = GROUP_WIDTH // n
    for e in range(n):
        r.out_w_part[e] = out_grad[e * group_rows : (e + 1) * group_rows]
    bundles = (
        (lambda t: r.out_w_part.at[t], r.out_w_recv, r.bso, r.bro),
        (lambda t: r.small_part, r.small_recv, r.bss, r.brs),
    )

    def each_bundle(act):
        for q in range(p.share):
            t = q * p.reps + p.h

            @pl.when(t != i)
            def _():
                for src, dst, ss, rs in bundles:
                    act(rcopy(src(t), dst.at[p.m], ss.at[q], rs.at[p.m], t, j))

    to_owner.pass_on()
    bulk.go(PACE_BACK[4])
    each_bundle(lambda copy: copy.start())
    r.out_w_recv[p.m] = r.out_w_part[i]
    r.small_recv[p.m] = r.small_part[...]
    back, gain_rows = rms_back(r.global_in[...], r.norm_in_gain[...], to_owner.total())
    r.line[j] = (r.global_grad[...] + back).astype(bf16)
    line = Exchange(p, lambda t: r.line.at[j], lambda s: r.line.at[s], r.bs5, r.br5).start()
    r.gains[0:1, :] = jnp.sum(gain_rows, axis=0, keepdims=True)
    others = [(p.mine + d) % p.half for d in range(1, p.half)]

    def gains_copy(q):
        return rcopy(r.gains, r.gains_plane.at[p.mine], r.bsh.at[q], r.brh.at[p.mine], q * 2 + p.c, j)

    for q in others:
        gains_copy(q).start()
    r.gains_plane[p.mine] = r.gains[...]
    local_line.start()
    block_line.start()
    r.local_all[j] = r.local[j]
    r.block_all[j] = r.block[j]
    line.wait_all()
    slot = lambda s: r.plane.at[s]
    plane = PlaneGather(p, r.line, slot, r.bsp, r.brp, r.bspr).start()
    keep_line = load(r.line, r.plane.at[i])
    proj_plane.relay()
    r.qkv_sum[...] = sum_qkv.finish()
    ao = sum_ao.finish().astype(bf16)
    for t in range(mpn):
        r.ao[t] = ao[:, t * width : (t + 1) * width]
    ao_line = Exchange(p, lambda t: r.ao.at[t], lambda s: r.ao_all.at[s], r.bs8, r.br8).start()
    r.ao_all[j] = r.ao[j]
    bulk.go(len(bulk.exchanges))
    for q in others:
        rcopy(r.gains, r.gains_plane.at[q], r.bsh.at[q], r.brh.at[q], q * 2 + p.c, j).wait_recv()
    r.gains_pair[0] = sum(r.gains_plane[s] for s in range(p.half))
    pair_copy = rcopy(r.gains_pair.at[0], r.gains_pair.at[1], r.bsq.at[0], r.brq.at[0], p.other, j)
    pair_copy.start()
    plane.relay()
    pair_copy.wait()
    r.gains_pair[0] = r.gains_pair[0] + r.gains_pair[1]
    width_i = r.gains_all.shape[1]
    first = i * feature // width_i * width_i
    r.gains_all[...] = r.gains_pair[0, :, pl.ds(pl.multiple_of(first, 128), width_i)]
    gains_line = Exchange(p, lambda t: r.gains_all, lambda s: r.gains_line.at[s], r.bsg, r.brg).start()
    plane.finish()
    local_line.wait_all()
    block_line.wait_all()
    ao_line.wait_all()
    for s in range(mpn):
        @pl.when(s * p.reps + p.h != i)
        def _():
            for src, dst, ss, rs in bundles:
                rcopy(src(0), dst.at[s], ss.at[0], rs.at[s], s * p.reps + p.h, j).wait_recv()
    proj_plane.finish()
    gains_line.wait_all()
    r.gains_line[j] = r.gains_all[...]
    gains_line.sent()
    r.gains_all[...] = sum(r.gains_line[s] for s in range(mpn))
    bulk.wait(0, len(bulk.exchanges))
    keep_line.wait()
    keep_proj.wait()
    for thing in (
        sum_in, sum_down, sum_ao, sum_qkv, bulk, up_line, att_line, cast, to_owner, line, local_line,
        block_line, plane, proj_plane, ao_line,
    ):
        thing.sent()
    for q in others:
        gains_copy(q).wait_send()
    each_bundle(lambda copy: copy.wait_send())


def backward_kernel(n, mpn, spill, r):
    p = place_of(n, mpn, False)
    load = Loads(r.b_load)

    def read(view):
        if not spill:
            return view[...]
        copy = pltpu.make_async_copy(view, r.stage.at[0], r.sem_stage.at[0])
        copy.start()
        copy.wait()
        return r.stage[0]

    def write(view, value):
        if not spill:
            view[...] = value
            return
        r.stage[1] = value
        copy = pltpu.make_async_copy(r.stage.at[1], view, r.sem_stage.at[1])
        copy.start()
        copy.wait()

    per = r.w_grad.shape[1] // mpn
    keep_w = load(r.w_grad.at[:, pl.ds(pl.multiple_of(p.j * per, per), per)], r.g_recv.at[p.j])
    loads = dict(
        bytes=[load(r.byte_input.at[p.j], r.own_bytes)],
        qkv=[load(r.qkv_weight, r.qkv_v)],
        mixer=[load(r.out_weight, r.out_v), load(r.in_weight, r.in_v)],
    )

    def ready(what):
        for copy in loads[what]:
            copy.wait()

    barrier = pltpu.get_barrier_semaphore()
    pl.semaphore_wait(barrier, greet_all(p, barrier))
    bulk = grad_pieces(p, r, 1, lambda w, at, cols: r.w_grad.at[w, at, cols], *r.w_grad.shape[1:])
    sum_in, sum_down = ffn_sums(p, r, read, write)
    sum_in.start()
    sum_in.spread()
    sum_down.start()
    dim = r.after.shape[1]
    own_slab = lambda k: r.own_bytes[:, k * dim : (k + 1) * dim]
    backward_steps(p, r, load, own_slab, ready, sum_in, sum_down, bulk)
    keep_w.wait()


def backward_results(n, mpn, a):
    micro, patches, cols = a.byte_input.shape
    dim = a.norm_in_gain.shape[1]
    rows = patches * (cols // dim)
    width = a.qkv_weight.shape[2]
    hidden = a.ffn_weight.shape[2]
    feature = dim // n
    return dict(
        g_recv=((mpn, 3, dim // mpn, hidden), bf16, ANY),
        plane=((n, mpn, patches, dim), bf16, ANY),
        qkv_sum=((3, feature, width), f32, VMEM),
        ao_all=((mpn, feature, width), bf16, VMEM),
        proj_all=((n, n * patches // (n // mpn), a.in_weight.shape[0]), bf16, ANY),
        out_w_recv=((mpn, GROUP_WIDTH // n, dim), bf16, VMEM),
        small_recv=((mpn, 16, CONV_CH), f32, VMEM),
        gains_all=((8, max(feature, 128)), f32, VMEM),
        local_all=((mpn, rows // mpn, dim), bf16, VMEM),
        block_all=((mpn, rows, width), bf16, VMEM),
    )


def backward_scratch(n, mpn, a):
    micro, patches, cols = a.byte_input.shape
    dim = a.norm_in_gain.shape[1]
    rows = patches * (cols // dim)
    width = a.qkv_weight.shape[2]
    hidden = a.ffn_weight.shape[2]
    half, share = n // 2, mpn
    feature = dim // n
    pieces = max(hidden // FFN_COLS, 1) * 3 * WEIGHT_CUTS
    line, plane = DMA((mpn,)), DMA((half,))
    return dict(
        local_in=pltpu.VMEM((rows, dim), f32),
        after_grad=pltpu.VMEM((rows, dim), f32),
        branch=pltpu.VMEM((rows, dim), bf16),
        up=pltpu.VMEM((mpn, rows, width), bf16),
        up_recv=pltpu.VMEM((mpn, rows, width), bf16),
        qkv_low=pltpu.VMEM((3, micro, rows, width), bf16),
        att_part=pltpu.VMEM((micro, rows, dim), bf16),
        att_recv=pltpu.VMEM((mpn, rows, dim), bf16),
        qkv_part=pltpu.VMEM((3, dim, width), bf16),
        qkv_pre=pltpu.VMEM((half, 3, feature, width), bf16),
        qkv_recv=pltpu.VMEM((half, 3, feature, width), bf16),
        ao_part=pltpu.VMEM((dim, mpn * width), bf16),
        ao_pre=pltpu.VMEM((half, feature, mpn * width), bf16),
        ao_recv=pltpu.VMEM((half, feature, mpn * width), bf16),
        ao=pltpu.VMEM((mpn, feature, width), bf16),
        block=pltpu.VMEM((mpn, rows, width), bf16),
        local=pltpu.VMEM((mpn, rows // mpn, dim), bf16),
        b_low=pltpu.VMEM((patches, dim), bf16),
        global_grad=pltpu.VMEM((patches, dim), f32),
        mixer=pltpu.VMEM((n, patches, dim), bf16),
        b_part=pltpu.VMEM((n, patches, dim), bf16),
        b_mid=pltpu.VMEM((mpn, patches, dim), bf16),
        b_recv=pltpu.VMEM((mpn, patches, dim), bf16),
        line=pltpu.VMEM((mpn, patches, dim), bf16),
        proj_grad=pltpu.VMEM((n * patches, a.in_weight.shape[0]), bf16),
        out_w_part=pltpu.VMEM((n, GROUP_WIDTH // n, dim), bf16),
        small_part=pltpu.VMEM((16, CONV_CH), f32),
        gains=pltpu.VMEM((8, dim), f32),
        gains_line=pltpu.VMEM((mpn, 8, max(feature, 128)), f32),
        gains_plane=pltpu.VMEM((half, 8, dim), f32),
        gains_pair=pltpu.VMEM((2, 8, dim), f32),
        b_load=DMA((16,)),
        bs_in=DMA((4, half)), bs_down=DMA((4, half)), bs_ao=DMA((4, half)), bs_qkv=DMA((4, half)),
        bs1=line, br1=line, bs2=line, br2=line, bs3=DMA((n,)), br3=DMA((n,)), bsc=plane, bs4=line, br4=line, bs9=line, br9=line,
        bs5=line, br5=line, bs6=line, br6=line, bs7=line, br7=line, bs8=line, br8=line,
        bsp=plane, brp=DMA((n,)), bspr=plane,
        bsg=line, brg=line, bsh=plane, brh=plane, bsq=DMA((1,)), brq=DMA((1,)),
        bsz=DMA((1,)), bsi=plane, bri=DMA((n,)), bsir=plane, bso=DMA((share,)), bro=line, bss=DMA((share,)), brs=line,
        bsw=DMA((pieces, mpn)), brw=DMA((pieces, mpn)),
    )


def sum_buffers(n, a, make):
    micro, patches, cols = a.byte_input.shape
    dim = a.norm_in_gain.shape[1]
    shape = (n // 2, patches * (cols // dim), dim)
    return {name: make(shape) for name in ("in_pre", "in_recv", "down_pre", "down_recv")}


def backward(n, mpn, a):
    spill = a.in_part.size * 2 > SPILL_BYTES
    ins = dict(seq_lengths=(a.seq_lengths, SMEM))
    for name in ("byte_input", "w_grad", "in_weight", "out_weight", "qkv_weight"):
        ins[name] = (getattr(a, name), ANY)
    for name in ("in_part", "down_part"):
        ins[name] = (getattr(a, name), ANY if spill else VMEM)
    for name in SMALL_PARAMS + (
        "after", "own_grad", "heads_own", "qkv", "attn_in", "ao_sorted", "global_in", "global_own", "normed",
        "projected", "mixer_y", "mixer_low",
    ):
        ins[name] = (getattr(a, name), VMEM)
    outs = backward_results(n, mpn, a)
    scratch = backward_scratch(n, mpn, a)
    scratch.update(
        own_bytes=pltpu.VMEM(a.byte_input.shape[1:], bf16),
        in_v=pltpu.VMEM(a.in_weight.shape, bf16),
        out_v=pltpu.VMEM(a.out_weight.shape, bf16),
        qkv_v=pltpu.VMEM(a.qkv_weight.shape, bf16),
    )
    if spill:
        outs.update(sum_buffers(n, a, lambda shape: (shape, bf16, ANY)))
        scratch.update(stage=pltpu.VMEM((2,) + a.in_part.shape[1:], bf16), sem_stage=DMA((2,)))
    else:
        scratch.update(sum_buffers(n, a, lambda shape: pltpu.VMEM(shape, bf16)))
    return launch(
        "backward", partial(backward_kernel, n, mpn, spill), ins, outs, scratch, remote_params(1, 63)
    )


def ffn_steps(p, r, st, load, sum_in, sum_down, bulk, grad_of):
    n, half = p.n, p.half
    rows, dim = r.own_grad.shape
    hidden = r.w_v.shape[2]
    cols = hidden // st.halves
    per = dim // p.mpn
    pair = 2 * rows
    st.grads.finish()
    grads_all = lambda: r.grad_rows[...].reshape(n * rows, dim)
    rows_all = lambda: r.ffn_rows[...].reshape(n * rows, dim)
    kept = []
    if st.halves == 1:
        st.rows.relay()
        st.rows.finish()
    count = len(st.bulk.exchanges) // st.halves
    for hh in range(st.halves):
        at = slice(hh * cols, (hh + 1) * cols)
        last = hh == st.halves - 1
        if last:
            st.bulk.go(len(st.bulk.exchanges))
        st.bulk.wait(hh * count, (hh + 1) * count)
        if hh == 0:
            for copy in st.kept:
                copy.wait()

        def compute(q):
            here = r.ffn_rows[pl.ds(2 * q, 2)].reshape(pair, dim)
            up = r.grad_rows[pl.ds(2 * q, 2)].reshape(pair, dim)
            gate = dot(here, r.w_v[0, :, at])
            other = dot(here, r.w_v[1, :, at])
            act, slope = silu_pair(gate)
            hidden_low = (act * other).astype(bf16)
            here_at = pl.ds(pl.multiple_of(q * pair, pair), pair)
            r.hidden_low[hh, here_at, :] = hidden_low
            down = dot(hidden_low, r.w_v[2, :, at], ((1,), (1,)))
            hidden_grad = dot(up, r.w_v[2, :, at])
            gate_grad = (hidden_grad * other * slope).astype(bf16)
            up_grad = (hidden_grad * act).astype(bf16)
            r.gate_low[hh, here_at, :] = gate_grad
            r.up_low[hh, here_at, :] = up_grad
            back = dot(gate_grad, r.w_v[0, :, at], ((1,), (1,))) + dot(up_grad, r.w_v[1, :, at], ((1,), (1,)))
            if hh > 0:
                back = back + r.in_part[pl.ds(2 * q, 2)].reshape(pair, dim).astype(f32)
                down = down + r.down_part[pl.ds(2 * q, 2)].reshape(pair, dim).astype(f32)
            r.in_part[pl.ds(2 * q, 2)] = back.astype(bf16).reshape(2, rows, dim)
            r.down_part[pl.ds(2 * q, 2)] = down.astype(bf16).reshape(2, rows, dim)

        def first_pass(d, _):
            q = (p.mine + half - d) % half

            @pl.when(d > 0)
            def _():
                st.rows.relay_one(q)

            st.rows.wait_across(q)
            compute(q)
            return 0

        def last_pass(d, _):
            q = (p.mine + d) % half
            compute(q)
            sum_in.first(q).start()

            @pl.when(d > 1)
            def _():
                sum_in.spread_one((p.mine + d - 1) % half)

            return 0

        if last:
            lax.fori_loop(1, half + 1, last_pass, 0)
            sum_down.start()
        else:
            lax.fori_loop(0, half, first_pass, 0)
        everything = slice(0, dim)
        grad_of(0, everything, at)[...] = dot(rows_all(), r.gate_low[hh], ((0,), (0,))).astype(bf16)
        grad_of(1, everything, at)[...] = dot(rows_all(), r.up_low[hh], ((0,), (0,))).astype(bf16)
        grad_of(2, everything, at)[...] = dot(grads_all(), r.hidden_low[hh], ((0,), (0,))).astype(bf16)
        mine = pl.ds(pl.multiple_of(p.j * per, per), per)
        kept += [load(grad_of(w, mine, at), r.g_recv.at[p.j, w, :, at]) for w in range(3)]
        if not last:
            bulk.go(PACE_FFN)
    return kept


def layer_kernel(n, mpn, r):
    p = place_of(n, mpn, mpn == 4)
    dim = r.after.shape[1]

    def put_rows(ref):
        def put(s, value):
            ref[s] = value

        return put

    r.grad_rows_own = put_rows(r.grad_rows)
    r.ffn_rows_own = put_rows(r.ffn_rows)
    per = r.ffn_weight.shape[1]

    def land(s, w, rows, cols):
        first = (0 if rows.start is None else rows.start) + s * per
        size = per if rows.start is None else rows.stop - rows.start
        return r.w_v.at[w, pl.ds(pl.multiple_of(first, size), size), cols]

    load = Loads(r.sem_load)
    st = forward_steps(p, r, load, land)
    hidden = r.w_v.shape[2]

    def grad_of(w, at, cols):
        first = w % 2 * hidden
        return r.pw.at[w // 2, at, first + cols.start : first + cols.stop]

    bulk = grad_pieces(p, r, st.halves, grad_of, dim, hidden)
    sum_in, sum_down = ffn_sums(p, r, plain_get, plain_put)
    load = Loads(r.b_load)
    kept = ffn_steps(p, r, st, load, sum_in, sum_down, bulk, grad_of)
    own_slab = lambda k: r.bytes_v[p.j, :, k * dim : (k + 1) * dim]
    backward_steps(p, r, load, own_slab, lambda what: None, sum_in, sum_down, bulk)
    st.settle()
    for copy in kept:
        copy.wait()


def layer(n, mpn, a):
    dim = a.norm_in_gain.shape[1]
    hidden = a.ffn_weight.shape[2]
    halves = max(hidden // FFN_COLS, 1)
    large, small = forward_results(n, mpn, a)
    rows = small["own_grad"][0][0]
    outs = {name: large.pop(name) + (ANY,) for name in ("bytes_part", "normed_cols")}
    outs.update(backward_results(n, mpn, a))
    large.pop("w_all")
    scratch = forward_scratch(n, mpn, a)
    scratch.update(backward_scratch(n, mpn, a))
    for name, (shape, dtype) in (*large.items(), *small.items()):
        scratch[name] = pltpu.VMEM(shape, dtype)
    scratch.update(sum_buffers(n, a, lambda shape: pltpu.VMEM(shape, bf16)))
    scratch.update(
        g_held=pltpu.VMEM((halves * 3 * WEIGHT_CUTS, dim // mpn // WEIGHT_CUTS, hidden // halves), bf16),
        att_held=pltpu.VMEM((rows, dim), bf16),
        bsr=DMA((halves * 3 * WEIGHT_CUTS,)),
        w_v=pltpu.VMEM((3, dim, hidden), bf16),
        in_part=pltpu.VMEM((n, rows, dim), bf16),
        down_part=pltpu.VMEM((n, rows, dim), bf16),
        gate_low=pltpu.VMEM((halves, n * rows, hidden // halves), bf16),
        up_low=pltpu.VMEM((halves, n * rows, hidden // halves), bf16),
        hidden_low=pltpu.VMEM((halves, n * rows, hidden // halves), bf16),
    )
    return launch(
        "layer", partial(layer_kernel, n, mpn), forward_ins(a), outs, scratch, remote_params(2, 63)
    )


def finish_kernel(line, r):
    i, j = lax.axis_index("dp"), lax.axis_index("mp")
    mpn, patches, dim = r.plane.shape[1:]
    n = r.plane.shape[0]
    features = r.bytes_part.shape[-1]
    positions = r.patch_weight.shape[0]
    feature = dim // n
    everyone = r.plane[...].reshape(n * mpn * patches, dim)
    own = r.plane[i].reshape(mpn * patches, dim)
    for k in range(positions):
        mine = r.bytes_part[:, k].reshape(n * mpn * patches, features)
        got = dot(mine, everyone, ((0,), (0,)))
        if features != feature:
            cut = features // feature
            got = sum(
                jnp.where(i % cut == e, got[e * feature : (e + 1) * feature], 0.0) for e in range(cut)
            )
        r.patch_grad[k] = got
        piece = dot(own, r.patch_weight[k], ((1,), (1,)))
        for m in range(mpn):
            r.input_grad[m, :, k * dim : (k + 1) * dim] = (
                piece[m * patches : (m + 1) * patches]
                + r.local_all[m, k * patches : (k + 1) * patches, :].astype(f32)
            )
    for w in range(3):
        r.ffn_grad[w] = sum(
            jnp.where(absent(line, j, s), 0.0, r.g_recv[s, w].astype(f32)) for s in range(mpn)
        )
    r.ao_grad[...] = sum(r.ao_all[s].astype(f32) for s in range(mpn)).T
    columns = r.in_grad.shape[0]
    got = dot(
        r.proj_all[...].reshape(n * mpn * patches, columns),
        r.normed_cols[...].reshape(n * mpn * patches, features), ((0,), (0,)),
    )
    if features != feature:
        cut = features // feature
        got = sum(jnp.where(i % cut == e, got[:, e * feature : (e + 1) * feature], 0.0) for e in range(cut))
    r.in_grad[...] = got
    r.out_grad[...] = sum(r.out_w_recv[s].astype(f32) for s in range(mpn))
    small = sum(r.small_recv[s] for s in range(mpn))

    def chosen(values, size):
        whole = values.shape[1]
        at = lax.broadcasted_iota(jnp.int32, (whole, size), 0)
        want = lax.broadcasted_iota(jnp.int32, (whole, size), 1) + i * size % whole
        return dot(values, (at == want).astype(f32), precision=highest)

    conv = chosen(small, CONV_CH // n)
    r.conv_w_grad[...] = conv[:CONV]
    r.conv_b_grad[...] = conv[CONV : CONV + 1]
    group = chosen(small[:, :GROUP_WIDTH], GROUP_WIDTH // n)
    r.group_grad[...] = group[CONV + 1 : CONV + 2]
    heads = lax.broadcasted_iota(jnp.int32, (GROUP_WIDTH, GROUP_HEADS), 0) // HEAD_DIM
    pick = heads == lax.broadcasted_iota(jnp.int32, (GROUP_WIDTH, GROUP_HEADS), 1)
    skip = dot(small[:, :GROUP_WIDTH], pick.astype(f32), precision=highest)
    r.skip_grad[...] = skip[CONV + 2 : CONV + 3]
    r.step_grad[...] = small[CONV + 3 : CONV + 4, :GROUP_HEADS]
    r.decay_grad[...] = small[CONV + 4 : CONV + 5, :GROUP_HEADS]
    gains = chosen(r.gains_all[...], feature)
    r.norm_in_grad[...] = gains[0:1]
    r.attn_gain_grad[...] = gains[1:2]
    r.ffn_gain_grad[...] = gains[2:3]
    r.qkv_grad[...] = r.qkv_sum[...]
    r.block_out[...] = r.block_all[...]


def finish(a, line):
    n, mpn, patches, dim = a.plane.shape
    positions = a.patch_weight.shape[0]
    feature = dim // n
    columns = a.in_weight.shape[0]
    names = (
        "plane", "bytes_part", "patch_weight", "local_all", "g_recv", "ao_all", "proj_all", "normed_cols", "out_w_recv",
        "small_recv", "gains_all", "qkv_sum", "block_all",
    )
    row = lambda size: ((1, size), f32, VMEM)
    outs = dict(
        patch_grad=((positions, feature, dim), f32, VMEM),
        input_grad=((mpn, patches, positions * dim), f32, VMEM),
        ffn_grad=(a.g_recv.shape[1:], f32, VMEM),
        ao_grad=(a.ao_all.shape[:0:-1], f32, VMEM),
        in_grad=((columns, feature), f32, VMEM),
        out_grad=(a.out_w_recv.shape[1:], f32, VMEM),
        conv_w_grad=((CONV, CONV_CH // n), f32, VMEM),
        conv_b_grad=row(CONV_CH // n),
        group_grad=row(GROUP_WIDTH // n),
        skip_grad=row(GROUP_HEADS),
        step_grad=row(GROUP_HEADS),
        decay_grad=row(GROUP_HEADS),
        norm_in_grad=row(feature),
        attn_gain_grad=row(feature),
        ffn_gain_grad=row(feature),
        qkv_grad=(a.qkv_sum.shape, f32, VMEM),
        block_out=(a.block_all.shape, bf16, VMEM),
    )
    ins = {name: (getattr(a, name), VMEM) for name in names}
    return launch("finish", partial(finish_kernel, line), ins, outs, {}, plain_params())


def body(
    byte_input,
    seq_lengths,
    patch_weight,
    norm_in_gain,
    in_weight,
    conv_weight,
    conv_bias,
    step_bias,
    log_decay,
    skip_gain,
    group_gain,
    out_weight,
    attn_gain,
    qkv_weight,
    attn_out_weight,
    ffn_gain,
    ffn_weight,
    out_grad,
):
    n, mpn = lax.axis_size("dp"), lax.axis_size("mp")
    row = lambda v: v.reshape(1, -1)
    a = SimpleNamespace(
        byte_input=byte_input,
        seq_lengths=seq_lengths,
        patch_weight=patch_weight,
        norm_in_gain=row(norm_in_gain),
        in_weight=in_weight[0].T,
        taps=conv_weight[0].T,
        conv_bias=conv_bias,
        step_bias=step_bias,
        log_decay=log_decay,
        skip=row(jnp.repeat(skip_gain[0], HEAD_DIM)),
        group_gain=group_gain,
        out_weight=out_weight[0],
        attn_gain=row(attn_gain),
        qkv_weight=qkv_weight,
        attn_out_weight=attn_out_weight,
        ffn_gain=row(ffn_gain),
        ffn_weight=ffn_weight,
        out_grad=out_grad,
    )
    dim, hidden = ffn_gain.shape[0], ffn_weight.shape[2]
    fits = n * out_grad.shape[1] * dim * 2 <= SPILL_BYTES and 2 * hidden <= dim
    if fits:
        a.__dict__.update(layer(n, mpn, a).__dict__)
    else:
        a.__dict__.update(forward(n, mpn, a).__dict__)
        a.down_part, a.in_part, a.w_grad = ffn(a.ffn_rows, a.grad_rows, a.w_all)
        a.__dict__.update(backward(n, mpn, a).__dict__)
    f = finish(a, fits and mpn == 4)
    return (
        f.block_out,
        f.input_grad,
        f.patch_grad,
        f.norm_in_grad[0],
        f.in_grad.T[None],
        f.conv_w_grad.T[None],
        f.conv_b_grad,
        f.step_grad,
        f.decay_grad,
        f.skip_grad,
        f.group_grad,
        f.out_grad[None],
        f.attn_gain_grad[0],
        f.qkv_grad,
        f.ao_grad,
        f.ffn_gain_grad[0],
        f.ffn_grad,
    )


def solution(mesh):
    in_specs = (
        P(None, "dp", None),
        P(),
        P("mp", None, None),
        P(),
        P("mp", None, None),
        P("mp", None, None),
        P("mp", None),
        P("mp", None),
        P("mp", None),
        P("mp", None),
        P("mp", None),
        P("mp", None, None),
        P(),
        P(None, None, "mp"),
        P("mp", None),
        P(),
        P(None, "mp", "dp"),
        P(None, "dp", None),
    )
    out_specs = (
        P(None, "dp", "mp"),
        P(None, "dp", "mp"),
        P("mp", "dp", None),
        P("dp"),
        P("mp", "dp", None),
        P("mp", "dp", None),
        P("mp", "dp"),
        P("mp", None),
        P("mp", None),
        P("mp", None),
        P("mp", "dp"),
        P("mp", "dp", None),
        P("dp"),
        P(None, "dp", "mp"),
        P("mp", "dp"),
        P("dp"),
        P(None, "mp", "dp"),
    )
    return jax.shard_map(body, mesh=mesh, in_specs=in_specs, out_specs=out_specs, check_vma=False)
```

```python
from functools import partial
from types import SimpleNamespace

import jax
import jax.numpy as jnp
from jax import lax
from jax.experimental import pallas as pl
from jax.experimental.pallas import tpu as pltpu
from jax.sharding import PartitionSpec as P

STATE = 128
CONV = 4
SEQS = 3
GROUP_WIDTH = 512
GROUP_HEADS = 8
HEAD_DIM = 64
ATT_DIM = 64
CONV_CH = 768

norm_eps = 1e-06
highest = lax.Precision.HIGHEST
large_negative = -1e30
f32 = jnp.float32
bf16 = jnp.bfloat16
MESH = pl.DeviceIdType.MESH
VMEM = pl.BlockSpec(memory_space=pltpu.VMEM)
ANY = pl.BlockSpec(memory_space=pl.ANY)
SMEM = pl.BlockSpec(memory_space=pltpu.SMEM)
DMA = pltpu.SemaphoreType.DMA
SMALL_PARAMS = (
    "norm_in_gain", "taps", "conv_bias", "step_bias", "log_decay", "skip", "group_gain", "attn_gain", "ffn_gain"
)
SPILL_BYTES = 4 * 2**20
FFN_COLS = 256
WEIGHT_CUTS = 2
PACE = (1, 1, 1, 1, 1, 2, 6, 0)
PACE_FFN = 6
RELAY_WEIGHTS = ((2, 8), (3, 10))
RELAY_GRADS = (3, 6)
PACE_BACK = (0, 3, 3, 0, 0)


def dot(a, b, dims=((1,), (0,)), precision=None):
    return lax.dot_general(
        a, b, (dims, ((), ())), preferred_element_type=f32, precision=precision
    )


def inv_rms(values):
    return lax.rsqrt(jnp.mean(values * values, axis=-1, keepdims=True) + norm_eps)


def rms_back(values, gain, upstream):
    scale = inv_rms(values)
    weighted = upstream * gain
    inner = jnp.mean(weighted * values, axis=-1, keepdims=True)
    back = scale * weighted - values * (inner * scale * scale * scale)
    return back, upstream * (values * scale)


def silu_pair(values):
    sig = jax.nn.sigmoid(values)
    return values * sig, sig * (1.0 + values * (1.0 - sig))


def rcopy(src, dst, send_sem, recv_sem, dp, mp):
    return pltpu.make_async_remote_copy(
        src_ref=src,
        dst_ref=dst,
        send_sem=send_sem,
        recv_sem=recv_sem,
        device_id={"dp": dp, "mp": mp},
        device_id_type=MESH,
    )


def greet(barrier, dp, mp):
    pl.semaphore_signal(barrier, inc=1, device_id={"dp": dp, "mp": mp}, device_id_type=MESH)


def plain_params(mib=56):
    return pltpu.CompilerParams(vmem_limit_bytes=mib * 2**20)


def remote_params(cid, mib=40):
    return pltpu.CompilerParams(
        collective_id=cid, has_side_effects=True, vmem_limit_bytes=mib * 2**20
    )


def launch(name, kernel, ins, outs, scratch, params):
    names = [*ins, *outs, *scratch]

    def run(*refs):
        kernel(SimpleNamespace(**dict(zip(names, refs))))

    results = pl.pallas_call(
        run,
        out_shape=tuple(jax.ShapeDtypeStruct(shape, dtype) for shape, dtype, _ in outs.values()),
        in_specs=[spec for _, spec in ins.values()],
        out_specs=tuple(spec for _, _, spec in outs.values()),
        scratch_shapes=list(scratch.values()),
        compiler_params=params,
        name=name,
    )(*[array for array, _ in ins.values()])
    return SimpleNamespace(**dict(zip(outs, results)))


def place_of(n, mpn, line):
    i, j = lax.axis_index("dp"), lax.axis_index("mp")
    reps = n // mpn
    return SimpleNamespace(
        n=n, mpn=mpn, i=i, j=j, reps=reps, share=n // reps, half=n // 2,
        m=i // reps, h=i % reps, c=i % 2, mine=i // 2, other=i + 1 - 2 * (i % 2), inside=i // reps == j, line=line,
    )


def greet_all(p, barrier):
    for d in range(1, p.mpn):
        greet(barrier, p.i, (p.j + d) % p.mpn)
    for d in range(1, p.n):
        greet(barrier, (p.i + d) % p.n, p.j)
    for q in range(p.half):
        s = q * 2 + p.c

        @pl.when(jnp.logical_not((s == p.i) & p.inside))
        def _():
            greet(barrier, s, p.m)

    for h in range(0, p.reps, 2):
        for t in range(p.mpn):
            @pl.when(jnp.logical_not((p.j * p.reps + h + p.c == p.i) & (t == p.j)))
            def _():
                greet(barrier, p.j * p.reps + h + p.c, t)
    return p.mpn + p.n - 2 + p.half + p.reps // 2 * p.mpn - 2 * p.inside.astype(jnp.int32)


class Exchange:
    def __init__(self, p, src, dst, ss, rs):
        self.p, self.src, self.dst, self.ss, self.rs = p, src, dst, ss, rs

    def copy(self, t):
        p = self.p
        return rcopy(self.src(t), self.dst(p.j), self.ss.at[t], self.rs.at[p.j], p.i, t)

    def start(self):
        for d in range(1, self.p.mpn):
            self.copy((self.p.j + d) % self.p.mpn).start()
        return self

    def wait(self, d):
        s = (self.p.j + d) % self.p.mpn
        rcopy(self.dst(s), self.dst(s), self.ss.at[s], self.rs.at[s], self.p.i, s).wait_recv()
        return s

    def wait_all(self):
        for d in range(1, self.p.mpn):
            self.wait(d)

    def sent(self):
        for d in range(1, self.p.mpn):
            self.copy((self.p.j + d) % self.p.mpn).wait_send()


class LineGather(Exchange):
    def begin(self):
        for d in range(1, self.p.mpn):
            def send():
                self.copy((self.p.j + d) % self.p.mpn).start()

            self.unless_far(d, send)

    def unless_far(self, d, act):
        if d == 2 or not self.p.line:
            act()
        else:
            pl.when(self.p.j != (3 if d == 1 else 0))(act)

    def onward(self, at):
        s, t = (0, 3) if at == 2 else (3, 0)
        return rcopy(self.dst(s), self.dst(s), self.ss.at[at], self.rs.at[s], self.p.i, t)

    def relay(self):
        if not self.p.line:
            return
        for at in (1, 2):
            @pl.when(self.p.j == at)
            def _():
                self.wait(2)
                self.onward(at).start()

    def wait_all(self):
        for d in range(1, self.p.mpn):
            if d == 2 and self.p.line:
                @pl.when((self.p.j == 0) | (self.p.j == 3))
                def _():
                    self.wait(2)
            else:
                self.wait(d)

    def sent(self):
        for d in range(1, self.p.mpn):
            def done():
                self.copy((self.p.j + d) % self.p.mpn).wait_send()

            self.unless_far(d, done)
        if self.p.line:
            for at in (1, 2):
                @pl.when(self.p.j == at)
                def _():
                    self.onward(at).wait_send()


class LineReduce(Exchange):
    def __init__(self, p, src, dst, ss, rs, held, hs):
        super().__init__(p, src, dst, ss, rs)
        self.held, self.hs = held, hs

    def begin(self):
        p = self.p
        for d in range(1, p.mpn):
            t = (p.j + d) % p.mpn
            if not p.line:
                self.copy(t).start()
            elif d == 2:
                @pl.when((p.j == 0) | (p.j == 3))
                def _():
                    self.copy(t).start()
            else:
                end = 3 if d == 1 else 0

                @pl.when(p.j != end)
                def _():
                    self.copy(t).start()

                @pl.when(p.j == end)
                def _():
                    rcopy(self.src(t), self.held, self.ss.at[t], self.hs, p.i, 2 if end == 3 else 1).start()

    def send(self, t):
        p = self.p
        if not p.line:
            self.copy(t).start()
            return
        apart = jnp.abs(t - p.j)
        taking = (apart == 2) & ((p.j == 1) | (p.j == 2))

        @pl.when(apart == 3)
        def _():
            rcopy(self.src(t), self.held, self.ss.at[t], self.hs, p.i, jnp.where(p.j == 0, 1, 2)).start()

        @pl.when((apart < 3) & jnp.logical_not(taking))
        def _():
            self.copy(t).start()

        pl.when(taking)(self.relay)

    def relay(self):
        p = self.p
        if not p.line:
            return

        @pl.when((p.j == 1) | (p.j == 2))
        def _():
            t = (p.j + 2) % p.mpn
            rcopy(self.held, self.held, self.ss.at[t], self.hs, p.i, t).wait_recv()
            self.held[...] = (self.held[...].astype(f32) + self.src(t)[...].astype(f32)).astype(bf16)
            rcopy(self.held, self.dst(p.j), self.ss.at[t], self.rs.at[p.j], p.i, t).start()

    def wait_all(self):
        for d in range(1, self.p.mpn):
            if d == 2 or not self.p.line:
                self.wait(d)
            else:
                @pl.when(self.p.j != (3 if d == 1 else 0))
                def _():
                    self.wait(d)


def absent(line, j, s):
    return line & (((j == 3) & (s == 0)) | ((j == 0) & (s == 3)))


class Bulk:
    def __init__(self, exchanges):
        self.exchanges, self.begun, self.before, self.relayed = exchanges, 0, 0, 0

    def relay(self, last):
        last = min(last, self.begun)
        for exchange in self.exchanges[self.relayed : last]:
            exchange.relay()
        self.relayed = max(last, self.relayed)

    def go(self, count):
        count = min(count, len(self.exchanges) - self.begun)
        self.relay(self.before)
        self.before = self.begun
        for exchange in self.exchanges[self.begun : self.begun + count]:
            exchange.begin()
        self.begun += count

    def wait(self, first, last):
        self.relay(last)
        for exchange in self.exchanges[first:last]:
            exchange.wait_all()

    def sent(self):
        for exchange in self.exchanges:
            exchange.sent()


class PlaneGather:
    def __init__(self, p, own, slot, ss, rs, ssr):
        self.p, self.own, self.slot, self.ss, self.rs, self.ssr = p, own, slot, ss, rs, ssr

    def direct(self, q):
        p = self.p
        return rcopy(self.own, self.slot(p.i), self.ss.at[q], self.rs.at[p.i], q * 2 + p.c, p.j)

    def across(self, q):
        p = self.p
        s = q * 2 + p.c
        return rcopy(self.slot(s), self.slot(s), self.ssr.at[q], self.rs.at[s], p.other, p.j)

    def own_across(self):
        p = self.p
        return rcopy(self.own, self.slot(p.i), self.ssr.at[p.mine], self.rs.at[p.i], p.other, p.j)

    def others(self):
        return [(self.p.mine + d) % self.p.half for d in range(1, self.p.half)]

    def start(self):
        self.own_across().start()
        for q in self.others():
            self.direct(q).start()
        return self

    def relay_one(self, q):
        s = q * 2 + self.p.c
        rcopy(self.slot(s), self.slot(s), self.ss.at[q], self.rs.at[s], s, self.p.j).wait_recv()
        self.across(q).start()

    def wait_across(self, q):
        s = q * 2 + 1 - self.p.c
        rcopy(self.slot(s), self.slot(s), self.ssr.at[q], self.rs.at[s], self.p.other, self.p.j).wait_recv()

    def relay(self):
        for q in reversed(self.others()):
            self.relay_one(q)

    def finish(self):
        for q in range(self.p.half):
            self.wait_across(q)

    def sent(self):
        self.own_across().wait_send()
        for q in self.others():
            self.direct(q).wait_send()
            self.across(q).wait_send()


class Reduction:
    def __init__(self, p, block, value, pre, recv, ss, get, put):
        self.p, self.block, self.value, self.pre, self.recv, self.get, self.put = p, block, value, pre, recv, get, put
        self.ssa, self.rsa, self.ssb, self.rsb = (ss.at[k] for k in range(4))

    def first(self, q):
        p = self.p
        return rcopy(self.block(q * 2 + 1 - p.c), self.pre.at[q], self.ssa.at[q], self.rsa.at[q], p.other, p.j)

    def second(self, q):
        p = self.p
        return rcopy(self.pre.at[q], self.recv.at[p.mine], self.ssb.at[q], self.rsb.at[p.mine], q * 2 + p.c, p.j)

    def others(self):
        return [(self.p.mine + d) % self.p.half for d in range(1, self.p.half)]

    def start(self):
        for q in self.others() + [self.p.mine]:
            self.first(q).start()

    def spread_one(self, q):
        p = self.p
        rcopy(self.pre.at[q], self.pre.at[q], self.ssa.at[q], self.rsa.at[q], p.other, p.j).wait_recv()
        total = self.value(q * 2 + p.c).astype(f32)
        self.put(self.pre.at[q], (total + self.get(self.pre.at[q]).astype(f32)).astype(bf16))
        self.second(q).start()

    def spread(self):
        for q in self.others():
            self.spread_one(q)

    def finish(self):
        p, mine = self.p, self.p.mine
        rcopy(self.pre.at[mine], self.pre.at[mine], self.ssa.at[mine], self.rsa.at[mine], p.other, p.j).wait_recv()
        total = self.value(p.i).astype(f32)
        total = total + self.get(self.pre.at[mine]).astype(f32)
        for q in self.others():
            rcopy(self.recv.at[q], self.recv.at[q], self.ssb.at[q], self.rsb.at[q], q * 2 + p.c, p.j).wait_recv()
            total = total + self.get(self.recv.at[q]).astype(f32)
        return total

    def sent(self):
        for q in self.others() + [self.p.mine]:
            self.first(q).wait_send()
        for q in self.others():
            self.second(q).wait_send()


def plain_get(view):
    return view[...]


def plain_put(view, value):
    view[...] = value


class Cast:
    def __init__(self, p, low, dst, ss, rs, ssr):
        self.p, self.low, self.dst, self.ss, self.rs, self.ssr = p, low, dst, ss, rs, ssr

    def each(self, act):
        p = self.p
        for h in range(0, p.reps, 2):
            for t in range(p.mpn):
                to = p.j * p.reps + h + p.c

                @pl.when(jnp.logical_not((to == p.i) & (t == p.j)))
                def _():
                    act(rcopy(self.low, self.dst.at[p.i], self.ss.at[h // 2 * p.mpn + t], self.rs.at[p.i], to, t))

    def across(self, q):
        p = self.p
        s = q * 2 + p.c
        return rcopy(self.dst.at[s], self.dst.at[s], self.ssr.at[q], self.rs.at[s], p.other, p.j)

    def start(self):
        self.each(lambda copy: copy.start())

        @pl.when(self.p.inside)
        def _():
            self.dst[self.p.i] = self.low[...]

    def wait(self):
        p = self.p
        for q in range(p.half):
            s = q * 2 + p.c

            @pl.when(jnp.logical_not((s == p.i) & p.inside))
            def _():
                rcopy(self.low, self.dst.at[s], self.ss.at[0], self.rs.at[s], s, p.m).wait_recv()

            self.across(q).start()
        for q in range(p.half):
            s = q * 2 + 1 - p.c
            rcopy(self.dst.at[s], self.dst.at[s], self.ssr.at[q], self.rs.at[s], p.other, p.j).wait_recv()

    def sent(self):
        self.each(lambda copy: copy.wait_send())
        for q in range(self.p.half):
            self.across(q).wait_send()


class ToOwner:
    def __init__(self, p, part, mid, recv, ss, rs, ss_line, rs_line):
        self.p, self.part, self.mid, self.recv, self.ss, self.rs = p, part, mid, recv, ss, rs
        self.line = Exchange(p, lambda t: mid.at[t], lambda s: recv.at[s], ss_line, rs_line)

    def each(self, act):
        p = self.p
        for q in range(p.share):
            block = q * p.reps + p.h

            @pl.when(block != p.i)
            def _():
                act(rcopy(self.part.at[block], self.mid.at[p.m], self.ss.at[q], self.rs.at[p.m], block, p.j))

    def start(self):
        self.each(lambda copy: copy.start())
        self.mid[self.p.m] = self.part[self.p.i]

    def pass_on(self):
        p = self.p
        for s in range(p.mpn):
            @pl.when(s != p.m)
            def _():
                rcopy(
                    self.part.at[0], self.mid.at[s], self.ss.at[0], self.rs.at[s], s * p.reps + p.h, p.j
                ).wait_recv()
        self.line.start()
        self.recv[p.j] = self.mid[p.j]

    def total(self):
        self.line.wait_all()
        return sum(self.recv[s].astype(f32) for s in range(self.p.mpn))

    def sent(self):
        self.each(lambda copy: copy.wait_send())
        self.line.sent()


def perm_matrix(rows, patches, per, limit):
    at = lax.broadcasted_iota(jnp.int32, (rows, rows), 0)
    source = lax.broadcasted_iota(jnp.int32, (rows, rows), 1)
    return ((source == (at % patches) * per + at // patches) & (at % patches < limit)).astype(bf16)


class Loads:
    def __init__(self, sems):
        self.sems, self.count = sems, 0

    def __call__(self, src, dst):
        copy = pltpu.make_async_copy(src, dst, self.sems.at[self.count])
        self.count += 1
        copy.start()
        return copy


def own_lengths(r, m):
    return r.seq_lengths[m, 0], r.seq_lengths[m, 1], r.seq_lengths[m, 2]


def seg_starts(lengths, places):
    end0 = lengths[0]
    end1 = end0 + lengths[1]
    end2 = end1 + lengths[2]
    return jnp.where(
        places >= end2, end2, jnp.where(places >= end1, end1, jnp.where(places >= end0, end0, 0))
    )


def conv_taps(conv_in, pos, lag):
    moved = conv_in if lag == 0 else pltpu.roll(conv_in, lag, 0)
    return jnp.where(pos >= lag, moved, 0.0)


def mixer_state(lengths, projected, conv_weight, conv_bias, step_bias, log_decay):
    patches = projected.shape[0]
    places = lax.broadcasted_iota(jnp.int32, (patches, 1), 0)
    start = seg_starts(lengths, places)
    pos = places - start
    conv_in = projected[:, GROUP_WIDTH : GROUP_WIDTH + CONV_CH]
    conv_out = conv_bias
    for lag in range(CONV):
        conv_out = conv_out + conv_taps(conv_in, pos, lag) * conv_weight[CONV - 1 - lag][None]
    step_raw = projected[:, GROUP_WIDTH + CONV_CH :] + step_bias
    step = jnp.maximum(step_raw, 0.0) + jnp.log1p(jnp.exp(-jnp.abs(step_raw)))
    logd = -step * jnp.exp(log_decay)
    across = lax.broadcasted_iota(jnp.int32, (patches, patches), 1)
    down = lax.broadcasted_iota(jnp.int32, (patches, patches), 0)
    mask = (across >= start) & (across <= down)
    running = dot(mask.astype(f32), logd, precision=highest)
    return pos, conv_in, conv_out, step_raw, step, logd, mask, running


def head_decay(mask, running, running_t, h):
    return jnp.exp(
        jnp.where(mask, running[:, h : h + 1] - running_t[h : h + 1, :], large_negative)
    )


def att_mask(rows, patches):
    across = lax.broadcasted_iota(jnp.int32, (rows, rows), 1)
    down = lax.broadcasted_iota(jnp.int32, (rows, rows), 0)
    return (across % patches == down % patches) & (across <= down)


def soft_rows(mask, query, key):
    scores = dot(query, key, ((1,), (1,))) * ATT_DIM ** (-0.5)
    scores = jnp.where(mask, scores, large_negative)
    probs = jnp.exp(scores - jnp.max(scores, axis=1, keepdims=True))
    return probs / jnp.sum(probs, axis=1, keepdims=True)


def skip_columns(r):
    head = lax.broadcasted_iota(jnp.int32, (1, GROUP_WIDTH), 1) // HEAD_DIM
    return sum(jnp.where(head == h, r.skip[:, h : h + 1], 0.0) for h in range(GROUP_HEADS))


def mixer_fwd(r, lengths, normed):
    projected = dot(normed, r.in_v[...], ((1,), (1,)))
    r.projected[...] = projected
    _, _, conv_out, _, step, _, mask, running = mixer_state(
        lengths, projected, r.taps[...], r.conv_bias[...], r.step_bias[...], r.log_decay[...]
    )
    act = conv_out * jax.nn.sigmoid(conv_out)
    inputs = act[:, GROUP_WIDTH : GROUP_WIDTH + STATE]
    outputs = act[:, GROUP_WIDTH + STATE :]
    inner = dot(outputs, inputs, ((1,), (1,)))
    running_t, step_t = running.T, step.T
    pair = 2 * HEAD_DIM
    lane = lax.broadcasted_iota(jnp.int32, (1, pair), 1)
    pieces = []
    for c in range(GROUP_WIDTH // pair):
        values = act[:, c * pair : (c + 1) * pair]
        got = []
        for h in (2 * c, 2 * c + 1):
            weights = head_decay(mask, running, running_t, h) * inner * step_t[h : h + 1, :]
            got.append(dot(weights, values))
        pieces.append(jnp.where(lane < HEAD_DIM, got[0], got[1]))
    y = jnp.concatenate(pieces, axis=1) + skip_columns(r) * act[:, :GROUP_WIDTH]
    r.mixer_y[...] = y
    gate = projected[:, :GROUP_WIDTH]
    gated = y * (gate * jax.nn.sigmoid(gate))
    low = (gated * inv_rms(gated) * r.group_gain[...]).astype(bf16)
    r.mixer_low[...] = low
    return dot(low, r.out_v[...])


def forward_steps(p, r, load, land):
    n, mpn, i, j = p.n, p.mpn, p.i, p.j
    micro, patches, own_cols = r.own.shape
    positions, dim = r.pw.shape[0], r.pw.shape[1]
    slabs = r.bytes_v.shape[2] // dim
    rows = slabs * patches
    features = r.bytes_part.shape[-1]
    per, hidden = r.ffn_weight.shape[1:]

    load_own = load(r.byte_input.at[:, :, pl.ds(pl.multiple_of(j * own_cols, 128), own_cols)], r.own)
    load_pw = [load(r.patch_weight.at[k], r.pw.at[k]) for k in range(positions)]
    loads_small = load_small(r, load)
    load_grad = load(r.out_grad.at[j], r.grad_raw)
    load_in = load(r.in_weight, r.in_v)
    load_out = load(r.out_weight, r.out_v)
    load_bytes = load(r.byte_input, r.bytes_v)
    load_qkv = load(r.qkv_weight, r.qkv_v)
    kept = [load(r.ffn_weight.at[w], land(j, w, slice(None), slice(None))) for w in range(3)]

    barrier = pltpu.get_barrier_semaphore()
    count = greet_all(p, barrier)
    halves = max(hidden // FFN_COLS, 1)
    cuts = WEIGHT_CUTS if per // WEIGHT_CUTS >= 16 else 1
    step = per // cuts
    pieces = []
    for hh in range(halves):
        cols = slice(hh * (hidden // halves), (hh + 1) * (hidden // halves))
        for w in range(3):
            for k in range(cuts):
                at = slice(k * step, (k + 1) * step)
                pieces.append(LineGather(
                    p,
                    lambda t, w=w, at=at, cols=cols: r.ffn_weight.at[w, at, cols],
                    lambda s, w=w, at=at, cols=cols: land(s, w, at, cols),
                    r.ssw.at[len(pieces)],
                    r.rsw.at[len(pieces)],
                ))
    bulk = Bulk(pieces)
    pl.semaphore_wait(barrier, count)
    bulk.go(PACE[7])
    load_own.wait()
    sums = None
    for k in range(positions):
        load_pw[k].wait()
        term = dot(r.own[:, :, k * dim : (k + 1) * dim].reshape(micro * patches, dim), r.pw[k])
        sums = term if sums is None else sums + term
    for t in range(micro):
        r.part[t] = sums[t * patches : (t + 1) * patches]
        r.part_low[t] = sums[t * patches : (t + 1) * patches].astype(bf16)
    embed = Exchange(p, lambda t: r.part_low.at[t], lambda s: r.recv.at[s], r.ss1, r.rs1).start()
    bulk.go(PACE[0])
    load_grad.wait()
    perm = perm_matrix(rows, patches, slabs, sum(own_lengths(r, j)) - i * patches)
    r.own_grad[...] = dot(perm, r.grad_raw[...]).astype(bf16)
    r.grad_rows_own(i, r.own_grad[...])
    for copy in loads_small:
        copy.wait()
    total = r.part[j]
    for d in range(1, mpn):
        total = total + r.recv[embed.wait(d)].astype(f32)
    r.global_in[...] = total
    r.low[...] = (total * inv_rms(total) * r.norm_in_gain[...]).astype(bf16)
    cast = Cast(p, r.low, r.normed, r.ss2, r.rs2, r.ssc)
    cast.start()
    def columns_of(t, k):
        first = k * dim + t * (dim // n) // features * features
        return r.own.at[:, :, pl.ds(pl.multiple_of(first, 128), features)]

    def bytes_copy(t, k):
        return rcopy(columns_of(t, k), r.bytes_part.at[i, k], r.ssb.at[t, k], r.rsb.at[i, k], t, j)

    for d in range(1, n):
        for k in range(positions):
            bytes_copy((i + d) % n, k).start()
    kept += [load(columns_of(i, k), r.bytes_part.at[i, k]) for k in range(positions)]
    piece = r.out_proj.shape[0] // n
    at_piece = lambda s: pl.ds(pl.multiple_of(s * piece, piece), piece)
    kept_ao = load(r.out_proj.at[at_piece(i)], r.ao_sorted.at[j, at_piece(i)])
    ao_line = LineGather(
        p, lambda t: r.out_proj.at[at_piece(i)], lambda s: r.ao_sorted.at[s, at_piece(i)], r.ssa, r.rsa
    )
    ao_line.begin()
    bulk.go(PACE[1])
    load_in.wait()
    load_out.wait()
    cast.wait()
    feature = dim // n
    blocks = max(feature, 128)

    def normed_copy(q):
        t = q * p.reps + p.h
        return rcopy(normed_block(t), r.normed_cols.at[p.m], r.ssn.at[q], r.rsn.at[p.m], t, j)

    def normed_block(t):
        return r.normed.at[:, :, pl.ds(pl.multiple_of(t * feature // blocks * blocks, 128), blocks)]

    def each_normed(act, here):
        for q in range(p.share):
            at_home = q * p.reps + p.h == i
            pl.when(jnp.logical_not(at_home))(partial(act, q))
            pl.when(at_home)(here)

    def keep_normed():
        return pltpu.make_async_copy(normed_block(i), r.normed_cols.at[p.m], r.ssn.at[p.share])

    each_normed(lambda q: normed_copy(q).start(), lambda: keep_normed().start())
    bulk.go(PACE[2])

    part = mixer_fwd(r, own_lengths(r, p.m), r.normed[...].reshape(n * patches, dim))
    for b in range(n):
        r.mix_part[b] = part[b * patches : (b + 1) * patches].astype(bf16)
    to_owner = ToOwner(p, r.mix_part, r.mix_mid, r.mix_recv, r.ss3, r.rs3, r.sso, r.rso)
    to_owner.start()
    kept_ao.wait()
    ao_line.relay()
    to_owner.pass_on()
    bulk.go(PACE[3])
    ao_line.wait_all()
    ao_block = lambda s: r.ao_sorted.at[:, at_piece(s)]
    ao_plane = PlaneGather(p, ao_block(i), ao_block, r.ssap, r.rsap, r.ssar).start()
    grads = PlaneGather(p, r.own_grad, lambda s: r.grad_rows.at[s], r.ssg, r.rsg, r.ssgr).start()
    total = r.global_in[...] + to_owner.total()
    r.global_own[...] = total
    r.patch_all[j] = total.astype(bf16)
    patch_line = Exchange(p, lambda t: r.patch_all.at[j], lambda s: r.patch_all.at[s], r.ss4, r.rs4).start()
    bulk.go(PACE[4])
    load_bytes.wait()
    load_qkv.wait()
    patch_line.wait_all()

    mask = att_mask(rows, patches)
    pair = 2 * ATT_DIM
    width = r.qkv_v.shape[2]
    lane = lax.broadcasted_iota(jnp.int32, (1, pair), 1)
    heads_line = Exchange(p, lambda t: r.heads.at[t], lambda s: r.heads_own.at[s], r.ss5, r.rs5)

    def one_micro(d, _):
        m = (j + d) % mpn
        for k in range(slabs):
            here = r.bytes_v[m, :, k * dim : (k + 1) * dim].astype(f32) + r.patch_all[m].astype(f32)
            r.attn_in[m, k * patches : (k + 1) * patches, :] = (
                here * inv_rms(here) * r.attn_gain[...]
            ).astype(bf16)
        got = r.attn_in[m]
        for w in range(3):
            r.qkv[w, m] = dot(got, r.qkv_v[w]).astype(bf16)
        for c in range(width // pair):
            at = slice(c * pair, (c + 1) * pair)
            query, key, value = r.qkv[0, m, :, at], r.qkv[1, m, :, at], r.qkv[2, m, :, at]
            res = []
            for own in (lane < ATT_DIM, lane >= ATT_DIM):
                probs = soft_rows(mask, jnp.where(own, query, jnp.zeros_like(query)), key)
                res.append(dot(probs.astype(bf16), value))
            r.heads[m, :, at] = jnp.where(lane < ATT_DIM, res[0], res[1]).astype(bf16)

        @pl.when(d < mpn)
        def _():
            heads_line.copy(m).start()

        return 0

    lax.fori_loop(1, mpn + 1, one_micro, 0)
    bulk.go(PACE[5])
    r.heads_own[j] = r.heads[j]
    ao_plane.relay()
    ao_plane.finish()
    grads.relay()
    for k in range(slabs):
        here = r.bytes_v[j, :, k * dim : (k + 1) * dim].astype(f32) + r.global_own[...]
        r.after[k * patches : (k + 1) * patches, :] = here
    branch = None
    for d in range(mpn):
        s = j if d == 0 else heads_line.wait(d)
        term = dot(r.heads_own[s], r.ao_sorted[s])
        branch = term if branch is None else branch + term
    after = r.after[...] + branch
    r.after[...] = after
    r.ffn_own[...] = (after * inv_rms(after) * r.ffn_gain[...]).astype(bf16)
    rows_gather = PlaneGather(p, r.ffn_own, lambda s: r.ffn_rows.at[s], r.ssf, r.rsf, r.ssfr).start()
    r.ffn_rows_own(i, r.ffn_own[...])
    bulk.go(PACE[6])

    def settle():
        for d in range(1, n):
            s = (i + d) % n
            for k in range(positions):
                rcopy(r.bytes_part.at[s, k], r.bytes_part.at[s, k], r.ssb.at[s, k], r.rsb.at[s, k], s, j).wait_recv()
        for s in range(mpn):
            @pl.when(s * p.reps + p.h != i)
            def _():
                rcopy(
                    r.normed_cols.at[s], r.normed_cols.at[s], r.ssn.at[0], r.rsn.at[s], s * p.reps + p.h, j
                ).wait_recv()
        each_normed(lambda q: normed_copy(q).wait_send(), lambda: keep_normed().wait())
        for thing in (embed, grads, bulk, cast, ao_line, to_owner, ao_plane, patch_line, heads_line, rows_gather):
            thing.sent()
        for d in range(1, n):
            for k in range(positions):
                bytes_copy((i + d) % n, k).wait_send()

    return SimpleNamespace(grads=grads, rows=rows_gather, bulk=bulk, halves=halves, kept=kept, settle=settle)


def forward_kernel(n, mpn, r):
    p = place_of(n, mpn, False)
    load = Loads(r.sem_load)
    kept = []
    r.grad_rows_own = lambda s, value: kept.append(load(r.own_grad, r.grad_rows.at[s]))
    r.ffn_rows_own = lambda s, value: kept.append(load(r.ffn_own, r.ffn_rows.at[s]))
    st = forward_steps(p, r, load, lambda s, w, rows, cols: r.w_all.at[s, w, rows, cols])
    st.grads.finish()
    st.rows.relay()
    st.rows.finish()
    st.bulk.go(len(st.bulk.exchanges))
    st.bulk.wait(0, len(st.bulk.exchanges))
    st.settle()
    for copy in kept + st.kept:
        copy.wait()


def forward_ins(a):
    ins = dict(seq_lengths=(a.seq_lengths, SMEM))
    for name in ("byte_input", "patch_weight", "out_grad", "in_weight", "out_weight", "qkv_weight", "ffn_weight"):
        ins[name] = (getattr(a, name), ANY)
    ins["out_proj"] = (a.attn_out_weight, ANY)
    for name in SMALL_PARAMS:
        ins["given_" + name] = (getattr(a, name), ANY)
    return ins


def small_scratch(a):
    return {name: pltpu.VMEM(getattr(a, name).shape, f32) for name in SMALL_PARAMS}


def load_small(r, load):
    return [load(getattr(r, "given_" + name), getattr(r, name)) for name in SMALL_PARAMS]


def forward_results(n, mpn, a):
    micro, patches, cols = a.byte_input.shape
    dim = a.norm_in_gain.shape[1]
    rows = patches * (cols // dim)
    positions = a.patch_weight.shape[0]
    width = a.qkv_weight.shape[2]
    seq = n * patches
    large = dict(
        grad_rows=((n, rows, dim), bf16),
        ffn_rows=((n, rows, dim), bf16),
        w_all=((mpn,) + a.ffn_weight.shape, bf16),
        bytes_part=((n, positions, micro, patches, max(dim // n, 128)), bf16),
        normed_cols=((mpn, n, patches, max(dim // n, 128)), bf16),
    )
    small = dict(
        own_grad=((rows, dim), bf16),
        after=((rows, dim), f32),
        heads_own=((mpn, rows, width), bf16),
        qkv=((3, micro, rows, width), bf16),
        attn_in=((micro, rows, dim), bf16),
        ao_sorted=((mpn,) + a.attn_out_weight.shape, bf16),
        global_in=((patches, dim), f32),
        global_own=((patches, dim), f32),
        normed=((n, patches, dim), bf16),
        projected=((seq, a.in_weight.shape[0]), f32),
        mixer_y=((seq, GROUP_WIDTH), f32),
        mixer_low=((seq, GROUP_WIDTH), bf16),
    )
    return large, small


def forward_scratch(n, mpn, a):
    micro, patches, cols = a.byte_input.shape
    dim = a.norm_in_gain.shape[1]
    rows = patches * (cols // dim)
    positions = a.patch_weight.shape[0]
    width = a.qkv_weight.shape[2]
    half = n // 2
    pieces = max(a.ffn_weight.shape[2] // FFN_COLS, 1) * 3 * WEIGHT_CUTS
    line, plane = DMA((mpn,)), DMA((half,))
    return dict(
        **small_scratch(a),
        own=pltpu.VMEM((micro, patches, positions * dim), bf16),
        pw=pltpu.VMEM(a.patch_weight.shape, bf16),
        grad_raw=pltpu.VMEM((rows, dim), bf16),
        in_v=pltpu.VMEM(a.in_weight.shape, bf16),
        out_v=pltpu.VMEM(a.out_weight.shape, bf16),
        bytes_v=pltpu.VMEM(a.byte_input.shape, bf16),
        qkv_v=pltpu.VMEM(a.qkv_weight.shape, bf16),
        part=pltpu.VMEM((micro, patches, dim), f32),
        part_low=pltpu.VMEM((micro, patches, dim), bf16),
        recv=pltpu.VMEM((mpn, patches, dim), bf16),
        low=pltpu.VMEM((patches, dim), bf16),
        mix_part=pltpu.VMEM((n, patches, dim), bf16),
        mix_mid=pltpu.VMEM((mpn, patches, dim), bf16),
        mix_recv=pltpu.VMEM((mpn, patches, dim), bf16),
        patch_all=pltpu.VMEM((mpn, patches, dim), bf16),
        heads=pltpu.VMEM((micro, rows, width), bf16),
        ffn_own=pltpu.VMEM((rows, dim), bf16),
        sem_load=DMA((48,)),
        ss1=line, rs1=line, ss2=DMA((n,)), rs2=DMA((n,)), ssc=plane, ss3=line, rs3=line, sso=line, rso=line, ss4=line, rs4=line, ss5=line, rs5=line,
        ssg=plane, rsg=DMA((n,)), ssgr=plane, ssf=plane, rsf=DMA((n,)), ssfr=plane,
        ssb=DMA((n, positions)), rsb=DMA((n, positions)),
        ssn=DMA((mpn + 1,)), rsn=line, ssa=line, rsa=line, ssap=plane, rsap=DMA((n,)), ssar=plane,
        ssw=DMA((pieces, mpn)), rsw=DMA((pieces, mpn)),
    )


def forward(n, mpn, a):
    large, small = forward_results(n, mpn, a)
    outs = {name: value + (ANY,) for name, value in large.items()}
    outs.update({name: value + (VMEM,) for name, value in small.items()})
    return launch(
        "forward", partial(forward_kernel, n, mpn), forward_ins(a), outs, forward_scratch(n, mpn, a),
        remote_params(0, 62),
    )


def ffn_kernel(rows_in, grads_in, parts, down_out, in_grad, weight_grad, weight, gate_low, up_low, hidden_low):
    blocks, rows, dim = rows_in.shape
    per = parts.shape[2]
    for s in range(parts.shape[0]):
        for w in range(3):
            weight[w, s * per : (s + 1) * per, :] = parts[s, w]

    def step(b, _):
        here, up = rows_in[b], grads_in[b]
        gate = dot(here, weight[0])
        other = dot(here, weight[1])
        act, slope = silu_pair(gate)
        hidden = (act * other).astype(bf16)
        hidden_low[b] = hidden
        down_out[b] = dot(hidden, weight[2], ((1,), (1,))).astype(bf16)
        hidden_grad = dot(up, weight[2])
        gate_grad = (hidden_grad * other * slope).astype(bf16)
        up_grad = (hidden_grad * act).astype(bf16)
        gate_low[b] = gate_grad
        up_low[b] = up_grad
        back = dot(gate_grad, weight[0], ((1,), (1,))) + dot(up_grad, weight[1], ((1,), (1,)))
        in_grad[b] = back.astype(bf16)
        return 0

    lax.fori_loop(0, blocks, step, 0)
    hidden = weight.shape[2]
    everything = rows_in[...].reshape(blocks * rows, dim)
    weight_grad[0] = dot(everything, gate_low[...].reshape(blocks * rows, hidden), ((0,), (0,))).astype(bf16)
    weight_grad[1] = dot(everything, up_low[...].reshape(blocks * rows, hidden), ((0,), (0,))).astype(bf16)
    weight_grad[2] = dot(
        grads_in[...].reshape(blocks * rows, dim), hidden_low[...].reshape(blocks * rows, hidden), ((0,), (0,))
    ).astype(bf16)


def ffn(rows_in, grads_in, parts):
    blocks, rows, dim = rows_in.shape
    hidden = parts.shape[3]
    return pl.pallas_call(
        ffn_kernel,
        out_shape=(
            jax.ShapeDtypeStruct((blocks, rows, dim), bf16),
            jax.ShapeDtypeStruct((blocks, rows, dim), bf16),
            jax.ShapeDtypeStruct((3, dim, hidden), bf16),
        ),
        in_specs=[VMEM] * 3,
        out_specs=(VMEM,) * 3,
        scratch_shapes=[pltpu.VMEM((3, dim, hidden), bf16)] + [pltpu.VMEM((blocks, rows, hidden), bf16)] * 3,
        compiler_params=plain_params(60),
        name="ffn",
    )(rows_in, grads_in, parts)


def mixer_bwd(r, p, lengths, upstream):
    projected = r.projected[...]
    patches = projected.shape[0]
    pos, conv_in, conv_out, step_raw, step, logd, mask, running = mixer_state(
        lengths, projected, r.taps[...], r.conv_bias[...], r.step_bias[...], r.log_decay[...]
    )
    act, act_slope = silu_pair(conv_out)
    inputs = act[:, GROUP_WIDTH : GROUP_WIDTH + STATE]
    outputs = act[:, GROUP_WIDTH + STATE :]
    inner = dot(outputs, inputs, ((1,), (1,)))
    running_t, step_t = running.T, step.T
    normed_grad = dot(upstream, r.out_v[...], ((1,), (1,)))
    y = r.mixer_y[...]
    gate = projected[:, :GROUP_WIDTH]
    gate_act, gate_slope = silu_pair(gate)
    gated_grad, gain_rows = rms_back(y * gate_act, r.group_gain[...], normed_grad)
    y_grad = gated_grad * gate_act
    gate_grad = gated_grad * y * gate_slope
    values = act[:, :GROUP_WIDTH]
    skip_cols = jnp.sum(y_grad * values, axis=0, keepdims=True)
    pair = 2 * HEAD_DIM
    lane = lax.broadcasted_iota(jnp.int32, (1, pair), 1)
    inner_grad = jnp.zeros_like(inner)
    value_pieces, row_sums, col_sums = [], [], []
    for c in range(GROUP_WIDTH // pair):
        at = slice(c * pair, (c + 1) * pair)
        got = []
        for h in (2 * c, 2 * c + 1):
            own = (lane < HEAD_DIM) if h % 2 == 0 else (lane >= HEAD_DIM)
            mine = jnp.where(own, y_grad[:, at], 0.0)
            decay = head_decay(mask, running, running_t, h)
            step_row = step_t[h : h + 1, :]
            weight_grad = dot(mine, values[:, at], ((1,), (1,))) * decay
            scaled = weight_grad * step_row
            inner_grad = inner_grad + scaled
            col_sums.append(jnp.sum(weight_grad * inner, axis=0, keepdims=True))
            row_sums.append(jnp.sum(scaled * inner, axis=1, keepdims=True))
            weights = decay * inner * step_row
            got.append(dot(weights, mine, ((0,), (0,))))
        value_pieces.append(got[0] + got[1])
    values_grad = jnp.concatenate(value_pieces, axis=1) + skip_columns(r) * y_grad
    inputs_grad = dot(inner_grad, outputs, ((0,), (0,)))
    outputs_grad = dot(inner_grad, inputs)
    col_grad = jnp.concatenate(col_sums, axis=0).T
    running_grad = jnp.concatenate(row_sums, axis=1) - col_grad * step
    logd_grad = dot(mask.astype(f32), running_grad, ((0,), (0,)), precision=highest)
    step_grad = (col_grad - logd_grad * jnp.exp(r.log_decay[...])) * jax.nn.sigmoid(step_raw)
    conv_grad = jnp.concatenate([values_grad, inputs_grad, outputs_grad], axis=1) * act_slope
    conv_in_grad = jnp.zeros_like(conv_grad)
    small = r.small_part
    small[...] = jnp.zeros(small.shape, f32)
    for lag in range(CONV):
        small[CONV - 1 - lag : CONV - lag, :] = jnp.sum(
            conv_grad * conv_taps(conv_in, pos, lag), axis=0, keepdims=True
        )
        kept = jnp.where(pos >= lag, conv_grad, 0.0) * r.taps[CONV - 1 - lag : CONV - lag, :]
        conv_in_grad = conv_in_grad + (kept if lag == 0 else pltpu.roll(kept, patches - lag, 0))
    small[CONV : CONV + 1, :] = jnp.sum(conv_grad, axis=0, keepdims=True)
    small[CONV + 1 : CONV + 2, :GROUP_WIDTH] = jnp.sum(gain_rows, axis=0, keepdims=True)
    small[CONV + 2 : CONV + 3, :GROUP_WIDTH] = skip_cols
    small[CONV + 3 : CONV + 4, :GROUP_HEADS] = jnp.sum(step_grad, axis=0, keepdims=True)
    small[CONV + 4 : CONV + 5, :GROUP_HEADS] = jnp.sum(logd_grad * logd, axis=0, keepdims=True)
    return jnp.concatenate([gate_grad, conv_in_grad, step_grad], axis=1).astype(bf16)


def grad_pieces(p, r, halves, grad_of, dim, hidden):
    per = dim // p.mpn
    step = per // WEIGHT_CUTS
    pieces = []
    for hh in range(halves):
        cols = slice(hh * (hidden // halves), (hh + 1) * (hidden // halves))
        for w in range(3):
            for k in range(WEIGHT_CUTS):
                at = slice(k * step, (k + 1) * step)
                pieces.append(LineReduce(
                    p,
                    lambda t, w=w, k=k, cols=cols: grad_of(
                        w, pl.ds(pl.multiple_of(t * per + k * step, step), step), cols
                    ),
                    lambda s, w=w, at=at, cols=cols: r.g_recv.at[s, w, at, cols],
                    r.bsw.at[len(pieces)],
                    r.brw.at[len(pieces)],
                    r.g_held.at[len(pieces)] if p.line else None,
                    r.bsr.at[len(pieces)] if p.line else None,
                ))
    return Bulk(pieces)


def ffn_sums(p, r, get, put):
    in_block = lambda s: r.in_part.at[s]
    down_block = lambda s: r.down_part.at[s]
    return (
        Reduction(p, in_block, lambda s: get(in_block(s)), r.in_pre, r.in_recv, r.bs_in, get, put),
        Reduction(p, down_block, lambda s: get(down_block(s)), r.down_pre, r.down_recv, r.bs_down, get, put),
    )


def backward_steps(p, r, load, own_slab, ready, sum_in, sum_down, bulk):
    n, mpn, i, j = p.n, p.mpn, p.i, p.j
    micro, rows, dim = r.attn_in.shape
    patches = r.global_own.shape[0]
    slabs = rows // patches
    width = r.qkv_v.shape[2]
    feature = dim // n
    at_feature = lambda s: pl.ds(pl.multiple_of(s * feature, feature), feature)
    block_ao = lambda s: r.ao_part.at[at_feature(s)]
    block_qkv = lambda s: r.qkv_part.at[:, at_feature(s)]
    sum_ao = Reduction(
        p, block_ao, lambda s: block_ao(s)[...], r.ao_pre, r.ao_recv, r.bs_ao, plain_get, plain_put
    )
    sum_qkv = Reduction(
        p, block_qkv, lambda s: block_qkv(s)[...], r.qkv_pre, r.qkv_recv, r.bs_qkv, plain_get, plain_put
    )

    ready("bytes")
    for k in range(slabs):
        r.local_in[k * patches : (k + 1) * patches, :] = own_slab(k).astype(f32) + r.global_own[...]
    after = r.after[...]
    back, gain_rows = rms_back(after, r.ffn_gain[...], sum_in.finish())
    after_grad = r.own_grad[...].astype(f32) + back
    r.after_grad[...] = after_grad
    r.gains[...] = jnp.zeros(r.gains.shape, f32)
    r.gains[2:3, :] = jnp.sum(gain_rows, axis=0, keepdims=True)
    r.branch[...] = after_grad.astype(bf16)
    up_turn = jnp.where(j < mpn // 2, mpn - 1, 1)
    up_line = Exchange(p, lambda t: r.up.at[t], lambda s: r.up_recv.at[s], r.bs1, r.br1)
    for d in range(1, mpn + 1):
        t = (j + d * up_turn) % mpn
        r.up[t] = dot(r.branch[...], r.ao_sorted[t], ((1,), (1,))).astype(bf16)
        if d < mpn:
            up_line.copy(t).start()
    r.up_recv[j] = r.up[j]
    bulk.relay(RELAY_GRADS[1])
    bulk.go(PACE_BACK[0])
    sum_down.spread()
    ready("qkv")

    mask = att_mask(rows, patches)
    pair = 2 * ATT_DIM
    lane = lax.broadcasted_iota(jnp.int32, (1, pair), 1)
    att_line = LineReduce(
        p, lambda t: r.att_part.at[t], lambda s: r.att_recv.at[s], r.bs2, r.br2,
        r.att_held if p.line else None, r.bsz.at[0],
    )
    turn = jnp.where(j < mpn // 2, mpn - 1, 1)

    def one_micro(d, _):
        m = (j + d * turn) % mpn

        @pl.when(d > 0)
        def _():
            up_line.wait(d * turn)

        for c in range(width // pair):
            at = slice(c * pair, (c + 1) * pair)
            query, key, value = r.qkv[0, m, :, at], r.qkv[1, m, :, at], r.qkv[2, m, :, at]
            up = r.up_recv[m, :, at]
            got = [[], [], []]
            for own in (lane < ATT_DIM, lane >= ATT_DIM):
                mine = jnp.where(own, query, jnp.zeros_like(query))
                probs = soft_rows(mask, mine, key)
                my_up = jnp.where(own, up, jnp.zeros_like(up))
                probs_grad = dot(my_up, value, ((1,), (1,)))
                inner = jnp.sum(probs * probs_grad, axis=1, keepdims=True)
                score_grad = (probs * (probs_grad - inner) * ATT_DIM ** (-0.5)).astype(bf16)
                got[0].append(dot(score_grad, key))
                got[1].append(dot(score_grad, mine, ((0,), (0,))))
                got[2].append(dot(probs.astype(bf16), my_up, ((0,), (0,))))
            r.qkv_low[0, m, :, at] = jnp.where(lane < ATT_DIM, got[0][0], got[0][1]).astype(bf16)
            r.qkv_low[1, m, :, at] = (got[1][0] + got[1][1]).astype(bf16)
            r.qkv_low[2, m, :, at] = (got[2][0] + got[2][1]).astype(bf16)
        total = dot(r.qkv_low[0, m], r.qkv_v[0], ((1,), (1,)))
        total = total + dot(r.qkv_low[1, m], r.qkv_v[1], ((1,), (1,)))
        total = total + dot(r.qkv_low[2, m], r.qkv_v[2], ((1,), (1,)))
        r.att_part[m] = total.astype(bf16)

        @pl.when(d > 0)
        def _():
            att_line.send(m)

        return 0

    lax.fori_loop(0, mpn, one_micro, 0)

    everything = r.attn_in[...].reshape(micro * rows, dim)
    for w in range(3):
        r.qkv_part[w] = dot(
            everything, r.qkv_low[w].reshape(micro * rows, width), ((0,), (0,))
        ).astype(bf16)
    sum_qkv.start()
    sum_qkv.spread()
    for t in range(mpn):
        r.ao_part[:, t * width : (t + 1) * width] = dot(
            r.branch[...], r.heads_own[t], ((0,), (0,))
        ).astype(bf16)
    sum_ao.start()
    perm = perm_matrix(rows, patches, slabs, sum(own_lengths(r, j)) - i * patches)
    block = (r.after[...] + sum_down.finish()).astype(bf16)
    block = dot(perm, block, ((0,), (0,))).astype(bf16)
    for t in range(mpn):
        r.block[t] = block[:, t * width : (t + 1) * width]
    total = r.att_part[j].astype(f32)
    att_line.wait_all()
    for s in range(mpn):
        total = total + jnp.where((s == j) | absent(p.line, j, s), 0.0, r.att_recv[s].astype(f32))
    back, gain_rows = rms_back(r.local_in[...], r.attn_gain[...], total)
    local_grad = r.after_grad[...] + back
    global_grad = local_grad[:patches]
    for k in range(1, slabs):
        global_grad = global_grad + local_grad[k * patches : (k + 1) * patches]
    r.global_grad[...] = global_grad
    r.b_low[...] = global_grad.astype(bf16)
    cast = Cast(p, r.b_low, r.mixer, r.bs3, r.br3, r.bsc)
    cast.start()
    sum_ao.spread()
    bulk.go(PACE_BACK[1])
    r.gains[1:2, :] = jnp.sum(gain_rows, axis=0, keepdims=True)
    share_rows = rows // mpn
    for t in range(mpn):
        r.local[t] = local_grad[t * share_rows : (t + 1) * share_rows].astype(bf16)
    local_line = Exchange(p, lambda t: r.local.at[t], lambda s: r.local_all.at[s], r.bs6, r.br6)
    block_line = Exchange(p, lambda t: r.block.at[t], lambda s: r.block_all.at[s], r.bs7, r.br7)
    ready("mixer")
    cast.wait()
    bulk.go(PACE_BACK[2])

    upstream = r.mixer[...].reshape(n * patches, dim)
    proj_grad = mixer_bwd(r, p, own_lengths(r, p.m), upstream)
    part = dot(proj_grad, r.in_v[...])
    for b in range(n):
        r.b_part[b] = part[b * patches : (b + 1) * patches].astype(bf16)
    to_owner = ToOwner(p, r.b_part, r.b_mid, r.b_recv, r.bs4, r.br4, r.bs9, r.br9)
    to_owner.start()
    bulk.go(PACE_BACK[3])

    r.proj_grad[...] = proj_grad
    size = n * patches // p.reps
    proj_own = r.proj_grad.at[pl.ds(pl.multiple_of(p.h * size, size), size)]
    proj_plane = PlaneGather(p, proj_own, lambda s: r.proj_all.at[s], r.bsi, r.bri, r.bsir).start()
    keep_proj = load(proj_own, r.proj_all.at[i])
    out_grad = dot(r.mixer_low[...], upstream, ((0,), (0,))).astype(bf16)
    group_rows = GROUP_WIDTH // n
    for e in range(n):
        r.out_w_part[e] = out_grad[e * group_rows : (e + 1) * group_rows]
    bundles = (
        (lambda t: r.out_w_part.at[t], r.out_w_recv, r.bso, r.bro),
        (lambda t: r.small_part, r.small_recv, r.bss, r.brs),
    )

    def each_bundle(act):
        for q in range(p.share):
            t = q * p.reps + p.h

            @pl.when(t != i)
            def _():
                for src, dst, ss, rs in bundles:
                    act(rcopy(src(t), dst.at[p.m], ss.at[q], rs.at[p.m], t, j))

    to_owner.pass_on()
    bulk.go(PACE_BACK[4])
    each_bundle(lambda copy: copy.start())
    keeps = [load(r.out_w_part.at[i], r.out_w_recv.at[p.m]), load(r.small_part, r.small_recv.at[p.m])]
    back, gain_rows = rms_back(r.global_in[...], r.norm_in_gain[...], to_owner.total())
    r.line[j] = (r.global_grad[...] + back).astype(bf16)
    line = Exchange(p, lambda t: r.line.at[j], lambda s: r.line.at[s], r.bs5, r.br5).start()
    bulk.go(len(bulk.exchanges))
    r.gains[0:1, :] = jnp.sum(gain_rows, axis=0, keepdims=True)
    others = [(p.mine + d) % p.half for d in range(1, p.half)]

    def gains_copy(q):
        return rcopy(r.gains, r.gains_plane.at[p.mine], r.bsh.at[q], r.brh.at[p.mine], q * 2 + p.c, j)

    for q in others:
        gains_copy(q).start()
    r.gains_plane[p.mine] = r.gains[...]
    local_line.start()
    block_line.start()
    keeps += [load(r.local.at[j], r.local_all.at[j]), load(r.block.at[j], r.block_all.at[j])]
    line.wait_all()
    slot = lambda s: r.plane.at[s]
    plane = PlaneGather(p, r.line, slot, r.bsp, r.brp, r.bspr).start()
    keep_line = load(r.line, r.plane.at[i])
    bulk.relay(bulk.before)
    proj_plane.relay()
    r.qkv_total[...] = sum_qkv.finish()
    keeps.append(load(r.qkv_total, r.qkv_sum))
    ao = sum_ao.finish().astype(bf16)
    for t in range(mpn):
        r.ao[t] = ao[:, t * width : (t + 1) * width]
    ao_line = Exchange(p, lambda t: r.ao.at[t], lambda s: r.ao_all.at[s], r.bs8, r.br8).start()
    keeps.append(load(r.ao.at[j], r.ao_all.at[j]))
    bulk.relay(len(bulk.exchanges))
    for q in others:
        rcopy(r.gains, r.gains_plane.at[q], r.bsh.at[q], r.brh.at[q], q * 2 + p.c, j).wait_recv()
    r.gains_pair[0] = sum(r.gains_plane[s] for s in range(p.half))
    pair_copy = rcopy(r.gains_pair.at[0], r.gains_pair.at[1], r.bsq.at[0], r.brq.at[0], p.other, j)
    pair_copy.start()
    plane.relay()
    pair_copy.wait()
    r.gains_pair[0] = r.gains_pair[0] + r.gains_pair[1]
    width_i = r.gains_mine.shape[1]
    first = i * feature // width_i * width_i
    r.gains_mine[...] = r.gains_pair[0, :, pl.ds(pl.multiple_of(first, 128), width_i)]
    gains_line = Exchange(p, lambda t: r.gains_mine, lambda s: r.gains_line.at[s], r.bsg, r.brg).start()
    plane.finish()
    local_line.wait_all()
    block_line.wait_all()
    ao_line.wait_all()
    for s in range(mpn):
        @pl.when(s * p.reps + p.h != i)
        def _():
            for src, dst, ss, rs in bundles:
                rcopy(src(0), dst.at[s], ss.at[0], rs.at[s], s * p.reps + p.h, j).wait_recv()
    proj_plane.finish()
    gains_line.wait_all()
    r.gains_line[j] = r.gains_mine[...]
    gains_line.sent()
    r.gains_mine[...] = sum(r.gains_line[s] for s in range(mpn))
    keeps.append(load(r.gains_mine, r.gains_all))
    bulk.wait(0, len(bulk.exchanges))
    keep_line.wait()
    keep_proj.wait()
    for copy in keeps:
        copy.wait()
    for thing in (
        sum_in, sum_down, sum_ao, sum_qkv, bulk, up_line, att_line, cast, to_owner, line, local_line,
        block_line, plane, proj_plane, ao_line,
    ):
        thing.sent()
    for q in others:
        gains_copy(q).wait_send()
    each_bundle(lambda copy: copy.wait_send())


def backward_kernel(n, mpn, spill, r):
    p = place_of(n, mpn, False)
    load = Loads(r.b_load)

    def read(view):
        if not spill:
            return view[...]
        copy = pltpu.make_async_copy(view, r.stage.at[0], r.sem_stage.at[0])
        copy.start()
        copy.wait()
        return r.stage[0]

    def write(view, value):
        if not spill:
            view[...] = value
            return
        r.stage[1] = value
        copy = pltpu.make_async_copy(r.stage.at[1], view, r.sem_stage.at[1])
        copy.start()
        copy.wait()

    per = r.w_grad.shape[1] // mpn
    loads_small = load_small(r, load)
    keep_w = load(r.w_grad.at[:, pl.ds(pl.multiple_of(p.j * per, per), per)], r.g_recv.at[p.j])
    loads = dict(
        bytes=[load(r.byte_input.at[p.j], r.own_bytes)],
        qkv=[load(r.qkv_weight, r.qkv_v)],
        mixer=[load(r.out_weight, r.out_v), load(r.in_weight, r.in_v)],
    )

    def ready(what):
        for copy in loads[what]:
            copy.wait()

    barrier = pltpu.get_barrier_semaphore()
    pl.semaphore_wait(barrier, greet_all(p, barrier))
    for copy in loads_small:
        copy.wait()
    bulk = grad_pieces(p, r, 1, lambda w, at, cols: r.w_grad.at[w, at, cols], *r.w_grad.shape[1:])
    sum_in, sum_down = ffn_sums(p, r, read, write)
    sum_in.start()
    sum_in.spread()
    sum_down.start()
    dim = r.after.shape[1]
    own_slab = lambda k: r.own_bytes[:, k * dim : (k + 1) * dim]
    backward_steps(p, r, load, own_slab, ready, sum_in, sum_down, bulk)
    keep_w.wait()


def backward_results(n, mpn, a):
    micro, patches, cols = a.byte_input.shape
    dim = a.norm_in_gain.shape[1]
    rows = patches * (cols // dim)
    width = a.qkv_weight.shape[2]
    hidden = a.ffn_weight.shape[2]
    feature = dim // n
    return dict(
        g_recv=((mpn, 3, dim // mpn, hidden), bf16, ANY),
        plane=((n, mpn, patches, dim), bf16, ANY),
        qkv_sum=((3, feature, width), f32, ANY),
        ao_all=((mpn, feature, width), bf16, ANY),
        proj_all=((n, n * patches // (n // mpn), a.in_weight.shape[0]), bf16, ANY),
        out_w_recv=((mpn, GROUP_WIDTH // n, dim), bf16, ANY),
        small_recv=((mpn, 16, CONV_CH), f32, ANY),
        gains_all=((8, max(feature, 128)), f32, ANY),
        local_all=((mpn, rows // mpn, dim), bf16, ANY),
        block_all=((mpn, rows, width), bf16, ANY),
    )


def backward_scratch(n, mpn, a):
    micro, patches, cols = a.byte_input.shape
    dim = a.norm_in_gain.shape[1]
    rows = patches * (cols // dim)
    width = a.qkv_weight.shape[2]
    hidden = a.ffn_weight.shape[2]
    half, share = n // 2, mpn
    feature = dim // n
    pieces = max(hidden // FFN_COLS, 1) * 3 * WEIGHT_CUTS
    line, plane = DMA((mpn,)), DMA((half,))
    return dict(
        local_in=pltpu.VMEM((rows, dim), f32),
        after_grad=pltpu.VMEM((rows, dim), f32),
        branch=pltpu.VMEM((rows, dim), bf16),
        up=pltpu.VMEM((mpn, rows, width), bf16),
        up_recv=pltpu.VMEM((mpn, rows, width), bf16),
        qkv_low=pltpu.VMEM((3, micro, rows, width), bf16),
        att_part=pltpu.VMEM((micro, rows, dim), bf16),
        att_recv=pltpu.VMEM((mpn, rows, dim), bf16),
        qkv_part=pltpu.VMEM((3, dim, width), bf16),
        qkv_pre=pltpu.VMEM((half, 3, feature, width), bf16),
        qkv_recv=pltpu.VMEM((half, 3, feature, width), bf16),
        ao_part=pltpu.VMEM((dim, mpn * width), bf16),
        ao_pre=pltpu.VMEM((half, feature, mpn * width), bf16),
        ao_recv=pltpu.VMEM((half, feature, mpn * width), bf16),
        ao=pltpu.VMEM((mpn, feature, width), bf16),
        block=pltpu.VMEM((mpn, rows, width), bf16),
        local=pltpu.VMEM((mpn, rows // mpn, dim), bf16),
        b_low=pltpu.VMEM((patches, dim), bf16),
        global_grad=pltpu.VMEM((patches, dim), f32),
        mixer=pltpu.VMEM((n, patches, dim), bf16),
        b_part=pltpu.VMEM((n, patches, dim), bf16),
        b_mid=pltpu.VMEM((mpn, patches, dim), bf16),
        b_recv=pltpu.VMEM((mpn, patches, dim), bf16),
        line=pltpu.VMEM((mpn, patches, dim), bf16),
        proj_grad=pltpu.VMEM((n * patches, a.in_weight.shape[0]), bf16),
        out_w_part=pltpu.VMEM((n, GROUP_WIDTH // n, dim), bf16),
        small_part=pltpu.VMEM((16, CONV_CH), f32),
        qkv_total=pltpu.VMEM((3, feature, width), f32),
        gains=pltpu.VMEM((8, dim), f32),
        gains_mine=pltpu.VMEM((8, max(feature, 128)), f32),
        gains_line=pltpu.VMEM((mpn, 8, max(feature, 128)), f32),
        gains_plane=pltpu.VMEM((half, 8, dim), f32),
        gains_pair=pltpu.VMEM((2, 8, dim), f32),
        b_load=DMA((40,)),
        bs_in=DMA((4, half)), bs_down=DMA((4, half)), bs_ao=DMA((4, half)), bs_qkv=DMA((4, half)),
        bs1=line, br1=line, bs2=line, br2=line, bs3=DMA((n,)), br3=DMA((n,)), bsc=plane, bs4=line, br4=line, bs9=line, br9=line,
        bs5=line, br5=line, bs6=line, br6=line, bs7=line, br7=line, bs8=line, br8=line,
        bsp=plane, brp=DMA((n,)), bspr=plane,
        bsg=line, brg=line, bsh=plane, brh=plane, bsq=DMA((1,)), brq=DMA((1,)),
        bsz=DMA((1,)), bsi=plane, bri=DMA((n,)), bsir=plane, bso=DMA((share,)), bro=line, bss=DMA((share,)), brs=line,
        bsw=DMA((pieces, mpn)), brw=DMA((pieces, mpn)),
    )


def sum_buffers(n, a, make):
    micro, patches, cols = a.byte_input.shape
    dim = a.norm_in_gain.shape[1]
    shape = (n // 2, patches * (cols // dim), dim)
    return {name: make(shape) for name in ("in_pre", "in_recv", "down_pre", "down_recv")}


def backward(n, mpn, a):
    spill = a.in_part.size * 2 > SPILL_BYTES
    ins = dict(seq_lengths=(a.seq_lengths, SMEM))
    for name in ("byte_input", "w_grad", "in_weight", "out_weight", "qkv_weight"):
        ins[name] = (getattr(a, name), ANY)
    for name in ("in_part", "down_part"):
        ins[name] = (getattr(a, name), ANY if spill else VMEM)
    for name in SMALL_PARAMS:
        ins["given_" + name] = (getattr(a, name), ANY)
    for name in (
        "after", "own_grad", "heads_own", "qkv", "attn_in", "ao_sorted", "global_in", "global_own", "normed",
        "projected", "mixer_y", "mixer_low",
    ):
        ins[name] = (getattr(a, name), VMEM)
    outs = backward_results(n, mpn, a)
    scratch = backward_scratch(n, mpn, a)
    scratch.update(small_scratch(a))
    scratch.update(
        own_bytes=pltpu.VMEM(a.byte_input.shape[1:], bf16),
        in_v=pltpu.VMEM(a.in_weight.shape, bf16),
        out_v=pltpu.VMEM(a.out_weight.shape, bf16),
        qkv_v=pltpu.VMEM(a.qkv_weight.shape, bf16),
    )
    if spill:
        outs.update(sum_buffers(n, a, lambda shape: (shape, bf16, ANY)))
        scratch.update(stage=pltpu.VMEM((2,) + a.in_part.shape[1:], bf16), sem_stage=DMA((2,)))
    else:
        scratch.update(sum_buffers(n, a, lambda shape: pltpu.VMEM(shape, bf16)))
    return launch(
        "backward", partial(backward_kernel, n, mpn, spill), ins, outs, scratch, remote_params(1, 63)
    )


def ffn_steps(p, r, st, load, sum_in, sum_down, bulk, grad_of):
    n, half = p.n, p.half
    rows, dim = r.own_grad.shape
    hidden = r.w_v.shape[2]
    cols = hidden // st.halves
    per = dim // p.mpn
    pair = 2 * rows
    st.grads.finish()
    grads_all = lambda: r.grad_rows[...].reshape(n * rows, dim)
    rows_all = lambda: r.ffn_rows[...].reshape(n * rows, dim)
    kept = []
    if st.halves == 1:
        st.rows.relay()
        st.rows.finish()
    count = len(st.bulk.exchanges) // st.halves
    for hh in range(st.halves):
        at = slice(hh * cols, (hh + 1) * cols)
        last = hh == st.halves - 1
        if last:
            st.bulk.go(len(st.bulk.exchanges))
        st.bulk.wait(hh * count, (hh + 1) * count)
        if hh == 0:
            for copy in st.kept:
                copy.wait()

        def compute(q):
            here = r.ffn_rows[pl.ds(2 * q, 2)].reshape(pair, dim)
            up = r.grad_rows[pl.ds(2 * q, 2)].reshape(pair, dim)
            gate = dot(here, r.w_v[0, :, at])
            other = dot(here, r.w_v[1, :, at])
            act, slope = silu_pair(gate)
            hidden_low = (act * other).astype(bf16)
            here_at = pl.ds(pl.multiple_of(q * pair, pair), pair)
            r.hidden_low[hh, here_at, :] = hidden_low
            down = dot(hidden_low, r.w_v[2, :, at], ((1,), (1,)))
            hidden_grad = dot(up, r.w_v[2, :, at])
            gate_grad = (hidden_grad * other * slope).astype(bf16)
            up_grad = (hidden_grad * act).astype(bf16)
            r.gate_low[hh, here_at, :] = gate_grad
            r.up_low[hh, here_at, :] = up_grad
            back = dot(gate_grad, r.w_v[0, :, at], ((1,), (1,))) + dot(up_grad, r.w_v[1, :, at], ((1,), (1,)))
            if hh > 0:
                back = back + r.in_part[pl.ds(2 * q, 2)].reshape(pair, dim).astype(f32)
                down = down + r.down_part[pl.ds(2 * q, 2)].reshape(pair, dim).astype(f32)
            r.in_part[pl.ds(2 * q, 2)] = back.astype(bf16).reshape(2, rows, dim)
            r.down_part[pl.ds(2 * q, 2)] = down.astype(bf16).reshape(2, rows, dim)

        def first_pass(d, _):
            q = (p.mine + half - d) % half
            for turn, upto in RELAY_WEIGHTS:
                @pl.when(d == turn)
                def _():
                    st.bulk.relay(upto)

            @pl.when(d > 0)
            def _():
                st.rows.relay_one(q)

            st.rows.wait_across(q)
            compute(q)
            return 0

        def last_pass(d, _):
            q = (p.mine + d) % half
            compute(q)
            sum_in.first(q).start()

            @pl.when(d > 1)
            def _():
                sum_in.spread_one((p.mine + d - 1) % half)

            return 0

        if last:
            lax.fori_loop(1, half + 1, last_pass, 0)
            sum_down.start()
        else:
            lax.fori_loop(0, half, first_pass, 0)
        everything = slice(0, dim)
        grad_of(0, everything, at)[...] = dot(rows_all(), r.gate_low[hh], ((0,), (0,))).astype(bf16)
        grad_of(1, everything, at)[...] = dot(rows_all(), r.up_low[hh], ((0,), (0,))).astype(bf16)
        grad_of(2, everything, at)[...] = dot(grads_all(), r.hidden_low[hh], ((0,), (0,))).astype(bf16)
        mine = pl.ds(pl.multiple_of(p.j * per, per), per)
        kept += [load(grad_of(w, mine, at), r.g_recv.at[p.j, w, :, at]) for w in range(3)]
        if last:
            bulk.relay(RELAY_GRADS[0])
        else:
            bulk.go(PACE_FFN)
    return kept


def layer_kernel(n, mpn, r):
    p = place_of(n, mpn, mpn == 4)
    dim = r.after.shape[1]

    def put_rows(ref):
        def put(s, value):
            ref[s] = value

        return put

    r.grad_rows_own = put_rows(r.grad_rows)
    r.ffn_rows_own = put_rows(r.ffn_rows)
    per = r.ffn_weight.shape[1]

    def land(s, w, rows, cols):
        first = (0 if rows.start is None else rows.start) + s * per
        size = per if rows.start is None else rows.stop - rows.start
        return r.w_v.at[w, pl.ds(pl.multiple_of(first, size), size), cols]

    load = Loads(r.sem_load)
    st = forward_steps(p, r, load, land)
    hidden = r.w_v.shape[2]

    def grad_of(w, at, cols):
        first = w % 2 * hidden
        return r.pw.at[w // 2, at, first + cols.start : first + cols.stop]

    bulk = grad_pieces(p, r, st.halves, grad_of, dim, hidden)
    sum_in, sum_down = ffn_sums(p, r, plain_get, plain_put)
    load = Loads(r.b_load)
    kept = ffn_steps(p, r, st, load, sum_in, sum_down, bulk, grad_of)
    own_slab = lambda k: r.bytes_v[p.j, :, k * dim : (k + 1) * dim]
    backward_steps(p, r, load, own_slab, lambda what: None, sum_in, sum_down, bulk)
    st.settle()
    for copy in kept:
        copy.wait()


def layer(n, mpn, a):
    dim = a.norm_in_gain.shape[1]
    hidden = a.ffn_weight.shape[2]
    halves = max(hidden // FFN_COLS, 1)
    large, small = forward_results(n, mpn, a)
    rows = small["own_grad"][0][0]
    outs = {name: large.pop(name) + (ANY,) for name in ("bytes_part", "normed_cols")}
    outs.update(backward_results(n, mpn, a))
    large.pop("w_all")
    scratch = forward_scratch(n, mpn, a)
    scratch.update(backward_scratch(n, mpn, a))
    for name, (shape, dtype) in (*large.items(), *small.items()):
        scratch[name] = pltpu.VMEM(shape, dtype)
    scratch.update(sum_buffers(n, a, lambda shape: pltpu.VMEM(shape, bf16)))
    scratch.update(
        g_held=pltpu.VMEM((halves * 3 * WEIGHT_CUTS, dim // mpn // WEIGHT_CUTS, hidden // halves), bf16),
        att_held=pltpu.VMEM((rows, dim), bf16),
        bsr=DMA((halves * 3 * WEIGHT_CUTS,)),
        w_v=pltpu.VMEM((3, dim, hidden), bf16),
        in_part=pltpu.VMEM((n, rows, dim), bf16),
        down_part=pltpu.VMEM((n, rows, dim), bf16),
        gate_low=pltpu.VMEM((halves, n * rows, hidden // halves), bf16),
        up_low=pltpu.VMEM((halves, n * rows, hidden // halves), bf16),
        hidden_low=pltpu.VMEM((halves, n * rows, hidden // halves), bf16),
    )
    return launch(
        "layer", partial(layer_kernel, n, mpn), forward_ins(a), outs, scratch, remote_params(2, 63)
    )


def finish_kernel(line, r):
    i, j = lax.axis_index("dp"), lax.axis_index("mp")
    mpn, patches, dim = r.plane.shape[1:]
    n = r.plane.shape[0]
    features = r.bytes_part.shape[-1]
    positions = r.patch_weight.shape[0]
    feature = dim // n
    columns = r.in_grad.shape[0]
    load = Loads(r.sems)
    writes = []
    into = lambda name: load(getattr(r, name), getattr(r, name + "_v"))
    load_g = [load(r.g_recv.at[:, w], r.g_recv_v.at[w]) for w in range(3)]
    load_patch = [into("plane"), into("bytes_part")]
    load_in = [into("proj_all"), into("normed_cols")]
    load_rest = [into(name) for name in ("out_w_recv", "ao_all", "small_recv", "gains_all")]
    load_copied = [into("qkv_sum"), into("block_all")]
    load_input = [into("local_all")] + [load(r.patch_weight.at[k], r.patch_weight_v.at[k]) for k in range(positions)]

    def wait(copies):
        for copy in copies:
            copy.wait()

    def out(name, value, at=None):
        src, dst = getattr(r, name + "_v"), getattr(r, name)
        if at is not None:
            src, dst = src.at[at], dst.at[at]
        src[...] = value
        writes.append(load(src, dst))

    cut = features // feature
    for w in range(3):
        load_g[w].wait()
        out("ffn_grad", sum(
            jnp.where(absent(line, j, s), 0.0, r.g_recv_v[w, s].astype(f32)) for s in range(mpn)
        ), w)
    wait(load_patch)
    everyone = r.plane_v[...].reshape(n * mpn * patches, dim)
    for k in range(positions):
        mine = r.bytes_part_v[:, k].reshape(n * mpn * patches, features)
        got = dot(mine, everyone, ((0,), (0,)))
        if cut > 1:
            got = sum(jnp.where(i % cut == e, got[e * feature : (e + 1) * feature], 0.0) for e in range(cut))
        out("patch_grad", got, k)
    wait(load_in)
    got = dot(
        r.proj_all_v[...].reshape(n * mpn * patches, columns),
        r.normed_cols_v[...].reshape(n * mpn * patches, features), ((0,), (0,)),
    )
    if cut > 1:
        got = sum(jnp.where(i % cut == e, got[:, e * feature : (e + 1) * feature], 0.0) for e in range(cut))
    out("in_grad", got)
    wait(load_copied)
    writes += [load(r.qkv_sum_v, r.qkv_grad), load(r.block_all_v, r.block_out)]
    wait(load_rest)
    out("out_grad", sum(r.out_w_recv_v[s].astype(f32) for s in range(mpn)))
    out("ao_grad", sum(r.ao_all_v[s].astype(f32) for s in range(mpn)).T)
    small = sum(r.small_recv_v[s] for s in range(mpn))

    def chosen(values, size):
        whole = values.shape[1]
        at = lax.broadcasted_iota(jnp.int32, (whole, size), 0)
        want = lax.broadcasted_iota(jnp.int32, (whole, size), 1) + i * size % whole
        return dot(values, (at == want).astype(f32), precision=highest)

    conv = chosen(small, CONV_CH // n)
    out("conv_w_grad", conv[:CONV])
    out("conv_b_grad", conv[CONV : CONV + 1])
    out("group_grad", chosen(small[:, :GROUP_WIDTH], GROUP_WIDTH // n)[CONV + 1 : CONV + 2])
    heads = lax.broadcasted_iota(jnp.int32, (GROUP_WIDTH, GROUP_HEADS), 0) // HEAD_DIM
    pick = heads == lax.broadcasted_iota(jnp.int32, (GROUP_WIDTH, GROUP_HEADS), 1)
    out("skip_grad", dot(small[:, :GROUP_WIDTH], pick.astype(f32), precision=highest)[CONV + 2 : CONV + 3])
    out("step_grad", small[CONV + 3 : CONV + 4, :GROUP_HEADS])
    out("decay_grad", small[CONV + 4 : CONV + 5, :GROUP_HEADS])
    gains = chosen(r.gains_all_v[...], feature)
    out("norm_in_grad", gains[0:1])
    out("attn_gain_grad", gains[1:2])
    out("ffn_gain_grad", gains[2:3])
    wait(load_input)
    own = r.plane_v[i].reshape(mpn * patches, dim)
    for k in range(positions):
        piece = dot(own, r.patch_weight_v[k], ((1,), (1,)))
        for m in range(mpn):
            r.input_grad_v[m, :, k * dim : (k + 1) * dim] = (
                piece[m * patches : (m + 1) * patches]
                + r.local_all_v[m, k * patches : (k + 1) * patches, :].astype(f32)
            )
    writes.append(load(r.input_grad_v, r.input_grad))
    wait(writes)


def finish(a, line):
    n, mpn, patches, dim = a.plane.shape
    positions = a.patch_weight.shape[0]
    feature = dim // n
    columns = a.in_weight.shape[0]
    names = (
        "plane", "bytes_part", "patch_weight", "local_all", "g_recv", "ao_all", "proj_all", "normed_cols", "out_w_recv",
        "small_recv", "gains_all", "qkv_sum", "block_all",
    )
    large = dict(
        patch_grad=((positions, feature, dim), f32),
        input_grad=((mpn, patches, positions * dim), f32),
        ffn_grad=(a.g_recv.shape[1:], f32),
        ao_grad=(a.ao_all.shape[:0:-1], f32),
        in_grad=((columns, feature), f32),
        out_grad=(a.out_w_recv.shape[1:], f32),
    )
    row = lambda size: ((1, size), f32)
    large.update(
        conv_w_grad=((CONV, CONV_CH // n), f32),
        conv_b_grad=row(CONV_CH // n),
        group_grad=row(GROUP_WIDTH // n),
        skip_grad=row(GROUP_HEADS),
        step_grad=row(GROUP_HEADS),
        decay_grad=row(GROUP_HEADS),
        norm_in_grad=row(feature),
        attn_gain_grad=row(feature),
        ffn_gain_grad=row(feature),
    )
    outs = {name: value + (ANY,) for name, value in large.items()}
    outs.update(qkv_grad=(a.qkv_sum.shape, f32, ANY), block_out=(a.block_all.shape, bf16, ANY))
    scratch = {name + "_v": pltpu.VMEM(getattr(a, name).shape, getattr(a, name).dtype) for name in names}
    scratch["g_recv_v"] = pltpu.VMEM((3, mpn) + a.g_recv.shape[2:], bf16)
    scratch.update({name + "_v": pltpu.VMEM(*value) for name, value in large.items()})
    scratch["sems"] = DMA((48,))
    ins = {name: (getattr(a, name), ANY) for name in names}
    return launch("finish", partial(finish_kernel, line), ins, outs, scratch, plain_params(60))


def body(
    byte_input,
    seq_lengths,
    patch_weight,
    norm_in_gain,
    in_weight,
    conv_weight,
    conv_bias,
    step_bias,
    log_decay,
    skip_gain,
    group_gain,
    out_weight,
    attn_gain,
    qkv_weight,
    attn_out_weight,
    ffn_gain,
    ffn_weight,
    out_grad,
):
    n, mpn = lax.axis_size("dp"), lax.axis_size("mp")
    row = lambda v: v.reshape(1, -1)
    a = SimpleNamespace(
        byte_input=byte_input,
        seq_lengths=seq_lengths,
        patch_weight=patch_weight,
        norm_in_gain=row(norm_in_gain),
        in_weight=in_weight[0].T,
        taps=conv_weight[0].T,
        conv_bias=conv_bias,
        step_bias=step_bias,
        log_decay=log_decay,
        skip=skip_gain,
        group_gain=group_gain,
        out_weight=out_weight[0],
        attn_gain=row(attn_gain),
        qkv_weight=qkv_weight,
        attn_out_weight=attn_out_weight,
        ffn_gain=row(ffn_gain),
        ffn_weight=ffn_weight,
        out_grad=out_grad,
    )
    dim, hidden = ffn_gain.shape[0], ffn_weight.shape[2]
    fits = n * out_grad.shape[1] * dim * 2 <= SPILL_BYTES and 2 * hidden <= dim
    if fits:
        a.__dict__.update(layer(n, mpn, a).__dict__)
    else:
        a.__dict__.update(forward(n, mpn, a).__dict__)
        a.down_part, a.in_part, a.w_grad = ffn(a.ffn_rows, a.grad_rows, a.w_all)
        a.__dict__.update(backward(n, mpn, a).__dict__)
    f = finish(a, fits and mpn == 4)
    return (
        f.block_out,
        f.input_grad,
        f.patch_grad,
        f.norm_in_grad[0],
        f.in_grad.T[None],
        f.conv_w_grad.T[None],
        f.conv_b_grad,
        f.step_grad,
        f.decay_grad,
        f.skip_grad,
        f.group_grad,
        f.out_grad[None],
        f.attn_gain_grad[0],
        f.qkv_grad,
        f.ao_grad,
        f.ffn_gain_grad[0],
        f.ffn_grad,
    )


def solution(mesh):
    in_specs = (
        P(None, "dp", None),
        P(),
        P("mp", None, None),
        P(),
        P("mp", None, None),
        P("mp", None, None),
        P("mp", None),
        P("mp", None),
        P("mp", None),
        P("mp", None),
        P("mp", None),
        P("mp", None, None),
        P(),
        P(None, None, "mp"),
        P("mp", None),
        P(),
        P(None, "mp", "dp"),
        P(None, "dp", None),
    )
    out_specs = (
        P(None, "dp", "mp"),
        P(None, "dp", "mp"),
        P("mp", "dp", None),
        P("dp"),
        P("mp", "dp", None),
        P("mp", "dp", None),
        P("mp", "dp"),
        P("mp", None),
        P("mp", None),
        P("mp", None),
        P("mp", "dp"),
        P("mp", "dp", None),
        P("dp"),
        P(None, "dp", "mp"),
        P("mp", "dp"),
        P("dp"),
        P(None, "mp", "dp"),
    )
    return jax.shard_map(body, mesh=mesh, in_specs=in_specs, out_specs=out_specs, check_vma=False)
```

```python
from functools import partial
from types import SimpleNamespace

import jax
import jax.numpy as jnp
from jax import lax
from jax.experimental import pallas as pl
from jax.experimental.pallas import tpu as pltpu
from jax.sharding import PartitionSpec as P

STATE = 128
CONV = 4
SEQS = 3
GROUP_WIDTH = 512
GROUP_HEADS = 8
HEAD_DIM = 64
ATT_DIM = 64
CONV_CH = 768

norm_eps = 1e-06
highest = lax.Precision.HIGHEST
large_negative = -1e30
f32 = jnp.float32
bf16 = jnp.bfloat16
MESH = pl.DeviceIdType.MESH
VMEM = pl.BlockSpec(memory_space=pltpu.VMEM)
ANY = pl.BlockSpec(memory_space=pl.ANY)
SMEM = pl.BlockSpec(memory_space=pltpu.SMEM)
DMA = pltpu.SemaphoreType.DMA
SMALL_PARAMS = (
    "norm_in_gain", "taps", "conv_bias", "step_bias", "log_decay", "skip", "group_gain", "attn_gain", "ffn_gain"
)
SPILL_BYTES = 4 * 2**20
FFN_COLS = 256
WEIGHT_CUTS = 2
PACE = (1, 1, 1, 1, 1, 2, 6, 0)
PACE_FFN = 6
RELAY_WEIGHTS = ((2, 8), (3, 10))
RELAY_GRADS = (4, 6, 6, 6, 9, 10, 11, 12)
PACE_BACK = (0, 5, 0, 0, 1)


def dot(a, b, dims=((1,), (0,)), precision=None):
    return lax.dot_general(
        a, b, (dims, ((), ())), preferred_element_type=f32, precision=precision
    )


def inv_rms(values):
    return lax.rsqrt(jnp.mean(values * values, axis=-1, keepdims=True) + norm_eps)


def rms_back(values, gain, upstream):
    scale = inv_rms(values)
    weighted = upstream * gain
    inner = jnp.mean(weighted * values, axis=-1, keepdims=True)
    back = scale * weighted - values * (inner * scale * scale * scale)
    return back, upstream * (values * scale)


def silu_pair(values):
    sig = jax.nn.sigmoid(values)
    return values * sig, sig * (1.0 + values * (1.0 - sig))


def rcopy(src, dst, send_sem, recv_sem, dp, mp):
    return pltpu.make_async_remote_copy(
        src_ref=src,
        dst_ref=dst,
        send_sem=send_sem,
        recv_sem=recv_sem,
        device_id={"dp": dp, "mp": mp},
        device_id_type=MESH,
    )


def greet(barrier, dp, mp):
    pl.semaphore_signal(barrier, inc=1, device_id={"dp": dp, "mp": mp}, device_id_type=MESH)


def plain_params(mib=56):
    return pltpu.CompilerParams(vmem_limit_bytes=mib * 2**20)


def remote_params(cid, mib=40):
    return pltpu.CompilerParams(
        collective_id=cid, has_side_effects=True, vmem_limit_bytes=mib * 2**20
    )


def launch(name, kernel, ins, outs, scratch, params):
    names = [*ins, *outs, *scratch]

    def run(*refs):
        kernel(SimpleNamespace(**dict(zip(names, refs))))

    results = pl.pallas_call(
        run,
        out_shape=tuple(jax.ShapeDtypeStruct(shape, dtype) for shape, dtype, _ in outs.values()),
        in_specs=[spec for _, spec in ins.values()],
        out_specs=tuple(spec for _, _, spec in outs.values()),
        scratch_shapes=list(scratch.values()),
        compiler_params=params,
        name=name,
    )(*[array for array, _ in ins.values()])
    return SimpleNamespace(**dict(zip(outs, results)))


def place_of(n, mpn, line):
    i, j = lax.axis_index("dp"), lax.axis_index("mp")
    reps = n // mpn
    return SimpleNamespace(
        n=n, mpn=mpn, i=i, j=j, reps=reps, share=n // reps, half=n // 2,
        m=i // reps, h=i % reps, c=i % 2, mine=i // 2, other=i + 1 - 2 * (i % 2), inside=i // reps == j, line=line,
    )


def greet_all(p, barrier):
    for d in range(1, p.mpn):
        greet(barrier, p.i, (p.j + d) % p.mpn)
    for d in range(1, p.n):
        greet(barrier, (p.i + d) % p.n, p.j)
    for q in range(p.half):
        s = q * 2 + p.c

        @pl.when(jnp.logical_not((s == p.i) & p.inside))
        def _():
            greet(barrier, s, p.m)

    for h in range(0, p.reps, 2):
        for t in range(p.mpn):
            @pl.when(jnp.logical_not((p.j * p.reps + h + p.c == p.i) & (t == p.j)))
            def _():
                greet(barrier, p.j * p.reps + h + p.c, t)
    return p.mpn + p.n - 2 + p.half + p.reps // 2 * p.mpn - 2 * p.inside.astype(jnp.int32)


class Exchange:
    def __init__(self, p, src, dst, ss, rs):
        self.p, self.src, self.dst, self.ss, self.rs = p, src, dst, ss, rs

    def copy(self, t):
        p = self.p
        return rcopy(self.src(t), self.dst(p.j), self.ss.at[t], self.rs.at[p.j], p.i, t)

    def start(self):
        for d in range(1, self.p.mpn):
            self.copy((self.p.j + d) % self.p.mpn).start()
        return self

    def wait(self, d):
        s = (self.p.j + d) % self.p.mpn
        rcopy(self.dst(s), self.dst(s), self.ss.at[s], self.rs.at[s], self.p.i, s).wait_recv()
        return s

    def wait_all(self):
        for d in range(1, self.p.mpn):
            self.wait(d)

    def sent(self):
        for d in range(1, self.p.mpn):
            self.copy((self.p.j + d) % self.p.mpn).wait_send()


class LineGather(Exchange):
    def begin(self):
        for d in range(1, self.p.mpn):
            def send():
                self.copy((self.p.j + d) % self.p.mpn).start()

            self.unless_far(d, send)

    def unless_far(self, d, act):
        if d == 2 or not self.p.line:
            act()
        else:
            pl.when(self.p.j != (3 if d == 1 else 0))(act)

    def onward(self, at):
        s, t = (0, 3) if at == 2 else (3, 0)
        return rcopy(self.dst(s), self.dst(s), self.ss.at[at], self.rs.at[s], self.p.i, t)

    def relay(self):
        if not self.p.line:
            return
        for at in (1, 2):
            @pl.when(self.p.j == at)
            def _():
                self.wait(2)
                self.onward(at).start()

    def wait_all(self):
        for d in range(1, self.p.mpn):
            if d == 2 and self.p.line:
                @pl.when((self.p.j == 0) | (self.p.j == 3))
                def _():
                    self.wait(2)
            else:
                self.wait(d)

    def sent(self):
        for d in range(1, self.p.mpn):
            def done():
                self.copy((self.p.j + d) % self.p.mpn).wait_send()

            self.unless_far(d, done)
        if self.p.line:
            for at in (1, 2):
                @pl.when(self.p.j == at)
                def _():
                    self.onward(at).wait_send()


class LineReduce(Exchange):
    def __init__(self, p, src, dst, ss, rs, held, hs):
        super().__init__(p, src, dst, ss, rs)
        self.held, self.hs = held, hs

    def begin(self):
        p = self.p
        for d in range(1, p.mpn):
            t = (p.j + d) % p.mpn
            if not p.line:
                self.copy(t).start()
            elif d == 2:
                @pl.when((p.j == 0) | (p.j == 3))
                def _():
                    self.copy(t).start()
            else:
                end = 3 if d == 1 else 0

                @pl.when(p.j != end)
                def _():
                    self.copy(t).start()

                @pl.when(p.j == end)
                def _():
                    rcopy(self.src(t), self.held, self.ss.at[t], self.hs, p.i, 2 if end == 3 else 1).start()

    def send(self, t):
        p = self.p
        if not p.line:
            self.copy(t).start()
            return
        apart = jnp.abs(t - p.j)
        taking = (apart == 2) & ((p.j == 1) | (p.j == 2))

        @pl.when(apart == 3)
        def _():
            rcopy(self.src(t), self.held, self.ss.at[t], self.hs, p.i, jnp.where(p.j == 0, 1, 2)).start()

        @pl.when((apart < 3) & jnp.logical_not(taking))
        def _():
            self.copy(t).start()

        pl.when(taking)(self.relay)

    def relay(self):
        p = self.p
        if not p.line:
            return

        @pl.when((p.j == 1) | (p.j == 2))
        def _():
            t = (p.j + 2) % p.mpn
            rcopy(self.held, self.held, self.ss.at[t], self.hs, p.i, t).wait_recv()
            self.held[...] = (self.held[...].astype(f32) + self.src(t)[...].astype(f32)).astype(bf16)
            rcopy(self.held, self.dst(p.j), self.ss.at[t], self.rs.at[p.j], p.i, t).start()

    def wait_all(self):
        for d in range(1, self.p.mpn):
            if d == 2 or not self.p.line:
                self.wait(d)
            else:
                @pl.when(self.p.j != (3 if d == 1 else 0))
                def _():
                    self.wait(d)


def absent(line, j, s):
    return line & (((j == 3) & (s == 0)) | ((j == 0) & (s == 3)))


class Bulk:
    def __init__(self, exchanges):
        self.exchanges, self.begun, self.before, self.relayed = exchanges, 0, 0, 0

    def relay(self, last):
        last = min(last, self.begun)
        for exchange in self.exchanges[self.relayed : last]:
            exchange.relay()
        self.relayed = max(last, self.relayed)

    def go(self, count, relay=None):
        count = min(count, len(self.exchanges) - self.begun)
        self.relay(self.before if relay is None else relay)
        self.before = self.begun
        for exchange in self.exchanges[self.begun : self.begun + count]:
            exchange.begin()
        self.begun += count

    def wait(self, first, last):
        self.relay(last)
        for exchange in self.exchanges[first:last]:
            exchange.wait_all()

    def sent(self):
        for exchange in self.exchanges:
            exchange.sent()


class PlaneGather:
    def __init__(self, p, own, slot, ss, rs, ssr):
        self.p, self.own, self.slot, self.ss, self.rs, self.ssr = p, own, slot, ss, rs, ssr

    def direct(self, q):
        p = self.p
        return rcopy(self.own, self.slot(p.i), self.ss.at[q], self.rs.at[p.i], q * 2 + p.c, p.j)

    def across(self, q):
        p = self.p
        s = q * 2 + p.c
        return rcopy(self.slot(s), self.slot(s), self.ssr.at[q], self.rs.at[s], p.other, p.j)

    def own_across(self):
        p = self.p
        return rcopy(self.own, self.slot(p.i), self.ssr.at[p.mine], self.rs.at[p.i], p.other, p.j)

    def others(self):
        return [(self.p.mine + d) % self.p.half for d in range(1, self.p.half)]

    def start(self):
        self.own_across().start()
        for q in self.others():
            self.direct(q).start()
        return self

    def relay_one(self, q):
        s = q * 2 + self.p.c
        rcopy(self.slot(s), self.slot(s), self.ss.at[q], self.rs.at[s], s, self.p.j).wait_recv()
        self.across(q).start()

    def wait_across(self, q):
        s = q * 2 + 1 - self.p.c
        rcopy(self.slot(s), self.slot(s), self.ssr.at[q], self.rs.at[s], self.p.other, self.p.j).wait_recv()

    def relay(self):
        for q in reversed(self.others()):
            self.relay_one(q)

    def finish(self):
        for q in range(self.p.half):
            self.wait_across(q)

    def sent(self):
        self.own_across().wait_send()
        for q in self.others():
            self.direct(q).wait_send()
            self.across(q).wait_send()


class Reduction:
    def __init__(self, p, block, value, pre, recv, ss, get, put):
        self.p, self.block, self.value, self.pre, self.recv, self.get, self.put = p, block, value, pre, recv, get, put
        self.ssa, self.rsa, self.ssb, self.rsb = (ss.at[k] for k in range(4))

    def first(self, q):
        p = self.p
        return rcopy(self.block(q * 2 + 1 - p.c), self.pre.at[q], self.ssa.at[q], self.rsa.at[q], p.other, p.j)

    def second(self, q):
        p = self.p
        return rcopy(self.pre.at[q], self.recv.at[p.mine], self.ssb.at[q], self.rsb.at[p.mine], q * 2 + p.c, p.j)

    def others(self):
        return [(self.p.mine + d) % self.p.half for d in range(1, self.p.half)]

    def start(self):
        for q in self.others() + [self.p.mine]:
            self.first(q).start()

    def spread_one(self, q):
        p = self.p
        rcopy(self.pre.at[q], self.pre.at[q], self.ssa.at[q], self.rsa.at[q], p.other, p.j).wait_recv()
        total = self.value(q * 2 + p.c).astype(f32)
        self.put(self.pre.at[q], (total + self.get(self.pre.at[q]).astype(f32)).astype(bf16))
        self.second(q).start()

    def spread(self):
        for q in self.others():
            self.spread_one(q)

    def finish(self):
        p, mine = self.p, self.p.mine
        rcopy(self.pre.at[mine], self.pre.at[mine], self.ssa.at[mine], self.rsa.at[mine], p.other, p.j).wait_recv()
        total = self.value(p.i).astype(f32)
        total = total + self.get(self.pre.at[mine]).astype(f32)
        for q in self.others():
            rcopy(self.recv.at[q], self.recv.at[q], self.ssb.at[q], self.rsb.at[q], q * 2 + p.c, p.j).wait_recv()
            total = total + self.get(self.recv.at[q]).astype(f32)
        return total

    def sent(self):
        for q in self.others() + [self.p.mine]:
            self.first(q).wait_send()
        for q in self.others():
            self.second(q).wait_send()


def plain_get(view):
    return view[...]


def plain_put(view, value):
    view[...] = value


class Cast:
    def __init__(self, p, low, dst, ss, rs, ssr):
        self.p, self.low, self.dst, self.ss, self.rs, self.ssr = p, low, dst, ss, rs, ssr

    def each(self, act):
        p = self.p
        for h in range(0, p.reps, 2):
            for t in range(p.mpn):
                to = p.j * p.reps + h + p.c

                @pl.when(jnp.logical_not((to == p.i) & (t == p.j)))
                def _():
                    act(rcopy(self.low, self.dst.at[p.i], self.ss.at[h // 2 * p.mpn + t], self.rs.at[p.i], to, t))

    def across(self, q):
        p = self.p
        s = q * 2 + p.c
        return rcopy(self.dst.at[s], self.dst.at[s], self.ssr.at[q], self.rs.at[s], p.other, p.j)

    def start(self):
        self.each(lambda copy: copy.start())

        @pl.when(self.p.inside)
        def _():
            self.dst[self.p.i] = self.low[...]

    def wait(self):
        p = self.p
        for q in range(p.half):
            s = q * 2 + p.c

            @pl.when(jnp.logical_not((s == p.i) & p.inside))
            def _():
                rcopy(self.low, self.dst.at[s], self.ss.at[0], self.rs.at[s], s, p.m).wait_recv()

            self.across(q).start()
        for q in range(p.half):
            s = q * 2 + 1 - p.c
            rcopy(self.dst.at[s], self.dst.at[s], self.ssr.at[q], self.rs.at[s], p.other, p.j).wait_recv()

    def sent(self):
        self.each(lambda copy: copy.wait_send())
        for q in range(self.p.half):
            self.across(q).wait_send()


class ToOwner:
    def __init__(self, p, part, mid, recv, ss, rs, ss_line, rs_line):
        self.p, self.part, self.mid, self.recv, self.ss, self.rs = p, part, mid, recv, ss, rs
        self.line = Exchange(p, lambda t: mid.at[t], lambda s: recv.at[s], ss_line, rs_line)

    def each(self, act):
        p = self.p
        for q in range(p.share):
            block = q * p.reps + p.h

            @pl.when(block != p.i)
            def _():
                act(rcopy(self.part.at[block], self.mid.at[p.m], self.ss.at[q], self.rs.at[p.m], block, p.j))

    def start(self):
        self.each(lambda copy: copy.start())
        self.mid[self.p.m] = self.part[self.p.i]

    def pass_on(self):
        p = self.p
        for s in range(p.mpn):
            @pl.when(s != p.m)
            def _():
                rcopy(
                    self.part.at[0], self.mid.at[s], self.ss.at[0], self.rs.at[s], s * p.reps + p.h, p.j
                ).wait_recv()
        self.line.start()
        self.recv[p.j] = self.mid[p.j]

    def total(self):
        self.line.wait_all()
        return sum(self.recv[s].astype(f32) for s in range(self.p.mpn))

    def sent(self):
        self.each(lambda copy: copy.wait_send())
        self.line.sent()


def perm_matrix(rows, patches, per, limit):
    at = lax.broadcasted_iota(jnp.int32, (rows, rows), 0)
    source = lax.broadcasted_iota(jnp.int32, (rows, rows), 1)
    return ((source == (at % patches) * per + at // patches) & (at % patches < limit)).astype(bf16)


class Loads:
    def __init__(self, sems):
        self.sems, self.count = sems, 0

    def __call__(self, src, dst):
        copy = pltpu.make_async_copy(src, dst, self.sems.at[self.count])
        self.count += 1
        copy.start()
        return copy


def own_lengths(r, m):
    return r.seq_lengths[m, 0], r.seq_lengths[m, 1], r.seq_lengths[m, 2]


def seg_starts(lengths, places):
    end0 = lengths[0]
    end1 = end0 + lengths[1]
    end2 = end1 + lengths[2]
    return jnp.where(
        places >= end2, end2, jnp.where(places >= end1, end1, jnp.where(places >= end0, end0, 0))
    )


def conv_taps(conv_in, pos, lag):
    moved = conv_in if lag == 0 else pltpu.roll(conv_in, lag, 0)
    return jnp.where(pos >= lag, moved, 0.0)


def mixer_state(lengths, projected, conv_weight, conv_bias, step_bias, log_decay):
    patches = projected.shape[0]
    places = lax.broadcasted_iota(jnp.int32, (patches, 1), 0)
    start = seg_starts(lengths, places)
    pos = places - start
    conv_in = projected[:, GROUP_WIDTH : GROUP_WIDTH + CONV_CH]
    conv_out = conv_bias
    for lag in range(CONV):
        conv_out = conv_out + conv_taps(conv_in, pos, lag) * conv_weight[CONV - 1 - lag][None]
    step_raw = projected[:, GROUP_WIDTH + CONV_CH :] + step_bias
    step = jnp.maximum(step_raw, 0.0) + jnp.log1p(jnp.exp(-jnp.abs(step_raw)))
    logd = -step * jnp.exp(log_decay)
    across = lax.broadcasted_iota(jnp.int32, (patches, patches), 1)
    down = lax.broadcasted_iota(jnp.int32, (patches, patches), 0)
    mask = (across >= start) & (across <= down)
    running = dot(mask.astype(f32), logd, precision=highest)
    return pos, conv_in, conv_out, step_raw, step, logd, mask, running


def head_decay(mask, running, running_t, h):
    return jnp.exp(
        jnp.where(mask, running[:, h : h + 1] - running_t[h : h + 1, :], large_negative)
    )


def att_mask(rows, patches):
    across = lax.broadcasted_iota(jnp.int32, (rows, rows), 1)
    down = lax.broadcasted_iota(jnp.int32, (rows, rows), 0)
    return (across % patches == down % patches) & (across <= down)


def soft_rows(mask, query, key):
    scores = dot(query, key, ((1,), (1,))) * ATT_DIM ** (-0.5)
    scores = jnp.where(mask, scores, large_negative)
    probs = jnp.exp(scores - jnp.max(scores, axis=1, keepdims=True))
    return probs / jnp.sum(probs, axis=1, keepdims=True)


def skip_columns(r):
    head = lax.broadcasted_iota(jnp.int32, (1, GROUP_WIDTH), 1) // HEAD_DIM
    return sum(jnp.where(head == h, r.skip[:, h : h + 1], 0.0) for h in range(GROUP_HEADS))


def mixer_fwd(r, lengths, normed):
    projected = dot(normed, r.in_v[...], ((1,), (1,)))
    r.projected[...] = projected
    _, _, conv_out, _, step, _, mask, running = mixer_state(
        lengths, projected, r.taps[...], r.conv_bias[...], r.step_bias[...], r.log_decay[...]
    )
    act = conv_out * jax.nn.sigmoid(conv_out)
    inputs = act[:, GROUP_WIDTH : GROUP_WIDTH + STATE]
    outputs = act[:, GROUP_WIDTH + STATE :]
    inner = dot(outputs, inputs, ((1,), (1,)))
    running_t, step_t = running.T, step.T
    pair = 2 * HEAD_DIM
    lane = lax.broadcasted_iota(jnp.int32, (1, pair), 1)
    pieces = []
    for c in range(GROUP_WIDTH // pair):
        values = act[:, c * pair : (c + 1) * pair]
        got = []
        for h in (2 * c, 2 * c + 1):
            weights = head_decay(mask, running, running_t, h) * inner * step_t[h : h + 1, :]
            got.append(dot(weights, values))
        pieces.append(jnp.where(lane < HEAD_DIM, got[0], got[1]))
    y = jnp.concatenate(pieces, axis=1) + skip_columns(r) * act[:, :GROUP_WIDTH]
    r.mixer_y[...] = y
    gate = projected[:, :GROUP_WIDTH]
    gated = y * (gate * jax.nn.sigmoid(gate))
    low = (gated * inv_rms(gated) * r.group_gain[...]).astype(bf16)
    r.mixer_low[...] = low
    return dot(low, r.out_v[...])


def forward_steps(p, r, load, land):
    n, mpn, i, j = p.n, p.mpn, p.i, p.j
    micro, patches, own_cols = r.own.shape
    positions, dim = r.pw.shape[0], r.pw.shape[1]
    slabs = r.bytes_v.shape[2] // dim
    rows = slabs * patches
    features = r.bytes_part.shape[-1]
    per, hidden = r.ffn_weight.shape[1:]

    load_own = load(r.byte_input.at[:, :, pl.ds(pl.multiple_of(j * own_cols, 128), own_cols)], r.own)
    load_pw = [load(r.patch_weight.at[k], r.pw.at[k]) for k in range(positions)]
    loads_small = load_small(r, load)
    load_grad = load(r.out_grad.at[j], r.grad_raw)
    load_in = load(r.in_weight, r.in_v)
    load_out = load(r.out_weight, r.out_v)
    load_bytes = load(r.byte_input, r.bytes_v)
    load_qkv = load(r.qkv_weight, r.qkv_v)
    kept = [load(r.ffn_weight.at[w], land(j, w, slice(None), slice(None))) for w in range(3)]

    barrier = pltpu.get_barrier_semaphore()
    count = greet_all(p, barrier)
    halves = max(hidden // FFN_COLS, 1)
    cuts = WEIGHT_CUTS if per // WEIGHT_CUTS >= 16 else 1
    step = per // cuts
    pieces = []
    for hh in range(halves):
        cols = slice(hh * (hidden // halves), (hh + 1) * (hidden // halves))
        for w in range(3):
            for k in range(cuts):
                at = slice(k * step, (k + 1) * step)
                pieces.append(LineGather(
                    p,
                    lambda t, w=w, at=at, cols=cols: r.ffn_weight.at[w, at, cols],
                    lambda s, w=w, at=at, cols=cols: land(s, w, at, cols),
                    r.ssw.at[len(pieces)],
                    r.rsw.at[len(pieces)],
                ))
    bulk = Bulk(pieces)
    pl.semaphore_wait(barrier, count)
    bulk.go(PACE[7])
    load_own.wait()
    sums = None
    for k in range(positions):
        load_pw[k].wait()
        term = dot(r.own[:, :, k * dim : (k + 1) * dim].reshape(micro * patches, dim), r.pw[k])
        sums = term if sums is None else sums + term
    for t in range(micro):
        r.part[t] = sums[t * patches : (t + 1) * patches]
        r.part_low[t] = sums[t * patches : (t + 1) * patches].astype(bf16)
    embed = Exchange(p, lambda t: r.part_low.at[t], lambda s: r.recv.at[s], r.ss1, r.rs1).start()
    bulk.go(PACE[0])
    load_grad.wait()
    perm = perm_matrix(rows, patches, slabs, sum(own_lengths(r, j)) - i * patches)
    r.own_grad[...] = dot(perm, r.grad_raw[...]).astype(bf16)
    r.grad_rows_own(i, r.own_grad[...])
    for copy in loads_small:
        copy.wait()
    total = r.part[j]
    for d in range(1, mpn):
        total = total + r.recv[embed.wait(d)].astype(f32)
    r.global_in[...] = total
    r.low[...] = (total * inv_rms(total) * r.norm_in_gain[...]).astype(bf16)
    cast = Cast(p, r.low, r.normed, r.ss2, r.rs2, r.ssc)
    cast.start()
    def columns_of(t, k):
        first = k * dim + t * (dim // n) // features * features
        return r.own.at[:, :, pl.ds(pl.multiple_of(first, 128), features)]

    def bytes_copy(t, k):
        return rcopy(columns_of(t, k), r.bytes_part.at[i, k], r.ssb.at[t, k], r.rsb.at[i, k], t, j)

    for d in range(1, n):
        for k in range(positions):
            bytes_copy((i + d) % n, k).start()
    kept += [load(columns_of(i, k), r.bytes_part.at[i, k]) for k in range(positions)]
    piece = r.out_proj.shape[0] // n
    at_piece = lambda s: pl.ds(pl.multiple_of(s * piece, piece), piece)
    kept_ao = load(r.out_proj.at[at_piece(i)], r.ao_sorted.at[j, at_piece(i)])
    ao_line = LineGather(
        p, lambda t: r.out_proj.at[at_piece(i)], lambda s: r.ao_sorted.at[s, at_piece(i)], r.ssa, r.rsa
    )
    ao_line.begin()
    bulk.go(PACE[1])
    load_in.wait()
    load_out.wait()
    cast.wait()
    feature = dim // n
    blocks = max(feature, 128)

    def normed_copy(q):
        t = q * p.reps + p.h
        return rcopy(normed_block(t), r.normed_cols.at[p.m], r.ssn.at[q], r.rsn.at[p.m], t, j)

    def normed_block(t):
        return r.normed.at[:, :, pl.ds(pl.multiple_of(t * feature // blocks * blocks, 128), blocks)]

    def each_normed(act, here):
        for q in range(p.share):
            at_home = q * p.reps + p.h == i
            pl.when(jnp.logical_not(at_home))(partial(act, q))
            pl.when(at_home)(here)

    def keep_normed():
        return pltpu.make_async_copy(normed_block(i), r.normed_cols.at[p.m], r.ssn.at[p.share])

    each_normed(lambda q: normed_copy(q).start(), lambda: keep_normed().start())
    bulk.go(PACE[2])

    part = mixer_fwd(r, own_lengths(r, p.m), r.normed[...].reshape(n * patches, dim))
    for b in range(n):
        r.mix_part[b] = part[b * patches : (b + 1) * patches].astype(bf16)
    to_owner = ToOwner(p, r.mix_part, r.mix_mid, r.mix_recv, r.ss3, r.rs3, r.sso, r.rso)
    to_owner.start()
    kept_ao.wait()
    ao_line.relay()
    to_owner.pass_on()
    bulk.go(PACE[3])
    ao_line.wait_all()
    ao_block = lambda s: r.ao_sorted.at[:, at_piece(s)]
    ao_plane = PlaneGather(p, ao_block(i), ao_block, r.ssap, r.rsap, r.ssar).start()
    grads = PlaneGather(p, r.own_grad, lambda s: r.grad_rows.at[s], r.ssg, r.rsg, r.ssgr).start()
    total = r.global_in[...] + to_owner.total()
    r.global_own[...] = total
    r.patch_all[j] = total.astype(bf16)
    patch_line = Exchange(p, lambda t: r.patch_all.at[j], lambda s: r.patch_all.at[s], r.ss4, r.rs4).start()
    bulk.go(PACE[4])
    load_bytes.wait()
    load_qkv.wait()
    patch_line.wait_all()

    mask = att_mask(rows, patches)
    pair = 2 * ATT_DIM
    width = r.qkv_v.shape[2]
    lane = lax.broadcasted_iota(jnp.int32, (1, pair), 1)
    heads_line = Exchange(p, lambda t: r.heads.at[t], lambda s: r.heads_own.at[s], r.ss5, r.rs5)

    def one_micro(d, _):
        m = (j + d) % mpn
        for k in range(slabs):
            here = r.bytes_v[m, :, k * dim : (k + 1) * dim].astype(f32) + r.patch_all[m].astype(f32)
            r.attn_in[m, k * patches : (k + 1) * patches, :] = (
                here * inv_rms(here) * r.attn_gain[...]
            ).astype(bf16)
        got = r.attn_in[m]
        for w in range(3):
            r.qkv[w, m] = dot(got, r.qkv_v[w]).astype(bf16)
        for c in range(width // pair):
            at = slice(c * pair, (c + 1) * pair)
            query, key, value = r.qkv[0, m, :, at], r.qkv[1, m, :, at], r.qkv[2, m, :, at]
            res = []
            for own in (lane < ATT_DIM, lane >= ATT_DIM):
                probs = soft_rows(mask, jnp.where(own, query, jnp.zeros_like(query)), key)
                res.append(dot(probs.astype(bf16), value))
            r.heads[m, :, at] = jnp.where(lane < ATT_DIM, res[0], res[1]).astype(bf16)

        @pl.when(d < mpn)
        def _():
            heads_line.copy(m).start()

        return 0

    lax.fori_loop(1, mpn + 1, one_micro, 0)
    bulk.go(PACE[5])
    r.heads_own[j] = r.heads[j]
    ao_plane.relay()
    ao_plane.finish()
    grads.relay()
    for k in range(slabs):
        here = r.bytes_v[j, :, k * dim : (k + 1) * dim].astype(f32) + r.global_own[...]
        r.after[k * patches : (k + 1) * patches, :] = here
    branch = None
    for d in range(mpn):
        s = j if d == 0 else heads_line.wait(d)
        term = dot(r.heads_own[s], r.ao_sorted[s])
        branch = term if branch is None else branch + term
    after = r.after[...] + branch
    r.after[...] = after
    r.ffn_own[...] = (after * inv_rms(after) * r.ffn_gain[...]).astype(bf16)
    rows_gather = PlaneGather(p, r.ffn_own, lambda s: r.ffn_rows.at[s], r.ssf, r.rsf, r.ssfr).start()
    r.ffn_rows_own(i, r.ffn_own[...])
    bulk.go(PACE[6])

    def settle():
        for d in range(1, n):
            s = (i + d) % n
            for k in range(positions):
                rcopy(r.bytes_part.at[s, k], r.bytes_part.at[s, k], r.ssb.at[s, k], r.rsb.at[s, k], s, j).wait_recv()
        for s in range(mpn):
            @pl.when(s * p.reps + p.h != i)
            def _():
                rcopy(
                    r.normed_cols.at[s], r.normed_cols.at[s], r.ssn.at[0], r.rsn.at[s], s * p.reps + p.h, j
                ).wait_recv()
        each_normed(lambda q: normed_copy(q).wait_send(), lambda: keep_normed().wait())
        for thing in (embed, bulk, cast, ao_line, to_owner, ao_plane, patch_line, heads_line):
            thing.sent()
        for d in range(1, n):
            for k in range(positions):
                bytes_copy((i + d) % n, k).wait_send()

    return SimpleNamespace(grads=grads, rows=rows_gather, bulk=bulk, halves=halves, kept=kept, settle=settle)


def forward_kernel(n, mpn, r):
    p = place_of(n, mpn, False)
    load = Loads(r.sem_load)
    kept = []
    r.grad_rows_own = lambda s, value: kept.append(load(r.own_grad, r.grad_rows.at[s]))
    r.ffn_rows_own = lambda s, value: kept.append(load(r.ffn_own, r.ffn_rows.at[s]))
    st = forward_steps(p, r, load, lambda s, w, rows, cols: r.w_all.at[s, w, rows, cols])
    st.grads.finish()
    st.rows.relay()
    st.rows.finish()
    st.bulk.go(len(st.bulk.exchanges))
    st.bulk.wait(0, len(st.bulk.exchanges))
    st.settle()
    st.rows.sent()
    st.grads.sent()
    for copy in kept + st.kept:
        copy.wait()


def forward_ins(a):
    ins = dict(seq_lengths=(a.seq_lengths, SMEM))
    for name in ("byte_input", "patch_weight", "out_grad", "in_weight", "out_weight", "qkv_weight", "ffn_weight"):
        ins[name] = (getattr(a, name), ANY)
    ins["out_proj"] = (a.attn_out_weight, ANY)
    for name in SMALL_PARAMS:
        ins["given_" + name] = (getattr(a, name), ANY)
    return ins


def small_scratch(a):
    return {name: pltpu.VMEM(getattr(a, name).shape, f32) for name in SMALL_PARAMS}


def load_small(r, load):
    return [load(getattr(r, "given_" + name), getattr(r, name)) for name in SMALL_PARAMS]


def forward_results(n, mpn, a):
    micro, patches, cols = a.byte_input.shape
    dim = a.norm_in_gain.shape[1]
    rows = patches * (cols // dim)
    positions = a.patch_weight.shape[0]
    width = a.qkv_weight.shape[2]
    seq = n * patches
    large = dict(
        grad_rows=((n, rows, dim), bf16),
        ffn_rows=((n, rows, dim), bf16),
        w_all=((mpn,) + a.ffn_weight.shape, bf16),
        bytes_part=((n, positions, micro, patches, max(dim // n, 128)), bf16),
        normed_cols=((mpn, n, patches, max(dim // n, 128)), bf16),
    )
    small = dict(
        own_grad=((rows, dim), bf16),
        after=((rows, dim), f32),
        heads_own=((mpn, rows, width), bf16),
        qkv=((3, micro, rows, width), bf16),
        attn_in=((micro, rows, dim), bf16),
        ao_sorted=((mpn,) + a.attn_out_weight.shape, bf16),
        global_in=((patches, dim), f32),
        global_own=((patches, dim), f32),
        normed=((n, patches, dim), bf16),
        projected=((seq, a.in_weight.shape[0]), f32),
        mixer_y=((seq, GROUP_WIDTH), f32),
        mixer_low=((seq, GROUP_WIDTH), bf16),
    )
    return large, small


def forward_scratch(n, mpn, a):
    micro, patches, cols = a.byte_input.shape
    dim = a.norm_in_gain.shape[1]
    rows = patches * (cols // dim)
    positions = a.patch_weight.shape[0]
    width = a.qkv_weight.shape[2]
    half = n // 2
    pieces = max(a.ffn_weight.shape[2] // FFN_COLS, 1) * 3 * WEIGHT_CUTS
    line, plane = DMA((mpn,)), DMA((half,))
    return dict(
        **small_scratch(a),
        own=pltpu.VMEM((micro, patches, positions * dim), bf16),
        pw=pltpu.VMEM(a.patch_weight.shape, bf16),
        grad_raw=pltpu.VMEM((rows, dim), bf16),
        in_v=pltpu.VMEM(a.in_weight.shape, bf16),
        out_v=pltpu.VMEM(a.out_weight.shape, bf16),
        bytes_v=pltpu.VMEM(a.byte_input.shape, bf16),
        qkv_v=pltpu.VMEM(a.qkv_weight.shape, bf16),
        part=pltpu.VMEM((micro, patches, dim), f32),
        part_low=pltpu.VMEM((micro, patches, dim), bf16),
        recv=pltpu.VMEM((mpn, patches, dim), bf16),
        low=pltpu.VMEM((patches, dim), bf16),
        mix_part=pltpu.VMEM((n, patches, dim), bf16),
        mix_mid=pltpu.VMEM((mpn, patches, dim), bf16),
        mix_recv=pltpu.VMEM((mpn, patches, dim), bf16),
        patch_all=pltpu.VMEM((mpn, patches, dim), bf16),
        heads=pltpu.VMEM((micro, rows, width), bf16),
        ffn_own=pltpu.VMEM((rows, dim), bf16),
        sem_load=DMA((48,)),
        ss1=line, rs1=line, ss2=DMA((n,)), rs2=DMA((n,)), ssc=plane, ss3=line, rs3=line, sso=line, rso=line, ss4=line, rs4=line, ss5=line, rs5=line,
        ssg=plane, rsg=DMA((n,)), ssgr=plane, ssf=plane, rsf=DMA((n,)), ssfr=plane,
        ssb=DMA((n, positions)), rsb=DMA((n, positions)),
        ssn=DMA((mpn + 1,)), rsn=line, ssa=line, rsa=line, ssap=plane, rsap=DMA((n,)), ssar=plane,
        ssw=DMA((pieces, mpn)), rsw=DMA((pieces, mpn)),
    )


def forward(n, mpn, a):
    large, small = forward_results(n, mpn, a)
    outs = {name: value + (ANY,) for name, value in large.items()}
    outs.update({name: value + (VMEM,) for name, value in small.items()})
    return launch(
        "forward", partial(forward_kernel, n, mpn), forward_ins(a), outs, forward_scratch(n, mpn, a),
        remote_params(0, 62),
    )


def ffn_kernel(rows_in, grads_in, parts, down_out, in_grad, weight_grad, weight, gate_low, up_low, hidden_low):
    blocks, rows, dim = rows_in.shape
    per = parts.shape[2]
    for s in range(parts.shape[0]):
        for w in range(3):
            weight[w, s * per : (s + 1) * per, :] = parts[s, w]

    def step(b, _):
        here, up = rows_in[b], grads_in[b]
        gate = dot(here, weight[0])
        other = dot(here, weight[1])
        act, slope = silu_pair(gate)
        hidden = (act * other).astype(bf16)
        hidden_low[b] = hidden
        down_out[b] = dot(hidden, weight[2], ((1,), (1,))).astype(bf16)
        hidden_grad = dot(up, weight[2])
        gate_grad = (hidden_grad * other * slope).astype(bf16)
        up_grad = (hidden_grad * act).astype(bf16)
        gate_low[b] = gate_grad
        up_low[b] = up_grad
        back = dot(gate_grad, weight[0], ((1,), (1,))) + dot(up_grad, weight[1], ((1,), (1,)))
        in_grad[b] = back.astype(bf16)
        return 0

    lax.fori_loop(0, blocks, step, 0)
    hidden = weight.shape[2]
    everything = rows_in[...].reshape(blocks * rows, dim)
    weight_grad[0] = dot(everything, gate_low[...].reshape(blocks * rows, hidden), ((0,), (0,))).astype(bf16)
    weight_grad[1] = dot(everything, up_low[...].reshape(blocks * rows, hidden), ((0,), (0,))).astype(bf16)
    weight_grad[2] = dot(
        grads_in[...].reshape(blocks * rows, dim), hidden_low[...].reshape(blocks * rows, hidden), ((0,), (0,))
    ).astype(bf16)


def ffn(rows_in, grads_in, parts):
    blocks, rows, dim = rows_in.shape
    hidden = parts.shape[3]
    return pl.pallas_call(
        ffn_kernel,
        out_shape=(
            jax.ShapeDtypeStruct((blocks, rows, dim), bf16),
            jax.ShapeDtypeStruct((blocks, rows, dim), bf16),
            jax.ShapeDtypeStruct((3, dim, hidden), bf16),
        ),
        in_specs=[VMEM] * 3,
        out_specs=(VMEM,) * 3,
        scratch_shapes=[pltpu.VMEM((3, dim, hidden), bf16)] + [pltpu.VMEM((blocks, rows, hidden), bf16)] * 3,
        compiler_params=plain_params(60),
        name="ffn",
    )(rows_in, grads_in, parts)


def mixer_bwd(r, p, lengths, upstream):
    projected = r.projected[...]
    patches = projected.shape[0]
    pos, conv_in, conv_out, step_raw, step, logd, mask, running = mixer_state(
        lengths, projected, r.taps[...], r.conv_bias[...], r.step_bias[...], r.log_decay[...]
    )
    act, act_slope = silu_pair(conv_out)
    inputs = act[:, GROUP_WIDTH : GROUP_WIDTH + STATE]
    outputs = act[:, GROUP_WIDTH + STATE :]
    inner = dot(outputs, inputs, ((1,), (1,)))
    running_t, step_t = running.T, step.T
    normed_grad = dot(upstream, r.out_v[...], ((1,), (1,)))
    y = r.mixer_y[...]
    gate = projected[:, :GROUP_WIDTH]
    gate_act, gate_slope = silu_pair(gate)
    gated_grad, gain_rows = rms_back(y * gate_act, r.group_gain[...], normed_grad)
    y_grad = gated_grad * gate_act
    gate_grad = gated_grad * y * gate_slope
    values = act[:, :GROUP_WIDTH]
    skip_cols = jnp.sum(y_grad * values, axis=0, keepdims=True)
    pair = 2 * HEAD_DIM
    lane = lax.broadcasted_iota(jnp.int32, (1, pair), 1)
    inner_grad = jnp.zeros_like(inner)
    value_pieces, row_sums, col_sums = [], [], []
    for c in range(GROUP_WIDTH // pair):
        at = slice(c * pair, (c + 1) * pair)
        got = []
        for h in (2 * c, 2 * c + 1):
            own = (lane < HEAD_DIM) if h % 2 == 0 else (lane >= HEAD_DIM)
            mine = jnp.where(own, y_grad[:, at], 0.0)
            decay = head_decay(mask, running, running_t, h)
            step_row = step_t[h : h + 1, :]
            weight_grad = dot(mine, values[:, at], ((1,), (1,))) * decay
            scaled = weight_grad * step_row
            inner_grad = inner_grad + scaled
            col_sums.append(jnp.sum(weight_grad * inner, axis=0, keepdims=True))
            row_sums.append(jnp.sum(scaled * inner, axis=1, keepdims=True))
            weights = decay * inner * step_row
            got.append(dot(weights, mine, ((0,), (0,))))
        value_pieces.append(got[0] + got[1])
    values_grad = jnp.concatenate(value_pieces, axis=1) + skip_columns(r) * y_grad
    inputs_grad = dot(inner_grad, outputs, ((0,), (0,)))
    outputs_grad = dot(inner_grad, inputs)
    col_grad = jnp.concatenate(col_sums, axis=0).T
    running_grad = jnp.concatenate(row_sums, axis=1) - col_grad * step
    logd_grad = dot(mask.astype(f32), running_grad, ((0,), (0,)), precision=highest)
    step_grad = (col_grad - logd_grad * jnp.exp(r.log_decay[...])) * jax.nn.sigmoid(step_raw)
    conv_grad = jnp.concatenate([values_grad, inputs_grad, outputs_grad], axis=1) * act_slope
    conv_in_grad = jnp.zeros_like(conv_grad)
    small = r.small_part
    small[...] = jnp.zeros(small.shape, f32)
    for lag in range(CONV):
        small[CONV - 1 - lag : CONV - lag, :] = jnp.sum(
            conv_grad * conv_taps(conv_in, pos, lag), axis=0, keepdims=True
        )
        kept = jnp.where(pos >= lag, conv_grad, 0.0) * r.taps[CONV - 1 - lag : CONV - lag, :]
        conv_in_grad = conv_in_grad + (kept if lag == 0 else pltpu.roll(kept, patches - lag, 0))
    small[CONV : CONV + 1, :] = jnp.sum(conv_grad, axis=0, keepdims=True)
    small[CONV + 1 : CONV + 2, :GROUP_WIDTH] = jnp.sum(gain_rows, axis=0, keepdims=True)
    small[CONV + 2 : CONV + 3, :GROUP_WIDTH] = skip_cols
    small[CONV + 3 : CONV + 4, :GROUP_HEADS] = jnp.sum(step_grad, axis=0, keepdims=True)
    small[CONV + 4 : CONV + 5, :GROUP_HEADS] = jnp.sum(logd_grad * logd, axis=0, keepdims=True)
    return jnp.concatenate([gate_grad, conv_in_grad, step_grad], axis=1).astype(bf16)


def grad_pieces(p, r, halves, grad_of, dim, hidden):
    per = dim // p.mpn
    step = per // WEIGHT_CUTS
    pieces = []
    for hh in range(halves):
        cols = slice(hh * (hidden // halves), (hh + 1) * (hidden // halves))
        for w in range(3):
            for k in range(WEIGHT_CUTS):
                at = slice(k * step, (k + 1) * step)
                pieces.append(LineReduce(
                    p,
                    lambda t, w=w, k=k, cols=cols: grad_of(
                        w, pl.ds(pl.multiple_of(t * per + k * step, step), step), cols
                    ),
                    lambda s, w=w, at=at, cols=cols: r.g_recv.at[s, w, at, cols],
                    r.bsw.at[len(pieces)],
                    r.brw.at[len(pieces)],
                    r.g_held.at[len(pieces)] if p.line else None,
                    r.bsr.at[len(pieces)] if p.line else None,
                ))
    return Bulk(pieces)


def ffn_sums(p, r, get, put):
    in_block = lambda s: r.in_part.at[s]
    down_block = lambda s: r.down_part.at[s]
    return (
        Reduction(p, in_block, lambda s: get(in_block(s)), r.in_pre, r.in_recv, r.bs_in, get, put),
        Reduction(p, down_block, lambda s: get(down_block(s)), r.down_pre, r.down_recv, r.bs_down, get, put),
    )


def backward_steps(p, r, load, own_slab, ready, sum_in, sum_down, bulk, pieces_of=None):
    n, mpn, i, j = p.n, p.mpn, p.i, p.j
    micro, rows, dim = r.attn_in.shape
    patches = r.global_own.shape[0]
    slabs = rows // patches
    width = r.qkv_v.shape[2]
    feature = dim // n
    at_feature = lambda s: pl.ds(pl.multiple_of(s * feature, feature), feature)
    block_ao = lambda s: r.ao_part.at[at_feature(s)]
    block_qkv = lambda s: r.qkv_part.at[:, at_feature(s)]
    sum_ao = Reduction(
        p, block_ao, lambda s: block_ao(s)[...], r.ao_pre, r.ao_recv, r.bs_ao, plain_get, plain_put
    )
    sum_qkv = Reduction(
        p, block_qkv, lambda s: block_qkv(s)[...], r.qkv_pre, r.qkv_recv, r.bs_qkv, plain_get, plain_put
    )

    ready("bytes")
    for k in range(slabs):
        r.local_in[k * patches : (k + 1) * patches, :] = own_slab(k).astype(f32) + r.global_own[...]
    after = r.after[...]
    back, gain_rows = rms_back(after, r.ffn_gain[...], sum_in.finish())
    after_grad = r.own_grad[...].astype(f32) + back
    r.after_grad[...] = after_grad
    r.gains[...] = jnp.zeros(r.gains.shape, f32)
    r.gains[2:3, :] = jnp.sum(gain_rows, axis=0, keepdims=True)
    r.branch[...] = after_grad.astype(bf16)
    up_turn = jnp.where(j < mpn // 2, mpn - 1, 1)
    up_line = Exchange(p, lambda t: r.up.at[t], lambda s: r.up_recv.at[s], r.bs1, r.br1)
    for d in range(1, mpn + 1):
        t = (j + d * up_turn) % mpn
        r.up[t] = dot(r.branch[...], r.ao_sorted[t], ((1,), (1,))).astype(bf16)
        if d < mpn:
            up_line.copy(t).start()
    r.up_recv[j] = r.up[j]
    bulk.go(PACE_BACK[0], RELAY_GRADS[1])
    sum_down.spread()
    ready("qkv")

    mask = att_mask(rows, patches)
    pair = 2 * ATT_DIM
    lane = lax.broadcasted_iota(jnp.int32, (1, pair), 1)
    att_line = LineReduce(
        p, lambda t: r.att_part.at[t], lambda s: r.att_recv.at[s], r.bs2, r.br2,
        r.att_held if p.line else None, r.bsz.at[0],
    )
    turn = jnp.where(j < mpn // 2, mpn - 1, 1)

    def one_micro(d, _):
        m = (j + d * turn) % mpn

        @pl.when(d > 0)
        def _():
            up_line.wait(d * turn)

        for c in range(width // pair):
            at = slice(c * pair, (c + 1) * pair)
            query, key, value = r.qkv[0, m, :, at], r.qkv[1, m, :, at], r.qkv[2, m, :, at]
            up = r.up_recv[m, :, at]
            got = [[], [], []]
            for own in (lane < ATT_DIM, lane >= ATT_DIM):
                mine = jnp.where(own, query, jnp.zeros_like(query))
                probs = soft_rows(mask, mine, key)
                my_up = jnp.where(own, up, jnp.zeros_like(up))
                probs_grad = dot(my_up, value, ((1,), (1,)))
                inner = jnp.sum(probs * probs_grad, axis=1, keepdims=True)
                score_grad = (probs * (probs_grad - inner) * ATT_DIM ** (-0.5)).astype(bf16)
                got[0].append(dot(score_grad, key))
                got[1].append(dot(score_grad, mine, ((0,), (0,))))
                got[2].append(dot(probs.astype(bf16), my_up, ((0,), (0,))))
            r.qkv_low[0, m, :, at] = jnp.where(lane < ATT_DIM, got[0][0], got[0][1]).astype(bf16)
            r.qkv_low[1, m, :, at] = (got[1][0] + got[1][1]).astype(bf16)
            r.qkv_low[2, m, :, at] = (got[2][0] + got[2][1]).astype(bf16)
        total = dot(r.qkv_low[0, m], r.qkv_v[0], ((1,), (1,)))
        total = total + dot(r.qkv_low[1, m], r.qkv_v[1], ((1,), (1,)))
        total = total + dot(r.qkv_low[2, m], r.qkv_v[2], ((1,), (1,)))
        r.att_part[m] = total.astype(bf16)

        @pl.when(d > 0)
        def _():
            att_line.send(m)

        return 0

    lax.fori_loop(0, mpn, one_micro, 0)

    everything = r.attn_in[...].reshape(micro * rows, dim)
    for w in range(3):
        r.qkv_part[w] = dot(
            everything, r.qkv_low[w].reshape(micro * rows, width), ((0,), (0,))
        ).astype(bf16)
    sum_qkv.start()
    sum_qkv.spread()
    for t in range(mpn):
        r.ao_part[:, t * width : (t + 1) * width] = dot(
            r.branch[...], r.heads_own[t], ((0,), (0,))
        ).astype(bf16)
    sum_ao.start()
    perm = perm_matrix(rows, patches, slabs, sum(own_lengths(r, j)) - i * patches)
    block = (r.after[...] + sum_down.finish()).astype(bf16)
    block = dot(perm, block, ((0,), (0,))).astype(bf16)
    for t in range(mpn):
        r.block[t] = block[:, t * width : (t + 1) * width]
    total = r.att_part[j].astype(f32)
    att_line.wait_all()
    for s in range(mpn):
        total = total + jnp.where((s == j) | absent(p.line, j, s), 0.0, r.att_recv[s].astype(f32))
    back, gain_rows = rms_back(r.local_in[...], r.attn_gain[...], total)
    local_grad = r.after_grad[...] + back
    global_grad = local_grad[:patches]
    for k in range(1, slabs):
        global_grad = global_grad + local_grad[k * patches : (k + 1) * patches]
    r.global_grad[...] = global_grad
    r.b_low[...] = global_grad.astype(bf16)
    cast = Cast(p, r.b_low, r.mixer, r.bs3, r.br3, r.bsc)
    cast.start()
    sum_ao.spread()
    bulk.go(PACE_BACK[1], RELAY_GRADS[2])
    r.gains[1:2, :] = jnp.sum(gain_rows, axis=0, keepdims=True)
    share_rows = rows // mpn
    for t in range(mpn):
        r.local[t] = local_grad[t * share_rows : (t + 1) * share_rows].astype(bf16)
    local_line = Exchange(p, lambda t: r.local.at[t], lambda s: r.local_all.at[s], r.bs6, r.br6)
    block_line = Exchange(p, lambda t: r.block.at[t], lambda s: r.block_all.at[s], r.bs7, r.br7)
    ready("mixer")
    cast.wait()
    bulk.go(PACE_BACK[2], RELAY_GRADS[3])

    upstream = r.mixer[...].reshape(n * patches, dim)
    proj_grad = mixer_bwd(r, p, own_lengths(r, p.m), upstream)
    part = dot(proj_grad, r.in_v[...])
    for b in range(n):
        r.b_part[b] = part[b * patches : (b + 1) * patches].astype(bf16)
    to_owner = ToOwner(p, r.b_part, r.b_mid, r.b_recv, r.bs4, r.br4, r.bs9, r.br9)
    to_owner.start()
    bulk.go(PACE_BACK[3], RELAY_GRADS[4])

    r.proj_grad[...] = proj_grad
    size = n * patches // p.reps
    proj_own = r.proj_grad.at[pl.ds(pl.multiple_of(p.h * size, size), size)]
    proj_plane = PlaneGather(p, proj_own, lambda s: r.proj_all.at[s], r.bsi, r.bri, r.bsir).start()
    keep_proj = load(proj_own, r.proj_all.at[i])
    out_grad = dot(r.mixer_low[...], upstream, ((0,), (0,))).astype(bf16)
    group_rows = GROUP_WIDTH // n
    for e in range(n):
        r.out_w_part[e] = out_grad[e * group_rows : (e + 1) * group_rows]
    bundles = (
        (lambda t: r.out_w_part.at[t], r.out_w_recv, r.bso, r.bro),
        (lambda t: r.small_part, r.small_recv, r.bss, r.brs),
    )

    def each_bundle(act):
        for q in range(p.share):
            t = q * p.reps + p.h

            @pl.when(t != i)
            def _():
                for src, dst, ss, rs in bundles:
                    act(rcopy(src(t), dst.at[p.m], ss.at[q], rs.at[p.m], t, j))

    to_owner.pass_on()
    bulk.go(PACE_BACK[4], RELAY_GRADS[5])
    each_bundle(lambda copy: copy.start())
    keeps = [load(r.out_w_part.at[i], r.out_w_recv.at[p.m]), load(r.small_part, r.small_recv.at[p.m])]
    back, gain_rows = rms_back(r.global_in[...], r.norm_in_gain[...], to_owner.total())
    r.line[j] = (r.global_grad[...] + back).astype(bf16)
    line = Exchange(p, lambda t: r.line.at[j], lambda s: r.line.at[s], r.bs5, r.br5).start()
    bulk.go(len(bulk.exchanges), RELAY_GRADS[6])
    r.gains[0:1, :] = jnp.sum(gain_rows, axis=0, keepdims=True)
    others = [(p.mine + d) % p.half for d in range(1, p.half)]

    def gains_copy(q):
        return rcopy(r.gains, r.gains_plane.at[p.mine], r.bsh.at[q], r.brh.at[p.mine], q * 2 + p.c, j)

    for q in others:
        gains_copy(q).start()
    r.gains_plane[p.mine] = r.gains[...]
    local_line.start()
    block_line.start()
    keeps += [load(r.local.at[j], r.local_all.at[j]), load(r.block.at[j], r.block_all.at[j])]
    line.wait_all()
    slot = lambda s: r.plane.at[s]
    plane = PlaneGather(p, r.line, slot, r.bsp, r.brp, r.bspr).start()
    keep_line = load(r.line, r.plane.at[i])
    bulk.relay(RELAY_GRADS[7])
    proj_plane.relay()
    r.qkv_total[...] = sum_qkv.finish()
    keeps.append(load(r.qkv_total, r.qkv_sum))
    ao = sum_ao.finish().astype(bf16)
    for t in range(mpn):
        r.ao[t] = ao[:, t * width : (t + 1) * width]
    ao_line = Exchange(p, lambda t: r.ao.at[t], lambda s: r.ao_all.at[s], r.bs8, r.br8).start()
    keeps.append(load(r.ao.at[j], r.ao_all.at[j]))
    bulk.relay(len(bulk.exchanges))
    if pieces_of is not None:
        keeps.append(pieces_of())
    for q in others:
        rcopy(r.gains, r.gains_plane.at[q], r.bsh.at[q], r.brh.at[q], q * 2 + p.c, j).wait_recv()
    r.gains_pair[0] = sum(r.gains_plane[s] for s in range(p.half))
    pair_copy = rcopy(r.gains_pair.at[0], r.gains_pair.at[1], r.bsq.at[0], r.brq.at[0], p.other, j)
    pair_copy.start()
    plane.relay()
    pair_copy.wait()
    r.gains_pair[0] = r.gains_pair[0] + r.gains_pair[1]
    width_i = r.gains_mine.shape[1]
    first = i * feature // width_i * width_i
    r.gains_mine[...] = r.gains_pair[0, :, pl.ds(pl.multiple_of(first, 128), width_i)]
    gains_line = Exchange(p, lambda t: r.gains_mine, lambda s: r.gains_line.at[s], r.bsg, r.brg).start()
    plane.finish()
    local_line.wait_all()
    block_line.wait_all()
    ao_line.wait_all()
    for s in range(mpn):
        @pl.when(s * p.reps + p.h != i)
        def _():
            for src, dst, ss, rs in bundles:
                rcopy(src(0), dst.at[s], ss.at[0], rs.at[s], s * p.reps + p.h, j).wait_recv()
    proj_plane.finish()
    gains_line.wait_all()
    r.gains_line[j] = r.gains_mine[...]
    gains_line.sent()
    r.gains_mine[...] = sum(r.gains_line[s] for s in range(mpn))
    keeps.append(load(r.gains_mine, r.gains_all))
    bulk.wait(0, len(bulk.exchanges))
    keep_line.wait()
    keep_proj.wait()
    for copy in keeps:
        copy.wait()
    for thing in (
        sum_in, sum_down, sum_ao, sum_qkv, bulk, up_line, att_line, cast, to_owner, line, local_line,
        block_line, plane, proj_plane, ao_line,
    ):
        thing.sent()
    for q in others:
        gains_copy(q).wait_send()
    each_bundle(lambda copy: copy.wait_send())


def backward_kernel(n, mpn, spill, r):
    p = place_of(n, mpn, False)
    load = Loads(r.b_load)

    def read(view):
        if not spill:
            return view[...]
        copy = pltpu.make_async_copy(view, r.stage.at[0], r.sem_stage.at[0])
        copy.start()
        copy.wait()
        return r.stage[0]

    def write(view, value):
        if not spill:
            view[...] = value
            return
        r.stage[1] = value
        copy = pltpu.make_async_copy(r.stage.at[1], view, r.sem_stage.at[1])
        copy.start()
        copy.wait()

    per = r.w_grad.shape[1] // mpn
    loads_small = load_small(r, load)
    keep_w = load(r.w_grad.at[:, pl.ds(pl.multiple_of(p.j * per, per), per)], r.g_recv.at[p.j])
    loads = dict(
        bytes=[load(r.byte_input.at[p.j], r.own_bytes)],
        qkv=[load(r.qkv_weight, r.qkv_v)],
        mixer=[load(r.out_weight, r.out_v), load(r.in_weight, r.in_v)],
    )

    def ready(what):
        for copy in loads[what]:
            copy.wait()

    barrier = pltpu.get_barrier_semaphore()
    pl.semaphore_wait(barrier, greet_all(p, barrier))
    for copy in loads_small:
        copy.wait()
    bulk = grad_pieces(p, r, 1, lambda w, at, cols: r.w_grad.at[w, at, cols], *r.w_grad.shape[1:])
    sum_in, sum_down = ffn_sums(p, r, read, write)
    sum_in.start()
    sum_in.spread()
    sum_down.start()
    dim = r.after.shape[1]
    own_slab = lambda k: r.own_bytes[:, k * dim : (k + 1) * dim]
    backward_steps(p, r, load, own_slab, ready, sum_in, sum_down, bulk)
    keep_w.wait()


def backward_results(n, mpn, a):
    micro, patches, cols = a.byte_input.shape
    dim = a.norm_in_gain.shape[1]
    rows = patches * (cols // dim)
    width = a.qkv_weight.shape[2]
    hidden = a.ffn_weight.shape[2]
    feature = dim // n
    return dict(
        g_recv=((mpn, 3, dim // mpn, hidden), bf16, ANY),
        plane=((n, mpn, patches, dim), bf16, ANY),
        qkv_sum=((3, feature, width), f32, ANY),
        ao_all=((mpn, feature, width), bf16, ANY),
        proj_all=((n, n * patches // (n // mpn), a.in_weight.shape[0]), bf16, ANY),
        out_w_recv=((mpn, GROUP_WIDTH // n, dim), bf16, ANY),
        small_recv=((mpn, 16, CONV_CH), f32, ANY),
        gains_all=((8, max(feature, 128)), f32, ANY),
        local_all=((mpn, rows // mpn, dim), bf16, ANY),
        block_all=((mpn, rows, width), bf16, ANY),
    )


def backward_scratch(n, mpn, a):
    micro, patches, cols = a.byte_input.shape
    dim = a.norm_in_gain.shape[1]
    rows = patches * (cols // dim)
    width = a.qkv_weight.shape[2]
    hidden = a.ffn_weight.shape[2]
    half, share = n // 2, mpn
    feature = dim // n
    pieces = max(hidden // FFN_COLS, 1) * 3 * WEIGHT_CUTS
    line, plane = DMA((mpn,)), DMA((half,))
    return dict(
        local_in=pltpu.VMEM((rows, dim), f32),
        after_grad=pltpu.VMEM((rows, dim), f32),
        branch=pltpu.VMEM((rows, dim), bf16),
        up=pltpu.VMEM((mpn, rows, width), bf16),
        up_recv=pltpu.VMEM((mpn, rows, width), bf16),
        qkv_low=pltpu.VMEM((3, micro, rows, width), bf16),
        att_part=pltpu.VMEM((micro, rows, dim), bf16),
        att_recv=pltpu.VMEM((mpn, rows, dim), bf16),
        qkv_part=pltpu.VMEM((3, dim, width), bf16),
        qkv_pre=pltpu.VMEM((half, 3, feature, width), bf16),
        qkv_recv=pltpu.VMEM((half, 3, feature, width), bf16),
        ao_part=pltpu.VMEM((dim, mpn * width), bf16),
        ao_pre=pltpu.VMEM((half, feature, mpn * width), bf16),
        ao_recv=pltpu.VMEM((half, feature, mpn * width), bf16),
        ao=pltpu.VMEM((mpn, feature, width), bf16),
        block=pltpu.VMEM((mpn, rows, width), bf16),
        local=pltpu.VMEM((mpn, rows // mpn, dim), bf16),
        b_low=pltpu.VMEM((patches, dim), bf16),
        global_grad=pltpu.VMEM((patches, dim), f32),
        mixer=pltpu.VMEM((n, patches, dim), bf16),
        b_part=pltpu.VMEM((n, patches, dim), bf16),
        b_mid=pltpu.VMEM((mpn, patches, dim), bf16),
        b_recv=pltpu.VMEM((mpn, patches, dim), bf16),
        line=pltpu.VMEM((mpn, patches, dim), bf16),
        proj_grad=pltpu.VMEM((n * patches, a.in_weight.shape[0]), bf16),
        out_w_part=pltpu.VMEM((n, GROUP_WIDTH // n, dim), bf16),
        small_part=pltpu.VMEM((16, CONV_CH), f32),
        qkv_total=pltpu.VMEM((3, feature, width), f32),
        gains=pltpu.VMEM((8, dim), f32),
        gains_mine=pltpu.VMEM((8, max(feature, 128)), f32),
        gains_line=pltpu.VMEM((mpn, 8, max(feature, 128)), f32),
        gains_plane=pltpu.VMEM((half, 8, dim), f32),
        gains_pair=pltpu.VMEM((2, 8, dim), f32),
        b_load=DMA((64,)),
        bs_in=DMA((4, half)), bs_down=DMA((4, half)), bs_ao=DMA((4, half)), bs_qkv=DMA((4, half)),
        bs1=line, br1=line, bs2=line, br2=line, bs3=DMA((n,)), br3=DMA((n,)), bsc=plane, bs4=line, br4=line, bs9=line, br9=line,
        bs5=line, br5=line, bs6=line, br6=line, bs7=line, br7=line, bs8=line, br8=line,
        bsp=plane, brp=DMA((n,)), bspr=plane,
        bsg=line, brg=line, bsh=plane, brh=plane, bsq=DMA((1,)), brq=DMA((1,)),
        bsz=DMA((1,)), bsi=plane, bri=DMA((n,)), bsir=plane, bso=DMA((share,)), bro=line, bss=DMA((share,)), brs=line,
        bsw=DMA((pieces, mpn)), brw=DMA((pieces, mpn)),
    )


def sum_buffers(n, a, make):
    micro, patches, cols = a.byte_input.shape
    dim = a.norm_in_gain.shape[1]
    shape = (n // 2, patches * (cols // dim), dim)
    return {name: make(shape) for name in ("in_pre", "in_recv", "down_pre", "down_recv")}


def backward(n, mpn, a):
    spill = a.in_part.size * 2 > SPILL_BYTES
    ins = dict(seq_lengths=(a.seq_lengths, SMEM))
    for name in ("byte_input", "w_grad", "in_weight", "out_weight", "qkv_weight"):
        ins[name] = (getattr(a, name), ANY)
    for name in ("in_part", "down_part"):
        ins[name] = (getattr(a, name), ANY if spill else VMEM)
    for name in SMALL_PARAMS:
        ins["given_" + name] = (getattr(a, name), ANY)
    for name in (
        "after", "own_grad", "heads_own", "qkv", "attn_in", "ao_sorted", "global_in", "global_own", "normed",
        "projected", "mixer_y", "mixer_low",
    ):
        ins[name] = (getattr(a, name), VMEM)
    outs = backward_results(n, mpn, a)
    scratch = backward_scratch(n, mpn, a)
    scratch.update(small_scratch(a))
    scratch.update(
        own_bytes=pltpu.VMEM(a.byte_input.shape[1:], bf16),
        in_v=pltpu.VMEM(a.in_weight.shape, bf16),
        out_v=pltpu.VMEM(a.out_weight.shape, bf16),
        qkv_v=pltpu.VMEM(a.qkv_weight.shape, bf16),
    )
    if spill:
        outs.update(sum_buffers(n, a, lambda shape: (shape, bf16, ANY)))
        scratch.update(stage=pltpu.VMEM((2,) + a.in_part.shape[1:], bf16), sem_stage=DMA((2,)))
    else:
        scratch.update(sum_buffers(n, a, lambda shape: pltpu.VMEM(shape, bf16)))
    return launch(
        "backward", partial(backward_kernel, n, mpn, spill), ins, outs, scratch, remote_params(1, 63)
    )


def ffn_steps(p, r, st, load, sum_in, sum_down, bulk, grad_of):
    n, half = p.n, p.half
    rows, dim = r.own_grad.shape
    hidden = r.w_v.shape[2]
    cols = hidden // st.halves
    per = dim // p.mpn
    pair = 2 * rows
    st.grads.finish()
    grads_all = lambda: r.grad_rows[...].reshape(n * rows, dim)
    rows_all = lambda: r.ffn_rows[...].reshape(n * rows, dim)
    kept = []
    if st.halves == 1:
        st.rows.relay()
        st.rows.finish()
    count = len(st.bulk.exchanges) // st.halves
    for hh in range(st.halves):
        at = slice(hh * cols, (hh + 1) * cols)
        last = hh == st.halves - 1
        if last:
            st.bulk.go(len(st.bulk.exchanges))
        st.bulk.wait(hh * count, (hh + 1) * count)
        if hh == 0:
            for copy in st.kept:
                copy.wait()

        def compute(q):
            here = r.ffn_rows[pl.ds(2 * q, 2)].reshape(pair, dim)
            up = r.grad_rows[pl.ds(2 * q, 2)].reshape(pair, dim)
            gate = dot(here, r.w_v[0, :, at])
            other = dot(here, r.w_v[1, :, at])
            act, slope = silu_pair(gate)
            hidden_low = (act * other).astype(bf16)
            here_at = pl.ds(pl.multiple_of(q * pair, pair), pair)
            r.hidden_low[hh, here_at, :] = hidden_low
            down = dot(hidden_low, r.w_v[2, :, at], ((1,), (1,)))
            hidden_grad = dot(up, r.w_v[2, :, at])
            gate_grad = (hidden_grad * other * slope).astype(bf16)
            up_grad = (hidden_grad * act).astype(bf16)
            r.gate_low[hh, here_at, :] = gate_grad
            r.up_low[hh, here_at, :] = up_grad
            back = dot(gate_grad, r.w_v[0, :, at], ((1,), (1,))) + dot(up_grad, r.w_v[1, :, at], ((1,), (1,)))
            if hh > 0:
                back = back + r.in_part[pl.ds(2 * q, 2)].reshape(pair, dim).astype(f32)
                down = down + r.down_part[pl.ds(2 * q, 2)].reshape(pair, dim).astype(f32)
            r.in_part[pl.ds(2 * q, 2)] = back.astype(bf16).reshape(2, rows, dim)
            r.down_part[pl.ds(2 * q, 2)] = down.astype(bf16).reshape(2, rows, dim)

        def first_pass(d, _):
            q = (p.mine + half - d) % half
            for turn, upto in RELAY_WEIGHTS:
                @pl.when(d == turn)
                def _():
                    st.bulk.relay(upto)

            @pl.when(d > 0)
            def _():
                st.rows.relay_one(q)

            st.rows.wait_across(q)
            compute(q)
            return 0

        def last_pass(d, _):
            q = (p.mine + d) % half
            compute(q)
            sum_in.first(q).start()

            @pl.when(d > 1)
            def _():
                sum_in.spread_one((p.mine + d - 1) % half)

            return 0

        if last:
            lax.fori_loop(1, half + 1, last_pass, 0)
            sum_down.start()
        else:
            lax.fori_loop(0, half, first_pass, 0)
        everything = slice(0, dim)
        grad_of(0, everything, at)[...] = dot(rows_all(), r.gate_low[hh], ((0,), (0,))).astype(bf16)
        grad_of(1, everything, at)[...] = dot(rows_all(), r.up_low[hh], ((0,), (0,))).astype(bf16)
        grad_of(2, everything, at)[...] = dot(grads_all(), r.hidden_low[hh], ((0,), (0,))).astype(bf16)
        mine = pl.ds(pl.multiple_of(p.j * per, per), per)
        kept += [load(grad_of(w, mine, at), r.g_recv.at[p.j, w, :, at]) for w in range(3)]
        if last:
            bulk.relay(RELAY_GRADS[0])
        else:
            bulk.go(PACE_FFN)
    return kept


def layer_kernel(n, mpn, r):
    p = place_of(n, mpn, mpn == 4)
    dim = r.after.shape[1]

    def put_rows(ref):
        def put(s, value):
            ref[s] = value

        return put

    r.grad_rows_own = put_rows(r.grad_rows)
    r.ffn_rows_own = put_rows(r.ffn_rows)
    per = r.ffn_weight.shape[1]

    def land(s, w, rows, cols):
        first = (0 if rows.start is None else rows.start) + s * per
        size = per if rows.start is None else rows.stop - rows.start
        return r.w_v.at[w, pl.ds(pl.multiple_of(first, size), size), cols]

    load = Loads(r.sem_load)
    st = forward_steps(p, r, load, land)
    hidden = r.w_v.shape[2]

    def grad_of(w, at, cols):
        first = w % 2 * hidden
        return r.pw.at[w // 2, at, first + cols.start : first + cols.stop]

    bulk = grad_pieces(p, r, st.halves, grad_of, dim, hidden)
    sum_in, sum_down = ffn_sums(p, r, plain_get, plain_put)
    load = Loads(r.b_load)
    kept = ffn_steps(p, r, st, load, sum_in, sum_down, bulk, grad_of)
    own_slab = lambda k: r.bytes_v[p.j, :, k * dim : (k + 1) * dim]
    st.rows.sent()
    st.grads.sent()
    rows = r.own_grad.shape[0]
    positions = r.patch_weight.shape[0]
    places = (r.ffn_rows, r.grad_rows)
    again = [
        load(r.patch_weight.at[k, s * rows : (s + 1) * rows], places[k].at[s])
        for k in range(positions) for s in range(dim // rows)
    ]

    def pieces_of():
        for copy in again:
            copy.wait()
        own = r.line[...].reshape(-1, dim)
        for k in range(positions):
            r.piece_v[:, k * dim : (k + 1) * dim] = dot(
                own, places[k][: dim // rows].reshape(dim, dim), ((1,), (1,))
            )
        return load(r.piece_v, r.piece)

    backward_steps(p, r, load, own_slab, lambda what: None, sum_in, sum_down, bulk, pieces_of)
    st.settle()
    for copy in kept:
        copy.wait()


def layer(n, mpn, a):
    dim = a.norm_in_gain.shape[1]
    hidden = a.ffn_weight.shape[2]
    halves = max(hidden // FFN_COLS, 1)
    large, small = forward_results(n, mpn, a)
    rows = small["own_grad"][0][0]
    outs = {name: large.pop(name) + (ANY,) for name in ("bytes_part", "normed_cols")}
    outs.update(backward_results(n, mpn, a))
    patches, cols = a.byte_input.shape[1:]
    piece = ((mpn * patches, a.patch_weight.shape[0] * dim), f32)
    outs.update(piece=piece + (ANY,))
    large.pop("w_all")
    scratch = forward_scratch(n, mpn, a)
    scratch.update(backward_scratch(n, mpn, a))
    scratch.update(piece_v=pltpu.VMEM(*piece))
    for name, (shape, dtype) in (*large.items(), *small.items()):
        scratch[name] = pltpu.VMEM(shape, dtype)
    scratch.update(sum_buffers(n, a, lambda shape: pltpu.VMEM(shape, bf16)))
    scratch.update(
        g_held=pltpu.VMEM((halves * 3 * WEIGHT_CUTS, dim // mpn // WEIGHT_CUTS, hidden // halves), bf16),
        att_held=pltpu.VMEM((rows, dim), bf16),
        bsr=DMA((halves * 3 * WEIGHT_CUTS,)),
        w_v=pltpu.VMEM((3, dim, hidden), bf16),
        in_part=pltpu.VMEM((n, rows, dim), bf16),
        down_part=pltpu.VMEM((n, rows, dim), bf16),
        gate_low=pltpu.VMEM((halves, n * rows, hidden // halves), bf16),
        up_low=pltpu.VMEM((halves, n * rows, hidden // halves), bf16),
        hidden_low=pltpu.VMEM((halves, n * rows, hidden // halves), bf16),
    )
    return launch(
        "layer", partial(layer_kernel, n, mpn), forward_ins(a), outs, scratch, remote_params(2, 63)
    )


def finish_kernel(line, r):
    i, j = lax.axis_index("dp"), lax.axis_index("mp")
    mpn, patches, dim = r.plane.shape[1:]
    n = r.plane.shape[0]
    features = r.bytes_part.shape[-1]
    positions = r.bytes_part.shape[1]
    feature = dim // n
    columns = r.in_grad.shape[0]
    load = Loads(r.sems)
    writes = []
    into = lambda name: load(getattr(r, name), getattr(r, name + "_v"))
    load_g = [load(r.g_recv.at[:, w], r.g_recv_v.at[w]) for w in range(3)]
    load_patch = [into("plane"), into("bytes_part")]
    load_in = [into("proj_all"), into("normed_cols")]
    load_rest = [into(name) for name in ("out_w_recv", "ao_all", "small_recv", "gains_all")]
    load_copied = [into("qkv_sum"), into("block_all")]
    given = hasattr(r, "piece")
    load_input = [into("local_all"), into("piece" if given else "patch_weight")]

    def wait(copies):
        for copy in copies:
            copy.wait()

    def out(name, value, at=None):
        src, dst = getattr(r, name + "_v"), getattr(r, name)
        if at is not None:
            src, dst = src.at[at], dst.at[at]
        src[...] = value
        writes.append(load(src, dst))

    cut = features // feature
    for w in range(3):
        load_g[w].wait()
        out("ffn_grad", sum(
            jnp.where(absent(line, j, s), 0.0, r.g_recv_v[w, s].astype(f32)) for s in range(mpn)
        ), w)
    wait(load_patch)
    everyone = r.plane_v[...].reshape(n * mpn * patches, dim)
    for k in range(positions):
        mine = r.bytes_part_v[:, k].reshape(n * mpn * patches, features)
        got = dot(mine, everyone, ((0,), (0,)))
        if cut > 1:
            got = sum(jnp.where(i % cut == e, got[e * feature : (e + 1) * feature], 0.0) for e in range(cut))
        out("patch_grad", got, k)
    wait(load_in)
    got = dot(
        r.proj_all_v[...].reshape(n * mpn * patches, columns),
        r.normed_cols_v[...].reshape(n * mpn * patches, features), ((0,), (0,)),
    )
    if cut > 1:
        got = sum(jnp.where(i % cut == e, got[:, e * feature : (e + 1) * feature], 0.0) for e in range(cut))
    out("in_grad", got)
    wait(load_copied)
    writes += [load(r.qkv_sum_v, r.qkv_grad), load(r.block_all_v, r.block_out)]
    wait(load_rest)
    out("out_grad", sum(r.out_w_recv_v[s].astype(f32) for s in range(mpn)))
    out("ao_grad", sum(r.ao_all_v[s].astype(f32) for s in range(mpn)).T)
    small = sum(r.small_recv_v[s] for s in range(mpn))

    def chosen(values, size):
        whole = values.shape[1]
        at = lax.broadcasted_iota(jnp.int32, (whole, size), 0)
        want = lax.broadcasted_iota(jnp.int32, (whole, size), 1) + i * size % whole
        return dot(values, (at == want).astype(f32), precision=highest)

    conv = chosen(small, CONV_CH // n)
    out("conv_w_grad", conv[:CONV])
    out("conv_b_grad", conv[CONV : CONV + 1])
    out("group_grad", chosen(small[:, :GROUP_WIDTH], GROUP_WIDTH // n)[CONV + 1 : CONV + 2])
    heads = lax.broadcasted_iota(jnp.int32, (GROUP_WIDTH, GROUP_HEADS), 0) // HEAD_DIM
    pick = heads == lax.broadcasted_iota(jnp.int32, (GROUP_WIDTH, GROUP_HEADS), 1)
    out("skip_grad", dot(small[:, :GROUP_WIDTH], pick.astype(f32), precision=highest)[CONV + 2 : CONV + 3])
    out("step_grad", small[CONV + 3 : CONV + 4, :GROUP_HEADS])
    out("decay_grad", small[CONV + 4 : CONV + 5, :GROUP_HEADS])
    gains = chosen(r.gains_all_v[...], feature)
    out("norm_in_grad", gains[0:1])
    out("attn_gain_grad", gains[1:2])
    out("ffn_gain_grad", gains[2:3])
    wait(load_input)
    own = r.plane_v[i].reshape(mpn * patches, dim)
    for k in range(positions):
        if given:
            piece = r.piece_v[:, k * dim : (k + 1) * dim]
        else:
            piece = dot(own, r.patch_weight_v[k], ((1,), (1,)))
        for m in range(mpn):
            r.input_grad_v[m, :, k * dim : (k + 1) * dim] = (
                piece[m * patches : (m + 1) * patches]
                + r.local_all_v[m, k * patches : (k + 1) * patches, :].astype(f32)
            )
    writes.append(load(r.input_grad_v, r.input_grad))
    wait(writes)


def finish(a, line):
    n, mpn, patches, dim = a.plane.shape
    positions = a.patch_weight.shape[0]
    feature = dim // n
    columns = a.in_weight.shape[0]
    names = (
        "plane", "bytes_part", "piece" if hasattr(a, "piece") else "patch_weight", "local_all", "g_recv", "ao_all", "proj_all", "normed_cols", "out_w_recv",
        "small_recv", "gains_all", "qkv_sum", "block_all",
    )
    large = dict(
        patch_grad=((positions, feature, dim), f32),
        input_grad=((mpn, patches, positions * dim), f32),
        ffn_grad=(a.g_recv.shape[1:], f32),
        ao_grad=(a.ao_all.shape[:0:-1], f32),
        in_grad=((columns, feature), f32),
        out_grad=(a.out_w_recv.shape[1:], f32),
    )
    row = lambda size: ((1, size), f32)
    large.update(
        conv_w_grad=((CONV, CONV_CH // n), f32),
        conv_b_grad=row(CONV_CH // n),
        group_grad=row(GROUP_WIDTH // n),
        skip_grad=row(GROUP_HEADS),
        step_grad=row(GROUP_HEADS),
        decay_grad=row(GROUP_HEADS),
        norm_in_grad=row(feature),
        attn_gain_grad=row(feature),
        ffn_gain_grad=row(feature),
    )
    outs = {name: value + (ANY,) for name, value in large.items()}
    outs.update(qkv_grad=(a.qkv_sum.shape, f32, ANY), block_out=(a.block_all.shape, bf16, ANY))
    scratch = {name + "_v": pltpu.VMEM(getattr(a, name).shape, getattr(a, name).dtype) for name in names}
    scratch["g_recv_v"] = pltpu.VMEM((3, mpn) + a.g_recv.shape[2:], bf16)
    scratch.update({name + "_v": pltpu.VMEM(*value) for name, value in large.items()})
    scratch["sems"] = DMA((48,))
    ins = {name: (getattr(a, name), ANY) for name in names}
    return launch("finish", partial(finish_kernel, line), ins, outs, scratch, plain_params(60))


def body(
    byte_input,
    seq_lengths,
    patch_weight,
    norm_in_gain,
    in_weight,
    conv_weight,
    conv_bias,
    step_bias,
    log_decay,
    skip_gain,
    group_gain,
    out_weight,
    attn_gain,
    qkv_weight,
    attn_out_weight,
    ffn_gain,
    ffn_weight,
    out_grad,
):
    n, mpn = lax.axis_size("dp"), lax.axis_size("mp")
    row = lambda v: v.reshape(1, -1)
    a = SimpleNamespace(
        byte_input=byte_input,
        seq_lengths=seq_lengths,
        patch_weight=patch_weight,
        norm_in_gain=row(norm_in_gain),
        in_weight=in_weight[0].T,
        taps=conv_weight[0].T,
        conv_bias=conv_bias,
        step_bias=step_bias,
        log_decay=log_decay,
        skip=skip_gain,
        group_gain=group_gain,
        out_weight=out_weight[0],
        attn_gain=row(attn_gain),
        qkv_weight=qkv_weight,
        attn_out_weight=attn_out_weight,
        ffn_gain=row(ffn_gain),
        ffn_weight=ffn_weight,
        out_grad=out_grad,
    )
    dim, hidden = ffn_gain.shape[0], ffn_weight.shape[2]
    rows = out_grad.shape[1]
    fits = n * rows * dim * 2 <= SPILL_BYTES and 2 * hidden <= dim
    fits = fits and dim % rows == 0 and dim // rows <= n and patch_weight.shape[0] <= 2
    if fits:
        a.__dict__.update(layer(n, mpn, a).__dict__)
    else:
        a.__dict__.update(forward(n, mpn, a).__dict__)
        a.down_part, a.in_part, a.w_grad = ffn(a.ffn_rows, a.grad_rows, a.w_all)
        a.__dict__.update(backward(n, mpn, a).__dict__)
    f = finish(a, fits and mpn == 4)
    return (
        f.block_out,
        f.input_grad,
        f.patch_grad,
        f.norm_in_grad[0],
        f.in_grad.T[None],
        f.conv_w_grad.T[None],
        f.conv_b_grad,
        f.step_grad,
        f.decay_grad,
        f.skip_grad,
        f.group_grad,
        f.out_grad[None],
        f.attn_gain_grad[0],
        f.qkv_grad,
        f.ao_grad,
        f.ffn_gain_grad[0],
        f.ffn_grad,
    )


def solution(mesh):
    in_specs = (
        P(None, "dp", None),
        P(),
        P("mp", None, None),
        P(),
        P("mp", None, None),
        P("mp", None, None),
        P("mp", None),
        P("mp", None),
        P("mp", None),
        P("mp", None),
        P("mp", None),
        P("mp", None, None),
        P(),
        P(None, None, "mp"),
        P("mp", None),
        P(),
        P(None, "mp", "dp"),
        P(None, "dp", None),
    )
    out_specs = (
        P(None, "dp", "mp"),
        P(None, "dp", "mp"),
        P("mp", "dp", None),
        P("dp"),
        P("mp", "dp", None),
        P("mp", "dp", None),
        P("mp", "dp"),
        P("mp", None),
        P("mp", None),
        P("mp", None),
        P("mp", "dp"),
        P("mp", "dp", None),
        P("dp"),
        P(None, "dp", "mp"),
        P("mp", "dp"),
        P("dp"),
        P(None, "mp", "dp"),
    )
    return jax.shard_map(body, mesh=mesh, in_specs=in_specs, out_specs=out_specs, check_vma=False)
```

```python
from functools import partial
from types import SimpleNamespace

import jax
import jax.numpy as jnp
from jax import lax
from jax.experimental import pallas as pl
from jax.experimental.pallas import tpu as pltpu
from jax.sharding import PartitionSpec as P

STATE = 128
CONV = 4
SEQS = 3
GROUP_WIDTH = 512
GROUP_HEADS = 8
HEAD_DIM = 64
ATT_DIM = 64
CONV_CH = 768

norm_eps = 1e-06
highest = lax.Precision.HIGHEST
large_negative = -1e30
f32 = jnp.float32
bf16 = jnp.bfloat16
MESH = pl.DeviceIdType.MESH
VMEM = pl.BlockSpec(memory_space=pltpu.VMEM)
ANY = pl.BlockSpec(memory_space=pl.ANY)
SMEM = pl.BlockSpec(memory_space=pltpu.SMEM)
DMA = pltpu.SemaphoreType.DMA
SMALL_PARAMS = (
    "norm_in_gain", "taps", "conv_bias", "step_bias", "log_decay", "skip", "group_gain", "attn_gain", "ffn_gain"
)
SPILL_BYTES = 4 * 2**20
FFN_COLS = 256
WEIGHT_CUTS = 2
PACE = (1, 1, 1, 1, 1, 2, 6, 0)
PACE_FFN = 6
RELAY_WEIGHTS = ((2, 8), (3, 10))
RELAY_GRADS = (4, 6, 6, 7, 9, 10, 11, 12)
PACE_BACK = (0, 6, 0, 0, 0)


def dot(a, b, dims=((1,), (0,)), precision=None):
    return lax.dot_general(
        a, b, (dims, ((), ())), preferred_element_type=f32, precision=precision
    )


def inv_rms(values):
    return lax.rsqrt(jnp.mean(values * values, axis=-1, keepdims=True) + norm_eps)


def rms_back(values, gain, upstream):
    scale = inv_rms(values)
    weighted = upstream * gain
    inner = jnp.mean(weighted * values, axis=-1, keepdims=True)
    back = scale * weighted - values * (inner * scale * scale * scale)
    return back, upstream * (values * scale)


def silu_pair(values):
    sig = jax.nn.sigmoid(values)
    return values * sig, sig * (1.0 + values * (1.0 - sig))


def rcopy(src, dst, send_sem, recv_sem, dp, mp):
    return pltpu.make_async_remote_copy(
        src_ref=src,
        dst_ref=dst,
        send_sem=send_sem,
        recv_sem=recv_sem,
        device_id={"dp": dp, "mp": mp},
        device_id_type=MESH,
    )


def greet(barrier, dp, mp):
    pl.semaphore_signal(barrier, inc=1, device_id={"dp": dp, "mp": mp}, device_id_type=MESH)


def plain_params(mib=56):
    return pltpu.CompilerParams(vmem_limit_bytes=mib * 2**20)


def remote_params(cid, mib=40):
    return pltpu.CompilerParams(
        collective_id=cid, has_side_effects=True, vmem_limit_bytes=mib * 2**20
    )


def launch(name, kernel, ins, outs, scratch, params):
    names = [*ins, *outs, *scratch]

    def run(*refs):
        kernel(SimpleNamespace(**dict(zip(names, refs))))

    results = pl.pallas_call(
        run,
        out_shape=tuple(jax.ShapeDtypeStruct(shape, dtype) for shape, dtype, _ in outs.values()),
        in_specs=[spec for _, spec in ins.values()],
        out_specs=tuple(spec for _, _, spec in outs.values()),
        scratch_shapes=list(scratch.values()),
        compiler_params=params,
        name=name,
    )(*[array for array, _ in ins.values()])
    return SimpleNamespace(**dict(zip(outs, results)))


def place_of(n, mpn, line):
    i, j = lax.axis_index("dp"), lax.axis_index("mp")
    reps = n // mpn
    return SimpleNamespace(
        n=n, mpn=mpn, i=i, j=j, reps=reps, share=n // reps, half=n // 2,
        m=i // reps, h=i % reps, c=i % 2, mine=i // 2, other=i + 1 - 2 * (i % 2), inside=i // reps == j, line=line,
    )


def greet_all(p, barrier):
    for d in range(1, p.mpn):
        greet(barrier, p.i, (p.j + d) % p.mpn)
    for d in range(1, p.n):
        greet(barrier, (p.i + d) % p.n, p.j)
    for q in range(p.half):
        s = q * 2 + p.c

        @pl.when(jnp.logical_not((s == p.i) & p.inside))
        def _():
            greet(barrier, s, p.m)

    for h in range(0, p.reps, 2):
        for t in range(p.mpn):
            @pl.when(jnp.logical_not((p.j * p.reps + h + p.c == p.i) & (t == p.j)))
            def _():
                greet(barrier, p.j * p.reps + h + p.c, t)
    return p.mpn + p.n - 2 + p.half + p.reps // 2 * p.mpn - 2 * p.inside.astype(jnp.int32)


class Exchange:
    def __init__(self, p, src, dst, ss, rs):
        self.p, self.src, self.dst, self.ss, self.rs = p, src, dst, ss, rs

    def copy(self, t):
        p = self.p
        return rcopy(self.src(t), self.dst(p.j), self.ss.at[t], self.rs.at[p.j], p.i, t)

    def start(self):
        for d in range(1, self.p.mpn):
            self.copy((self.p.j + d) % self.p.mpn).start()
        return self

    def wait(self, d):
        s = (self.p.j + d) % self.p.mpn
        rcopy(self.dst(s), self.dst(s), self.ss.at[s], self.rs.at[s], self.p.i, s).wait_recv()
        return s

    def wait_all(self):
        for d in range(1, self.p.mpn):
            self.wait(d)

    def sent(self):
        for d in range(1, self.p.mpn):
            self.copy((self.p.j + d) % self.p.mpn).wait_send()


class LineGather(Exchange):
    def begin(self):
        for d in range(1, self.p.mpn):
            def send():
                self.copy((self.p.j + d) % self.p.mpn).start()

            self.unless_far(d, send)

    def unless_far(self, d, act):
        if d == 2 or not self.p.line:
            act()
        else:
            pl.when(self.p.j != (3 if d == 1 else 0))(act)

    def onward(self, at):
        s, t = (0, 3) if at == 2 else (3, 0)
        return rcopy(self.dst(s), self.dst(s), self.ss.at[at], self.rs.at[s], self.p.i, t)

    def relay(self):
        if not self.p.line:
            return
        for at in (1, 2):
            @pl.when(self.p.j == at)
            def _():
                self.wait(2)
                self.onward(at).start()

    def wait_all(self):
        for d in range(1, self.p.mpn):
            if d == 2 and self.p.line:
                @pl.when((self.p.j == 0) | (self.p.j == 3))
                def _():
                    self.wait(2)
            else:
                self.wait(d)

    def sent(self):
        for d in range(1, self.p.mpn):
            def done():
                self.copy((self.p.j + d) % self.p.mpn).wait_send()

            self.unless_far(d, done)
        if self.p.line:
            for at in (1, 2):
                @pl.when(self.p.j == at)
                def _():
                    self.onward(at).wait_send()


class LineReduce(Exchange):
    def __init__(self, p, src, dst, ss, rs, held, hs):
        super().__init__(p, src, dst, ss, rs)
        self.held, self.hs = held, hs

    def begin(self):
        p = self.p
        for d in range(1, p.mpn):
            t = (p.j + d) % p.mpn
            if not p.line:
                self.copy(t).start()
            elif d == 2:
                @pl.when((p.j == 0) | (p.j == 3))
                def _():
                    self.copy(t).start()
            else:
                end = 3 if d == 1 else 0

                @pl.when(p.j != end)
                def _():
                    self.copy(t).start()

                @pl.when(p.j == end)
                def _():
                    rcopy(self.src(t), self.held, self.ss.at[t], self.hs, p.i, 2 if end == 3 else 1).start()

    def send(self, t):
        p = self.p
        if not p.line:
            self.copy(t).start()
            return
        apart = jnp.abs(t - p.j)
        taking = (apart == 2) & ((p.j == 1) | (p.j == 2))

        @pl.when(apart == 3)
        def _():
            rcopy(self.src(t), self.held, self.ss.at[t], self.hs, p.i, jnp.where(p.j == 0, 1, 2)).start()

        @pl.when((apart < 3) & jnp.logical_not(taking))
        def _():
            self.copy(t).start()

        pl.when(taking)(self.relay)

    def relay(self):
        p = self.p
        if not p.line:
            return

        @pl.when((p.j == 1) | (p.j == 2))
        def _():
            t = (p.j + 2) % p.mpn
            rcopy(self.held, self.held, self.ss.at[t], self.hs, p.i, t).wait_recv()
            self.held[...] = (self.held[...].astype(f32) + self.src(t)[...].astype(f32)).astype(bf16)
            rcopy(self.held, self.dst(p.j), self.ss.at[t], self.rs.at[p.j], p.i, t).start()

    def wait_all(self):
        for d in range(1, self.p.mpn):
            if d == 2 or not self.p.line:
                self.wait(d)
            else:
                @pl.when(self.p.j != (3 if d == 1 else 0))
                def _():
                    self.wait(d)


def absent(line, j, s):
    return line & (((j == 3) & (s == 0)) | ((j == 0) & (s == 3)))


class Bulk:
    def __init__(self, exchanges):
        self.exchanges, self.begun, self.before, self.relayed = exchanges, 0, 0, 0

    def relay(self, last):
        last = min(last, self.begun)
        for exchange in self.exchanges[self.relayed : last]:
            exchange.relay()
        self.relayed = max(last, self.relayed)

    def go(self, count, relay=None):
        count = min(count, len(self.exchanges) - self.begun)
        self.relay(self.before if relay is None else relay)
        self.before = self.begun
        for exchange in self.exchanges[self.begun : self.begun + count]:
            exchange.begin()
        self.begun += count

    def wait(self, first, last):
        self.relay(last)
        for exchange in self.exchanges[first:last]:
            exchange.wait_all()

    def sent(self):
        for exchange in self.exchanges:
            exchange.sent()


class PlaneGather:
    def __init__(self, p, own, slot, ss, rs, ssr):
        self.p, self.own, self.slot, self.ss, self.rs, self.ssr = p, own, slot, ss, rs, ssr

    def direct(self, q):
        p = self.p
        return rcopy(self.own, self.slot(p.i), self.ss.at[q], self.rs.at[p.i], q * 2 + p.c, p.j)

    def across(self, q):
        p = self.p
        s = q * 2 + p.c
        return rcopy(self.slot(s), self.slot(s), self.ssr.at[q], self.rs.at[s], p.other, p.j)

    def own_across(self):
        p = self.p
        return rcopy(self.own, self.slot(p.i), self.ssr.at[p.mine], self.rs.at[p.i], p.other, p.j)

    def others(self):
        return [(self.p.mine + d) % self.p.half for d in range(1, self.p.half)]

    def start(self):
        self.own_across().start()
        for q in self.others():
            self.direct(q).start()
        return self

    def relay_one(self, q):
        s = q * 2 + self.p.c
        rcopy(self.slot(s), self.slot(s), self.ss.at[q], self.rs.at[s], s, self.p.j).wait_recv()
        self.across(q).start()

    def wait_across(self, q):
        s = q * 2 + 1 - self.p.c
        rcopy(self.slot(s), self.slot(s), self.ssr.at[q], self.rs.at[s], self.p.other, self.p.j).wait_recv()

    def relay(self):
        for q in reversed(self.others()):
            self.relay_one(q)

    def finish(self):
        for q in range(self.p.half):
            self.wait_across(q)

    def sent(self):
        self.own_across().wait_send()
        for q in self.others():
            self.direct(q).wait_send()
            self.across(q).wait_send()


class Reduction:
    def __init__(self, p, block, value, pre, recv, ss, get, put):
        self.p, self.block, self.value, self.pre, self.recv, self.get, self.put = p, block, value, pre, recv, get, put
        self.ssa, self.rsa, self.ssb, self.rsb = (ss.at[k] for k in range(4))

    def first(self, q):
        p = self.p
        return rcopy(self.block(q * 2 + 1 - p.c), self.pre.at[q], self.ssa.at[q], self.rsa.at[q], p.other, p.j)

    def second(self, q):
        p = self.p
        return rcopy(self.pre.at[q], self.recv.at[p.mine], self.ssb.at[q], self.rsb.at[p.mine], q * 2 + p.c, p.j)

    def others(self):
        return [(self.p.mine + d) % self.p.half for d in range(1, self.p.half)]

    def start(self):
        for q in self.others() + [self.p.mine]:
            self.first(q).start()

    def spread_one(self, q):
        p = self.p
        rcopy(self.pre.at[q], self.pre.at[q], self.ssa.at[q], self.rsa.at[q], p.other, p.j).wait_recv()
        total = self.value(q * 2 + p.c).astype(f32)
        self.put(self.pre.at[q], (total + self.get(self.pre.at[q]).astype(f32)).astype(bf16))
        self.second(q).start()

    def spread(self):
        for q in self.others():
            self.spread_one(q)

    def finish(self):
        p, mine = self.p, self.p.mine
        rcopy(self.pre.at[mine], self.pre.at[mine], self.ssa.at[mine], self.rsa.at[mine], p.other, p.j).wait_recv()
        total = self.value(p.i).astype(f32)
        total = total + self.get(self.pre.at[mine]).astype(f32)
        for q in self.others():
            rcopy(self.recv.at[q], self.recv.at[q], self.ssb.at[q], self.rsb.at[q], q * 2 + p.c, p.j).wait_recv()
            total = total + self.get(self.recv.at[q]).astype(f32)
        return total

    def sent(self):
        for q in self.others() + [self.p.mine]:
            self.first(q).wait_send()
        for q in self.others():
            self.second(q).wait_send()


def plain_get(view):
    return view[...]


def plain_put(view, value):
    view[...] = value


class Cast:
    def __init__(self, p, low, dst, ss, rs, ssr):
        self.p, self.low, self.dst, self.ss, self.rs, self.ssr = p, low, dst, ss, rs, ssr

    def each(self, act):
        p = self.p
        for h in range(0, p.reps, 2):
            for t in range(p.mpn):
                to = p.j * p.reps + h + p.c

                @pl.when(jnp.logical_not((to == p.i) & (t == p.j)))
                def _():
                    act(rcopy(self.low, self.dst.at[p.i], self.ss.at[h // 2 * p.mpn + t], self.rs.at[p.i], to, t))

    def across(self, q):
        p = self.p
        s = q * 2 + p.c
        return rcopy(self.dst.at[s], self.dst.at[s], self.ssr.at[q], self.rs.at[s], p.other, p.j)

    def start(self):
        self.each(lambda copy: copy.start())

        @pl.when(self.p.inside)
        def _():
            self.dst[self.p.i] = self.low[...]

    def wait(self):
        p = self.p
        for q in range(p.half):
            s = q * 2 + p.c

            @pl.when(jnp.logical_not((s == p.i) & p.inside))
            def _():
                rcopy(self.low, self.dst.at[s], self.ss.at[0], self.rs.at[s], s, p.m).wait_recv()

            self.across(q).start()
        for q in range(p.half):
            s = q * 2 + 1 - p.c
            rcopy(self.dst.at[s], self.dst.at[s], self.ssr.at[q], self.rs.at[s], p.other, p.j).wait_recv()

    def sent(self):
        self.each(lambda copy: copy.wait_send())
        for q in range(self.p.half):
            self.across(q).wait_send()


class ToOwner:
    def __init__(self, p, part, mid, recv, ss, rs, ss_line, rs_line):
        self.p, self.part, self.mid, self.recv, self.ss, self.rs = p, part, mid, recv, ss, rs
        self.line = Exchange(p, lambda t: mid.at[t], lambda s: recv.at[s], ss_line, rs_line)

    def each(self, act):
        p = self.p
        for q in range(p.share):
            block = q * p.reps + p.h

            @pl.when(block != p.i)
            def _():
                act(rcopy(self.part.at[block], self.mid.at[p.m], self.ss.at[q], self.rs.at[p.m], block, p.j))

    def start(self):
        self.each(lambda copy: copy.start())
        self.mid[self.p.m] = self.part[self.p.i]

    def pass_on(self):
        p = self.p
        for s in range(p.mpn):
            @pl.when(s != p.m)
            def _():
                rcopy(
                    self.part.at[0], self.mid.at[s], self.ss.at[0], self.rs.at[s], s * p.reps + p.h, p.j
                ).wait_recv()
        self.line.start()
        self.recv[p.j] = self.mid[p.j]

    def total(self):
        self.line.wait_all()
        return sum(self.recv[s].astype(f32) for s in range(self.p.mpn))

    def sent(self):
        self.each(lambda copy: copy.wait_send())
        self.line.sent()


def perm_matrix(rows, patches, per, limit):
    at = lax.broadcasted_iota(jnp.int32, (rows, rows), 0)
    source = lax.broadcasted_iota(jnp.int32, (rows, rows), 1)
    return ((source == (at % patches) * per + at // patches) & (at % patches < limit)).astype(bf16)


class Loads:
    def __init__(self, sems):
        self.sems, self.count = sems, 0

    def __call__(self, src, dst):
        copy = pltpu.make_async_copy(src, dst, self.sems.at[self.count])
        self.count += 1
        copy.start()
        return copy


def own_lengths(r, m):
    return r.seq_lengths[m, 0], r.seq_lengths[m, 1], r.seq_lengths[m, 2]


def seg_starts(lengths, places):
    end0 = lengths[0]
    end1 = end0 + lengths[1]
    end2 = end1 + lengths[2]
    return jnp.where(
        places >= end2, end2, jnp.where(places >= end1, end1, jnp.where(places >= end0, end0, 0))
    )


def conv_taps(conv_in, pos, lag):
    moved = conv_in if lag == 0 else pltpu.roll(conv_in, lag, 0)
    return jnp.where(pos >= lag, moved, 0.0)


def mixer_state(lengths, projected, conv_weight, conv_bias, step_bias, log_decay):
    patches = projected.shape[0]
    places = lax.broadcasted_iota(jnp.int32, (patches, 1), 0)
    start = seg_starts(lengths, places)
    pos = places - start
    conv_in = projected[:, GROUP_WIDTH : GROUP_WIDTH + CONV_CH]
    conv_out = conv_bias
    for lag in range(CONV):
        conv_out = conv_out + conv_taps(conv_in, pos, lag) * conv_weight[CONV - 1 - lag][None]
    step_raw = projected[:, GROUP_WIDTH + CONV_CH :] + step_bias
    step = jnp.maximum(step_raw, 0.0) + jnp.log1p(jnp.exp(-jnp.abs(step_raw)))
    logd = -step * jnp.exp(log_decay)
    across = lax.broadcasted_iota(jnp.int32, (patches, patches), 1)
    down = lax.broadcasted_iota(jnp.int32, (patches, patches), 0)
    mask = (across >= start) & (across <= down)
    running = dot(mask.astype(f32), logd, precision=highest)
    return pos, conv_in, conv_out, step_raw, step, logd, mask, running


def head_decay(mask, running, running_t, h):
    return jnp.exp(
        jnp.where(mask, running[:, h : h + 1] - running_t[h : h + 1, :], large_negative)
    )


def att_mask(rows, patches):
    across = lax.broadcasted_iota(jnp.int32, (rows, rows), 1)
    down = lax.broadcasted_iota(jnp.int32, (rows, rows), 0)
    return (across % patches == down % patches) & (across <= down)


def soft_rows(mask, query, key):
    scores = dot(query, key, ((1,), (1,))) * ATT_DIM ** (-0.5)
    scores = jnp.where(mask, scores, large_negative)
    probs = jnp.exp(scores - jnp.max(scores, axis=1, keepdims=True))
    return probs / jnp.sum(probs, axis=1, keepdims=True)


def skip_columns(r):
    head = lax.broadcasted_iota(jnp.int32, (1, GROUP_WIDTH), 1) // HEAD_DIM
    return sum(jnp.where(head == h, r.skip[:, h : h + 1], 0.0) for h in range(GROUP_HEADS))


def mixer_fwd(r, lengths, normed):
    projected = dot(normed, r.in_v[...], ((1,), (1,)))
    r.projected[...] = projected
    _, _, conv_out, _, step, _, mask, running = mixer_state(
        lengths, projected, r.taps[...], r.conv_bias[...], r.step_bias[...], r.log_decay[...]
    )
    act = conv_out * jax.nn.sigmoid(conv_out)
    inputs = act[:, GROUP_WIDTH : GROUP_WIDTH + STATE]
    outputs = act[:, GROUP_WIDTH + STATE :]
    inner = dot(outputs, inputs, ((1,), (1,)))
    running_t, step_t = running.T, step.T
    pair = 2 * HEAD_DIM
    lane = lax.broadcasted_iota(jnp.int32, (1, pair), 1)
    pieces = []
    for c in range(GROUP_WIDTH // pair):
        values = act[:, c * pair : (c + 1) * pair]
        got = []
        for h in (2 * c, 2 * c + 1):
            weights = head_decay(mask, running, running_t, h) * inner * step_t[h : h + 1, :]
            got.append(dot(weights, values))
        pieces.append(jnp.where(lane < HEAD_DIM, got[0], got[1]))
    y = jnp.concatenate(pieces, axis=1) + skip_columns(r) * act[:, :GROUP_WIDTH]
    r.mixer_y[...] = y
    gate = projected[:, :GROUP_WIDTH]
    gated = y * (gate * jax.nn.sigmoid(gate))
    low = (gated * inv_rms(gated) * r.group_gain[...]).astype(bf16)
    r.mixer_low[...] = low
    return dot(low, r.out_v[...])


def forward_steps(p, r, load, land):
    n, mpn, i, j = p.n, p.mpn, p.i, p.j
    micro, patches, own_cols = r.own.shape
    positions, dim = r.pw.shape[0], r.pw.shape[1]
    slabs = r.bytes_v.shape[2] // dim
    rows = slabs * patches
    features = r.bytes_part.shape[-1]
    per, hidden = r.ffn_weight.shape[1:]

    load_own = load(r.byte_input.at[:, :, pl.ds(pl.multiple_of(j * own_cols, 128), own_cols)], r.own)
    load_pw = [load(r.patch_weight.at[k], r.pw.at[k]) for k in range(positions)]
    loads_small = load_small(r, load)
    load_grad = load(r.out_grad.at[j], r.grad_raw)
    load_in = load(r.in_weight, r.in_v)
    load_out = load(r.out_weight, r.out_v)
    load_bytes = load(r.byte_input, r.bytes_v)
    load_qkv = load(r.qkv_weight, r.qkv_v)
    kept = [load(r.ffn_weight.at[w], land(j, w, slice(None), slice(None))) for w in range(3)]

    barrier = pltpu.get_barrier_semaphore()
    count = greet_all(p, barrier)
    halves = max(hidden // FFN_COLS, 1)
    cuts = WEIGHT_CUTS if per // WEIGHT_CUTS >= 16 else 1
    step = per // cuts
    pieces = []
    for hh in range(halves):
        cols = slice(hh * (hidden // halves), (hh + 1) * (hidden // halves))
        for w in range(3):
            for k in range(cuts):
                at = slice(k * step, (k + 1) * step)
                pieces.append(LineGather(
                    p,
                    lambda t, w=w, at=at, cols=cols: r.ffn_weight.at[w, at, cols],
                    lambda s, w=w, at=at, cols=cols: land(s, w, at, cols),
                    r.ssw.at[len(pieces)],
                    r.rsw.at[len(pieces)],
                ))
    bulk = Bulk(pieces)
    pl.semaphore_wait(barrier, count)
    bulk.go(PACE[7])
    load_own.wait()
    sums = None
    for k in range(positions):
        load_pw[k].wait()
        term = dot(r.own[:, :, k * dim : (k + 1) * dim].reshape(micro * patches, dim), r.pw[k])
        sums = term if sums is None else sums + term
    for t in range(micro):
        r.part[t] = sums[t * patches : (t + 1) * patches]
        r.part_low[t] = sums[t * patches : (t + 1) * patches].astype(bf16)
    embed = Exchange(p, lambda t: r.part_low.at[t], lambda s: r.recv.at[s], r.ss1, r.rs1).start()
    bulk.go(PACE[0])
    load_grad.wait()
    perm = perm_matrix(rows, patches, slabs, sum(own_lengths(r, j)) - i * patches)
    r.own_grad[...] = dot(perm, r.grad_raw[...]).astype(bf16)
    r.grad_rows_own(i, r.own_grad[...])
    for copy in loads_small:
        copy.wait()
    total = r.part[j]
    for d in range(1, mpn):
        total = total + r.recv[embed.wait(d)].astype(f32)
    r.global_in[...] = total
    r.low[...] = (total * inv_rms(total) * r.norm_in_gain[...]).astype(bf16)
    cast = Cast(p, r.low, r.normed, r.ss2, r.rs2, r.ssc)
    cast.start()
    def columns_of(t, k):
        first = k * dim + t * (dim // n) // features * features
        return r.own.at[:, :, pl.ds(pl.multiple_of(first, 128), features)]

    def bytes_copy(t, k):
        return rcopy(columns_of(t, k), r.bytes_part.at[i, k], r.ssb.at[t, k], r.rsb.at[i, k], t, j)

    for d in range(1, n):
        for k in range(positions):
            bytes_copy((i + d) % n, k).start()
    kept += [load(columns_of(i, k), r.bytes_part.at[i, k]) for k in range(positions)]
    piece = r.out_proj.shape[0] // n
    at_piece = lambda s: pl.ds(pl.multiple_of(s * piece, piece), piece)
    kept_ao = load(r.out_proj.at[at_piece(i)], r.ao_sorted.at[j, at_piece(i)])
    ao_line = LineGather(
        p, lambda t: r.out_proj.at[at_piece(i)], lambda s: r.ao_sorted.at[s, at_piece(i)], r.ssa, r.rsa
    )
    ao_line.begin()
    bulk.go(PACE[1])
    load_in.wait()
    load_out.wait()
    cast.wait()
    feature = dim // n
    blocks = max(feature, 128)

    def normed_copy(q):
        t = q * p.reps + p.h
        return rcopy(normed_block(t), r.normed_cols.at[p.m], r.ssn.at[q], r.rsn.at[p.m], t, j)

    def normed_block(t):
        return r.normed.at[:, :, pl.ds(pl.multiple_of(t * feature // blocks * blocks, 128), blocks)]

    def each_normed(act, here):
        for q in range(p.share):
            at_home = q * p.reps + p.h == i
            pl.when(jnp.logical_not(at_home))(partial(act, q))
            pl.when(at_home)(here)

    def keep_normed():
        return pltpu.make_async_copy(normed_block(i), r.normed_cols.at[p.m], r.ssn.at[p.share])

    each_normed(lambda q: normed_copy(q).start(), lambda: keep_normed().start())
    bulk.go(PACE[2])

    part = mixer_fwd(r, own_lengths(r, p.m), r.normed[...].reshape(n * patches, dim))
    for b in range(n):
        r.mix_part[b] = part[b * patches : (b + 1) * patches].astype(bf16)
    to_owner = ToOwner(p, r.mix_part, r.mix_mid, r.mix_recv, r.ss3, r.rs3, r.sso, r.rso)
    to_owner.start()
    kept_ao.wait()
    ao_line.relay()
    to_owner.pass_on()
    bulk.go(PACE[3])
    ao_line.wait_all()
    ao_block = lambda s: r.ao_sorted.at[:, at_piece(s)]
    ao_plane = PlaneGather(p, ao_block(i), ao_block, r.ssap, r.rsap, r.ssar).start()
    grads = PlaneGather(p, r.own_grad, lambda s: r.grad_rows.at[s], r.ssg, r.rsg, r.ssgr).start()
    total = r.global_in[...] + to_owner.total()
    r.global_own[...] = total
    r.patch_all[j] = total.astype(bf16)
    patch_line = Exchange(p, lambda t: r.patch_all.at[j], lambda s: r.patch_all.at[s], r.ss4, r.rs4).start()
    bulk.go(PACE[4])
    load_bytes.wait()
    load_qkv.wait()
    patch_line.wait_all()

    mask = att_mask(rows, patches)
    pair = 2 * ATT_DIM
    width = r.qkv_v.shape[2]
    lane = lax.broadcasted_iota(jnp.int32, (1, pair), 1)
    heads_line = Exchange(p, lambda t: r.heads.at[t], lambda s: r.heads_own.at[s], r.ss5, r.rs5)

    def one_micro(d, _):
        m = (j + d) % mpn
        for k in range(slabs):
            here = r.bytes_v[m, :, k * dim : (k + 1) * dim].astype(f32) + r.patch_all[m].astype(f32)
            r.attn_in[m, k * patches : (k + 1) * patches, :] = (
                here * inv_rms(here) * r.attn_gain[...]
            ).astype(bf16)
        got = r.attn_in[m]
        for w in range(3):
            r.qkv[w, m] = dot(got, r.qkv_v[w]).astype(bf16)
        for c in range(width // pair):
            at = slice(c * pair, (c + 1) * pair)
            query, key, value = r.qkv[0, m, :, at], r.qkv[1, m, :, at], r.qkv[2, m, :, at]
            res = []
            for own in (lane < ATT_DIM, lane >= ATT_DIM):
                probs = soft_rows(mask, jnp.where(own, query, jnp.zeros_like(query)), key)
                res.append(dot(probs.astype(bf16), value))
            r.heads[m, :, at] = jnp.where(lane < ATT_DIM, res[0], res[1]).astype(bf16)

        @pl.when(d < mpn)
        def _():
            heads_line.copy(m).start()

        return 0

    lax.fori_loop(1, mpn + 1, one_micro, 0)
    bulk.go(PACE[5])
    r.heads_own[j] = r.heads[j]
    ao_plane.relay()
    ao_plane.finish()
    for k in range(slabs):
        here = r.bytes_v[j, :, k * dim : (k + 1) * dim].astype(f32) + r.global_own[...]
        r.after[k * patches : (k + 1) * patches, :] = here
    branch = None
    for d in range(mpn):
        s = j if d == 0 else heads_line.wait(d)
        term = dot(r.heads_own[s], r.ao_sorted[s])
        branch = term if branch is None else branch + term
    after = r.after[...] + branch
    r.after[...] = after
    r.ffn_own[...] = (after * inv_rms(after) * r.ffn_gain[...]).astype(bf16)
    rows_gather = PlaneGather(p, r.ffn_own, lambda s: r.ffn_rows.at[s], r.ssf, r.rsf, r.ssfr).start()
    r.ffn_rows_own(i, r.ffn_own[...])
    grads.relay()
    bulk.go(PACE[6])

    def settle():
        for d in range(1, n):
            s = (i + d) % n
            for k in range(positions):
                rcopy(r.bytes_part.at[s, k], r.bytes_part.at[s, k], r.ssb.at[s, k], r.rsb.at[s, k], s, j).wait_recv()
        for s in range(mpn):
            @pl.when(s * p.reps + p.h != i)
            def _():
                rcopy(
                    r.normed_cols.at[s], r.normed_cols.at[s], r.ssn.at[0], r.rsn.at[s], s * p.reps + p.h, j
                ).wait_recv()
        each_normed(lambda q: normed_copy(q).wait_send(), lambda: keep_normed().wait())
        for thing in (embed, bulk, cast, ao_line, to_owner, ao_plane, patch_line, heads_line):
            thing.sent()
        for d in range(1, n):
            for k in range(positions):
                bytes_copy((i + d) % n, k).wait_send()

    return SimpleNamespace(grads=grads, rows=rows_gather, bulk=bulk, halves=halves, kept=kept, settle=settle)


def forward_kernel(n, mpn, r):
    p = place_of(n, mpn, False)
    load = Loads(r.sem_load)
    kept = []
    r.grad_rows_own = lambda s, value: kept.append(load(r.own_grad, r.grad_rows.at[s]))
    r.ffn_rows_own = lambda s, value: kept.append(load(r.ffn_own, r.ffn_rows.at[s]))
    st = forward_steps(p, r, load, lambda s, w, rows, cols: r.w_all.at[s, w, rows, cols])
    st.grads.finish()
    st.rows.relay()
    st.rows.finish()
    st.bulk.go(len(st.bulk.exchanges))
    st.bulk.wait(0, len(st.bulk.exchanges))
    st.settle()
    st.rows.sent()
    st.grads.sent()
    for copy in kept + st.kept:
        copy.wait()


def forward_ins(a):
    ins = dict(seq_lengths=(a.seq_lengths, SMEM))
    for name in ("byte_input", "patch_weight", "out_grad", "in_weight", "out_weight", "qkv_weight", "ffn_weight"):
        ins[name] = (getattr(a, name), ANY)
    ins["out_proj"] = (a.attn_out_weight, ANY)
    for name in SMALL_PARAMS:
        ins["given_" + name] = (getattr(a, name), ANY)
    return ins


def small_scratch(a):
    return {name: pltpu.VMEM(getattr(a, name).shape, f32) for name in SMALL_PARAMS}


def load_small(r, load):
    return [load(getattr(r, "given_" + name), getattr(r, name)) for name in SMALL_PARAMS]


def forward_results(n, mpn, a):
    micro, patches, cols = a.byte_input.shape
    dim = a.norm_in_gain.shape[1]
    rows = patches * (cols // dim)
    positions = a.patch_weight.shape[0]
    width = a.qkv_weight.shape[2]
    seq = n * patches
    large = dict(
        grad_rows=((n, rows, dim), bf16),
        ffn_rows=((n, rows, dim), bf16),
        w_all=((mpn,) + a.ffn_weight.shape, bf16),
        bytes_part=((n, positions, micro, patches, max(dim // n, 128)), bf16),
        normed_cols=((mpn, n, patches, max(dim // n, 128)), bf16),
    )
    small = dict(
        own_grad=((rows, dim), bf16),
        after=((rows, dim), f32),
        heads_own=((mpn, rows, width), bf16),
        qkv=((3, micro, rows, width), bf16),
        attn_in=((micro, rows, dim), bf16),
        ao_sorted=((mpn,) + a.attn_out_weight.shape, bf16),
        global_in=((patches, dim), f32),
        global_own=((patches, dim), f32),
        normed=((n, patches, dim), bf16),
        projected=((seq, a.in_weight.shape[0]), f32),
        mixer_y=((seq, GROUP_WIDTH), f32),
        mixer_low=((seq, GROUP_WIDTH), bf16),
    )
    return large, small


def forward_scratch(n, mpn, a):
    micro, patches, cols = a.byte_input.shape
    dim = a.norm_in_gain.shape[1]
    rows = patches * (cols // dim)
    positions = a.patch_weight.shape[0]
    width = a.qkv_weight.shape[2]
    half = n // 2
    pieces = max(a.ffn_weight.shape[2] // FFN_COLS, 1) * 3 * WEIGHT_CUTS
    line, plane = DMA((mpn,)), DMA((half,))
    return dict(
        **small_scratch(a),
        own=pltpu.VMEM((micro, patches, positions * dim), bf16),
        pw=pltpu.VMEM(a.patch_weight.shape, bf16),
        grad_raw=pltpu.VMEM((rows, dim), bf16),
        in_v=pltpu.VMEM(a.in_weight.shape, bf16),
        out_v=pltpu.VMEM(a.out_weight.shape, bf16),
        bytes_v=pltpu.VMEM(a.byte_input.shape, bf16),
        qkv_v=pltpu.VMEM(a.qkv_weight.shape, bf16),
        part=pltpu.VMEM((micro, patches, dim), f32),
        part_low=pltpu.VMEM((micro, patches, dim), bf16),
        recv=pltpu.VMEM((mpn, patches, dim), bf16),
        low=pltpu.VMEM((patches, dim), bf16),
        mix_part=pltpu.VMEM((n, patches, dim), bf16),
        mix_mid=pltpu.VMEM((mpn, patches, dim), bf16),
        mix_recv=pltpu.VMEM((mpn, patches, dim), bf16),
        patch_all=pltpu.VMEM((mpn, patches, dim), bf16),
        heads=pltpu.VMEM((micro, rows, width), bf16),
        ffn_own=pltpu.VMEM((rows, dim), bf16),
        sem_load=DMA((48,)),
        ss1=line, rs1=line, ss2=DMA((n,)), rs2=DMA((n,)), ssc=plane, ss3=line, rs3=line, sso=line, rso=line, ss4=line, rs4=line, ss5=line, rs5=line,
        ssg=plane, rsg=DMA((n,)), ssgr=plane, ssf=plane, rsf=DMA((n,)), ssfr=plane,
        ssb=DMA((n, positions)), rsb=DMA((n, positions)),
        ssn=DMA((mpn + 1,)), rsn=line, ssa=line, rsa=line, ssap=plane, rsap=DMA((n,)), ssar=plane,
        ssw=DMA((pieces, mpn)), rsw=DMA((pieces, mpn)),
    )


def forward(n, mpn, a):
    large, small = forward_results(n, mpn, a)
    outs = {name: value + (ANY,) for name, value in large.items()}
    outs.update({name: value + (VMEM,) for name, value in small.items()})
    return launch(
        "forward", partial(forward_kernel, n, mpn), forward_ins(a), outs, forward_scratch(n, mpn, a),
        remote_params(0, 62),
    )


def ffn_kernel(rows_in, grads_in, parts, down_out, in_grad, weight_grad, weight, gate_low, up_low, hidden_low):
    blocks, rows, dim = rows_in.shape
    per = parts.shape[2]
    for s in range(parts.shape[0]):
        for w in range(3):
            weight[w, s * per : (s + 1) * per, :] = parts[s, w]

    def step(b, _):
        here, up = rows_in[b], grads_in[b]
        gate = dot(here, weight[0])
        other = dot(here, weight[1])
        act, slope = silu_pair(gate)
        hidden = (act * other).astype(bf16)
        hidden_low[b] = hidden
        down_out[b] = dot(hidden, weight[2], ((1,), (1,))).astype(bf16)
        hidden_grad = dot(up, weight[2])
        gate_grad = (hidden_grad * other * slope).astype(bf16)
        up_grad = (hidden_grad * act).astype(bf16)
        gate_low[b] = gate_grad
        up_low[b] = up_grad
        back = dot(gate_grad, weight[0], ((1,), (1,))) + dot(up_grad, weight[1], ((1,), (1,)))
        in_grad[b] = back.astype(bf16)
        return 0

    lax.fori_loop(0, blocks, step, 0)
    hidden = weight.shape[2]
    everything = rows_in[...].reshape(blocks * rows, dim)
    weight_grad[0] = dot(everything, gate_low[...].reshape(blocks * rows, hidden), ((0,), (0,))).astype(bf16)
    weight_grad[1] = dot(everything, up_low[...].reshape(blocks * rows, hidden), ((0,), (0,))).astype(bf16)
    weight_grad[2] = dot(
        grads_in[...].reshape(blocks * rows, dim), hidden_low[...].reshape(blocks * rows, hidden), ((0,), (0,))
    ).astype(bf16)


def ffn(rows_in, grads_in, parts):
    blocks, rows, dim = rows_in.shape
    hidden = parts.shape[3]
    return pl.pallas_call(
        ffn_kernel,
        out_shape=(
            jax.ShapeDtypeStruct((blocks, rows, dim), bf16),
            jax.ShapeDtypeStruct((blocks, rows, dim), bf16),
            jax.ShapeDtypeStruct((3, dim, hidden), bf16),
        ),
        in_specs=[VMEM] * 3,
        out_specs=(VMEM,) * 3,
        scratch_shapes=[pltpu.VMEM((3, dim, hidden), bf16)] + [pltpu.VMEM((blocks, rows, hidden), bf16)] * 3,
        compiler_params=plain_params(60),
        name="ffn",
    )(rows_in, grads_in, parts)


def mixer_bwd(r, p, lengths, upstream):
    projected = r.projected[...]
    patches = projected.shape[0]
    pos, conv_in, conv_out, step_raw, step, logd, mask, running = mixer_state(
        lengths, projected, r.taps[...], r.conv_bias[...], r.step_bias[...], r.log_decay[...]
    )
    act, act_slope = silu_pair(conv_out)
    inputs = act[:, GROUP_WIDTH : GROUP_WIDTH + STATE]
    outputs = act[:, GROUP_WIDTH + STATE :]
    inner = dot(outputs, inputs, ((1,), (1,)))
    running_t, step_t = running.T, step.T
    normed_grad = dot(upstream, r.out_v[...], ((1,), (1,)))
    y = r.mixer_y[...]
    gate = projected[:, :GROUP_WIDTH]
    gate_act, gate_slope = silu_pair(gate)
    gated_grad, gain_rows = rms_back(y * gate_act, r.group_gain[...], normed_grad)
    y_grad = gated_grad * gate_act
    gate_grad = gated_grad * y * gate_slope
    values = act[:, :GROUP_WIDTH]
    skip_cols = jnp.sum(y_grad * values, axis=0, keepdims=True)
    pair = 2 * HEAD_DIM
    lane = lax.broadcasted_iota(jnp.int32, (1, pair), 1)
    inner_grad = jnp.zeros_like(inner)
    value_pieces, row_sums, col_sums = [], [], []
    for c in range(GROUP_WIDTH // pair):
        at = slice(c * pair, (c + 1) * pair)
        got = []
        for h in (2 * c, 2 * c + 1):
            own = (lane < HEAD_DIM) if h % 2 == 0 else (lane >= HEAD_DIM)
            mine = jnp.where(own, y_grad[:, at], 0.0)
            decay = head_decay(mask, running, running_t, h)
            step_row = step_t[h : h + 1, :]
            weight_grad = dot(mine, values[:, at], ((1,), (1,))) * decay
            scaled = weight_grad * step_row
            inner_grad = inner_grad + scaled
            col_sums.append(jnp.sum(weight_grad * inner, axis=0, keepdims=True))
            row_sums.append(jnp.sum(scaled * inner, axis=1, keepdims=True))
            weights = decay * inner * step_row
            got.append(dot(weights, mine, ((0,), (0,))))
        value_pieces.append(got[0] + got[1])
    values_grad = jnp.concatenate(value_pieces, axis=1) + skip_columns(r) * y_grad
    inputs_grad = dot(inner_grad, outputs, ((0,), (0,)))
    outputs_grad = dot(inner_grad, inputs)
    col_grad = jnp.concatenate(col_sums, axis=0).T
    running_grad = jnp.concatenate(row_sums, axis=1) - col_grad * step
    logd_grad = dot(mask.astype(f32), running_grad, ((0,), (0,)), precision=highest)
    step_grad = (col_grad - logd_grad * jnp.exp(r.log_decay[...])) * jax.nn.sigmoid(step_raw)
    conv_grad = jnp.concatenate([values_grad, inputs_grad, outputs_grad], axis=1) * act_slope
    conv_in_grad = jnp.zeros_like(conv_grad)
    small = r.small_part
    small[...] = jnp.zeros(small.shape, f32)
    for lag in range(CONV):
        small[CONV - 1 - lag : CONV - lag, :] = jnp.sum(
            conv_grad * conv_taps(conv_in, pos, lag), axis=0, keepdims=True
        )
        kept = jnp.where(pos >= lag, conv_grad, 0.0) * r.taps[CONV - 1 - lag : CONV - lag, :]
        conv_in_grad = conv_in_grad + (kept if lag == 0 else pltpu.roll(kept, patches - lag, 0))
    small[CONV : CONV + 1, :] = jnp.sum(conv_grad, axis=0, keepdims=True)
    small[CONV + 1 : CONV + 2, :GROUP_WIDTH] = jnp.sum(gain_rows, axis=0, keepdims=True)
    small[CONV + 2 : CONV + 3, :GROUP_WIDTH] = skip_cols
    small[CONV + 3 : CONV + 4, :GROUP_HEADS] = jnp.sum(step_grad, axis=0, keepdims=True)
    small[CONV + 4 : CONV + 5, :GROUP_HEADS] = jnp.sum(logd_grad * logd, axis=0, keepdims=True)
    return jnp.concatenate([gate_grad, conv_in_grad, step_grad], axis=1).astype(bf16)


def grad_pieces(p, r, halves, grad_of, dim, hidden):
    per = dim // p.mpn
    step = per // WEIGHT_CUTS
    pieces = []
    for hh in range(halves):
        cols = slice(hh * (hidden // halves), (hh + 1) * (hidden // halves))
        for w in range(3):
            for k in range(WEIGHT_CUTS):
                at = slice(k * step, (k + 1) * step)
                pieces.append(LineReduce(
                    p,
                    lambda t, w=w, k=k, cols=cols: grad_of(
                        w, pl.ds(pl.multiple_of(t * per + k * step, step), step), cols
                    ),
                    lambda s, w=w, at=at, cols=cols: r.g_recv.at[s, w, at, cols],
                    r.bsw.at[len(pieces)],
                    r.brw.at[len(pieces)],
                    r.g_held.at[len(pieces)] if p.line else None,
                    r.bsr.at[len(pieces)] if p.line else None,
                ))
    return Bulk(pieces)


def ffn_sums(p, r, get, put):
    in_block = lambda s: r.in_part.at[s]
    down_block = lambda s: r.down_part.at[s]
    return (
        Reduction(p, in_block, lambda s: get(in_block(s)), r.in_pre, r.in_recv, r.bs_in, get, put),
        Reduction(p, down_block, lambda s: get(down_block(s)), r.down_pre, r.down_recv, r.bs_down, get, put),
    )


def backward_steps(p, r, load, own_slab, ready, sum_in, sum_down, bulk, pieces_of=None):
    n, mpn, i, j = p.n, p.mpn, p.i, p.j
    micro, rows, dim = r.attn_in.shape
    patches = r.global_own.shape[0]
    slabs = rows // patches
    width = r.qkv_v.shape[2]
    feature = dim // n
    at_feature = lambda s: pl.ds(pl.multiple_of(s * feature, feature), feature)
    block_ao = lambda s: r.ao_part.at[at_feature(s)]
    block_qkv = lambda s: r.qkv_part.at[:, at_feature(s)]
    sum_ao = Reduction(
        p, block_ao, lambda s: block_ao(s)[...], r.ao_pre, r.ao_recv, r.bs_ao, plain_get, plain_put
    )
    sum_qkv = Reduction(
        p, block_qkv, lambda s: block_qkv(s)[...], r.qkv_pre, r.qkv_recv, r.bs_qkv, plain_get, plain_put
    )

    ready("bytes")
    for k in range(slabs):
        r.local_in[k * patches : (k + 1) * patches, :] = own_slab(k).astype(f32) + r.global_own[...]
    after = r.after[...]
    back, gain_rows = rms_back(after, r.ffn_gain[...], sum_in.finish())
    after_grad = r.own_grad[...].astype(f32) + back
    r.after_grad[...] = after_grad
    r.gains[...] = jnp.zeros(r.gains.shape, f32)
    r.gains[2:3, :] = jnp.sum(gain_rows, axis=0, keepdims=True)
    r.branch[...] = after_grad.astype(bf16)
    up_turn = jnp.where(j < mpn // 2, mpn - 1, 1)
    up_line = Exchange(p, lambda t: r.up.at[t], lambda s: r.up_recv.at[s], r.bs1, r.br1)
    for d in range(1, mpn + 1):
        t = (j + d * up_turn) % mpn
        r.up[t] = dot(r.branch[...], r.ao_sorted[t], ((1,), (1,))).astype(bf16)
        if d < mpn:
            up_line.copy(t).start()
    r.up_recv[j] = r.up[j]
    bulk.go(PACE_BACK[0], RELAY_GRADS[1])
    sum_down.spread()
    ready("qkv")

    mask = att_mask(rows, patches)
    pair = 2 * ATT_DIM
    lane = lax.broadcasted_iota(jnp.int32, (1, pair), 1)
    att_line = LineReduce(
        p, lambda t: r.att_part.at[t], lambda s: r.att_recv.at[s], r.bs2, r.br2,
        r.att_held if p.line else None, r.bsz.at[0],
    )
    turn = jnp.where(j < mpn // 2, mpn - 1, 1)

    def one_micro(d, _):
        m = (j + d * turn) % mpn

        @pl.when(d > 0)
        def _():
            up_line.wait(d * turn)

        for c in range(width // pair):
            at = slice(c * pair, (c + 1) * pair)
            query, key, value = r.qkv[0, m, :, at], r.qkv[1, m, :, at], r.qkv[2, m, :, at]
            up = r.up_recv[m, :, at]
            got = [[], [], []]
            for own in (lane < ATT_DIM, lane >= ATT_DIM):
                mine = jnp.where(own, query, jnp.zeros_like(query))
                probs = soft_rows(mask, mine, key)
                my_up = jnp.where(own, up, jnp.zeros_like(up))
                probs_grad = dot(my_up, value, ((1,), (1,)))
                inner = jnp.sum(probs * probs_grad, axis=1, keepdims=True)
                score_grad = (probs * (probs_grad - inner) * ATT_DIM ** (-0.5)).astype(bf16)
                got[0].append(dot(score_grad, key))
                got[1].append(dot(score_grad, mine, ((0,), (0,))))
                got[2].append(dot(probs.astype(bf16), my_up, ((0,), (0,))))
            r.qkv_low[0, m, :, at] = jnp.where(lane < ATT_DIM, got[0][0], got[0][1]).astype(bf16)
            r.qkv_low[1, m, :, at] = (got[1][0] + got[1][1]).astype(bf16)
            r.qkv_low[2, m, :, at] = (got[2][0] + got[2][1]).astype(bf16)
        total = dot(r.qkv_low[0, m], r.qkv_v[0], ((1,), (1,)))
        total = total + dot(r.qkv_low[1, m], r.qkv_v[1], ((1,), (1,)))
        total = total + dot(r.qkv_low[2, m], r.qkv_v[2], ((1,), (1,)))
        r.att_part[m] = total.astype(bf16)

        @pl.when(d > 0)
        def _():
            att_line.send(m)

        return 0

    lax.fori_loop(0, mpn, one_micro, 0)

    everything = r.attn_in[...].reshape(micro * rows, dim)
    for w in range(3):
        r.qkv_part[w] = dot(
            everything, r.qkv_low[w].reshape(micro * rows, width), ((0,), (0,))
        ).astype(bf16)
    sum_qkv.start()
    sum_qkv.spread()
    for t in range(mpn):
        r.ao_part[:, t * width : (t + 1) * width] = dot(
            r.branch[...], r.heads_own[t], ((0,), (0,))
        ).astype(bf16)
    sum_ao.start()
    perm = perm_matrix(rows, patches, slabs, sum(own_lengths(r, j)) - i * patches)
    block = (r.after[...] + sum_down.finish()).astype(bf16)
    block = dot(perm, block, ((0,), (0,))).astype(bf16)
    for t in range(mpn):
        r.block[t] = block[:, t * width : (t + 1) * width]
    total = r.att_part[j].astype(f32)
    att_line.wait_all()
    for s in range(mpn):
        total = total + jnp.where((s == j) | absent(p.line, j, s), 0.0, r.att_recv[s].astype(f32))
    back, gain_rows = rms_back(r.local_in[...], r.attn_gain[...], total)
    local_grad = r.after_grad[...] + back
    global_grad = local_grad[:patches]
    for k in range(1, slabs):
        global_grad = global_grad + local_grad[k * patches : (k + 1) * patches]
    r.global_grad[...] = global_grad
    r.b_low[...] = global_grad.astype(bf16)
    cast = Cast(p, r.b_low, r.mixer, r.bs3, r.br3, r.bsc)
    cast.start()
    sum_ao.spread()
    bulk.go(PACE_BACK[1], RELAY_GRADS[2])
    r.gains[1:2, :] = jnp.sum(gain_rows, axis=0, keepdims=True)
    share_rows = rows // mpn
    for t in range(mpn):
        r.local[t] = local_grad[t * share_rows : (t + 1) * share_rows].astype(bf16)
    local_line = Exchange(p, lambda t: r.local.at[t], lambda s: r.local_all.at[s], r.bs6, r.br6)
    block_line = Exchange(p, lambda t: r.block.at[t], lambda s: r.block_all.at[s], r.bs7, r.br7)
    ready("mixer")
    cast.wait()
    bulk.go(PACE_BACK[2], RELAY_GRADS[3])

    upstream = r.mixer[...].reshape(n * patches, dim)
    proj_grad = mixer_bwd(r, p, own_lengths(r, p.m), upstream)
    part = dot(proj_grad, r.in_v[...])
    for b in range(n):
        r.b_part[b] = part[b * patches : (b + 1) * patches].astype(bf16)
    to_owner = ToOwner(p, r.b_part, r.b_mid, r.b_recv, r.bs4, r.br4, r.bs9, r.br9)
    to_owner.start()
    bulk.go(PACE_BACK[3], RELAY_GRADS[4])

    r.proj_grad[...] = proj_grad
    size = n * patches // p.reps
    proj_own = r.proj_grad.at[pl.ds(pl.multiple_of(p.h * size, size), size)]
    proj_plane = PlaneGather(p, proj_own, lambda s: r.proj_all.at[s], r.bsi, r.bri, r.bsir).start()
    keep_proj = load(proj_own, r.proj_all.at[i])
    out_grad = dot(r.mixer_low[...], upstream, ((0,), (0,))).astype(bf16)
    group_rows = GROUP_WIDTH // n
    for e in range(n):
        r.out_w_part[e] = out_grad[e * group_rows : (e + 1) * group_rows]
    bundles = (
        (lambda t: r.out_w_part.at[t], r.out_w_recv, r.bso, r.bro),
        (lambda t: r.small_part, r.small_recv, r.bss, r.brs),
    )

    def each_bundle(act):
        for q in range(p.share):
            t = q * p.reps + p.h

            @pl.when(t != i)
            def _():
                for src, dst, ss, rs in bundles:
                    act(rcopy(src(t), dst.at[p.m], ss.at[q], rs.at[p.m], t, j))

    to_owner.pass_on()
    bulk.go(PACE_BACK[4], RELAY_GRADS[5])
    each_bundle(lambda copy: copy.start())
    keeps = [load(r.out_w_part.at[i], r.out_w_recv.at[p.m]), load(r.small_part, r.small_recv.at[p.m])]
    back, gain_rows = rms_back(r.global_in[...], r.norm_in_gain[...], to_owner.total())
    r.line[j] = (r.global_grad[...] + back).astype(bf16)
    line = Exchange(p, lambda t: r.line.at[j], lambda s: r.line.at[s], r.bs5, r.br5).start()
    bulk.go(len(bulk.exchanges), RELAY_GRADS[6])
    r.gains[0:1, :] = jnp.sum(gain_rows, axis=0, keepdims=True)
    others = [(p.mine + d) % p.half for d in range(1, p.half)]

    def gains_copy(q):
        return rcopy(r.gains, r.gains_plane.at[p.mine], r.bsh.at[q], r.brh.at[p.mine], q * 2 + p.c, j)

    for q in others:
        gains_copy(q).start()
    r.gains_plane[p.mine] = r.gains[...]
    local_line.start()
    block_line.start()
    keeps += [load(r.local.at[j], r.local_all.at[j]), load(r.block.at[j], r.block_all.at[j])]
    line.wait_all()
    slot = lambda s: r.plane.at[s]
    plane = PlaneGather(p, r.line, slot, r.bsp, r.brp, r.bspr).start()
    keep_line = load(r.line, r.plane.at[i])
    bulk.relay(RELAY_GRADS[7])
    proj_plane.relay()
    r.qkv_total[...] = sum_qkv.finish()
    keeps.append(load(r.qkv_total, r.qkv_sum))
    ao = sum_ao.finish().astype(bf16)
    for t in range(mpn):
        r.ao[t] = ao[:, t * width : (t + 1) * width]
    ao_line = Exchange(p, lambda t: r.ao.at[t], lambda s: r.ao_all.at[s], r.bs8, r.br8).start()
    keeps.append(load(r.ao.at[j], r.ao_all.at[j]))
    bulk.relay(len(bulk.exchanges))
    if pieces_of is not None:
        keeps.append(pieces_of())
    for q in others:
        rcopy(r.gains, r.gains_plane.at[q], r.bsh.at[q], r.brh.at[q], q * 2 + p.c, j).wait_recv()
    r.gains_pair[0] = sum(r.gains_plane[s] for s in range(p.half))
    pair_copy = rcopy(r.gains_pair.at[0], r.gains_pair.at[1], r.bsq.at[0], r.brq.at[0], p.other, j)
    pair_copy.start()
    plane.relay()
    pair_copy.wait()
    r.gains_pair[0] = r.gains_pair[0] + r.gains_pair[1]
    width_i = r.gains_mine.shape[1]
    first = i * feature // width_i * width_i
    r.gains_mine[...] = r.gains_pair[0, :, pl.ds(pl.multiple_of(first, 128), width_i)]
    gains_line = Exchange(p, lambda t: r.gains_mine, lambda s: r.gains_line.at[s], r.bsg, r.brg).start()
    plane.finish()
    local_line.wait_all()
    block_line.wait_all()
    ao_line.wait_all()
    for s in range(mpn):
        @pl.when(s * p.reps + p.h != i)
        def _():
            for src, dst, ss, rs in bundles:
                rcopy(src(0), dst.at[s], ss.at[0], rs.at[s], s * p.reps + p.h, j).wait_recv()
    proj_plane.finish()
    gains_line.wait_all()
    r.gains_line[j] = r.gains_mine[...]
    gains_line.sent()
    r.gains_mine[...] = sum(r.gains_line[s] for s in range(mpn))
    keeps.append(load(r.gains_mine, r.gains_all))
    bulk.wait(0, len(bulk.exchanges))
    keep_line.wait()
    keep_proj.wait()
    for copy in keeps:
        copy.wait()
    for thing in (
        sum_in, sum_down, sum_ao, sum_qkv, bulk, up_line, att_line, cast, to_owner, line, local_line,
        block_line, plane, proj_plane, ao_line,
    ):
        thing.sent()
    for q in others:
        gains_copy(q).wait_send()
    each_bundle(lambda copy: copy.wait_send())


def backward_kernel(n, mpn, spill, r):
    p = place_of(n, mpn, False)
    load = Loads(r.b_load)

    def read(view):
        if not spill:
            return view[...]
        copy = pltpu.make_async_copy(view, r.stage.at[0], r.sem_stage.at[0])
        copy.start()
        copy.wait()
        return r.stage[0]

    def write(view, value):
        if not spill:
            view[...] = value
            return
        r.stage[1] = value
        copy = pltpu.make_async_copy(r.stage.at[1], view, r.sem_stage.at[1])
        copy.start()
        copy.wait()

    per = r.w_grad.shape[1] // mpn
    loads_small = load_small(r, load)
    keep_w = load(r.w_grad.at[:, pl.ds(pl.multiple_of(p.j * per, per), per)], r.g_recv.at[p.j])
    loads = dict(
        bytes=[load(r.byte_input.at[p.j], r.own_bytes)],
        qkv=[load(r.qkv_weight, r.qkv_v)],
        mixer=[load(r.out_weight, r.out_v), load(r.in_weight, r.in_v)],
    )

    def ready(what):
        for copy in loads[what]:
            copy.wait()

    barrier = pltpu.get_barrier_semaphore()
    pl.semaphore_wait(barrier, greet_all(p, barrier))
    for copy in loads_small:
        copy.wait()
    bulk = grad_pieces(p, r, 1, lambda w, at, cols: r.w_grad.at[w, at, cols], *r.w_grad.shape[1:])
    sum_in, sum_down = ffn_sums(p, r, read, write)
    sum_in.start()
    sum_in.spread()
    sum_down.start()
    dim = r.after.shape[1]
    own_slab = lambda k: r.own_bytes[:, k * dim : (k + 1) * dim]
    backward_steps(p, r, load, own_slab, ready, sum_in, sum_down, bulk)
    keep_w.wait()


def backward_results(n, mpn, a):
    micro, patches, cols = a.byte_input.shape
    dim = a.norm_in_gain.shape[1]
    rows = patches * (cols // dim)
    width = a.qkv_weight.shape[2]
    hidden = a.ffn_weight.shape[2]
    feature = dim // n
    return dict(
        g_recv=((mpn, 3, dim // mpn, hidden), bf16, ANY),
        plane=((n, mpn, patches, dim), bf16, ANY),
        qkv_sum=((3, feature, width), f32, ANY),
        ao_all=((mpn, feature, width), bf16, ANY),
        proj_all=((n, n * patches // (n // mpn), a.in_weight.shape[0]), bf16, ANY),
        out_w_recv=((mpn, GROUP_WIDTH // n, dim), bf16, ANY),
        small_recv=((mpn, 16, CONV_CH), f32, ANY),
        gains_all=((8, max(feature, 128)), f32, ANY),
        local_all=((mpn, rows // mpn, dim), bf16, ANY),
        block_all=((mpn, rows, width), bf16, ANY),
    )


def backward_scratch(n, mpn, a):
    micro, patches, cols = a.byte_input.shape
    dim = a.norm_in_gain.shape[1]
    rows = patches * (cols // dim)
    width = a.qkv_weight.shape[2]
    hidden = a.ffn_weight.shape[2]
    half, share = n // 2, mpn
    feature = dim // n
    pieces = max(hidden // FFN_COLS, 1) * 3 * WEIGHT_CUTS
    line, plane = DMA((mpn,)), DMA((half,))
    return dict(
        local_in=pltpu.VMEM((rows, dim), f32),
        after_grad=pltpu.VMEM((rows, dim), f32),
        branch=pltpu.VMEM((rows, dim), bf16),
        up=pltpu.VMEM((mpn, rows, width), bf16),
        up_recv=pltpu.VMEM((mpn, rows, width), bf16),
        qkv_low=pltpu.VMEM((3, micro, rows, width), bf16),
        att_part=pltpu.VMEM((micro, rows, dim), bf16),
        att_recv=pltpu.VMEM((mpn, rows, dim), bf16),
        qkv_part=pltpu.VMEM((3, dim, width), bf16),
        qkv_pre=pltpu.VMEM((half, 3, feature, width), bf16),
        qkv_recv=pltpu.VMEM((half, 3, feature, width), bf16),
        ao_part=pltpu.VMEM((dim, mpn * width), bf16),
        ao_pre=pltpu.VMEM((half, feature, mpn * width), bf16),
        ao_recv=pltpu.VMEM((half, feature, mpn * width), bf16),
        ao=pltpu.VMEM((mpn, feature, width), bf16),
        block=pltpu.VMEM((mpn, rows, width), bf16),
        local=pltpu.VMEM((mpn, rows // mpn, dim), bf16),
        b_low=pltpu.VMEM((patches, dim), bf16),
        global_grad=pltpu.VMEM((patches, dim), f32),
        mixer=pltpu.VMEM((n, patches, dim), bf16),
        b_part=pltpu.VMEM((n, patches, dim), bf16),
        b_mid=pltpu.VMEM((mpn, patches, dim), bf16),
        b_recv=pltpu.VMEM((mpn, patches, dim), bf16),
        line=pltpu.VMEM((mpn, patches, dim), bf16),
        proj_grad=pltpu.VMEM((n * patches, a.in_weight.shape[0]), bf16),
        out_w_part=pltpu.VMEM((n, GROUP_WIDTH // n, dim), bf16),
        small_part=pltpu.VMEM((16, CONV_CH), f32),
        qkv_total=pltpu.VMEM((3, feature, width), f32),
        gains=pltpu.VMEM((8, dim), f32),
        gains_mine=pltpu.VMEM((8, max(feature, 128)), f32),
        gains_line=pltpu.VMEM((mpn, 8, max(feature, 128)), f32),
        gains_plane=pltpu.VMEM((half, 8, dim), f32),
        gains_pair=pltpu.VMEM((2, 8, dim), f32),
        b_load=DMA((64,)),
        bs_in=DMA((4, half)), bs_down=DMA((4, half)), bs_ao=DMA((4, half)), bs_qkv=DMA((4, half)),
        bs1=line, br1=line, bs2=line, br2=line, bs3=DMA((n,)), br3=DMA((n,)), bsc=plane, bs4=line, br4=line, bs9=line, br9=line,
        bs5=line, br5=line, bs6=line, br6=line, bs7=line, br7=line, bs8=line, br8=line,
        bsp=plane, brp=DMA((n,)), bspr=plane,
        bsg=line, brg=line, bsh=plane, brh=plane, bsq=DMA((1,)), brq=DMA((1,)),
        bsz=DMA((1,)), bsi=plane, bri=DMA((n,)), bsir=plane, bso=DMA((share,)), bro=line, bss=DMA((share,)), brs=line,
        bsw=DMA((pieces, mpn)), brw=DMA((pieces, mpn)),
    )


def sum_buffers(n, a, make):
    micro, patches, cols = a.byte_input.shape
    dim = a.norm_in_gain.shape[1]
    shape = (n // 2, patches * (cols // dim), dim)
    return {name: make(shape) for name in ("in_pre", "in_recv", "down_pre", "down_recv")}


def backward(n, mpn, a):
    spill = a.in_part.size * 2 > SPILL_BYTES
    ins = dict(seq_lengths=(a.seq_lengths, SMEM))
    for name in ("byte_input", "w_grad", "in_weight", "out_weight", "qkv_weight"):
        ins[name] = (getattr(a, name), ANY)
    for name in ("in_part", "down_part"):
        ins[name] = (getattr(a, name), ANY if spill else VMEM)
    for name in SMALL_PARAMS:
        ins["given_" + name] = (getattr(a, name), ANY)
    for name in (
        "after", "own_grad", "heads_own", "qkv", "attn_in", "ao_sorted", "global_in", "global_own", "normed",
        "projected", "mixer_y", "mixer_low",
    ):
        ins[name] = (getattr(a, name), VMEM)
    outs = backward_results(n, mpn, a)
    scratch = backward_scratch(n, mpn, a)
    scratch.update(small_scratch(a))
    scratch.update(
        own_bytes=pltpu.VMEM(a.byte_input.shape[1:], bf16),
        in_v=pltpu.VMEM(a.in_weight.shape, bf16),
        out_v=pltpu.VMEM(a.out_weight.shape, bf16),
        qkv_v=pltpu.VMEM(a.qkv_weight.shape, bf16),
    )
    if spill:
        outs.update(sum_buffers(n, a, lambda shape: (shape, bf16, ANY)))
        scratch.update(stage=pltpu.VMEM((2,) + a.in_part.shape[1:], bf16), sem_stage=DMA((2,)))
    else:
        scratch.update(sum_buffers(n, a, lambda shape: pltpu.VMEM(shape, bf16)))
    return launch(
        "backward", partial(backward_kernel, n, mpn, spill), ins, outs, scratch, remote_params(1, 63)
    )


def ffn_steps(p, r, st, load, sum_in, sum_down, bulk, grad_of):
    n, half = p.n, p.half
    rows, dim = r.own_grad.shape
    hidden = r.w_v.shape[2]
    cols = hidden // st.halves
    per = dim // p.mpn
    pair = 2 * rows
    st.grads.finish()
    grads_all = lambda: r.grad_rows[...].reshape(n * rows, dim)
    rows_all = lambda: r.ffn_rows[...].reshape(n * rows, dim)
    kept = []
    if st.halves == 1:
        st.rows.relay()
        st.rows.finish()
    count = len(st.bulk.exchanges) // st.halves
    for hh in range(st.halves):
        at = slice(hh * cols, (hh + 1) * cols)
        last = hh == st.halves - 1
        if last:
            st.bulk.go(len(st.bulk.exchanges))
        st.bulk.wait(hh * count, (hh + 1) * count)
        if hh == 0:
            for copy in st.kept:
                copy.wait()

        def compute(q):
            here = r.ffn_rows[pl.ds(2 * q, 2)].reshape(pair, dim)
            up = r.grad_rows[pl.ds(2 * q, 2)].reshape(pair, dim)
            gate = dot(here, r.w_v[0, :, at])
            other = dot(here, r.w_v[1, :, at])
            act, slope = silu_pair(gate)
            hidden_low = (act * other).astype(bf16)
            here_at = pl.ds(pl.multiple_of(q * pair, pair), pair)
            r.hidden_low[hh, here_at, :] = hidden_low
            down = dot(hidden_low, r.w_v[2, :, at], ((1,), (1,)))
            hidden_grad = dot(up, r.w_v[2, :, at])
            gate_grad = (hidden_grad * other * slope).astype(bf16)
            up_grad = (hidden_grad * act).astype(bf16)
            r.gate_low[hh, here_at, :] = gate_grad
            r.up_low[hh, here_at, :] = up_grad
            back = dot(gate_grad, r.w_v[0, :, at], ((1,), (1,))) + dot(up_grad, r.w_v[1, :, at], ((1,), (1,)))
            if hh > 0:
                back = back + r.in_part[pl.ds(2 * q, 2)].reshape(pair, dim).astype(f32)
                down = down + r.down_part[pl.ds(2 * q, 2)].reshape(pair, dim).astype(f32)
            r.in_part[pl.ds(2 * q, 2)] = back.astype(bf16).reshape(2, rows, dim)
            r.down_part[pl.ds(2 * q, 2)] = down.astype(bf16).reshape(2, rows, dim)

        def first_pass(d, _):
            q = (p.mine + half - d) % half
            for turn, upto in RELAY_WEIGHTS:
                @pl.when(d == turn)
                def _():
                    st.bulk.relay(upto)

            @pl.when(d > 0)
            def _():
                st.rows.relay_one(q)

            st.rows.wait_across(q)
            compute(q)
            return 0

        def last_pass(d, _):
            q = (p.mine + d) % half
            compute(q)
            sum_in.first(q).start()

            @pl.when(d > 1)
            def _():
                sum_in.spread_one((p.mine + d - 1) % half)

            return 0

        if last:
            lax.fori_loop(1, half + 1, last_pass, 0)
            sum_down.start()
        else:
            lax.fori_loop(0, half, first_pass, 0)
        everything = slice(0, dim)
        grad_of(0, everything, at)[...] = dot(rows_all(), r.gate_low[hh], ((0,), (0,))).astype(bf16)
        grad_of(1, everything, at)[...] = dot(rows_all(), r.up_low[hh], ((0,), (0,))).astype(bf16)
        grad_of(2, everything, at)[...] = dot(grads_all(), r.hidden_low[hh], ((0,), (0,))).astype(bf16)
        mine = pl.ds(pl.multiple_of(p.j * per, per), per)
        kept += [load(grad_of(w, mine, at), r.g_recv.at[p.j, w, :, at]) for w in range(3)]
        if last:
            bulk.relay(RELAY_GRADS[0])
        else:
            bulk.go(PACE_FFN)
    return kept


def layer_kernel(n, mpn, r):
    p = place_of(n, mpn, mpn == 4)
    dim = r.after.shape[1]

    def put_rows(ref):
        def put(s, value):
            ref[s] = value

        return put

    r.grad_rows_own = put_rows(r.grad_rows)
    r.ffn_rows_own = put_rows(r.ffn_rows)
    per = r.ffn_weight.shape[1]

    def land(s, w, rows, cols):
        first = (0 if rows.start is None else rows.start) + s * per
        size = per if rows.start is None else rows.stop - rows.start
        return r.w_v.at[w, pl.ds(pl.multiple_of(first, size), size), cols]

    load = Loads(r.sem_load)
    st = forward_steps(p, r, load, land)
    hidden = r.w_v.shape[2]

    def grad_of(w, at, cols):
        first = w % 2 * hidden
        return r.pw.at[w // 2, at, first + cols.start : first + cols.stop]

    bulk = grad_pieces(p, r, st.halves, grad_of, dim, hidden)
    sum_in, sum_down = ffn_sums(p, r, plain_get, plain_put)
    load = Loads(r.b_load)
    kept = ffn_steps(p, r, st, load, sum_in, sum_down, bulk, grad_of)
    own_slab = lambda k: r.bytes_v[p.j, :, k * dim : (k + 1) * dim]
    st.rows.sent()
    st.grads.sent()
    rows = r.own_grad.shape[0]
    positions = r.patch_weight.shape[0]
    places = (r.ffn_rows, r.grad_rows)
    again = [
        load(r.patch_weight.at[k, s * rows : (s + 1) * rows], places[k].at[s])
        for k in range(positions) for s in range(dim // rows)
    ]

    def pieces_of():
        for copy in again:
            copy.wait()
        own = r.line[...].reshape(-1, dim)
        for k in range(positions):
            r.piece_v[:, k * dim : (k + 1) * dim] = dot(
                own, places[k][: dim // rows].reshape(dim, dim), ((1,), (1,))
            )
        return load(r.piece_v, r.piece)

    backward_steps(p, r, load, own_slab, lambda what: None, sum_in, sum_down, bulk, pieces_of)
    st.settle()
    for copy in kept:
        copy.wait()


def layer(n, mpn, a):
    dim = a.norm_in_gain.shape[1]
    hidden = a.ffn_weight.shape[2]
    halves = max(hidden // FFN_COLS, 1)
    large, small = forward_results(n, mpn, a)
    rows = small["own_grad"][0][0]
    outs = {name: large.pop(name) + (ANY,) for name in ("bytes_part", "normed_cols")}
    outs.update(backward_results(n, mpn, a))
    patches, cols = a.byte_input.shape[1:]
    piece = ((mpn * patches, a.patch_weight.shape[0] * dim), f32)
    outs.update(piece=piece + (ANY,))
    large.pop("w_all")
    scratch = forward_scratch(n, mpn, a)
    scratch.update(backward_scratch(n, mpn, a))
    scratch.update(piece_v=pltpu.VMEM(*piece))
    for name, (shape, dtype) in (*large.items(), *small.items()):
        scratch[name] = pltpu.VMEM(shape, dtype)
    scratch.update(sum_buffers(n, a, lambda shape: pltpu.VMEM(shape, bf16)))
    scratch.update(
        g_held=pltpu.VMEM((halves * 3 * WEIGHT_CUTS, dim // mpn // WEIGHT_CUTS, hidden // halves), bf16),
        att_held=pltpu.VMEM((rows, dim), bf16),
        bsr=DMA((halves * 3 * WEIGHT_CUTS,)),
        w_v=pltpu.VMEM((3, dim, hidden), bf16),
        in_part=pltpu.VMEM((n, rows, dim), bf16),
        down_part=pltpu.VMEM((n, rows, dim), bf16),
        gate_low=pltpu.VMEM((halves, n * rows, hidden // halves), bf16),
        up_low=pltpu.VMEM((halves, n * rows, hidden // halves), bf16),
        hidden_low=pltpu.VMEM((halves, n * rows, hidden // halves), bf16),
    )
    return launch(
        "layer", partial(layer_kernel, n, mpn), forward_ins(a), outs, scratch, remote_params(2, 63)
    )


def finish_kernel(line, r):
    i, j = lax.axis_index("dp"), lax.axis_index("mp")
    mpn, patches, dim = r.plane.shape[1:]
    n = r.plane.shape[0]
    features = r.bytes_part.shape[-1]
    positions = r.bytes_part.shape[1]
    feature = dim // n
    columns = r.in_grad.shape[0]
    load = Loads(r.sems)
    writes = []
    into = lambda name: load(getattr(r, name), getattr(r, name + "_v"))
    load_g = [load(r.g_recv.at[:, w], r.g_recv_v.at[w]) for w in range(3)]
    load_patch = [into("plane"), into("bytes_part")]
    load_in = [into("proj_all"), into("normed_cols")]
    load_rest = [into(name) for name in ("out_w_recv", "ao_all", "small_recv", "gains_all")]
    load_copied = [into("qkv_sum"), into("block_all")]
    given = hasattr(r, "piece")
    load_input = [into("local_all"), into("piece" if given else "patch_weight")]

    def wait(copies):
        for copy in copies:
            copy.wait()

    def out(name, value, at=None):
        src, dst = getattr(r, name + "_v"), getattr(r, name)
        if at is not None:
            src, dst = src.at[at], dst.at[at]
        src[...] = value
        writes.append(load(src, dst))

    cut = features // feature
    for w in range(3):
        load_g[w].wait()
        out("ffn_grad", sum(
            jnp.where(absent(line, j, s), 0.0, r.g_recv_v[w, s].astype(f32)) for s in range(mpn)
        ), w)
    wait(load_patch)
    everyone = r.plane_v[...].reshape(n * mpn * patches, dim)
    for k in range(positions):
        mine = r.bytes_part_v[:, k].reshape(n * mpn * patches, features)
        got = dot(mine, everyone, ((0,), (0,)))
        if cut > 1:
            got = sum(jnp.where(i % cut == e, got[e * feature : (e + 1) * feature], 0.0) for e in range(cut))
        out("patch_grad", got, k)
    wait(load_in)
    got = dot(
        r.proj_all_v[...].reshape(n * mpn * patches, columns),
        r.normed_cols_v[...].reshape(n * mpn * patches, features), ((0,), (0,)),
    )
    if cut > 1:
        got = sum(jnp.where(i % cut == e, got[:, e * feature : (e + 1) * feature], 0.0) for e in range(cut))
    out("in_grad", got)
    wait(load_copied)
    writes += [load(r.qkv_sum_v, r.qkv_grad), load(r.block_all_v, r.block_out)]
    wait(load_rest)
    out("out_grad", sum(r.out_w_recv_v[s].astype(f32) for s in range(mpn)))
    out("ao_grad", sum(r.ao_all_v[s].astype(f32) for s in range(mpn)).T)
    small = sum(r.small_recv_v[s] for s in range(mpn))

    def chosen(values, size):
        whole = values.shape[1]
        at = lax.broadcasted_iota(jnp.int32, (whole, size), 0)
        want = lax.broadcasted_iota(jnp.int32, (whole, size), 1) + i * size % whole
        return dot(values, (at == want).astype(f32), precision=highest)

    conv = chosen(small, CONV_CH // n)
    out("conv_w_grad", conv[:CONV])
    out("conv_b_grad", conv[CONV : CONV + 1])
    out("group_grad", chosen(small[:, :GROUP_WIDTH], GROUP_WIDTH // n)[CONV + 1 : CONV + 2])
    heads = lax.broadcasted_iota(jnp.int32, (GROUP_WIDTH, GROUP_HEADS), 0) // HEAD_DIM
    pick = heads == lax.broadcasted_iota(jnp.int32, (GROUP_WIDTH, GROUP_HEADS), 1)
    out("skip_grad", dot(small[:, :GROUP_WIDTH], pick.astype(f32), precision=highest)[CONV + 2 : CONV + 3])
    out("step_grad", small[CONV + 3 : CONV + 4, :GROUP_HEADS])
    out("decay_grad", small[CONV + 4 : CONV + 5, :GROUP_HEADS])
    gains = chosen(r.gains_all_v[...], feature)
    out("norm_in_grad", gains[0:1])
    out("attn_gain_grad", gains[1:2])
    out("ffn_gain_grad", gains[2:3])
    wait(load_input)
    own = r.plane_v[i].reshape(mpn * patches, dim)
    for k in range(positions):
        if given:
            piece = r.piece_v[:, k * dim : (k + 1) * dim]
        else:
            piece = dot(own, r.patch_weight_v[k], ((1,), (1,)))
        for m in range(mpn):
            r.input_grad_v[m, :, k * dim : (k + 1) * dim] = (
                piece[m * patches : (m + 1) * patches]
                + r.local_all_v[m, k * patches : (k + 1) * patches, :].astype(f32)
            )
    writes.append(load(r.input_grad_v, r.input_grad))
    wait(writes)


def finish(a, line):
    n, mpn, patches, dim = a.plane.shape
    positions = a.patch_weight.shape[0]
    feature = dim // n
    columns = a.in_weight.shape[0]
    names = (
        "plane", "bytes_part", "piece" if hasattr(a, "piece") else "patch_weight", "local_all", "g_recv", "ao_all", "proj_all", "normed_cols", "out_w_recv",
        "small_recv", "gains_all", "qkv_sum", "block_all",
    )
    large = dict(
        patch_grad=((positions, feature, dim), f32),
        input_grad=((mpn, patches, positions * dim), f32),
        ffn_grad=(a.g_recv.shape[1:], f32),
        ao_grad=(a.ao_all.shape[:0:-1], f32),
        in_grad=((columns, feature), f32),
        out_grad=(a.out_w_recv.shape[1:], f32),
    )
    row = lambda size: ((1, size), f32)
    large.update(
        conv_w_grad=((CONV, CONV_CH // n), f32),
        conv_b_grad=row(CONV_CH // n),
        group_grad=row(GROUP_WIDTH // n),
        skip_grad=row(GROUP_HEADS),
        step_grad=row(GROUP_HEADS),
        decay_grad=row(GROUP_HEADS),
        norm_in_grad=row(feature),
        attn_gain_grad=row(feature),
        ffn_gain_grad=row(feature),
    )
    outs = {name: value + (ANY,) for name, value in large.items()}
    outs.update(qkv_grad=(a.qkv_sum.shape, f32, ANY), block_out=(a.block_all.shape, bf16, ANY))
    scratch = {name + "_v": pltpu.VMEM(getattr(a, name).shape, getattr(a, name).dtype) for name in names}
    scratch["g_recv_v"] = pltpu.VMEM((3, mpn) + a.g_recv.shape[2:], bf16)
    scratch.update({name + "_v": pltpu.VMEM(*value) for name, value in large.items()})
    scratch["sems"] = DMA((48,))
    ins = {name: (getattr(a, name), ANY) for name in names}
    return launch("finish", partial(finish_kernel, line), ins, outs, scratch, plain_params(60))


def body(
    byte_input,
    seq_lengths,
    patch_weight,
    norm_in_gain,
    in_weight,
    conv_weight,
    conv_bias,
    step_bias,
    log_decay,
    skip_gain,
    group_gain,
    out_weight,
    attn_gain,
    qkv_weight,
    attn_out_weight,
    ffn_gain,
    ffn_weight,
    out_grad,
):
    n, mpn = lax.axis_size("dp"), lax.axis_size("mp")
    row = lambda v: v.reshape(1, -1)
    a = SimpleNamespace(
        byte_input=byte_input,
        seq_lengths=seq_lengths,
        patch_weight=patch_weight,
        norm_in_gain=row(norm_in_gain),
        in_weight=in_weight[0].T,
        taps=conv_weight[0].T,
        conv_bias=conv_bias,
        step_bias=step_bias,
        log_decay=log_decay,
        skip=skip_gain,
        group_gain=group_gain,
        out_weight=out_weight[0],
        attn_gain=row(attn_gain),
        qkv_weight=qkv_weight,
        attn_out_weight=attn_out_weight,
        ffn_gain=row(ffn_gain),
        ffn_weight=ffn_weight,
        out_grad=out_grad,
    )
    dim, hidden = ffn_gain.shape[0], ffn_weight.shape[2]
    rows = out_grad.shape[1]
    fits = n * rows * dim * 2 <= SPILL_BYTES and 2 * hidden <= dim
    fits = fits and dim % rows == 0 and dim // rows <= n and patch_weight.shape[0] <= 2
    if fits:
        a.__dict__.update(layer(n, mpn, a).__dict__)
    else:
        a.__dict__.update(forward(n, mpn, a).__dict__)
        a.down_part, a.in_part, a.w_grad = ffn(a.ffn_rows, a.grad_rows, a.w_all)
        a.__dict__.update(backward(n, mpn, a).__dict__)
    f = finish(a, fits and mpn == 4)
    return (
        f.block_out,
        f.input_grad,
        f.patch_grad,
        f.norm_in_grad[0],
        f.in_grad.T[None],
        f.conv_w_grad.T[None],
        f.conv_b_grad,
        f.step_grad,
        f.decay_grad,
        f.skip_grad,
        f.group_grad,
        f.out_grad[None],
        f.attn_gain_grad[0],
        f.qkv_grad,
        f.ao_grad,
        f.ffn_gain_grad[0],
        f.ffn_grad,
    )


def solution(mesh):
    in_specs = (
        P(None, "dp", None),
        P(),
        P("mp", None, None),
        P(),
        P("mp", None, None),
        P("mp", None, None),
        P("mp", None),
        P("mp", None),
        P("mp", None),
        P("mp", None),
        P("mp", None),
        P("mp", None, None),
        P(),
        P(None, None, "mp"),
        P("mp", None),
        P(),
        P(None, "mp", "dp"),
        P(None, "dp", None),
    )
    out_specs = (
        P(None, "dp", "mp"),
        P(None, "dp", "mp"),
        P("mp", "dp", None),
        P("dp"),
        P("mp", "dp", None),
        P("mp", "dp", None),
        P("mp", "dp"),
        P("mp", None),
        P("mp", None),
        P("mp", None),
        P("mp", "dp"),
        P("mp", "dp", None),
        P("dp"),
        P(None, "dp", "mp"),
        P("mp", "dp"),
        P("dp"),
        P(None, "mp", "dp"),
    )
    return jax.shard_map(body, mesh=mesh, in_specs=in_specs, out_specs=out_specs, check_vma=False)
```
